128 devices in a mesh: ctx: 8 (over x, y_lo), exp: 16 (over y_hi, z, core).
Axes of the slice: x: 4, y: 4 (y_hi: 2, y_lo: 2; y = y_hi * 2 + y_lo), z: 4, core: 2. Of those that a mesh axis runs over, the one named last changes fastest.
Arguments:
- tokens: bfloat16 [16, 1024, 1280], P('exp', 'ctx'), may hold values from -6 to 6
- lengths: int32 [16], P('exp'), may hold values from 512 to 1024, as said below
- routes: int32 [16, 1024, 7], P('exp', 'ctx'), may hold values from 0 to 31, all different within a row; in each aligned block of 128 rows (0 to 127, 128 to 255, ..., all dimensions but the last counted through in order) at most 42 rows name the same one
- route_gates: float32 [16, 1024, 7], P('exp', 'ctx'), may hold values from 0.25 to 1
- attn_gain: float32 [1280], replicated, may hold values from 0.1 to 1.9
- w_query: bfloat16 [1280, 1280], replicated, may hold values from -0.15625 to 0.15625
- w_key: bfloat16 [1280, 1280], replicated, may hold values from -0.15625 to 0.15625
- w_value: bfloat16 [1280, 1280], replicated, may hold values from -0.15625 to 0.15625
- w_out: bfloat16 [1280, 1280], replicated, may hold values from -2 to 2
- ffn_gain: float32 [1280], replicated, may hold values from 0.1 to 1.9
- shared_gate: bfloat16 [1280, 896], replicated, may hold values from -0.15625 to 0.15625
- shared_up: bfloat16 [1280, 896], replicated, may hold values from -0.15625 to 0.15625
- shared_down: bfloat16 [896, 1280], replicated, may hold values from -0.1875 to 0.1875
- expert_gate: bfloat16 [32, 1280, 896], P('exp'), may hold values from -0.15625 to 0.15625
- expert_up: bfloat16 [32, 1280, 896], P('exp'), may hold values from -0.15625 to 0.15625
- expert_down: bfloat16 [32, 896, 1280], P('exp'), may hold values from -0.1875 to 0.1875
- cotangent: bfloat16 [16, 1024, 1280], P('exp', 'ctx'), may hold values from -6 to 6
Outputs:
- block_out: float32 [16, 1024, 1280], P('exp', 'ctx')
- input_grad: float32 [16, 1024, 1280], P('exp', 'ctx')
- attn_gain_grad: float32 [1280], P(('ctx', 'exp'))
- w_query_grad: float32 [1280, 1280], P(('ctx', 'exp'))
- w_key_grad: float32 [1280, 1280], P(('ctx', 'exp'))
- w_value_grad: float32 [1280, 1280], P(('ctx', 'exp'))
- w_out_grad: float32 [1280, 1280], P(('ctx', 'exp'))
- ffn_gain_grad: float32 [1280], P(('ctx', 'exp'))
- shared_gate_grad: float32 [1280, 896], P(('ctx', 'exp'))
- shared_up_grad: float32 [1280, 896], P(('ctx', 'exp'))
- shared_down_grad: float32 [896, 1280], P(('ctx', 'exp'))
- expert_gate_grad: float32 [32, 1280, 896], P('exp', 'ctx')
- expert_up_grad: float32 [32, 1280, 896], P('exp', 'ctx')
- expert_down_grad: float32 [32, 896, 1280], P('exp', 'ctx')
The draws below stay inside these ranges and needn't reach their ends.
Inputs may be any that keep to these rules, and one draw needn't show every extreme that they name: `lengths`: each sequence has 512 to 1024 live tokens, and some sequence has exactly 1024. `routes`: a row names 7 different experts; within the 128 rows of one device no expert is named more than 42 times, a bound that some block reaches; every expert is named somewhere.
All inputs are finite; a program needn't handle non-finite values.
Results may differ from the reference program's by a relative error of at most 0.025.
Values may be sent and summed in bfloat16 or wider, within the bound.
A program may use at most 320 MiB of HBM per device.

```python
import math
import jax
import jax.numpy as jnp
import numpy as np
from jax import lax

HEADS = 10
HEAD_DIM = 128
D = 1280
FF = 896
TOP = 7
SEQ_LEN = 1024
ROWS = 128
SEQS = 16
EXPERTS = 32
CAP = 42
N_CTX = 8


def draw_lengths(key, part):
    key = jax.random.fold_in(key, 11)
    first_key, second_key = jax.random.split(key)
    drawn = jax.random.randint(first_key, (SEQS,), SEQ_LEN // 2, SEQ_LEN + 1)
    chosen = jax.random.randint(second_key, (), 0, SEQS)
    return jnp.where(jnp.arange(SEQS) == chosen, SEQ_LEN, drawn).astype(jnp.int32)


def block_scale(own_key, dims, cuts, least, high):
    level, own = 1.0, jax.random.fold_in(own_key, 6)
    for dim, shards_of in cuts:
        draws = jnp.exp(jax.random.uniform(jax.random.fold_in(own, dim), (shards_of,), jnp.float32, least / len(cuts), high / len(cuts)))
        level = level * jnp.repeat(draws, dims[dim] // shards_of).reshape([-1 if axis == dim else 1 for axis in range(len(dims))])
    return level


def routed_block(own_key, own, number, rows, amount, top, most, slope):
    ranking = jax.random.permutation(own_key, amount)
    heavy_load, common = shares(amount, rows * top, most, slope, True), shares(amount, rows * top, most, slope, False)
    places = jnp.arange(amount)

    def named(tallies, offset_by):
        used = int((tallies > 0).sum())
        fixed = max(1, used // 4)
        shifted = fixed + (places - fixed + offset_by * (used - fixed)) % max(1, amount - fixed)
        return jnp.zeros((amount,), jnp.int32).at[ranking[jnp.where(places < fixed, places, shifted)]].set(jnp.asarray(tallies, jnp.int32))

    tallies = jnp.where(number % 4 == 0, named(heavy_load, number // 4), named(common, number - number // 4 - 1))
    mixed = jax.random.permutation(jax.random.fold_in(own, 3), amount)
    source_of, taker = mixed[0:amount // 2 * 2:2], mixed[1:amount // 2 * 2:2]
    margin = jnp.minimum(tallies[source_of] - 1, most - tallies[taker]) // 2
    margin = jnp.where((source_of == ranking[0]) | (taker == ranking[0]) | (tallies[taker] == 0), 0, jnp.maximum(margin, 0))
    shifted = jax.random.randint(jax.random.fold_in(own, 4), (amount // 2,), 0, 1 << 20) % (margin + 1)
    tallies = tallies.at[source_of].add(-shifted).at[taker].add(shifted)
    members = jnp.searchsorted(jnp.cumsum(tallies), jnp.arange(rows * top), side="right").astype(jnp.int32)
    table = members.reshape(top, rows).T
    table = table[jax.random.permutation(jax.random.fold_in(own, 1), rows)]
    offset_by = jax.random.randint(jax.random.fold_in(own, 2), (rows, 1), 0, top)
    return jnp.take_along_axis(table, (jnp.arange(top)[None, :] + offset_by) % top, axis=1)


def shares(count, total, most, lean, full):
    weights = [(1 << 20) // math.isqrt(rank ** lean) + 1 for rank in range(1, count + 1)]
    largest = most if full else min(most, max(-(-total // count), total * weights[0] // sum(weights)))
    least = 1 if total - largest >= count - 1 else 0
    given, spare = [largest] + [least] * (count - 1), total - largest - least * (count - 1)
    while spare > 0:
        free = [i for i in range(1, count) if given[i] < largest] or [i for i in range(1, count) if given[i] < most]
        mass, left = sum([weights[i] for i in free]), spare
        for i in free:
            extra = min(most - given[i], max(1, left * weights[i] // mass), spare)
            given[i] = given[i] + extra
            spare = spare - extra
    return np.array(given)


def normal_values(own_key, shape, deviation, most, pieces=(), kind=jnp.bfloat16):
    array = jax.random.normal(own_key, shape, jnp.float32) * deviation
    if len(pieces) > 0:
        array = block_scale(own_key, shape, pieces, -0.22, 0.18) * array
    return jnp.clip(array, min=-most, max=most).astype(kind)


def setup_inputs(seed: int = 0) -> dict:
    seeds = jax.random.split(jax.random.key(seed), 18)
    tokens = normal_values(seeds[0], (SEQS, SEQ_LEN, D), 1.0, 6.0, ((0, 16), (1, 8)))
    lengths = draw_lengths(jax.random.fold_in(seeds[17], 71), 0)
    routes_keys = jax.random.split(jax.random.fold_in(seeds[2], 1), SEQS * SEQ_LEN // ROWS)
    routes_turns = jax.random.permutation(jax.random.fold_in(seeds[2], 3), SEQS * SEQ_LEN // ROWS)
    routes = jax.vmap(lambda own, number: routed_block(jax.random.fold_in(seeds[2], 2), own, number, ROWS, EXPERTS, TOP, CAP, 1))(routes_keys, routes_turns).reshape((SEQS, SEQ_LEN, TOP))
    route_gates = jnp.clip(jnp.exp(math.log(1.0) - 1.3862944 * jax.random.uniform(seeds[3], (SEQS, SEQ_LEN, TOP), jnp.float32) ** block_scale(seeds[3], (SEQS, SEQ_LEN, TOP), ((0, 16), (1, 8)), -0.2, 0.2)), 0.25, 1.0)
    attn_gain = jnp.clip(1.0 + 0.18 * jax.random.normal(seeds[4], (D,), jnp.float32), 0.1, 1.9)
    w_query = normal_values(seeds[5], (D, D), D ** -0.5, 0.15625)
    w_key = normal_values(seeds[6], (D, D), D ** -0.5, 0.15625)
    w_value = normal_values(seeds[7], (D, D), D ** -0.5, 0.15625)
    w_out = normal_values(seeds[8], (D, D), (max(1, D // 128)) ** -0.5, 2.0)
    ffn_gain = jnp.clip(1.0 + 0.18 * jax.random.normal(seeds[9], (D,), jnp.float32), 0.1, 1.9)
    shared_gate = normal_values(seeds[10], (D, FF), D ** -0.5, 0.15625)
    shared_up = normal_values(seeds[11], (D, FF), D ** -0.5, 0.15625)
    shared_down = normal_values(seeds[12], (FF, D), FF ** -0.5, 0.1875)
    expert_gate = normal_values(seeds[13], (EXPERTS, D, FF), D ** -0.5, 0.15625, ((0, 16),))
    expert_up = normal_values(seeds[14], (EXPERTS, D, FF), D ** -0.5, 0.15625, ((0, 16),))
    expert_down = normal_values(seeds[15], (EXPERTS, FF, D), FF ** -0.5, 0.1875, ((0, 16),))
    cotangent = normal_values(seeds[16], (SEQS, SEQ_LEN, D), 1.0, 6.0, ((0, 16), (1, 8)))
    return {"tokens": tokens, "lengths": lengths, "routes": routes, "route_gates": route_gates, "attn_gain": attn_gain, "w_query": w_query, "w_key": w_key, "w_value": w_value, "w_out": w_out, "ffn_gain": ffn_gain, "shared_gate": shared_gate, "shared_up": shared_up, "shared_down": shared_down, "expert_gate": expert_gate, "expert_up": expert_up, "expert_down": expert_down, "cotangent": cotangent}


@jax.custom_vjp
def low(v):
    return lax.optimization_barrier(v.astype(jnp.bfloat16)).astype(jnp.float32)

@jax.custom_vjp
def low_back(v):
    return v

def low_keep(v):
    return (low(v), None)

def low_pass(kept, grad):
    return (grad,)

def back_keep(v):
    return (v, None)

def back_low(kept, grad):
    return (low(grad),)
low.defvjp(low_keep, low_pass)
low_back.defvjp(back_keep, back_low)

def product(left, right):
    return jnp.dot(left, right, precision=lax.Precision.HIGHEST, preferred_element_type=jnp.float32)

def norm_rows(values, gain_vec):
    return values * lax.rsqrt(lax.optimization_barrier(jnp.mean(values * values, axis=-1, keepdims=True)) + 1e-06) * gain_vec

def angles(positions):
    half_dim = HEAD_DIM // 2
    frequency = jnp.exp(jnp.arange(half_dim, dtype=jnp.float32) * (-2.0 * math.log(10000.0) / HEAD_DIM))
    turn_angle = positions.astype(jnp.float32)[:, None] * frequency[None, :]
    return (jnp.cos(turn_angle)[:, None, :], jnp.sin(turn_angle)[:, None, :])

def rotate(values, turn_cos, turn_sin):
    half_dim = values.shape[-1] // 2
    lower_half = values[..., :half_dim]
    upper_half = values[..., half_dim:]
    return jnp.concatenate([lower_half * turn_cos - upper_half * turn_sin, upper_half * turn_cos + lower_half * turn_sin], axis=-1)

def sequence_forward(params, resident, gate_rows, route_rows, seq_length):
    attn_gain, w_query, w_key, w_value, w_out, ffn_gain, shared_gate, shared_up, shared_down, expert_gate, expert_up, expert_down = params
    positions = jnp.arange(SEQ_LEN, dtype=jnp.int32)
    row_live = positions < seq_length
    turn_cos, turn_sin = angles(positions)
    normed_one = low(norm_rows(resident, attn_gain))
    query_heads = low(rotate(low_back(product(normed_one, w_query)).reshape(SEQ_LEN, HEADS, HEAD_DIM), turn_cos, turn_sin))
    key_heads = low(rotate(low_back(product(normed_one, w_key)).reshape(SEQ_LEN, HEADS, HEAD_DIM), turn_cos, turn_sin))
    value_heads = low(low_back(product(normed_one, w_value))).reshape(SEQ_LEN, HEADS, HEAD_DIM)
    raw_scores = low_back(jnp.einsum('qhd,khd->hqk', query_heads, key_heads, precision=lax.Precision.HIGHEST) * HEAD_DIM ** (-0.5))
    allowed = (positions[None, :] <= positions[:, None]) & (positions[None, :] < seq_length)
    scores = jnp.where(allowed[None], raw_scores, -1e+30)
    row_peak = lax.optimization_barrier(jnp.max(scores, axis=-1, keepdims=True))
    weights_raw = jnp.exp(scores - row_peak)
    attn_probs = weights_raw / lax.optimization_barrier(jnp.sum(weights_raw, axis=-1, keepdims=True))
    mixed_rows = jnp.einsum('hqk,khd->qhd', low(attn_probs), value_heads, precision=lax.Precision.HIGHEST).reshape(SEQ_LEN, D)
    hidden = resident + low_back(product(low(low_back(mixed_rows)), w_out))
    normed_two = low(norm_rows(hidden, ffn_gain))
    shared_act = low(jax.nn.silu(low_back(product(normed_two, shared_gate))) * low_back(product(normed_two, shared_up)))
    shared_out = product(shared_act, shared_down)
    pair_expert = route_rows.reshape(-1)
    member = (pair_expert[:, None] == jnp.arange(EXPERTS, dtype=jnp.int32)[None, :]).astype(jnp.int32)
    rank_in = lax.optimization_barrier(jnp.sum((jnp.cumsum(member, axis=0) - 1) * member, axis=1))
    slot_depth = N_CTX * CAP
    pair_slot = pair_expert * slot_depth + rank_in
    pair_owner = jnp.arange(SEQ_LEN * TOP, dtype=jnp.int32) // TOP
    pair_rows = low_back(normed_two[pair_owner])
    slot_table = jnp.zeros((EXPERTS * slot_depth, D), jnp.float32).at[pair_slot].set(pair_rows).reshape(EXPERTS, slot_depth, D)
    gate_pre = low_back(jnp.einsum('esd,edf->esf', slot_table, expert_gate, precision=lax.Precision.HIGHEST))
    up_pre = low_back(jnp.einsum('esd,edf->esf', slot_table, expert_up, precision=lax.Precision.HIGHEST))
    expert_act = low(jax.nn.silu(gate_pre) * up_pre)
    expert_rows = jnp.einsum('esf,efd->esd', expert_act, expert_down, precision=lax.Precision.HIGHEST).reshape(EXPERTS * slot_depth, D)
    pair_out = low(low_back(expert_rows[pair_slot]))
    pair_weight = gate_rows.reshape(-1) * row_live[pair_owner].astype(jnp.float32)
    routed = lax.optimization_barrier(jnp.sum((pair_out * pair_weight[:, None]).reshape(SEQ_LEN, TOP, D), axis=1))
    return hidden + shared_out + routed

def reference(tokens, lengths, routes, route_gates, attn_gain, w_query, w_key, w_value, w_out, ffn_gain, shared_gate, shared_up, shared_down, expert_gate, expert_up, expert_down, cotangent):
    params = tuple((weight.astype(jnp.float32) for weight in (attn_gain, w_query, w_key, w_value, w_out, ffn_gain, shared_gate, shared_up, shared_down, expert_gate, expert_up, expert_down)))
    resident_all = tokens.astype(jnp.float32)
    gate_all = route_gates.astype(jnp.float32)

    def forward(params, resident_all):

        def scan_step(carried, inputs):
            resident, gate_rows, route_rows, seq_length = inputs
            return (carried, jax.checkpoint(sequence_forward)(params, resident, gate_rows, route_rows, seq_length))
        _, outputs = lax.scan(scan_step, jnp.zeros((), jnp.int32), (resident_all, gate_all, routes, lengths))
        return outputs
    block_out, pullback = jax.vjp(forward, params, resident_all)
    param_grads, input_grad = pullback(cotangent.astype(jnp.float32))
    attn_gain_grad, w_query_grad, w_key_grad, w_value_grad, w_out_grad, ffn_gain_grad, shared_gate_grad, shared_up_grad, shared_down_grad, expert_gate_grad, expert_up_grad, expert_down_grad = param_grads
    return (block_out, input_grad, attn_gain_grad, w_query_grad, w_key_grad, w_value_grad, w_out_grad, ffn_gain_grad, shared_gate_grad, shared_up_grad, shared_down_grad, expert_gate_grad, expert_up_grad, expert_down_grad)
```

```python
import functools
import math

import jax
import jax.numpy as jnp
from jax import lax
from jax.experimental import pallas as pl
from jax.experimental.pallas import tpu as pltpu
from jax.sharding import PartitionSpec as P

MESH = pl.DeviceIdType.MESH
VMEM_LIMIT = 60 * 2**20
F32, BF16 = jnp.float32, jnp.bfloat16


def place():
    ctx, exp = lax.axis_index("ctx"), lax.axis_index("exp")
    return ctx // 2, (exp // 8) * 2 + ctx % 2, (exp // 2) % 4, exp % 2


def device(x, y, z, core):
    return (x * 2 + y % 2, (y // 2) * 8 + z * 2 + core)


def greet(devices):
    barrier = pltpu.get_barrier_semaphore()
    for target in devices:
        pl.semaphore_signal(barrier, inc=1, device_id=target, device_id_type=MESH)
    pl.semaphore_wait(barrier, len(devices))


class Copies:
    def __init__(self, send, recv, own):
        self.send, self.recv, self.own = send, recv, own
        self.remotes, self.locals = 0, 0
        self.started = []

    def remote(self, src, dst, target):
        index = self.remotes
        self.remotes += 1
        copy = pltpu.make_async_remote_copy(
            src_ref=src,
            dst_ref=dst,
            send_sem=self.send.at[index],
            recv_sem=self.recv.at[index],
            device_id=target,
            device_id_type=MESH,
        )
        copy.start()
        self.started.append(copy)
        return copy

    def local(self, src, dst):
        index = self.locals
        self.locals += 1
        copy = pltpu.make_async_copy(src, dst, self.own.at[index])
        copy.start()
        return copy

    def drain(self):
        for copy in self.started:
            copy.wait_send()


def each(shape, body):
    @pl.loop(0, math.prod(shape))
    def _(step):
        index = []
        for size in reversed(shape):
            index.append(step % size)
            step = step // size
        body(tuple(reversed(index)))


def add_into(out, shape, *terms, rows=None):
    def body(index):
        total = terms[0][index].astype(F32)
        for term in terms[1:]:
            total = total + term[index].astype(F32)
        out[index] = total.astype(out.dtype)

    if rows is None:
        each(shape, body)
    else:
        step, count = rows
        each(shape + (count,), lambda i: body(i[:-1] + (pl.ds(pl.multiple_of(i[-1] * step, step), step),)))


class RingSum:
    def __init__(self, copies, me, right, left, part, land, work, add, resident=None):
        self.copies, self.right, self.left, self.land, self.work, self.add = copies, right, left, land, work, add
        after, before, across = (me + 1) % 4, (me + 3) % 4, (me + 2) % 4
        self.one = copies.remote(part(across, 0), land.at[0], right)
        self.two = copies.remote(part(across, 1), land.at[1], left)
        self.three = copies.remote(part(after, 1), land.at[2], right)
        self.four = copies.remote(part(before, 0), land.at[4], left)
        self.resident = resident
        if resident is None:
            self.loads = [
                copies.local(part(after, 0), work.at[0]),
                copies.local(part(before, 1), work.at[1]),
                copies.local(part(me, 0), work.at[2]),
                copies.local(part(me, 1), work.at[3]),
            ]
            self.own = [work.at[i] for i in range(4)]
        else:
            self.loads = []
            self.own = [part(after, 0), part(before, 1), part(me, 0), part(me, 1)]

    def forward(self):
        for load in self.loads:
            load.wait()
        self.one.wait_recv()
        self.add(self.land.at[0], self.land.at[0], self.own[0])
        self.five = self.copies.remote(self.land.at[0], self.land.at[3], self.right)
        self.two.wait_recv()
        self.add(self.land.at[1], self.land.at[1], self.own[1])
        self.six = self.copies.remote(self.land.at[1], self.land.at[5], self.left)

    def finish(self, outs):
        for copy in (self.three, self.four, self.five, self.six):
            copy.wait_recv()
        self.add(outs[0], self.own[2], self.land.at[3], self.land.at[4])
        self.add(outs[1], self.own[3], self.land.at[2], self.land.at[5])


GRAD_REMOTES = 2 * 6 + 6 + 1 + 6 + 1 + 2 * 3 + 2 * 3 + 7
GRAD_LOCALS = 2 * 4 + 4 + 1


def grads_kernel(
    dense, gate, up, down, dense_out, gate_out, up_out, down_out,
    z_land, z_work, y_land, y_sum, x_land, total, stage, final_land,
    g_land, g_work, g_other, d_land, d_other, d_work, send, recv, own,
):
    x, y, z, core = place()
    y_half, y_low = y // 2, y % 2
    spot = z * 2 + core
    x_peers = [device((x + d) % 4, y, z, core) for d in (1, 2, 3)]
    y_peers = [device(x, (y + d) % 4, z, core) for d in (1, 2, 3)]
    spot_peers = [device(x, y, ((spot + d) % 8) // 2, (spot + d) % 2) for d in range(1, 8)]
    z_right, z_left = device(x, y, (z + 1) % 4, core), device(x, y, (z + 3) % 4, core)
    pair = device(x, y_half * 2 + 1 - y_low, z, core)
    greet(x_peers + y_peers + spot_peers)
    copies = Copies(send, recv, own)

    gate_rows = (16, 10)
    down_rows = (16, 7)

    def gate_add(out, *terms):
        add_into(out, (2, 2), *terms, rows=gate_rows)

    def dense_add(out, *terms):
        add_into(out, (2, 4, 4), *terms)

    def down_add(out, *terms):
        add_into(out, (), *terms, rows=down_rows)

    def gate_part(chunk, half):
        return (gate, up)[half].at[:, chunk]

    rings = [
        RingSum(copies, z, z_right, z_left, lambda c, h, t=t: dense.at[c, t, h], z_land.at[t], z_work.at[t], dense_add)
        for t in range(2)
    ]
    swap = copies.remote(down.at[:, :, 1 - y_low], d_other, pair)
    own_down = copies.local(down.at[:, :, y_low], d_work)
    gates = RingSum(copies, x, x_peers[0], x_peers[2], gate_part, g_land, g_work, gate_add)

    rings[0].forward()
    gates.forward()
    rings[1].forward()
    own_down.wait()
    swap.wait_recv()
    add_into(d_work, (2, 4), d_work, d_other, rows=down_rows)
    downs = RingSum(copies, x, x_peers[0], x_peers[2], lambda c, h: d_work.at[h, c], d_land, None, down_add, resident=True)

    def order(value):
        return (value % 2) * 2 + value // 2

    def start_y(t):
        rings[t].finish([z_work.at[t, 2], z_work.at[t, 3]])
        return [
            copies.remote(z_work.at[t, 2:4, :, :, order((y + d) % 4)], y_land.at[t, d - 1], y_peers[d - 1])
            for d in (1, 2, 3)
        ]

    def start_x(t, arrivals):
        for copy in arrivals:
            copy.wait_recv()
        mine = z_work.at[t, 2:4, :, :, order(y)]
        add_into(y_sum.at[t], (2, 2, 4), mine, y_land.at[t, 0], y_land.at[t, 1], y_land.at[t, 2])
        return [
            copies.remote(y_sum.at[t, :, :, (x + d) % 4], x_land.at[t, d - 1], x_peers[d - 1])
            for d in (1, 2, 3)
        ]

    y_first = start_y(0)
    downs.forward()
    gates.finish([g_work.at[2], g_work.at[3]])
    swap_gate = copies.remote(g_work.at[2:4, :, 1 - y_low], g_other, pair)
    x_first = start_x(0, y_first)
    y_second = start_y(1)
    downs.finish([down_out.at[0], down_out.at[1]])
    x_second = start_x(1, y_second)
    swap_gate.wait_recv()
    for index, out in enumerate((gate_out, up_out)):
        add_into(out, (2,), g_work.at[index + 2, :, y_low], g_other.at[index], rows=gate_rows)
    for t, arrivals in enumerate((x_first, x_second)):
        for copy in arrivals:
            copy.wait_recv()
        for half in range(2):
            for panel in range(2):
                value = y_sum[t, half, panel, x].astype(F32)
                for d in range(3):
                    value = value + x_land[t, d, half, panel].astype(F32)
                total[t * 4 + half * 2 + panel, 0:80] = value
                total[t * 4 + half * 2 + panel, 80:96] = jnp.zeros((16, 128), F32)
    for j in range(8):
        for panel in range(8):
            stage[j, panel] = total[panel, 10 * j : 10 * j + 16]
    finals = [
        copies.remote(stage.at[(spot + d) % 8], final_land.at[d], spot_peers[d - 1]) for d in range(1, 8)
    ]
    dense_out[spot] = stage[spot]
    for d, copy in enumerate(finals):
        copy.wait_recv()
        dense_out[(spot + 7 - d) % 8] = final_land[d + 1]
    copies.drain()


def sum_grads(dense, gate, up, down):
    scratch = [
        pltpu.VMEM((2, 6, 2, 4, 4, 80, 128), BF16),
        pltpu.VMEM((2, 4, 2, 4, 4, 80, 128), BF16),
        pltpu.VMEM((2, 3, 2, 2, 4, 80, 128), BF16),
        pltpu.VMEM((2, 2, 2, 4, 80, 128), BF16),
        pltpu.VMEM((2, 3, 2, 2, 80, 128), BF16),
        pltpu.VMEM((8, 96, 128), F32),
        pltpu.VMEM((8, 8, 16, 128), F32),
        pltpu.VMEM((8, 8, 16, 128), F32),
        pltpu.VMEM((6, 2, 2, 160, 896), BF16),
        pltpu.VMEM((4, 2, 2, 160, 896), BF16),
        pltpu.VMEM((2, 2, 160, 896), BF16),
        pltpu.VMEM((6, 112, 1280), BF16),
        pltpu.VMEM((2, 4, 112, 1280), BF16),
        pltpu.VMEM((2, 4, 112, 1280), BF16),
        pltpu.SemaphoreType.DMA((GRAD_REMOTES,)),
        pltpu.SemaphoreType.DMA((GRAD_REMOTES,)),
        pltpu.SemaphoreType.DMA((GRAD_LOCALS,)),
    ]
    vmem = pl.BlockSpec(memory_space=pltpu.VMEM)
    anywhere = pl.BlockSpec(memory_space=pl.ANY)
    return pl.pallas_call(
        grads_kernel,
        name="sum_grads",
        out_shape=(
            jax.ShapeDtypeStruct((8, 8, 16, 128), F32),
            jax.ShapeDtypeStruct((2, 160, 896), F32),
            jax.ShapeDtypeStruct((2, 160, 896), F32),
            jax.ShapeDtypeStruct((2, 112, 1280), F32),
        ),
        in_specs=[anywhere] * 4,
        out_specs=(vmem,) * 4,
        scratch_shapes=scratch,
        compiler_params=pltpu.CompilerParams(
            collective_id=0, has_side_effects=True, vmem_limit_bytes=VMEM_LIMIT
        ),
        cost_estimate=pl.CostEstimate(flops=10**8, bytes_accessed=4 * 10**8, transcendentals=0),
    )(
        dense.reshape(4, 2, 2, 2, 4, 4, 80, 128),
        gate.reshape(2, 4, 2, 160, 896),
        up.reshape(2, 4, 2, 160, 896),
        down.reshape(2, 4, 2, 112, 1280),
    )


def dense_kernel(left, right, gains, out):
    panel = pl.program_id(0)
    out[0] = lax.dot_general(
        left[0], right[...], (((0,), (0,)), ((), ())), preferred_element_type=F32
    ).astype(BF16)

    @pl.when(panel == 27)
    def _():
        out[0] = (out[0].astype(F32) + gains[...]).astype(BF16)


def dense_terms(left, right, gains):
    def group(p):
        return (p >= 15).astype(jnp.int32) + (p >= 20).astype(jnp.int32) + (p >= 27).astype(jnp.int32)

    return pl.pallas_call(
        dense_kernel,
        name="dense_terms",
        grid=(32,),
        out_shape=jax.ShapeDtypeStruct((32, 1280, 128), BF16),
        in_specs=[
            pl.BlockSpec((1, 256, 1280), lambda p: (group(p), 0, 0)),
            pl.BlockSpec((256, 128), lambda p: (0, p)),
            pl.BlockSpec((1280, 128), lambda p: (0, 0)),
        ],
        out_specs=pl.BlockSpec((1, 1280, 128), lambda p: (p, 0, 0)),
        compiler_params=pltpu.CompilerParams(vmem_limit_bytes=VMEM_LIMIT),
        cost_estimate=pl.CostEstimate(flops=2 * 256 * 1280 * 4096, bytes_accessed=15 * 10**6, transcendentals=0),
    )(left, right, gains)


def reduce_dense(normed_one, mixed, normed_two, shared_act, d_qkv, d_attn, d_gate, d_up, cot, attn_gain_term, ffn_gain_term):
    core = lax.axis_index("exp") % 2
    swap = [(e, e ^ 1) for e in range(lax.axis_size("exp"))]
    rows = normed_one.shape[0]
    padded = jnp.pad(shared_act.reshape(rows, 128, 7), ((0, 0), (0, 0), (0, 3))).reshape(rows, 1280)
    left = jnp.stack([normed_one, mixed, normed_two, padded])
    halves = [
        jnp.concatenate([d_qkv[:, :1920], d_attn[:, :640], d_gate, cot[:, :640]], axis=1),
        jnp.concatenate([d_qkv[:, 1920:], d_attn[:, 640:], d_up, cot[:, 640:]], axis=1),
    ]
    mine = jnp.where(core == 0, halves[0], halves[1])
    theirs = jnp.where(core == 0, halves[1], halves[0])
    gain_mine = jnp.where(core == 0, attn_gain_term, ffn_gain_term)
    gain_theirs = jnp.where(core == 0, ffn_gain_term, attn_gain_term)
    left = jnp.concatenate([left, lax.ppermute(left, "exp", swap)], axis=1)
    right = jnp.concatenate([mine, lax.ppermute(theirs, "exp", swap)], axis=0)
    gain = (gain_mine + lax.ppermute(gain_theirs, "exp", swap)).reshape(128, 1, 10)
    gains = jnp.pad(gain, ((0, 0), (7, 2), (0, 118))).reshape(1280, 128)
    return dense_terms(left, right, gains)


def unpack_dense(packed):
    panels = packed.reshape(4, 2, 8, 16, 128)[:, :, :, :10].transpose(1, 0, 2, 3, 4).reshape(2, 32, 10, 128)

    def joined(first, last):
        return panels[:, first:last].transpose(2, 0, 1, 3).reshape(10, -1)

    qkv, out = joined(0, 15), joined(15, 20)
    gate_up, down = joined(20, 27), joined(27, 32)[:7]
    return (
        panels[0, 27, 7, :10], qkv[:, :1280], qkv[:, 1280:2560], qkv[:, 2560:], out,
        panels[1, 27, 7, :10], gate_up[:, :896], gate_up[:, 896:], down,
    )

HEAD_DIM = 128


def norm_rows(values, gain_vec):
    return values * lax.rsqrt(jnp.mean(values * values, axis=-1, keepdims=True) + 1e-06) * gain_vec


def norm_back(values, gain_vec, upstream):
    factor = lax.rsqrt(jnp.mean(values * values, axis=-1, keepdims=True) + 1e-06)
    scaled = upstream * gain_vec
    inner_mean = jnp.mean(scaled * values, axis=-1, keepdims=True)
    gain_term = jnp.sum(upstream * values * factor, axis=0)
    return (factor * scaled - values * factor * factor * factor * inner_mean, gain_term)


def angles(positions, head_dim):
    half_dim = head_dim // 2
    frequency = jnp.exp(
        jnp.arange(half_dim, dtype=jnp.float32) * (-2.0 * math.log(10000.0) / head_dim)
    )
    turn_angle = positions.astype(jnp.float32)[:, None] * frequency[None, :]
    return (jnp.cos(turn_angle)[:, None, :], jnp.sin(turn_angle)[:, None, :])


def rotate(values, turn_cos, turn_sin):
    half_dim = values.shape[-1] // 2
    lower_half = values[..., :half_dim]
    upper_half = values[..., half_dim:]
    return jnp.concatenate(
        [
            lower_half * turn_cos - upper_half * turn_sin,
            upper_half * turn_cos + lower_half * turn_sin,
        ],
        axis=-1,
    )


def silu_slope(values):
    squash = jax.nn.sigmoid(values)
    return squash * (1.0 + values * (1.0 - squash))


def expert_forward(slot_items, expert_gate, expert_up):
    gate_pre = jnp.einsum(
        "sxcd,xdf->sxcf", slot_items, expert_gate, preferred_element_type=jnp.float32
    )
    up_pre = jnp.einsum("sxcd,xdf->sxcf", slot_items, expert_up, preferred_element_type=jnp.float32)
    activated = (jax.nn.silu(gate_pre) * up_pre).astype(jnp.bfloat16)
    return (gate_pre, up_pre, activated)


def local(
    tokens,
    lengths,
    routes,
    route_gates,
    attn_gain,
    w_query,
    w_key,
    w_value,
    w_out,
    ffn_gain,
    shared_gate,
    shared_up,
    shared_down,
    expert_gate,
    expert_up,
    expert_down,
    cotangent,
):
    resident = tokens[0].astype(jnp.float32)
    row_count, model_width = resident.shape
    head_dim = HEAD_DIM
    head_count = model_width // head_dim
    score_scale = head_dim ** (-0.5)
    ctx_count = lax.axis_size("ctx")
    exp_count = lax.axis_size("exp")
    seq_total = row_count * ctx_count
    positions = lax.axis_index("ctx") * row_count + jnp.arange(row_count, dtype=jnp.int32)
    seq_length = lengths[0]
    row_live = positions < seq_length
    turn_cos, turn_sin = angles(positions, head_dim)
    normed_one = norm_rows(resident, attn_gain).astype(jnp.bfloat16)
    query_pre = jnp.dot(normed_one, w_query, preferred_element_type=jnp.float32)
    key_pre = jnp.dot(normed_one, w_key, preferred_element_type=jnp.float32)
    query_heads = rotate(
        query_pre.reshape(row_count, head_count, head_dim), turn_cos, turn_sin
    ).astype(jnp.bfloat16)
    key_rows = (
        rotate(key_pre.reshape(row_count, head_count, head_dim), turn_cos, turn_sin)
        .astype(jnp.bfloat16)
        .reshape(row_count, model_width)
    )
    value_rows = jnp.dot(normed_one, w_value, preferred_element_type=jnp.float32).astype(
        jnp.bfloat16
    )
    whole_key, whole_value = (
        lax.all_gather(key_rows, "ctx", axis=0, tiled=True),
        lax.all_gather(value_rows, "ctx", axis=0, tiled=True),
    )
    key_heads = whole_key.reshape(seq_total, head_count, head_dim)
    value_heads = whole_value.reshape(seq_total, head_count, head_dim)
    key_positions = jnp.arange(seq_total, dtype=jnp.int32)
    allowed = (key_positions[None, :] <= positions[:, None]) & (key_positions[None, :] < seq_length)

    def scores_of(some_keys):
        raw_scores = (
            jnp.einsum("qhd,khd->hqk", query_heads, some_keys, preferred_element_type=jnp.float32)
            * score_scale
        )
        return jnp.where(allowed[None], raw_scores, -1e30)

    scores = scores_of(key_heads)
    row_peak = jnp.max(scores, axis=-1, keepdims=True)
    weights_raw = jnp.exp(scores - row_peak)
    row_total = jnp.sum(weights_raw, axis=-1, keepdims=True)
    attn_probs = weights_raw / row_total
    log_total = row_peak + jnp.log(row_total)
    mixed_rows = (
        jnp.einsum(
            "hqk,khd->qhd",
            attn_probs.astype(jnp.bfloat16),
            value_heads,
            preferred_element_type=jnp.float32,
        )
        .reshape(row_count, model_width)
        .astype(jnp.bfloat16)
    )
    hidden = resident + jnp.dot(mixed_rows, w_out, preferred_element_type=jnp.float32)
    normed_two = norm_rows(hidden, ffn_gain).astype(jnp.bfloat16)
    shared_gate_pre = jnp.dot(normed_two, shared_gate, preferred_element_type=jnp.float32)
    shared_up_pre = jnp.dot(normed_two, shared_up, preferred_element_type=jnp.float32)
    shared_act = (jax.nn.silu(shared_gate_pre) * shared_up_pre).astype(jnp.bfloat16)
    shared_out = jnp.dot(shared_act, shared_down, preferred_element_type=jnp.float32)
    top_count = routes.shape[2]
    exp_local = expert_gate.shape[0]
    expert_total = exp_local * exp_count
    slot_cap = 3 * row_count * top_count // (2 * expert_total)
    slot_count = expert_total * slot_cap
    pair_expert = routes[0].reshape(-1)
    pair_owner = jnp.arange(row_count * top_count, dtype=jnp.int32) // top_count
    pair_live = row_live[pair_owner]
    member = (
        (pair_expert[:, None] == jnp.arange(expert_total, dtype=jnp.int32)[None, :])
        & pair_live[:, None]
    ).astype(jnp.int32)
    rank_in = jnp.sum((jnp.cumsum(member, axis=0) - 1) * member, axis=1)
    pair_slot = jnp.where(pair_live, pair_expert * slot_cap + rank_in, slot_count)
    safe_slot = jnp.minimum(pair_slot, slot_count - 1)
    live_float = pair_live.astype(jnp.float32)
    pair_weight = route_gates[0].reshape(-1) * live_float

    def to_slots(pair_rows):
        placed = (
            jnp.zeros((slot_count, model_width), jnp.bfloat16)
            .at[pair_slot]
            .set(pair_rows, mode="drop")
        )
        return placed.reshape(exp_count, exp_local, slot_cap, model_width)

    slot_items = lax.all_to_all(
        to_slots(normed_two[pair_owner]), "exp", split_axis=0, concat_axis=0, tiled=True
    )
    gate_pre, up_pre, activated = expert_forward(slot_items, expert_gate, expert_up)
    produced = jnp.einsum(
        "sxcf,xfd->sxcd", activated, expert_down, preferred_element_type=jnp.float32
    ).astype(jnp.bfloat16)
    received, produced = (slot_items, produced)
    returned = lax.all_to_all(produced, "exp", split_axis=0, concat_axis=0, tiled=True).reshape(
        slot_count, model_width
    )
    pair_out = returned[safe_slot].astype(jnp.float32) * pair_weight[:, None]
    routed = jnp.sum(pair_out.reshape(row_count, top_count, model_width), axis=1)
    block_out = hidden + shared_out + routed
    grad_out = cotangent[0]
    grad_float = grad_out.astype(jnp.float32)
    d_shared_act = jnp.dot(grad_out, shared_down.T, preferred_element_type=jnp.float32)
    d_shared_gate = (d_shared_act * shared_up_pre * silu_slope(shared_gate_pre)).astype(
        jnp.bfloat16
    )
    d_shared_up = (d_shared_act * jax.nn.silu(shared_gate_pre)).astype(jnp.bfloat16)
    d_normed_two = jnp.dot(
        d_shared_gate, shared_gate.T, preferred_element_type=jnp.float32
    ) + jnp.dot(d_shared_up, shared_up.T, preferred_element_type=jnp.float32)
    d_pair = (grad_float[pair_owner] * pair_weight[:, None]).astype(jnp.bfloat16)
    d_incoming = lax.all_to_all(to_slots(d_pair), "exp", split_axis=0, concat_axis=0, tiled=True)
    gate_pre, up_pre, activated = expert_forward(received, expert_gate, expert_up)
    down_term = jnp.einsum(
        "sxcf,sxcd->xfd", activated, d_incoming, preferred_element_type=jnp.float32
    )
    d_activated = jnp.einsum(
        "sxcd,xfd->sxcf", d_incoming, expert_down, preferred_element_type=jnp.float32
    )
    d_gate_pre = (d_activated * up_pre * silu_slope(gate_pre)).astype(jnp.bfloat16)
    d_up_pre = (d_activated * jax.nn.silu(gate_pre)).astype(jnp.bfloat16)
    gate_term = jnp.einsum(
        "sxcd,sxcf->xdf", received, d_gate_pre, preferred_element_type=jnp.float32
    )
    up_term = jnp.einsum("sxcd,sxcf->xdf", received, d_up_pre, preferred_element_type=jnp.float32)
    d_received = (
        jnp.einsum("sxcf,xdf->sxcd", d_gate_pre, expert_gate, preferred_element_type=jnp.float32)
        + jnp.einsum("sxcf,xdf->sxcd", d_up_pre, expert_up, preferred_element_type=jnp.float32)
    ).astype(jnp.bfloat16)
    d_returned = lax.all_to_all(d_received, "exp", split_axis=0, concat_axis=0, tiled=True).reshape(
        slot_count, model_width
    )
    d_pair_rows = d_returned[safe_slot].astype(jnp.float32) * live_float[:, None]
    d_normed_two = d_normed_two + jnp.sum(
        d_pair_rows.reshape(row_count, top_count, model_width), axis=1
    )
    d_hidden, ffn_gain_term = norm_back(hidden, ffn_gain, d_normed_two)
    d_hidden = d_hidden + grad_float
    d_attn = d_hidden.astype(jnp.bfloat16)
    d_mixed = (
        jnp.dot(d_attn, w_out.T, preferred_element_type=jnp.float32)
        .astype(jnp.bfloat16)
        .reshape(row_count, head_count, head_dim)
    )
    again_key, again_value = (
        lax.all_gather(key_rows, "ctx", axis=0, tiled=True),
        lax.all_gather(value_rows, "ctx", axis=0, tiled=True),
    )
    back_key = again_key.reshape(seq_total, head_count, head_dim)
    back_value = again_value.reshape(seq_total, head_count, head_dim)
    back_probs = jnp.exp(scores_of(back_key) - log_total)
    d_probs = jnp.einsum("qhd,khd->hqk", d_mixed, back_value, preferred_element_type=jnp.float32)
    row_delta = jnp.sum(back_probs * d_probs, axis=-1, keepdims=True)
    d_scores = (back_probs * (d_probs - row_delta)).astype(jnp.bfloat16)
    d_query = (
        jnp.einsum("hqk,khd->qhd", d_scores, back_key, preferred_element_type=jnp.float32)
        * score_scale
    )
    key_grad_term = (
        jnp.einsum(
            "hqk,qhd->khd", d_scores, query_heads, preferred_element_type=jnp.float32
        ).reshape(seq_total, model_width)
        * score_scale
    )
    value_grad_term = jnp.einsum(
        "hqk,qhd->khd", back_probs.astype(jnp.bfloat16), d_mixed, preferred_element_type=jnp.float32
    ).reshape(seq_total, model_width)
    d_key, d_value = (
        lax.psum_scatter(
            key_grad_term.astype(jnp.bfloat16), "ctx", scatter_dimension=0, tiled=True
        ).astype(jnp.float32),
        lax.psum_scatter(
            value_grad_term.astype(jnp.bfloat16), "ctx", scatter_dimension=0, tiled=True
        ).astype(jnp.float32),
    )
    d_query_pre = (
        rotate(d_query, turn_cos, -turn_sin).reshape(row_count, model_width).astype(jnp.bfloat16)
    )
    d_key_pre = (
        rotate(d_key.reshape(row_count, head_count, head_dim), turn_cos, -turn_sin)
        .reshape(row_count, model_width)
        .astype(jnp.bfloat16)
    )
    d_value_low = d_value.astype(jnp.bfloat16)
    d_normed_one = (
        jnp.dot(d_query_pre, w_query.T, preferred_element_type=jnp.float32)
        + jnp.dot(d_key_pre, w_key.T, preferred_element_type=jnp.float32)
        + jnp.dot(d_value_low, w_value.T, preferred_element_type=jnp.float32)
    )
    d_resident, attn_gain_term = norm_back(resident, attn_gain, d_normed_one)
    input_grad = d_hidden + d_resident
    dense = reduce_dense(
        normed_one, mixed_rows, normed_two, shared_act,
        jnp.concatenate([d_query_pre, d_key_pre, d_value_low], axis=1),
        d_attn, d_shared_gate, d_shared_up, grad_out, attn_gain_term, ffn_gain_term,
    )
    packed, expert_gate_grad, expert_up_grad, expert_down_grad = sum_grads(
        dense, gate_term.astype(BF16), up_term.astype(BF16), down_term.astype(BF16)
    )
    (
        attn_gain_grad,
        w_query_grad,
        w_key_grad,
        w_value_grad,
        w_out_grad,
        ffn_gain_grad,
        shared_gate_grad,
        shared_up_grad,
        shared_down_grad,
    ) = unpack_dense(packed)
    return (
        block_out[None],
        input_grad[None],
        attn_gain_grad,
        w_query_grad,
        w_key_grad,
        w_value_grad,
        w_out_grad,
        ffn_gain_grad,
        shared_gate_grad,
        shared_up_grad,
        shared_down_grad,
        expert_gate_grad,
        expert_up_grad,
        expert_down_grad,
    )


def solution(mesh):
    in_specs = (
        P("exp", "ctx", None),
        P("exp"),
        P("exp", "ctx", None),
        P("exp", "ctx", None),
        P(),
        P(),
        P(),
        P(),
        P(),
        P(),
        P(),
        P(),
        P(),
        P("exp", None, None),
        P("exp", None, None),
        P("exp", None, None),
        P("exp", "ctx", None),
    )
    out_specs = (
        P("exp", "ctx", None),
        P("exp", "ctx", None),
        P(("ctx", "exp")),
        P(("ctx", "exp"), None),
        P(("ctx", "exp"), None),
        P(("ctx", "exp"), None),
        P(("ctx", "exp"), None),
        P(("ctx", "exp")),
        P(("ctx", "exp"), None),
        P(("ctx", "exp"), None),
        P(("ctx", "exp"), None),
        P("exp", "ctx", None),
        P("exp", "ctx", None),
        P("exp", "ctx", None),
    )
    return jax.shard_map(local, mesh=mesh, in_specs=in_specs, out_specs=out_specs, check_vma=False)
```

```python
import functools
import math

import jax
import jax.numpy as jnp
from jax import lax
from jax.experimental import pallas as pl
from jax.experimental.pallas import tpu as pltpu
from jax.sharding import PartitionSpec as P

MESH = pl.DeviceIdType.MESH
HEAD_DIM = 128
VMEM_LIMIT = 60 * 2**20
F32, BF16 = jnp.float32, jnp.bfloat16


def place():
    ctx, exp = lax.axis_index("ctx"), lax.axis_index("exp")
    return ctx // 2, (exp // 8) * 2 + ctx % 2, (exp // 2) % 4, exp % 2


def device(x, y, z, core):
    return (x * 2 + y % 2, (y // 2) * 8 + z * 2 + core)


def greet(devices):
    barrier = pltpu.get_barrier_semaphore()
    for target in devices:
        pl.semaphore_signal(barrier, inc=1, device_id=target, device_id_type=MESH)
    pl.semaphore_wait(barrier, len(devices))


class Copies:
    def __init__(self, send, recv, own):
        self.send, self.recv, self.own = send, recv, own
        self.remotes, self.locals = 0, 0
        self.started = []

    def remote(self, src, dst, target):
        index = self.remotes
        self.remotes += 1
        copy = pltpu.make_async_remote_copy(
            src_ref=src,
            dst_ref=dst,
            send_sem=self.send.at[index],
            recv_sem=self.recv.at[index],
            device_id=target,
            device_id_type=MESH,
        )
        copy.start()
        self.started.append(copy)
        return copy

    def local(self, src, dst):
        index = self.locals
        self.locals += 1
        copy = pltpu.make_async_copy(src, dst, self.own.at[index])
        copy.start()
        return copy

    def drain(self):
        for copy in self.started:
            copy.wait_send()


def each(shape, body):
    @pl.loop(0, math.prod(shape))
    def _(step):
        index = []
        for size in reversed(shape):
            index.append(step % size)
            step = step // size
        body(tuple(reversed(index)))


def add_into(out, shape, *terms, rows=None):
    def body(index):
        total = terms[0][index].astype(F32)
        for term in terms[1:]:
            total = total + term[index].astype(F32)
        out[index] = total.astype(out.dtype)

    if rows is None:
        each(shape, body)
    else:
        step, count = rows
        each(shape + (count,), lambda i: body(i[:-1] + (pl.ds(pl.multiple_of(i[-1] * step, step), step),)))


class RingSum:
    def __init__(self, copies, me, right, left, part, land, work, add, resident=None):
        self.copies, self.right, self.left, self.land, self.work, self.add = copies, right, left, land, work, add
        after, before, across = (me + 1) % 4, (me + 3) % 4, (me + 2) % 4
        self.one = copies.remote(part(across, 0), land.at[0], right)
        self.two = copies.remote(part(across, 1), land.at[1], left)
        self.three = copies.remote(part(after, 1), land.at[2], right)
        self.four = copies.remote(part(before, 0), land.at[4], left)
        self.resident = resident
        if resident is None:
            self.loads = [
                copies.local(part(after, 0), work.at[0]),
                copies.local(part(before, 1), work.at[1]),
                copies.local(part(me, 0), work.at[2]),
                copies.local(part(me, 1), work.at[3]),
            ]
            self.own = [work.at[i] for i in range(4)]
        else:
            self.loads = []
            self.own = [part(after, 0), part(before, 1), part(me, 0), part(me, 1)]

    def forward(self):
        for load in self.loads:
            load.wait()
        self.one.wait_recv()
        self.add(self.land.at[0], self.land.at[0], self.own[0])
        self.five = self.copies.remote(self.land.at[0], self.land.at[3], self.right)
        self.two.wait_recv()
        self.add(self.land.at[1], self.land.at[1], self.own[1])
        self.six = self.copies.remote(self.land.at[1], self.land.at[5], self.left)

    def finish(self, outs):
        for copy in (self.three, self.four, self.five, self.six):
            copy.wait_recv()
        self.add(outs[0], self.own[2], self.land.at[3], self.land.at[4])
        self.add(outs[1], self.own[3], self.land.at[2], self.land.at[5])


GRAD_REMOTES = 2 * 6 + 6 + 1 + 6 + 1 + 2 * 3 + 2 * 3 + 7
GRAD_LOCALS = 2 * 4 + 4 + 1


def grads_kernel(
    dense, gate, up, down, dense_out, gate_out, up_out, down_out,
    z_land, z_work, y_land, y_sum, x_land, total, stage, final_land,
    g_land, g_work, g_other, d_land, d_other, d_work, send, recv, own,
):
    x, y, z, core = place()
    y_half, y_low = y // 2, y % 2
    spot = z * 2 + core
    x_peers = [device((x + d) % 4, y, z, core) for d in (1, 2, 3)]
    y_peers = [device(x, (y + d) % 4, z, core) for d in (1, 2, 3)]
    spot_peers = [device(x, y, ((spot + d) % 8) // 2, (spot + d) % 2) for d in range(1, 8)]
    z_right, z_left = device(x, y, (z + 1) % 4, core), device(x, y, (z + 3) % 4, core)
    pair = device(x, y_half * 2 + 1 - y_low, z, core)
    greet(x_peers + y_peers + spot_peers)
    copies = Copies(send, recv, own)

    gate_rows = (16, 10)
    down_rows = (16, 7)

    def gate_add(out, *terms):
        add_into(out, (2, 2), *terms, rows=gate_rows)

    def dense_add(out, *terms):
        add_into(out, (2, 4, 4), *terms)

    def down_add(out, *terms):
        add_into(out, (), *terms, rows=down_rows)

    def gate_part(chunk, half):
        return (gate, up)[half].at[:, chunk]

    rings = [
        RingSum(copies, z, z_right, z_left, lambda c, h, t=t: dense.at[c, t, h], z_land.at[t], z_work.at[t], dense_add)
        for t in range(2)
    ]
    swap = copies.remote(down.at[:, :, 1 - y_low], d_other, pair)
    own_down = copies.local(down.at[:, :, y_low], d_work)
    gates = RingSum(copies, x, x_peers[0], x_peers[2], gate_part, g_land, g_work, gate_add)

    rings[0].forward()
    gates.forward()
    rings[1].forward()
    own_down.wait()
    swap.wait_recv()
    add_into(d_work, (2, 4), d_work, d_other, rows=down_rows)
    downs = RingSum(copies, x, x_peers[0], x_peers[2], lambda c, h: d_work.at[h, c], d_land, None, down_add, resident=True)

    def order(value):
        return (value % 2) * 2 + value // 2

    def start_y(t):
        rings[t].finish([z_work.at[t, 2], z_work.at[t, 3]])
        return [
            copies.remote(z_work.at[t, 2:4, :, :, order((y + d) % 4)], y_land.at[t, d - 1], y_peers[d - 1])
            for d in (1, 2, 3)
        ]

    def start_x(t, arrivals):
        for copy in arrivals:
            copy.wait_recv()
        mine = z_work.at[t, 2:4, :, :, order(y)]
        add_into(y_sum.at[t], (2, 2, 4), mine, y_land.at[t, 0], y_land.at[t, 1], y_land.at[t, 2])
        return [
            copies.remote(y_sum.at[t, :, :, (x + d) % 4], x_land.at[t, d - 1], x_peers[d - 1])
            for d in (1, 2, 3)
        ]

    y_first = start_y(0)
    downs.forward()
    gates.finish([g_work.at[2], g_work.at[3]])
    swap_gate = copies.remote(g_work.at[2:4, :, 1 - y_low], g_other, pair)
    x_first = start_x(0, y_first)
    y_second = start_y(1)
    downs.finish([down_out.at[0], down_out.at[1]])
    x_second = start_x(1, y_second)
    swap_gate.wait_recv()
    for index, out in enumerate((gate_out, up_out)):
        add_into(out, (2,), g_work.at[index + 2, :, y_low], g_other.at[index], rows=gate_rows)
    for t, arrivals in enumerate((x_first, x_second)):
        for copy in arrivals:
            copy.wait_recv()
        for half in range(2):
            for panel in range(2):
                value = y_sum[t, half, panel, x].astype(F32)
                for d in range(3):
                    value = value + x_land[t, d, half, panel].astype(F32)
                total[t * 4 + half * 2 + panel, 0:80] = value
                total[t * 4 + half * 2 + panel, 80:96] = jnp.zeros((16, 128), F32)
    for j in range(8):
        for panel in range(8):
            stage[j, panel] = total[panel, 10 * j : 10 * j + 16]
    finals = [
        copies.remote(stage.at[(spot + d) % 8], final_land.at[d], spot_peers[d - 1]) for d in range(1, 8)
    ]
    dense_out[spot] = stage[spot]
    for d, copy in enumerate(finals):
        copy.wait_recv()
        dense_out[(spot + 7 - d) % 8] = final_land[d + 1]
    copies.drain()


def sum_grads(dense, gate, up, down):
    scratch = [
        pltpu.VMEM((2, 6, 2, 4, 4, 80, 128), BF16),
        pltpu.VMEM((2, 4, 2, 4, 4, 80, 128), BF16),
        pltpu.VMEM((2, 3, 2, 2, 4, 80, 128), BF16),
        pltpu.VMEM((2, 2, 2, 4, 80, 128), BF16),
        pltpu.VMEM((2, 3, 2, 2, 80, 128), BF16),
        pltpu.VMEM((8, 96, 128), F32),
        pltpu.VMEM((8, 8, 16, 128), F32),
        pltpu.VMEM((8, 8, 16, 128), F32),
        pltpu.VMEM((6, 2, 2, 160, 896), BF16),
        pltpu.VMEM((4, 2, 2, 160, 896), BF16),
        pltpu.VMEM((2, 2, 160, 896), BF16),
        pltpu.VMEM((6, 112, 1280), BF16),
        pltpu.VMEM((2, 4, 112, 1280), BF16),
        pltpu.VMEM((2, 4, 112, 1280), BF16),
        pltpu.SemaphoreType.DMA((GRAD_REMOTES,)),
        pltpu.SemaphoreType.DMA((GRAD_REMOTES,)),
        pltpu.SemaphoreType.DMA((GRAD_LOCALS,)),
    ]
    vmem = pl.BlockSpec(memory_space=pltpu.VMEM)
    anywhere = pl.BlockSpec(memory_space=pl.ANY)
    return pl.pallas_call(
        grads_kernel,
        name="sum_grads",
        out_shape=(
            jax.ShapeDtypeStruct((8, 8, 16, 128), F32),
            jax.ShapeDtypeStruct((2, 160, 896), F32),
            jax.ShapeDtypeStruct((2, 160, 896), F32),
            jax.ShapeDtypeStruct((2, 112, 1280), F32),
        ),
        in_specs=[anywhere] * 4,
        out_specs=(vmem,) * 4,
        scratch_shapes=scratch,
        compiler_params=pltpu.CompilerParams(
            collective_id=0, has_side_effects=True, vmem_limit_bytes=VMEM_LIMIT
        ),
        cost_estimate=pl.CostEstimate(flops=10**8, bytes_accessed=4 * 10**8, transcendentals=0),
    )(
        dense.reshape(4, 2, 2, 2, 4, 4, 80, 128),
        gate.reshape(2, 4, 2, 160, 896),
        up.reshape(2, 4, 2, 160, 896),
        down.reshape(2, 4, 2, 112, 1280),
    )


def dense_kernel(left, right, gains, out):
    panel = pl.program_id(0)
    out[0] = lax.dot_general(
        left[0], right[...], (((0,), (0,)), ((), ())), preferred_element_type=F32
    ).astype(BF16)

    @pl.when(panel == 27)
    def _():
        out[0] = (out[0].astype(F32) + gains[...]).astype(BF16)


def dense_terms(left, right, gains):
    def group(p):
        return (p >= 15).astype(jnp.int32) + (p >= 20).astype(jnp.int32) + (p >= 27).astype(jnp.int32)

    return pl.pallas_call(
        dense_kernel,
        name="dense_terms",
        grid=(32,),
        out_shape=jax.ShapeDtypeStruct((32, 1280, 128), BF16),
        in_specs=[
            pl.BlockSpec((1, 256, 1280), lambda p: (group(p), 0, 0)),
            pl.BlockSpec((256, 128), lambda p: (0, p)),
            pl.BlockSpec((1280, 128), lambda p: (0, 0)),
        ],
        out_specs=pl.BlockSpec((1, 1280, 128), lambda p: (p, 0, 0)),
        compiler_params=pltpu.CompilerParams(vmem_limit_bytes=VMEM_LIMIT),
        cost_estimate=pl.CostEstimate(flops=2 * 256 * 1280 * 4096, bytes_accessed=15 * 10**6, transcendentals=0),
    )(left, right, gains)


def reduce_dense(normed_one, mixed, normed_two, shared_act, d_qkv, d_attn, d_gate, d_up, cot, attn_gain_term, ffn_gain_term):
    core = lax.axis_index("exp") % 2
    swap = [(e, e ^ 1) for e in range(lax.axis_size("exp"))]
    rows = normed_one.shape[0]
    padded = jnp.pad(shared_act.reshape(rows, 128, 7), ((0, 0), (0, 0), (0, 3))).reshape(rows, 1280)
    left = jnp.stack([normed_one, mixed, normed_two, padded])
    halves = [
        jnp.concatenate([d_qkv[:, :1920], d_attn[:, :640], d_gate, cot[:, :640]], axis=1),
        jnp.concatenate([d_qkv[:, 1920:], d_attn[:, 640:], d_up, cot[:, 640:]], axis=1),
    ]
    mine = jnp.where(core == 0, halves[0], halves[1])
    theirs = jnp.where(core == 0, halves[1], halves[0])
    gain_mine = jnp.where(core == 0, attn_gain_term, ffn_gain_term)
    gain_theirs = jnp.where(core == 0, ffn_gain_term, attn_gain_term)
    left = jnp.concatenate([left, lax.ppermute(left, "exp", swap)], axis=1)
    right = jnp.concatenate([mine, lax.ppermute(theirs, "exp", swap)], axis=0)
    gain = (gain_mine + lax.ppermute(gain_theirs, "exp", swap)).reshape(128, 1, 10)
    gains = jnp.pad(gain, ((0, 0), (7, 2), (0, 118))).reshape(1280, 128)
    return dense_terms(left, right, gains)


def unpack_dense(packed):
    panels = packed.reshape(4, 2, 8, 16, 128)[:, :, :, :10].transpose(1, 0, 2, 3, 4).reshape(2, 32, 10, 128)

    def joined(first, last):
        return panels[:, first:last].transpose(2, 0, 1, 3).reshape(10, -1)

    qkv, out = joined(0, 15), joined(15, 20)
    gate_up, down = joined(20, 27), joined(27, 32)[:7]
    return (
        panels[0, 27, 7, :10], qkv[:, :1280], qkv[:, 1280:2560], qkv[:, 2560:], out,
        panels[1, 27, 7, :10], gate_up[:, :896], gate_up[:, 896:], down,
    )


VMEM = pl.BlockSpec(memory_space=pltpu.VMEM)
ANYWHERE = pl.BlockSpec(memory_space=pl.ANY)
SMEM = pl.BlockSpec(memory_space=pltpu.SMEM)
EXTRA_HEAD = {8: 0, 9: 5}
SCALE = HEAD_DIM ** (-0.5)


def params(collective_id=None):
    if collective_id is None:
        return pltpu.CompilerParams(vmem_limit_bytes=VMEM_LIMIT)
    return pltpu.CompilerParams(
        collective_id=collective_id, has_side_effects=True, vmem_limit_bytes=VMEM_LIMIT
    )


def cost(flops, bytes_accessed):
    return pl.CostEstimate(flops=int(flops), bytes_accessed=int(bytes_accessed), transcendentals=0)


def dot(left, right):
    return jnp.dot(left, right, preferred_element_type=F32)


def dot_nt(left, right):
    return lax.dot_general(left, right, (((1,), (1,)), ((), ())), preferred_element_type=F32)


def dot_tn(left, right):
    return lax.dot_general(left, right, (((0,), (0,)), ((), ())), preferred_element_type=F32)


def normed(values, gain):
    return values * lax.rsqrt(jnp.mean(values * values, axis=-1, keepdims=True) + 1e-06) * gain


def normed_back(values, gain, upstream):
    factor = lax.rsqrt(jnp.mean(values * values, axis=-1, keepdims=True) + 1e-06)
    scaled = upstream * gain
    inner = jnp.mean(scaled * values, axis=-1, keepdims=True)
    term = jnp.sum(upstream * values * factor, axis=0, keepdims=True)
    return factor * scaled - values * factor * factor * factor * inner, term


def turned(values, cos, sin):
    return values * cos + pltpu.roll(values, HEAD_DIM // 2, 1) * sin


def turn_tables(positions):
    half = HEAD_DIM // 2
    frequency = jnp.exp(jnp.arange(half, dtype=F32) * (-2.0 * math.log(10000.0) / HEAD_DIM))
    angle = positions.astype(F32)[:, None] * frequency[None, :]
    cos, sin = jnp.cos(angle), jnp.sin(angle)
    return jnp.concatenate([cos, cos], axis=1), jnp.concatenate([-sin, sin], axis=1)


def project_kernel(tokens, gain, w_query, w_key, w_value, cos, sin, qkv, normed_one):
    @pl.when(pl.program_id(0) == 0)
    def _():
        normed_one[...] = normed(tokens[...].astype(F32), gain[...]).astype(BF16)

    rows = normed_one[...]
    query, key, value = dot(rows, w_query[...]), dot(rows, w_key[...]), dot(rows, w_value[...])
    for head in range(2):
        lanes = slice(head * HEAD_DIM, (head + 1) * HEAD_DIM)
        qkv[head, 0] = turned(query[:, lanes], cos[...], sin[...]).astype(BF16)
        qkv[head, 1] = turned(key[:, lanes], cos[...], sin[...]).astype(BF16)
        qkv[head, 2] = value[:, lanes].astype(BF16)


def project(tokens, gain, w_query, w_key, w_value, cos, sin):
    rows, width = tokens.shape
    whole = pl.BlockSpec((rows, width), lambda h: (0, 0))
    table = pl.BlockSpec((rows, HEAD_DIM), lambda h: (0, 0))
    columns = pl.BlockSpec((width, 2 * HEAD_DIM), lambda h: (0, h))
    return pl.pallas_call(
        project_kernel,
        name="project",
        grid=(5,),
        out_shape=(
            jax.ShapeDtypeStruct((10, 3, rows, HEAD_DIM), BF16),
            jax.ShapeDtypeStruct((rows, width), BF16),
        ),
        in_specs=[whole, pl.BlockSpec((1, width), lambda h: (0, 0)), columns, columns, columns, table, table],
        out_specs=(pl.BlockSpec((2, 3, rows, HEAD_DIM), lambda h: (h, 0, 0, 0)), whole),
        compiler_params=params(),
        cost_estimate=cost(6 * rows * width * width, 6 * width * width),
    )(tokens, gain, w_query, w_key, w_value, cos, sin)


def project_back_kernel(d_query, d_key, d_value, w_query, w_key, w_value, tokens, gain, d_hidden, input_grad, gain_term, total):
    step = pl.program_id(0)

    @pl.when(step == 0)
    def _():
        total[...] = jnp.zeros_like(total)

    total[...] += (
        dot_nt(d_query[...], w_query[...]) + dot_nt(d_key[...], w_key[...]) + dot_nt(d_value[...], w_value[...])
    )

    @pl.when(step == pl.num_programs(0) - 1)
    def _():
        grad, term = normed_back(tokens[...].astype(F32), gain[...], total[...])
        input_grad[...] = d_hidden[...] + grad
        gain_term[...] = term


def project_back(d_qkv, w_query, w_key, w_value, tokens, gain, d_hidden):
    rows, width = tokens.shape
    step = 2 * HEAD_DIM
    whole = pl.BlockSpec((rows, width), lambda h: (0, 0))
    line = pl.BlockSpec((1, width), lambda h: (0, 0))
    columns = pl.BlockSpec((width, step), lambda h: (0, h))
    return pl.pallas_call(
        project_back_kernel,
        name="project_back",
        grid=(5,),
        out_shape=(jax.ShapeDtypeStruct((rows, width), F32), jax.ShapeDtypeStruct((1, width), F32)),
        in_specs=[
            pl.BlockSpec((rows, step), lambda h: (0, h)),
            pl.BlockSpec((rows, step), lambda h: (0, h + 5)),
            pl.BlockSpec((rows, step), lambda h: (0, h + 10)),
            columns, columns, columns, whole, line, whole,
        ],
        out_specs=(whole, line),
        scratch_shapes=[pltpu.VMEM((rows, width), F32)],
        compiler_params=params(),
        cost_estimate=cost(6 * rows * width * width, 6 * width * width),
    )(d_qkv, d_qkv, d_qkv, w_query, w_key, w_value, tokens, gain, d_hidden)


def rank(y_half, z, core):
    return y_half * 8 + z * 2 + core


class Gather:
    def __init__(self, copies, where, src, out, cut):
        x, y, z, core = where
        self.copies, self.out, self.cut = copies, out, cut
        self.y_half, self.z, self.core = y // 2, z, core
        self.pair = device(x, y, z, 1 - core)
        self.across = device(x, (y + 2) % 4, z, core)
        self.right, self.left = device(x, y, (z + 1) % 4, core), device(x, y, (z + 3) % 4, core)
        me = rank(self.y_half, z, core)
        self.mine = copies.local(src, out.at[me])
        self.over = copies.remote(src, out.at[me], self.across)
        self.to_right = copies.remote(src, out.at[me], self.right)
        self.to_left = copies.remote(src, out.at[me], self.left)
        self.pairs = [copies.remote(src, out.at[me], self.pair)]

    def shard(self, other, dz):
        y_half = 1 - self.y_half if other else self.y_half
        return rank(y_half, (self.z + dz + 4) % 4, self.core)

    def half(self, index, which):
        rows = self.out.shape[1]
        return self.out.at[index, 0 : self.cut] if which == 0 else self.out.at[index, self.cut : rows]

    def send(self, ref, target):
        return self.copies.remote(ref, ref, target)

    def share(self, ref):
        self.pairs.append(self.send(ref, self.pair))

    def second(self):
        self.over.wait_recv()
        index = self.shard(True, 0)
        self.far_right = self.send(self.out.at[index], self.right)
        self.far_left = self.send(self.out.at[index], self.left)
        self.share(self.out.at[index])
        self.to_right.wait_recv()
        index = self.shard(False, -1)
        self.on_right = self.send(self.half(index, 0), self.right)
        self.share(self.out.at[index])
        self.to_left.wait_recv()
        index = self.shard(False, 1)
        self.on_left = self.send(self.half(index, 1), self.left)
        self.share(self.out.at[index])

    def third(self):
        self.far_right.wait_recv()
        index = self.shard(True, -1)
        self.far_on_right = self.send(self.half(index, 0), self.right)
        self.share(self.out.at[index])
        self.far_left.wait_recv()
        index = self.shard(True, 1)
        self.far_on_left = self.send(self.half(index, 1), self.left)
        self.share(self.out.at[index])

    def last(self):
        for copies, other in (((self.on_right, self.on_left), False), ((self.far_on_right, self.far_on_left), True)):
            for which, copy in enumerate(copies):
                copy.wait_recv()
                self.share(self.half(self.shard(other, 2), which))
        for copy in self.pairs:
            copy.wait_recv()
        self.mine.wait()


GATHER_REMOTES = 3 + 2 + 2 + 2 + 8 + 2


def exp_peers(where):
    x, y, z, core = where
    return [
        device(x, y, z, 1 - core),
        device(x, (y + 2) % 4, z, core),
        device(x, y, (z + 1) % 4, core),
        device(x, y, (z + 3) % 4, core),
    ]


def gather_kernel(src, out, send, recv, own):
    where = place()
    greet(exp_peers(where))
    copies = Copies(send, recv, own)
    gather = Gather(copies, where, src, out, src.shape[0] // 2)
    gather.second()
    gather.third()
    gather.last()
    copies.drain()


def gather_rows(rows, collective_id):
    return pl.pallas_call(
        gather_kernel,
        name="gather_rows",
        out_shape=jax.ShapeDtypeStruct((16,) + rows.shape, rows.dtype),
        in_specs=[ANYWHERE],
        out_specs=ANYWHERE,
        scratch_shapes=[
            pltpu.SemaphoreType.DMA((GATHER_REMOTES,)),
            pltpu.SemaphoreType.DMA((GATHER_REMOTES,)),
            pltpu.SemaphoreType.DMA((1,)),
        ],
        compiler_params=params(collective_id),
        cost_estimate=cost(10**6, 6 * 10**7),
    )(rows)


class Scatter:
    def __init__(self, copies, where, parts, pair_land, work, ring_land, far_land, y_land):
        x, y, z, core = where
        self.copies, self.work, self.pair_land = copies, work, pair_land
        self.ring_land, self.far_land, self.y_land = ring_land, far_land, y_land
        self.across = device(x, (y + 2) % 4, z, core)
        self.right, self.left = device(x, y, (z + 1) % 4, core), device(x, y, (z + 3) % 4, core)
        pair = device(x, y, z, 1 - core)
        self.pairs, self.loads = {}, {}
        for slot in ((0, 2), (1, 2), (0, 1), (0, 3), (1, 1), (1, 3), (0, 0), (1, 0)):
            y_half = 1 - y // 2 if slot[0] == 0 else y // 2
            at = (z + slot[1]) % 4
            self.pairs[slot] = copies.remote(parts.at[rank(y_half, at, 1 - core)], pair_land.at[slot], pair)
            self.loads[slot] = copies.local(parts.at[rank(y_half, at, core)], work.at[slot])

    def merge(self, slot):
        self.loads[slot].wait()
        self.pairs[slot].wait_recv()
        rows_add(self.work.at[slot], 0, 128, self.work.at[slot], self.pair_land.at[slot])

    def first(self):
        self.ring = {}
        for far in range(2):
            self.merge((far, 2))
            self.ring[far] = (
                self.copies.remote(self.work.at[far, 2, 0:64], self.ring_land.at[far, 0], self.right),
                self.copies.remote(self.work.at[far, 2, 64:128], self.ring_land.at[far, 1], self.left),
            )
        for far in range(2):
            self.merge((far, 1))
            self.merge((far, 3))
            self.merge((far, 0))

    def second(self):
        self.final = {}
        for far in range(2):
            self.ring[far][0].wait_recv()
            rows_add(self.work.at[far, 1, 0:64], 0, 64, self.work.at[far, 1, 0:64], self.ring_land.at[far, 0])
            to_right = self.copies.remote(self.work.at[far, 1], self.far_land.at[far, 0], self.right)
            self.ring[far][1].wait_recv()
            rows_add(self.work.at[far, 3, 64:128], 0, 64, self.work.at[far, 3, 64:128], self.ring_land.at[far, 1])
            to_left = self.copies.remote(self.work.at[far, 3], self.far_land.at[far, 1], self.left)
            self.final[far] = (to_right, to_left)

    def third(self):
        for far in range(2):
            for copy in self.final[far]:
                copy.wait_recv()
            rows_add(self.work.at[far, 0], 0, 128, self.work.at[far, 0], self.far_land.at[far, 0], self.far_land.at[far, 1])
            if far == 0:
                self.over = self.copies.remote(self.work.at[0, 0], self.y_land, self.across)

    def last(self, out):
        self.over.wait_recv()
        rows_add(out, 0, 128, self.work.at[1, 0], self.y_land)


def rows_add(out, first, rows, *terms):
    @pl.loop(0, rows // 16)
    def _(step):
        at = pl.ds(pl.multiple_of(step * 16, 16), 16)
        value = terms[0][at].astype(F32)
        for term in terms[1:]:
            value = value + term[at].astype(F32)
        out[at] = value.astype(out.dtype)


SCATTER_REMOTES, SCATTER_LOCALS = 8 + 4 + 4 + 1, 8
SCATTER_SCRATCH = [
    pltpu.VMEM((2, 4, 128, 1280), BF16),
    pltpu.VMEM((2, 4, 128, 1280), BF16),
    pltpu.VMEM((2, 2, 64, 1280), BF16),
    pltpu.VMEM((2, 2, 128, 1280), BF16),
    pltpu.VMEM((128, 1280), BF16),
]


def scatter_kernel(parts, out, *scratch):
    where = place()
    greet(exp_peers(where))
    copies = Copies(*scratch[5:])
    scatter = Scatter(copies, where, parts, *scratch[:5])
    scatter.first()
    scatter.second()
    scatter.third()
    scatter.last(out)
    copies.drain()


def scatter_rows(parts, collective_id):
    return pl.pallas_call(
        scatter_kernel,
        name="scatter_rows",
        out_shape=jax.ShapeDtypeStruct((128, 1280), F32),
        in_specs=[ANYWHERE],
        out_specs=VMEM,
        scratch_shapes=SCATTER_SCRATCH
        + [
            pltpu.SemaphoreType.DMA((SCATTER_REMOTES,)),
            pltpu.SemaphoreType.DMA((SCATTER_REMOTES,)),
            pltpu.SemaphoreType.DMA((SCATTER_LOCALS,)),
        ],
        compiler_params=params(collective_id),
        cost_estimate=cost(10**7, 10**8),
    )(parts)


def ctx_device(ctx):
    return (ctx, lax.axis_index("exp"))


def owns_extra(ctx):
    return (ctx == EXTRA_HEAD[8]) | (ctx == EXTRA_HEAD[9])


def extra_head(ctx):
    return 8 + (ctx == EXTRA_HEAD[9]).astype(jnp.int32)


class Exchange:
    def __init__(self, send, recv, own):
        self.send, self.recv, self.own = send, recv, own
        self.ctx = lax.axis_index("ctx")

    def copy(self, src, dst, slot, d):
        return pltpu.make_async_remote_copy(
            src_ref=src,
            dst_ref=dst,
            send_sem=self.send.at[slot, d],
            recv_sem=self.recv.at[slot, d],
            device_id=ctx_device((self.ctx + d) % 8),
            device_id_type=MESH,
        )


def to_owners(exchange, block, land):
    ctx = exchange.ctx
    for d in range(1, 8):
        peer = (ctx + d) % 8
        exchange.copy(block(peer), land(0, ctx), 0, d).start()

        @pl.when(owns_extra(peer))
        def _():
            exchange.copy(block(extra_head(peer)), land(1, ctx), 1, d).start()

    mine = [pltpu.make_async_copy(block(ctx), land(0, ctx), exchange.own.at[0])]
    mine[0].start()
    extra = pltpu.make_async_copy(block(extra_head(ctx)), land(1, ctx), exchange.own.at[1])

    @pl.when(owns_extra(ctx))
    def _():
        extra.start()

    def arrived():
        mine[0].wait()
        for d in range(1, 8):
            exchange.copy(block(0), land(0, ctx), 0, d).wait_recv()

        @pl.when(owns_extra(ctx))
        def _():
            extra.wait()
            for d in range(1, 8):
                exchange.copy(block(0), land(1, ctx), 1, d).wait_recv()

    def sent():
        for d in range(1, 8):
            exchange.copy(block(0), land(0, ctx), 0, d).wait_send()

            @pl.when(owns_extra((ctx + d) % 8))
            def _():
                exchange.copy(block(0), land(1, ctx), 1, d).wait_send()

    return arrived, sent


class Home:
    def __init__(self, exchange, block, land):
        self.exchange, self.block, self.land = exchange, block, land
        self.ctx = exchange.ctx

    def head(self, slot):
        return self.ctx if slot == 0 else extra_head(self.ctx)

    def start(self, slot):
        for d in range(1, 8):
            self.exchange.copy(self.block(slot, (self.ctx + d) % 8), self.land(self.head(slot)), slot, d).start()
        self.mine(slot).start()

    def mine(self, slot):
        return pltpu.make_async_copy(
            self.block(slot, self.ctx), self.land(self.head(slot)), self.exchange.own.at[slot]
        )

    def finish(self):
        self.mine(0).wait()
        for d in range(1, 8):
            copy = self.exchange.copy(self.block(0, 0), self.land(0), 0, d)
            copy.wait_send()
            copy.wait_recv()

            @pl.when(owns_extra((self.ctx + 8 - d) % 8))
            def _():
                self.exchange.copy(self.block(1, 0), self.land(0), 1, d).wait_recv()

        @pl.when(owns_extra(self.ctx))
        def _():
            self.mine(1).wait()
            for d in range(1, 8):
                self.exchange.copy(self.block(1, 0), self.land(0), 1, d).wait_send()


def attend_kernel(qkv, length, cot, mixed, heads, cots, land, result, home, s1, r1, o1, s2, r2, o2, s3, r3, o3):
    where = place()
    ctx = lax.axis_index("ctx")
    greet([ctx_device((ctx + d) % 8) for d in range(1, 8)] + exp_peers(where))
    arrived, sent = to_owners(
        Exchange(s1, r1, o1), lambda head: qkv.at[head], lambda slot, c: land.at[slot, :, c]
    )
    copies = Copies(s3, r3, o3)
    gather = Gather(copies, where, cot, cots, 80)
    back = Home(Exchange(s2, r2, o2), lambda slot, c: result.at[slot, c], lambda head: home.at[head])
    arrived()
    keep = pltpu.make_async_copy(land, heads, o3.at[1])

    def run(slot):
        for block in range(8):
            width = (block + 1) * 128
            query = land[slot, 0, block]
            key = land[slot, 1, 0 : block + 1].reshape(width, HEAD_DIM)
            value = land[slot, 2, 0 : block + 1].reshape(width, HEAD_DIM)
            column = lax.broadcasted_iota(jnp.int32, (128, width), 1)
            row = lax.broadcasted_iota(jnp.int32, (128, width), 0) + block * 128
            scores = jnp.where(
                (column <= row) & (column < length[0]), dot_nt(query, key) * SCALE, -1e30
            )
            weights = jnp.exp(scores - jnp.max(scores, axis=-1, keepdims=True))
            probs = weights / jnp.sum(weights, axis=-1, keepdims=True)
            result[slot, block] = dot(probs.astype(BF16), value).astype(BF16)
        back.start(slot)

    run(0)
    gather.second()

    @pl.when(owns_extra(ctx))
    def _():
        run(1)

    @pl.when(jnp.logical_not(owns_extra(ctx)))
    def _():
        land[1] = jnp.zeros_like(land[1])

    keep.start()
    gather.third()
    back.finish()
    for head in range(10):
        mixed[:, head * HEAD_DIM : (head + 1) * HEAD_DIM] = home[head]
    gather.last()
    sent()
    keep.wait()
    copies.drain()


def exchange_semaphores():
    return [
        pltpu.SemaphoreType.DMA((2, 8)),
        pltpu.SemaphoreType.DMA((2, 8)),
        pltpu.SemaphoreType.DMA((2,)),
    ]


def attend(qkv, length, cot, collective_id):
    return pl.pallas_call(
        attend_kernel,
        name="attend",
        out_shape=(
            jax.ShapeDtypeStruct((128, 1280), BF16),
            jax.ShapeDtypeStruct((2, 3, 8, 128, HEAD_DIM), BF16),
            jax.ShapeDtypeStruct((16,) + cot.shape, BF16),
        ),
        in_specs=[ANYWHERE, SMEM, ANYWHERE],
        out_specs=(VMEM, ANYWHERE, ANYWHERE),
        scratch_shapes=[
            pltpu.VMEM((2, 3, 8, 128, HEAD_DIM), BF16),
            pltpu.VMEM((2, 8, 128, HEAD_DIM), BF16),
            pltpu.VMEM((10, 128, HEAD_DIM), BF16),
        ]
        + exchange_semaphores()
        + exchange_semaphores()
        + [
            pltpu.SemaphoreType.DMA((GATHER_REMOTES,)),
            pltpu.SemaphoreType.DMA((GATHER_REMOTES,)),
            pltpu.SemaphoreType.DMA((2,)),
        ],
        compiler_params=params(collective_id),
        cost_estimate=cost(10**9, 10**8),
    )(qkv, length, cot)


def attend_back_kernel(
    d_mixed, heads, length, cos, sin, parts, d_qkv, routed, land, kept, d_key, d_value, result, home,
    a, b, c, d, e, s1, r1, o1, s2, r2, o2, s3, r3, o3, keep_sem,
):
    where = place()
    ctx = lax.axis_index("ctx")
    greet([ctx_device((ctx + step) % 8) for step in range(1, 8)] + exp_peers(where))
    arrived, sent = to_owners(
        Exchange(s1, r1, o1), lambda head: d_mixed.at[head], lambda slot, at: land.at[slot, at]
    )
    keep = pltpu.make_async_copy(heads, kept, keep_sem)
    keep.start()
    copies = Copies(s3, r3, o3)
    scatter = Scatter(copies, where, parts, a, b, c, d, e)
    back = Home(Exchange(s2, r2, o2), lambda slot, at: result.at[slot, :, at], lambda head: home.at[:, head])
    keep.wait()
    arrived()

    def run(slot):
        d_key[...] = jnp.zeros_like(d_key)
        d_value[...] = jnp.zeros_like(d_value)
        for block in range(8):
            width = (block + 1) * 128
            query, upstream = kept[slot, 0, block], land[slot, block]
            key = kept[slot, 1, 0 : block + 1].reshape(width, HEAD_DIM)
            value = kept[slot, 2, 0 : block + 1].reshape(width, HEAD_DIM)
            row = lax.broadcasted_iota(jnp.int32, (width, 128), 0)
            column = lax.broadcasted_iota(jnp.int32, (width, 128), 1) + block * 128
            scores = jnp.where(
                (row <= column) & (row < length[0]), dot_nt(key, query) * SCALE, -1e30
            )
            weights = jnp.exp(scores - jnp.max(scores, axis=0, keepdims=True))
            probs = weights / jnp.sum(weights, axis=0, keepdims=True)
            d_probs = dot_nt(value, upstream)
            delta = jnp.sum(probs * d_probs, axis=0, keepdims=True)
            d_scores = (probs * (d_probs - delta)).astype(BF16)
            rows = slice(block * 128, block * 128 + 128)
            d_query = dot_tn(d_scores, key) * SCALE
            result[slot, 0, block] = turned(d_query, cos[rows], sin[rows]).astype(BF16)
            d_key[0:width] += dot(d_scores, query)
            d_value[0:width] += dot(probs.astype(BF16), upstream)
        for block in range(8):
            rows = slice(block * 128, block * 128 + 128)
            result[slot, 1, block] = turned(d_key[rows] * SCALE, cos[rows], sin[rows]).astype(BF16)
            result[slot, 2, block] = d_value[rows].astype(BF16)
        back.start(slot)

    run(0)
    scatter.first()

    @pl.when(owns_extra(ctx))
    def _():
        run(1)

    scatter.second()
    scatter.third()
    back.finish()
    for head in range(10):
        for kind in range(3):
            at = kind * 1280 + head * HEAD_DIM
            d_qkv[:, at : at + HEAD_DIM] = home[kind, head]
    scatter.last(routed)
    sent()
    copies.drain()


def attend_back(d_mixed, heads, length, cos, sin, parts, collective_id):
    return pl.pallas_call(
        attend_back_kernel,
        name="attend_back",
        out_shape=(
            jax.ShapeDtypeStruct((128, 3840), BF16),
            jax.ShapeDtypeStruct((128, 1280), F32),
        ),
        in_specs=[ANYWHERE, ANYWHERE, SMEM, VMEM, VMEM, ANYWHERE],
        out_specs=(VMEM, VMEM),
        scratch_shapes=[
            pltpu.VMEM((2, 8, 128, HEAD_DIM), BF16),
            pltpu.VMEM((2, 3, 8, 128, HEAD_DIM), BF16),
            pltpu.VMEM((1024, HEAD_DIM), F32),
            pltpu.VMEM((1024, HEAD_DIM), F32),
            pltpu.VMEM((2, 3, 8, 128, HEAD_DIM), BF16),
            pltpu.VMEM((3, 10, 128, HEAD_DIM), BF16),
        ]
        + SCATTER_SCRATCH
        + exchange_semaphores()
        + exchange_semaphores()
        + [
            pltpu.SemaphoreType.DMA((SCATTER_REMOTES,)),
            pltpu.SemaphoreType.DMA((SCATTER_REMOTES,)),
            pltpu.SemaphoreType.DMA((SCATTER_LOCALS,)),
            pltpu.SemaphoreType.DMA,
        ],
        compiler_params=params(collective_id),
        cost_estimate=cost(10**9, 10**8),
    )(d_mixed, heads, length, cos, sin, parts)


def after_kernel(mixed, w_out, tokens, gain, hidden, normed_two):
    step = pl.program_id(0)
    size = w_out.shape[1]
    at = pl.ds(pl.multiple_of(step * size, size), size)
    hidden[:, at] = tokens[:, at].astype(F32) + dot(mixed[...], w_out[...])

    @pl.when(step == pl.num_programs(0) - 1)
    def _():
        normed_two[...] = normed(hidden[...], gain[...]).astype(BF16)


def after(mixed, w_out, tokens, gain):
    rows, width = tokens.shape
    whole = pl.BlockSpec((rows, width), lambda h: (0, 0))
    return pl.pallas_call(
        after_kernel,
        name="after",
        grid=(5,),
        out_shape=(jax.ShapeDtypeStruct((rows, width), F32), jax.ShapeDtypeStruct((rows, width), BF16)),
        in_specs=[whole, pl.BlockSpec((width, 256), lambda h: (0, h)), whole, pl.BlockSpec((1, width), lambda h: (0, 0))],
        out_specs=(whole, whole),
        compiler_params=params(),
        cost_estimate=cost(2 * rows * width * width, 2 * width * width),
    )(mixed, w_out, tokens, gain)


def gated(gate, up):
    squash = 1.0 / (1.0 + jnp.exp(-gate))
    silu = gate * squash
    slope = squash * (1.0 + gate * (1.0 - squash))
    return silu, slope


def shared_kernel(rows, cot, gate_w, up_w, down_w, act, d_gate, d_up, out, d_rows):
    @pl.when(pl.program_id(0) == 0)
    def _():
        out[...] = jnp.zeros_like(out)
        d_rows[...] = jnp.zeros_like(d_rows)

    gate, up = dot(rows[...], gate_w[...]), dot(rows[...], up_w[...])
    silu, slope = gated(gate, up)
    activated = (silu * up).astype(BF16)
    act[...] = activated
    out[...] += dot(activated, down_w[...])
    d_act = dot_nt(cot[...], down_w[...])
    gate_back = (d_act * up * slope).astype(BF16)
    up_back = (d_act * silu).astype(BF16)
    d_gate[...] = gate_back
    d_up[...] = up_back
    d_rows[...] += dot_nt(gate_back, gate_w[...]) + dot_nt(up_back, up_w[...])


def shared_expert(rows, cot, gate_w, up_w, down_w):
    count, width = rows.shape
    hidden = gate_w.shape[1]
    step = 128
    whole = pl.BlockSpec((count, width), lambda f: (0, 0))
    columns = pl.BlockSpec((width, step), lambda f: (0, f))
    narrow = pl.BlockSpec((count, step), lambda f: (0, f))
    return pl.pallas_call(
        shared_kernel,
        name="shared_expert",
        grid=(hidden // step,),
        out_shape=[jax.ShapeDtypeStruct((count, hidden), BF16)] * 3 + [jax.ShapeDtypeStruct((count, width), F32)] * 2,
        in_specs=[whole, whole, columns, columns, pl.BlockSpec((step, width), lambda f: (f, 0))],
        out_specs=[narrow] * 3 + [whole] * 2,
        compiler_params=params(),
        cost_estimate=cost(14 * count * width * hidden, 6 * width * hidden),
    )(rows, cot, gate_w, up_w, down_w)


def middle_kernel(d_shared, d_routed, hidden, gain, cot, w_out, d_mixed, d_hidden, d_attn, gain_term):
    @pl.when(pl.program_id(0) == 0)
    def _():
        grad, term = normed_back(hidden[...], gain[...], d_shared[...] + d_routed[...])
        whole = cot[...].astype(F32) + grad
        d_hidden[...] = whole
        d_attn[...] = whole.astype(BF16)
        gain_term[...] = term

    value = dot_nt(d_attn[...], w_out[...]).astype(BF16)
    d_mixed[0] = value[:, :HEAD_DIM]
    d_mixed[1] = value[:, HEAD_DIM:]


def middle(d_shared, d_routed, hidden, gain, cot, w_out):
    rows, width = hidden.shape
    whole = pl.BlockSpec((rows, width), lambda h: (0, 0))
    line = pl.BlockSpec((1, width), lambda h: (0, 0))
    return pl.pallas_call(
        middle_kernel,
        name="middle",
        grid=(5,),
        out_shape=(
            jax.ShapeDtypeStruct((10, rows, HEAD_DIM), BF16),
            jax.ShapeDtypeStruct((rows, width), F32),
            jax.ShapeDtypeStruct((rows, width), BF16),
            jax.ShapeDtypeStruct((1, width), F32),
        ),
        in_specs=[whole, whole, whole, line, whole, pl.BlockSpec((2 * HEAD_DIM, width), lambda h: (h, 0))],
        out_specs=(pl.BlockSpec((2, rows, HEAD_DIM), lambda h: (h, 0, 0)), whole, whole, line),
        compiler_params=params(),
        cost_estimate=cost(2 * rows * width * width, 2 * width * width),
    )(d_shared, d_routed, hidden, gain, cot, w_out)


SLOTS = 48
SLOT_ROWS = 16 * SLOTS


def chosen(meta, block, expert):
    weights = meta[block, expert : expert + 1]
    member = weights > 0
    before = lax.broadcasted_iota(jnp.int32, (128, 128), 0) < lax.broadcasted_iota(jnp.int32, (128, 128), 1)
    line = jnp.broadcast_to(jnp.where(member, 1.0, 0.0).astype(BF16), (8, 128))
    place_in = dot(line, jnp.where(before, 1.0, 0.0).astype(BF16))[0:1]
    slot = lax.broadcasted_iota(jnp.int32, (SLOTS, 128), 0).astype(F32)
    one_hot = jnp.where((slot == place_in) & member, 1.0, 0.0)
    return one_hot, jnp.sum(one_hot * weights, axis=1, keepdims=True)


def experts_kernel(
    meta, rows, cots, gate_w, up_w, down_w, out, d_rows, gate_grad, up_grad, down_grad,
    slot_rows, slot_cots, slot_out, slot_back, weight, act, d_gate, d_up, in_buf, out_buf, in_sem, out_sem,
):
    step = pl.program_id(0)

    def fetch(block, slot):
        return [
            pltpu.make_async_copy(rows.at[block], in_buf.at[slot, 0], in_sem.at[slot, 0]),
            pltpu.make_async_copy(cots.at[block, 0:128], in_buf.at[slot, 1], in_sem.at[slot, 1]),
        ]

    @pl.when(step == 0)
    def _():
        for copy in fetch(0, 0):
            copy.start()

        @pl.loop(0, 16)
        def _(block):
            slot = block % 2

            @pl.when(block < 15)
            def _():
                for copy in fetch(block + 1, 1 - slot):
                    copy.start()

            for copy in fetch(block, slot):
                copy.wait()
            picks = [chosen(meta, block, expert) for expert in range(2)]
            both = jnp.concatenate([pick[0] for pick in picks], axis=0).astype(BF16)
            column = jnp.concatenate([pick[1] for pick in picks], axis=0)
            picked = dot(both, in_buf[slot, 0]).astype(BF16)
            scaled = (dot(both, in_buf[slot, 1]) * column).astype(BF16)
            at = pl.ds(pl.multiple_of(block * SLOTS, SLOTS), SLOTS)
            for expert in range(2):
                part = slice(expert * SLOTS, (expert + 1) * SLOTS)
                slot_rows[expert, at] = picked[part]
                slot_cots[expert, at] = scaled[part]
                weight[expert, at] = jnp.broadcast_to(column[part], (SLOTS, 128))

    tile = 256

    @pl.loop(0, SLOT_ROWS // tile)
    def _(index):
        at = pl.ds(pl.multiple_of(index * tile, tile), tile)
        value, upstream = slot_rows[step, at], slot_cots[step, at]
        gate, up = dot(value, gate_w[0]), dot(value, up_w[0])
        silu, slope = gated(gate, up)
        activated = (silu * up).astype(BF16)
        act[at] = activated
        produced = dot(activated, down_w[0]).astype(BF16).astype(F32)
        slot_out[step, at] = (produced * weight[step, at][:, 0:1]).astype(BF16)
        d_act = dot_nt(upstream, down_w[0])
        gate_back = (d_act * up * slope).astype(BF16)
        up_back = (d_act * silu).astype(BF16)
        d_gate[at] = gate_back
        d_up[at] = up_back
        slot_back[step, at] = (dot_nt(gate_back, gate_w[0]) + dot_nt(up_back, up_w[0])).astype(BF16)

    @pl.loop(0, 5)
    def _(index):
        at = pl.ds(pl.multiple_of(index * 256, 256), 256)
        part = slot_rows[step, :, at]
        gate_grad[0, at] = dot_tn(part, d_gate[...]).astype(BF16)
        up_grad[0, at] = dot_tn(part, d_up[...]).astype(BF16)

    @pl.loop(0, 7)
    def _(index):
        at = pl.ds(pl.multiple_of(index * 128, 128), 128)
        down_grad[0, at] = dot_tn(act[:, at], slot_cots[step]).astype(BF16)

    @pl.when(step == 1)
    def _():
        def store(block, slot):
            return [
                pltpu.make_async_copy(out_buf.at[slot, 0], out.at[block], out_sem.at[slot, 0]),
                pltpu.make_async_copy(out_buf.at[slot, 1], d_rows.at[block], out_sem.at[slot, 1]),
            ]

        @pl.loop(0, 16)
        def _(block):
            slot = block % 2

            @pl.when(block >= 2)
            def _():
                for copy in store(block - 2, slot):
                    copy.wait()

            both = jnp.concatenate([chosen(meta, block, expert)[0] for expert in range(2)], axis=0).astype(BF16)
            at = pl.ds(pl.multiple_of(block * SLOTS, SLOTS), SLOTS)
            for index, source in enumerate((slot_out, slot_back)):
                value = jnp.concatenate([source[0, at], source[1, at]], axis=0)
                out_buf[slot, index] = dot_tn(both, value).astype(BF16)
            for copy in store(block, slot):
                copy.start()

        for block in (14, 15):
            for copy in store(block, block % 2):
                copy.wait()


def experts(meta, rows, cots, gate_w, up_w, down_w):
    width, hidden = gate_w.shape[1:]
    wide = pl.BlockSpec((1, width, hidden), lambda e: (e, 0, 0))
    deep = pl.BlockSpec((1, hidden, width), lambda e: (e, 0, 0))
    return pl.pallas_call(
        experts_kernel,
        name="experts",
        grid=(2,),
        out_shape=(
            jax.ShapeDtypeStruct((16, 128, width), BF16),
            jax.ShapeDtypeStruct((16, 128, width), BF16),
            jax.ShapeDtypeStruct(gate_w.shape, BF16),
            jax.ShapeDtypeStruct(up_w.shape, BF16),
            jax.ShapeDtypeStruct(down_w.shape, BF16),
        ),
        in_specs=[pl.BlockSpec((16, 2, 128), lambda e: (0, 0, 0)), ANYWHERE, ANYWHERE, wide, wide, deep],
        out_specs=(ANYWHERE, ANYWHERE, wide, wide, deep),
        scratch_shapes=[
            pltpu.VMEM((2, SLOT_ROWS, width), BF16),
            pltpu.VMEM((2, SLOT_ROWS, width), BF16),
            pltpu.VMEM((2, SLOT_ROWS, width), BF16),
            pltpu.VMEM((2, SLOT_ROWS, width), BF16),
            pltpu.VMEM((2, SLOT_ROWS, 128), F32),
            pltpu.VMEM((SLOT_ROWS, hidden), BF16),
            pltpu.VMEM((SLOT_ROWS, hidden), BF16),
            pltpu.VMEM((SLOT_ROWS, hidden), BF16),
            pltpu.VMEM((2, 2, 128, width), BF16),
            pltpu.VMEM((2, 2, 128, width), BF16),
            pltpu.SemaphoreType.DMA((2, 2)),
            pltpu.SemaphoreType.DMA((2, 2)),
        ],
        compiler_params=params(),
        cost_estimate=cost(18 * 2 * SLOT_ROWS * width * hidden, 6 * 10**7),
    )(meta, rows, cots, gate_w, up_w, down_w)


def with_weights(cot, routes, route_gates, row_live):
    routed = routes[:, :, None] == jnp.arange(32, dtype=jnp.int32)[None, None, :]
    live = jnp.where(row_live, 1.0, 0.0)
    table = jnp.sum(jnp.where(routed, route_gates[:, :, None], 0.0), axis=1) * live[:, None]
    table = table.T
    high = table.astype(BF16)
    low = (table - high.astype(F32)).astype(BF16)
    lines = jnp.stack([high, low]).reshape(4, 16, 128).transpose(1, 0, 2).reshape(16, 512)
    return jnp.concatenate([cot, jnp.pad(lines, ((0, 0), (0, 768)))], axis=0)


def read_weights(cots, exp):
    lines = cots[:, 128:144, :512].reshape(16, 16, 2, 2, 128).transpose(2, 0, 3, 1, 4).reshape(2, 16, 32, 128)
    mine = lax.dynamic_slice_in_dim(lines, exp * 2, 2, axis=2)
    return mine[0].astype(F32) + mine[1].astype(F32)


def local(
    tokens,
    lengths,
    routes,
    route_gates,
    attn_gain,
    w_query,
    w_key,
    w_value,
    w_out,
    ffn_gain,
    shared_gate,
    shared_up,
    shared_down,
    expert_gate,
    expert_up,
    expert_down,
    cotangent,
):
    resident, cot = tokens[0], cotangent[0]
    rows = resident.shape[0]
    attn_line, ffn_line = attn_gain[None], ffn_gain[None]
    ctx = lax.axis_index("ctx")
    positions = ctx * rows + jnp.arange(rows, dtype=jnp.int32)
    all_cos, all_sin = turn_tables(jnp.arange(8 * rows, dtype=jnp.int32))
    cos = lax.dynamic_slice_in_dim(all_cos, ctx * rows, rows)
    sin = lax.dynamic_slice_in_dim(all_sin, ctx * rows, rows)
    sent_cot = with_weights(cot, routes[0], route_gates[0], positions < lengths[0])

    qkv, normed_one = project(resident, attn_line, w_query, w_key, w_value, cos, sin)
    mixed, heads, cots = attend(qkv, lengths, sent_cot, 1)
    hidden, normed_two = after(mixed, w_out, resident, ffn_line)
    every_row = gather_rows(normed_two, 2)
    act, d_shared_gate, d_shared_up, shared_out, d_shared = shared_expert(
        normed_two, cot, shared_gate, shared_up, shared_down
    )
    parts, d_parts, gate_term, up_term, down_term = experts(
        read_weights(cots, lax.axis_index("exp")), every_row, cots, expert_gate, expert_up, expert_down
    )
    d_routed = scatter_rows(d_parts, 3)
    d_mixed, d_hidden, d_attn, ffn_term = middle(d_shared, d_routed, hidden, ffn_line, cot, w_out)
    d_qkv, routed = attend_back(d_mixed, heads, lengths, all_cos, -all_sin, parts, 4)
    block_out = hidden + shared_out + routed
    input_grad, attn_term = project_back(d_qkv, w_query, w_key, w_value, resident, attn_line, d_hidden)
    dense = reduce_dense(
        normed_one, mixed, normed_two, act, d_qkv, d_attn, d_shared_gate, d_shared_up, cot, attn_term[0], ffn_term[0]
    )
    packed, expert_gate_grad, expert_up_grad, expert_down_grad = sum_grads(dense, gate_term, up_term, down_term)
    return (
        block_out[None],
        input_grad[None],
        *unpack_dense(packed),
        expert_gate_grad,
        expert_up_grad,
        expert_down_grad,
    )


def solution(mesh):
    in_specs = (
        P("exp", "ctx", None),
        P("exp"),
        P("exp", "ctx", None),
        P("exp", "ctx", None),
        P(),
        P(),
        P(),
        P(),
        P(),
        P(),
        P(),
        P(),
        P(),
        P("exp", None, None),
        P("exp", None, None),
        P("exp", None, None),
        P("exp", "ctx", None),
    )
    out_specs = (
        P("exp", "ctx", None),
        P("exp", "ctx", None),
        P(("ctx", "exp")),
        P(("ctx", "exp"), None),
        P(("ctx", "exp"), None),
        P(("ctx", "exp"), None),
        P(("ctx", "exp"), None),
        P(("ctx", "exp")),
        P(("ctx", "exp"), None),
        P(("ctx", "exp"), None),
        P(("ctx", "exp"), None),
        P("exp", "ctx", None),
        P("exp", "ctx", None),
        P("exp", "ctx", None),
    )
    return jax.shard_map(local, mesh=mesh, in_specs=in_specs, out_specs=out_specs, check_vma=False)
```

```python
import functools
import math

import jax
import jax.numpy as jnp
import numpy as np
from jax import lax
from jax.experimental import pallas as pl
from jax.experimental.pallas import tpu as pltpu
from jax.sharding import PartitionSpec as P

MESH = pl.DeviceIdType.MESH
HEAD_DIM = 128
VMEM_LIMIT = 60 * 2**20
F32, BF16 = jnp.float32, jnp.bfloat16


def place():
    ctx, exp = lax.axis_index("ctx"), lax.axis_index("exp")
    return ctx // 2, (exp // 8) * 2 + ctx % 2, (exp // 2) % 4, exp % 2


def device(x, y, z, core):
    return (x * 2 + y % 2, (y // 2) * 8 + z * 2 + core)


def greet(devices):
    barrier = pltpu.get_barrier_semaphore()
    for target in devices:
        pl.semaphore_signal(barrier, inc=1, device_id=target, device_id_type=MESH)
    pl.semaphore_wait(barrier, len(devices))


class Copies:
    def __init__(self, send, recv, own):
        self.send, self.recv, self.own = send, recv, own
        self.remotes, self.locals = 0, 0
        self.started = []

    def remote(self, src, dst, target):
        index = self.remotes
        self.remotes += 1
        copy = pltpu.make_async_remote_copy(
            src_ref=src,
            dst_ref=dst,
            send_sem=self.send.at[index],
            recv_sem=self.recv.at[index],
            device_id=target,
            device_id_type=MESH,
        )
        copy.start()
        self.started.append(copy)
        return copy

    def local(self, src, dst):
        index = self.locals
        self.locals += 1
        copy = pltpu.make_async_copy(src, dst, self.own.at[index])
        copy.start()
        return copy

    def drain(self):
        for copy in self.started:
            copy.wait_send()


def each(shape, body):
    @pl.loop(0, math.prod(shape))
    def _(step):
        index = []
        for size in reversed(shape):
            index.append(step % size)
            step = step // size
        body(tuple(reversed(index)))


def add_into(out, shape, *terms, rows=None):
    def body(index):
        total = terms[0][index].astype(F32)
        for term in terms[1:]:
            total = total + term[index].astype(F32)
        out[index] = total.astype(out.dtype)

    if rows is None:
        each(shape, body)
    else:
        step, count = rows
        each(shape + (count,), lambda i: body(i[:-1] + (pl.ds(pl.multiple_of(i[-1] * step, step), step),)))


class RingSum:
    def __init__(self, copies, me, right, left, part, land, work, add, resident=None):
        self.copies, self.right, self.left, self.land, self.work, self.add = copies, right, left, land, work, add
        self.part = part
        self.after, self.before, across = (me + 1) % 4, (me + 3) % 4, (me + 2) % 4
        self.one = copies.remote(part(across, 0), land.at[0], right)
        self.two = copies.remote(part(across, 1), land.at[1], left)
        sources = [part(self.after, 0), part(self.before, 1), part(me, 0), part(me, 1)]
        if resident is None:
            self.loads = [copies.local(source, work.at[i]) for i, source in enumerate(sources)]
            self.own = [work.at[i] for i in range(4)]
        else:
            self.loads = []
            self.own = sources

    def raw(self):
        self.three = self.copies.remote(self.part(self.after, 1), self.land.at[2], self.right)
        self.four = self.copies.remote(self.part(self.before, 0), self.land.at[4], self.left)

    def forward(self):
        for load in self.loads:
            load.wait()
        self.one.wait_recv()
        self.add(self.land.at[0], self.land.at[0], self.own[0])
        self.five = self.copies.remote(self.land.at[0], self.land.at[3], self.right)
        self.two.wait_recv()
        self.add(self.land.at[1], self.land.at[1], self.own[1])
        self.six = self.copies.remote(self.land.at[1], self.land.at[5], self.left)

    def finish(self, outs):
        for copy in (self.three, self.four, self.five, self.six):
            copy.wait_recv()
        self.add(outs[0], self.own[2], self.land.at[3], self.land.at[4])
        self.add(outs[1], self.own[3], self.land.at[2], self.land.at[5])


GRAD_REMOTES = 5 * 6 + 3 + 3 * 5 + 3 * 4 + 6 + 3 * 4 + 7
GRAD_LOCALS = 5 * 4


def add_blocks(shape):
    def add(out, *terms):
        add_into(out, shape, *terms)

    return add


def half_rows(which, size):
    return pl.ds(pl.multiple_of(which * size, size), size)


def order(y):
    return (y % 2) * 2 + y // 2


def grads_kernel(
    late, first, second, gains, up, down_one, down, dense_out, up_out, down_out,
    z_land, z_work, s_land, s_work, y_land, y_sum, x_land, u_land, u_work, v_land, v_sum, w_land,
    t_land, t_work, tz_land, t_sum, tx_land,
    gx_land, gx_sum, gy_land, total, stage, final_land, up_other, one_other, d_land, d_work, d_other, send, recv, own,
):
    x, y, z, core = place()
    y_half, y_low = y // 2, y % 2
    spot = z * 2 + core
    x_peers = [device((x + d) % 4, y, z, core) for d in (1, 2, 3)]
    y_peers = [device(x, (y + d) % 4, z, core) for d in (1, 2, 3)]
    z_peers = [device(x, y, (z + d) % 4, core) for d in (1, 2, 3)]
    spot_peers = [device(x, y, ((spot + d) % 8) // 2, (spot + d) % 2) for d in range(1, 8)]
    pair = device(x, y_half * 2 + 1 - y_low, z, core)
    greet(x_peers + y_peers + spot_peers)
    copies = Copies(send, recv, own)

    def direct(part, me, land, peers):
        return [copies.remote(part((me + d) % 4), land.at[d - 1], peers[d - 1]) for d in (1, 2, 3)]

    def arrived(arrivals):
        for copy in arrivals:
            copy.wait_recv()

    rings = [
        RingSum(
            copies, z, z_peers[0], z_peers[2], lambda c, h: late.at[c, h],
            z_land, z_work, add_blocks((4, 4)),
        ),
        RingSum(
            copies, z, z_peers[0], z_peers[2], lambda c, h: late.at[c, 2, 2 * h : 2 * h + 2],
            s_land, s_work, add_blocks((2, 4)),
        ),
    ]
    rings[0].raw()
    side = RingSum(
        copies, x, x_peers[0], x_peers[2], lambda c, h: late.at[2 * h : 2 * h + 2, 3, c],
        u_land, u_work, add_blocks((2, 4)),
    )
    gain_x = direct(lambda c: gains.at[c], x, gx_land, x_peers)

    def down_add(out, *terms):
        add_into(out, (), *terms, rows=(16, 7))

    downs = RingSum(
        copies, x, x_peers[0], x_peers[2],
        lambda c, h: down.at[half_rows(2 * c + h, 112)], d_land, d_work, down_add,
    )
    side.raw()
    tall = RingSum(
        copies, y, y_peers[0], y_peers[2], lambda c, h: late.at[2 * h : 2 * h + 2, 4, :, order(c)],
        t_land, t_work, add_blocks((2, 4)),
    )
    tall.raw()
    y_copies = {
        0: direct(lambda c: first.at[:, :, order(c)], y, y_land.at[0], y_peers),
        1: direct(lambda c: second.at[:, order(c)], y, y_land.at[1, :, 0], y_peers),
    }
    swap_up = copies.remote(up.at[:, half_rows(1 - y_low, 160)], up_other, pair)
    swap_one = copies.remote(down_one.at[half_rows(1 - y_low, 112)], one_other, pair)

    side.forward()
    downs.raw()
    tall.forward()
    rings[0].forward()
    rings[1].raw()
    arrived(gain_x)
    gx_sum[...] = gains[x] + gx_land[0] + gx_land[1] + gx_land[2]
    gain_y = direct(lambda c: gx_sum.at[order(c)], y, gy_land, y_peers)
    downs.forward()
    rings[1].forward()

    x_copies = {}

    def start_x(t, mine):
        arrived(y_copies[t])
        add_into(y_sum.at[t], (2, 4), mine, y_land.at[t, 0], y_land.at[t, 1], y_land.at[t, 2])
        x_copies[t] = direct(lambda c: y_sum.at[t, :, c], x, x_land.at[t], x_peers)

    def start_x_one(t, mine):
        arrived(y_copies[t])
        add_into(y_sum.at[t, 0], (4,), mine, y_land.at[t, 0, 0], y_land.at[t, 1, 0], y_land.at[t, 2, 0])
        x_copies[t] = direct(lambda c: y_sum.at[t, 0, c], x, x_land.at[t, :, 0], x_peers)

    side.finish([u_work.at[2], u_work.at[3]])
    side_z = direct(lambda c: u_work.at[2 + c // 2, c % 2], z, v_land, z_peers)
    tall.finish([t_work.at[2], t_work.at[3]])
    tall_z = direct(lambda c: t_work.at[2 + c // 2, c % 2], z, tz_land, z_peers)
    start_x(0, first.at[:, :, order(y)])
    start_x_one(1, second.at[:, order(y)])
    rings[0].finish([z_work.at[2], z_work.at[3]])
    y_copies[2] = direct(lambda c: z_work.at[2:4, :, order(c)], y, y_land.at[2], y_peers)
    arrived(side_z)
    add_into(v_sum, (4,), u_work.at[2 + z // 2, z % 2], v_land.at[0], v_land.at[1], v_land.at[2])
    side_y = direct(lambda c: v_sum.at[order(c)], y, w_land, y_peers)
    arrived(tall_z)
    add_into(t_sum, (4,), t_work.at[2 + z // 2, z % 2], tz_land.at[0], tz_land.at[1], tz_land.at[2])
    tall_x = direct(lambda c: t_sum.at[c], x, tx_land, x_peers)
    downs.finish([d_work.at[2], d_work.at[3]])
    swap_down = copies.remote(d_work.at[2 + 1 - y_low], d_other, pair)
    start_x(2, z_work.at[2:4, :, order(y)])
    rings[1].finish([s_work.at[2], s_work.at[3]])
    y_copies[3] = [
        copies.remote(
            s_work.at[2 + half, :, order((y + d) % 4)], y_land.at[3, d - 1, 0, 2 * half : 2 * half + 2], y_peers[d - 1]
        )
        for half in range(2)
        for d in (1, 2, 3)
    ]
    swap_up.wait_recv()
    add_into(up_out, (2,), up.at[:, half_rows(y_low, 160)], up_other, rows=(16, 10))
    swap_one.wait_recv()
    add_into(down_out.at[0], (), down_one.at[half_rows(y_low, 112)], one_other, rows=(16, 7))
    arrived(y_copies[3])
    for half in range(2):
        pair_at = slice(2 * half, 2 * half + 2)
        add_into(
            y_sum.at[3, 0, pair_at], (2,), s_work.at[2 + half, :, order(y)],
            y_land.at[3, 0, 0, pair_at], y_land.at[3, 1, 0, pair_at], y_land.at[3, 2, 0, pair_at],
        )
    x_copies[3] = direct(lambda c: y_sum.at[3, 0, c], x, x_land.at[3, :, 0], x_peers)

    def summed(panel, first_part, land, *index):
        value = first_part.astype(F32)
        for d in range(3):
            value = value + land[(d,) + index].astype(F32)
        total[panel, 0:80] = value
        total[panel, 80:96] = jnp.zeros((16, 128), F32)

    arrived(gain_y)
    lines = gx_sum[order(y)] + gy_land[0] + gy_land[1] + gy_land[2]
    arrived(side_y)
    summed(6, v_sum[order(y)], w_land)
    arrived(tall_x)
    summed(7, t_sum[x], tx_land)
    for t, panels in ((0, (0, 1)), (1, (2,)), (2, (3, 4)), (3, (5,))):
        arrived(x_copies[t])
        for half, panel in enumerate(panels):
            summed(panel, y_sum[t, half, x], x_land.at[t], half)
    for j in range(8):
        for panel in range(8):
            stage[j, panel] = total[panel, 10 * j : 10 * j + 16]
        stage[j, 0, 10:11] = lines[j : j + 1]
    finals = [
        copies.remote(stage.at[(spot + d) % 8], final_land.at[d], spot_peers[d - 1]) for d in range(1, 8)
    ]
    swap_down.wait_recv()
    add_into(down_out.at[1], (), d_work.at[2 + y_low], d_other, rows=(16, 7))
    dense_out[spot] = stage[spot]
    for d, copy in enumerate(finals):
        copy.wait_recv()
        dense_out[(spot + 7 - d) % 8] = final_land[d + 1]
    copies.drain()


def sum_grads(late, first, second, gains, up, down_one, down):
    scratch = [
        pltpu.VMEM((6, 4, 4, 80, 128), BF16),
        pltpu.VMEM((4, 4, 4, 80, 128), BF16),
        pltpu.VMEM((6, 2, 4, 80, 128), BF16),
        pltpu.VMEM((4, 2, 4, 80, 128), BF16),
        pltpu.VMEM((4, 3, 2, 4, 80, 128), BF16),
        pltpu.VMEM((4, 2, 4, 80, 128), BF16),
        pltpu.VMEM((4, 3, 2, 80, 128), BF16),
        pltpu.VMEM((6, 2, 4, 80, 128), BF16),
        pltpu.VMEM((4, 2, 4, 80, 128), BF16),
        pltpu.VMEM((3, 4, 80, 128), BF16),
        pltpu.VMEM((4, 80, 128), BF16),
        pltpu.VMEM((3, 80, 128), BF16),
        pltpu.VMEM((6, 2, 4, 80, 128), BF16),
        pltpu.VMEM((4, 2, 4, 80, 128), BF16),
        pltpu.VMEM((3, 4, 80, 128), BF16),
        pltpu.VMEM((4, 80, 128), BF16),
        pltpu.VMEM((3, 80, 128), BF16),
        pltpu.VMEM((3, 4, 8, 128), F32),
        pltpu.VMEM((4, 8, 128), F32),
        pltpu.VMEM((3, 8, 128), F32),
        pltpu.VMEM((8, 96, 128), F32),
        pltpu.VMEM((8, 8, 16, 128), F32),
        pltpu.VMEM((8, 8, 16, 128), F32),
        pltpu.VMEM((2, 160, 896), BF16),
        pltpu.VMEM((112, 1280), BF16),
        pltpu.VMEM((6, 112, 1280), BF16),
        pltpu.VMEM((4, 112, 1280), BF16),
        pltpu.VMEM((112, 1280), BF16),
        pltpu.SemaphoreType.DMA((GRAD_REMOTES,)),
        pltpu.SemaphoreType.DMA((GRAD_REMOTES,)),
        pltpu.SemaphoreType.DMA((GRAD_LOCALS,)),
    ]
    return pl.pallas_call(
        grads_kernel,
        name="sum_grads",
        out_shape=(
            jax.ShapeDtypeStruct((8, 8, 16, 128), F32),
            jax.ShapeDtypeStruct((2, 160, 896), F32),
            jax.ShapeDtypeStruct((2, 112, 1280), F32),
        ),
        in_specs=[ANYWHERE, VMEM, VMEM, VMEM, VMEM, VMEM, ANYWHERE],
        out_specs=(VMEM,) * 3,
        scratch_shapes=scratch,
        compiler_params=params(0),
        cost_estimate=cost(10**8, 4 * 10**8),
    )(late.reshape(4, 5, 4, 4, 80, 128), first, second, gains, up, down_one, down)


def dense_kernel(groups, *refs):
    count = len(groups)
    sources, (out, right) = refs[: 4 * count], refs[4 * count :]
    core = lax.axis_index("exp") % 2

    @pl.when(pl.program_id(0) == 0)
    def _():
        for group, (first, last) in enumerate(groups):
            lanes = (last - first) * 128
            for half in range(2):
                source = sources[4 * group + 2 + half]
                if len(source.shape) == 3:
                    part = source[core]
                else:
                    part = source[:, pl.ds(pl.multiple_of(core * lanes, 128), lanes)]
                right[128 * half : 128 * half + 128, first * 128 : last * 128] = part

    for group, (first, last) in enumerate(groups):
        left = jnp.concatenate([sources[4 * group][...], sources[4 * group + 1][...]], axis=0)
        value = dot_tn(left, right[:, first * 128 : last * 128])
        for panel in range(first, last):
            out[panel] = value[:, (panel - first) * 128 : (panel - first + 1) * 128].astype(BF16)


def dense_terms(name, groups, sources):
    tile = 256
    panels = groups[-1][1]
    column = pl.BlockSpec((128, tile), lambda m: (0, m))
    specs = []
    for index, source in enumerate(sources):
        if index % 4 < 2:
            specs.append(column)
        else:
            specs.append(pl.BlockSpec(source.shape, lambda m, rank=source.ndim: (0,) * rank))
    return pl.pallas_call(
        functools.partial(dense_kernel, groups),
        name=name,
        grid=(1280 // tile,),
        out_shape=jax.ShapeDtypeStruct((panels, 1280, 128), BF16),
        in_specs=specs,
        out_specs=pl.BlockSpec((panels, tile, 128), lambda m: (0, m, 0)),
        scratch_shapes=[pltpu.VMEM((256, panels * 128), BF16)],
        compiler_params=params(),
        cost_estimate=cost(2 * 256 * 1280 * panels * 128, panels * 500000),
    )(*sources)


def partner(value):
    return lax.ppermute(value, "exp", [(e, e ^ 1) for e in range(lax.axis_size("exp"))])


def with_partner(*values):
    return [part for value in values for part in (value, partner(value))]


def gain_lines(attn_term, ffn_term):
    both = jnp.concatenate([attn_term, ffn_term]).reshape(2, 16, 8, 10).transpose(1, 2, 0, 3).reshape(4, 4, 8, 20)
    return jnp.pad(both, ((0, 0), (0, 0), (0, 0), (0, 108)))


def unpack_dense(packed):
    parts = packed.reshape(4, 2, 8, 16, 128)
    gains = jnp.sum(parts[:, :, 0, 10, :20], axis=(0, 1))
    parts = parts[:, :, :, :10].transpose(1, 0, 2, 3, 4)
    early = jnp.concatenate([parts[:, :, 0:2].reshape(2, 8, 10, 128), parts[:, :, 2]], axis=1)
    late = parts[:, :, 3:8].reshape(2, 20, 10, 128)

    def joined(panels):
        return panels.transpose(2, 0, 1, 3).reshape(10, -1)

    qkv, out = joined(late[:, 0:15]), joined(late[:, 15:20])
    gate_up, down = joined(early[:, 0:7]), joined(early[:, 7:12])[:7]
    return (
        gains[:10], qkv[:, :1280], qkv[:, 1280:2560], qkv[:, 2560:], out,
        gains[10:], gate_up[:, :896], gate_up[:, 896:], down,
    )


VMEM = pl.BlockSpec(memory_space=pltpu.VMEM)
ANYWHERE = pl.BlockSpec(memory_space=pl.ANY)
SMEM = pl.BlockSpec(memory_space=pltpu.SMEM)
EXTRA_HEAD = {8: 0, 9: 5}
SCALE = HEAD_DIM ** (-0.5)


def params(collective_id=None):
    if collective_id is None:
        return pltpu.CompilerParams(vmem_limit_bytes=VMEM_LIMIT)
    return pltpu.CompilerParams(
        collective_id=collective_id, has_side_effects=True, vmem_limit_bytes=VMEM_LIMIT
    )


def cost(flops, bytes_accessed):
    return pl.CostEstimate(flops=int(flops), bytes_accessed=int(bytes_accessed), transcendentals=0)


def dot(left, right):
    return jnp.dot(left, right, preferred_element_type=F32)


def dot_nt(left, right):
    return lax.dot_general(left, right, (((1,), (1,)), ((), ())), preferred_element_type=F32)


def dot_tn(left, right):
    return lax.dot_general(left, right, (((0,), (0,)), ((), ())), preferred_element_type=F32)


def normed(values, gain):
    return values * lax.rsqrt(jnp.mean(values * values, axis=-1, keepdims=True) + 1e-06) * gain


def normed_back(values, gain, upstream):
    factor = lax.rsqrt(jnp.mean(values * values, axis=-1, keepdims=True) + 1e-06)
    scaled = upstream * gain
    inner = jnp.mean(scaled * values, axis=-1, keepdims=True)
    term = jnp.sum(upstream * values * factor, axis=0, keepdims=True)
    return factor * scaled - values * factor * factor * factor * inner, term


def turned(values, cos, sin):
    return values * cos + pltpu.roll(values, HEAD_DIM // 2, 1) * sin


def turn_tables(count):
    half = HEAD_DIM // 2
    frequency = np.exp(np.arange(half, dtype=np.float32) * np.float32(-2.0 * math.log(10000.0) / HEAD_DIM))
    angle = np.arange(count, dtype=np.float32)[:, None] * frequency[None, :]
    cos, sin = np.cos(angle), np.sin(angle)
    return np.concatenate([cos, cos], axis=1), np.concatenate([-sin, sin], axis=1)


def project_kernel(tokens, gain, w_query, w_key, w_value, cos, sin, qkv, normed_one):
    @pl.when(pl.program_id(0) == 0)
    def _():
        normed_one[...] = normed(tokens[...].astype(F32), gain[...]).astype(BF16)

    rows = normed_one[...]
    query, key, value = dot(rows, w_query[...]), dot(rows, w_key[...]), dot(rows, w_value[...])
    for head in range(2):
        lanes = slice(head * HEAD_DIM, (head + 1) * HEAD_DIM)
        qkv[head, 0] = turned(query[:, lanes], cos[...], sin[...]).astype(BF16)
        qkv[head, 1] = turned(key[:, lanes], cos[...], sin[...]).astype(BF16)
        qkv[head, 2] = value[:, lanes].astype(BF16)


def project(tokens, gain, w_query, w_key, w_value, cos, sin):
    rows, width = tokens.shape
    whole = pl.BlockSpec((rows, width), lambda h: (0, 0))
    table = pl.BlockSpec((rows, HEAD_DIM), lambda h: (0, 0))
    columns = pl.BlockSpec((width, 2 * HEAD_DIM), lambda h: (0, h))
    return pl.pallas_call(
        project_kernel,
        name="project",
        grid=(5,),
        out_shape=(
            jax.ShapeDtypeStruct((10, 3, rows, HEAD_DIM), BF16),
            jax.ShapeDtypeStruct((rows, width), BF16),
        ),
        in_specs=[whole, pl.BlockSpec((1, width), lambda h: (0, 0)), columns, columns, columns, table, table],
        out_specs=(pl.BlockSpec((2, 3, rows, HEAD_DIM), lambda h: (h, 0, 0, 0)), whole),
        compiler_params=params(),
        cost_estimate=cost(6 * rows * width * width, 6 * width * width),
    )(tokens, gain, w_query, w_key, w_value, cos, sin)


def rank(y_half, z, core):
    return y_half * 8 + z * 2 + core


class Gather:
    def __init__(self, copies, where, src, out, cut):
        x, y, z, core = where
        self.copies, self.out, self.cut = copies, out, cut
        self.y_half, self.z, self.core = y // 2, z, core
        self.pair = device(x, y, z, 1 - core)
        self.across = device(x, (y + 2) % 4, z, core)
        self.right, self.left = device(x, y, (z + 1) % 4, core), device(x, y, (z + 3) % 4, core)
        me = rank(self.y_half, z, core)
        self.mine = copies.local(src, out.at[me])
        self.over = copies.remote(src, out.at[me], self.across)
        self.to_right = copies.remote(src, out.at[me], self.right)
        self.to_left = copies.remote(src, out.at[me], self.left)
        self.pairs = [copies.remote(src, out.at[me], self.pair)]

    def shard(self, other, dz):
        y_half = 1 - self.y_half if other else self.y_half
        return rank(y_half, (self.z + dz + 4) % 4, self.core)

    def half(self, index, which):
        rows = self.out.shape[1]
        return self.out.at[index, 0 : self.cut] if which == 0 else self.out.at[index, self.cut : rows]

    def send(self, ref, target):
        return self.copies.remote(ref, ref, target)

    def share(self, ref):
        self.pairs.append(self.send(ref, self.pair))

    def second(self):
        self.to_right.wait_recv()
        index = self.shard(False, -1)
        self.on_right = self.send(self.half(index, 0), self.right)
        self.share(self.out.at[index])
        self.to_left.wait_recv()
        index = self.shard(False, 1)
        self.on_left = self.send(self.half(index, 1), self.left)
        self.share(self.out.at[index])
        self.over.wait_recv()
        index = self.shard(True, 0)
        self.far_right = self.send(self.out.at[index], self.right)
        self.far_left = self.send(self.out.at[index], self.left)
        self.share(self.out.at[index])

    def third(self):
        self.far_right.wait_recv()
        index = self.shard(True, -1)
        self.far_on_right = self.send(self.half(index, 0), self.right)
        self.share(self.out.at[index])
        self.far_left.wait_recv()
        index = self.shard(True, 1)
        self.far_on_left = self.send(self.half(index, 1), self.left)
        self.share(self.out.at[index])

    def last(self):
        for copies, other in (((self.on_right, self.on_left), False), ((self.far_on_right, self.far_on_left), True)):
            for which, copy in enumerate(copies):
                copy.wait_recv()
                self.share(self.half(self.shard(other, 2), which))
        for copy in self.pairs:
            copy.wait_recv()
        self.mine.wait()


GATHER_REMOTES = 3 + 2 + 2 + 2 + 8 + 2


def exp_peers(where):
    x, y, z, core = where
    return [
        device(x, y, z, 1 - core),
        device(x, (y + 2) % 4, z, core),
        device(x, y, (z + 1) % 4, core),
        device(x, y, (z + 3) % 4, core),
    ]


def gather_kernel(
    rows, cot, meta, cots, gate_w, up_w, down_w,
    slot_rows, slot_cots, weight, act, d_gates, shared_out, d_shared,
    every, cots_in, gate, up, down, filled_rows, filled_cots, lines, send, recv, own, load_sem, keep_sem,
):
    where = place()
    loads = [
        pltpu.make_async_copy(src, dst, load_sem.at[i])
        for i, (src, dst) in enumerate(((gate_w, gate), (up_w, up), (down_w, down), (cots, cots_in)))
    ]
    for load in loads:
        load.start()
    greet(exp_peers(where))
    copies = Copies(send, recv, own)
    gather = Gather(copies, where, rows, every, rows.shape[0] // 2)
    lines[...] = slot_lines(meta).reshape(16, 2, 128)
    shared_out[...] = jnp.zeros_like(shared_out)
    d_shared[...] = jnp.zeros_like(d_shared)

    def shared(first, last):
        @pl.loop(first, last)
        def _(step):
            at = pl.ds(pl.multiple_of(step * 128, 128), 128)
            value = rows[...]
            gate_pre, up_pre = dot(value, gate[:, at]), dot(value, up[:, at])
            silu, slope = gated(gate_pre, up_pre)
            activated = (silu * up_pre).astype(BF16)
            act[:, at] = activated
            shared_out[...] += dot(activated, down[at])
            d_act = dot_nt(cot[...], down[at])
            gate_back = (d_act * up_pre * slope).astype(BF16)
            up_back = (d_act * silu).astype(BF16)
            d_gates[0, :, at] = gate_back
            d_gates[1, :, at] = up_back
            d_shared[...] += dot_nt(gate_back, gate[:, at]) + dot_nt(up_back, up[:, at])

    def hot(block):
        slot = lax.broadcasted_iota(jnp.int32, (SLOTS, 128), 0).astype(F32)
        return [jnp.where(slot == lines[block, e : e + 1], 1.0, 0.0) for e in range(2)]

    def fill(block, source, out, column=None):
        value = dot(jnp.concatenate(hot(block), axis=0).astype(BF16), source)
        if column is not None:
            value = value * column
        value = value.astype(BF16)
        at = pl.ds(pl.multiple_of(block * SLOTS, SLOTS), SLOTS)
        for expert in range(2):
            out[expert, at] = value[expert * SLOTS : (expert + 1) * SLOTS]

    def fill_cots(first, last):
        @pl.loop(first, last)
        def _(block):
            column = jnp.concatenate(
                [jnp.sum(one * meta[block, e : e + 1], axis=1, keepdims=True) for e, one in enumerate(hot(block))], axis=0
            )
            at = pl.ds(pl.multiple_of(block * SLOTS, SLOTS), SLOTS)
            for expert in range(2):
                weight[expert, at] = jnp.broadcast_to(column[expert * SLOTS : (expert + 1) * SLOTS], (SLOTS, 128))
            fill(block, cots_in[block, 0:128], filled_cots, column)

    for load in loads[:3]:
        load.wait()
    shared(0, 4)
    gather.second()
    shared(4, 7)
    loads[3].wait()
    fill_cots(0, 8)
    gather.third()
    fill_cots(8, 16)
    keep_cots = pltpu.make_async_copy(filled_cots, slot_cots, keep_sem.at[0])
    keep_cots.start()
    gather.last()

    @pl.loop(0, 16)
    def _(block):
        fill(block, every[block], filled_rows)

    keep_rows = pltpu.make_async_copy(filled_rows, slot_rows, keep_sem.at[1])
    keep_rows.start()
    copies.drain()
    keep_cots.wait()
    keep_rows.wait()


def gather_rows(rows, cot, meta, cots, gate_w, up_w, down_w, collective_id):
    count, width = rows.shape
    hidden = gate_w.shape[1]
    return pl.pallas_call(
        gather_kernel,
        name="gather_rows",
        out_shape=(
            jax.ShapeDtypeStruct((2, SLOT_ROWS, width), BF16),
            jax.ShapeDtypeStruct((2, SLOT_ROWS, width), BF16),
            jax.ShapeDtypeStruct((2, SLOT_ROWS, 128), F32),
            jax.ShapeDtypeStruct((count, hidden), BF16),
            jax.ShapeDtypeStruct((2, count, hidden), BF16),
            jax.ShapeDtypeStruct((count, width), F32),
            jax.ShapeDtypeStruct((count, width), F32),
        ),
        in_specs=[VMEM, VMEM, VMEM] + [ANYWHERE] * 4,
        out_specs=(ANYWHERE, ANYWHERE) + (VMEM,) * 5,
        scratch_shapes=[
            pltpu.VMEM((16, count, width), BF16),
            pltpu.VMEM(cots.shape, BF16),
            pltpu.VMEM(gate_w.shape, BF16),
            pltpu.VMEM(up_w.shape, BF16),
            pltpu.VMEM(down_w.shape, BF16),
            pltpu.VMEM((2, SLOT_ROWS, width), BF16),
            pltpu.VMEM((2, SLOT_ROWS, width), BF16),
            pltpu.VMEM((16, 2, 128), F32),
            pltpu.SemaphoreType.DMA((GATHER_REMOTES,)),
            pltpu.SemaphoreType.DMA((GATHER_REMOTES,)),
            pltpu.SemaphoreType.DMA((1,)),
            pltpu.SemaphoreType.DMA((4,)),
            pltpu.SemaphoreType.DMA((2,)),
        ],
        compiler_params=params(collective_id),
        cost_estimate=cost(10**9, 6 * 10**7),
    )(rows, cot, meta, cots, gate_w, up_w, down_w)


class Scatter:
    def __init__(self, copies, where, parts, pair_land, work, ring_land, far_land, y_land):
        x, y, z, core = where
        self.copies, self.work, self.pair_land = copies, work, pair_land
        self.ring_land, self.far_land, self.y_land = ring_land, far_land, y_land
        self.across = device(x, (y + 2) % 4, z, core)
        self.right, self.left = device(x, y, (z + 1) % 4, core), device(x, y, (z + 3) % 4, core)
        pair = device(x, y, z, 1 - core)
        self.pairs, self.loads = {}, {}
        for slot in ((0, 2), (1, 2), (0, 1), (0, 3), (1, 1), (1, 3), (0, 0), (1, 0)):
            y_half = 1 - y // 2 if slot[0] == 0 else y // 2
            at = (z + slot[1]) % 4
            self.pairs[slot] = copies.remote(parts.at[rank(y_half, at, 1 - core)], pair_land.at[slot], pair)
            self.loads[slot] = copies.local(parts.at[rank(y_half, at, core)], work.at[slot])

    def merge(self, slot):
        self.loads[slot].wait()
        self.pairs[slot].wait_recv()
        rows_add(self.work.at[slot], 0, 128, self.work.at[slot], self.pair_land.at[slot])

    def first(self):
        self.ring = {}
        for far in range(2):
            self.merge((far, 2))
            self.ring[far] = (
                self.copies.remote(self.work.at[far, 2, 0:64], self.ring_land.at[far, 0], self.right),
                self.copies.remote(self.work.at[far, 2, 64:128], self.ring_land.at[far, 1], self.left),
            )
        for far in range(2):
            self.merge((far, 1))
            self.merge((far, 3))
            self.merge((far, 0))

    def second(self):
        self.final = {}
        for far in range(2):
            self.ring[far][0].wait_recv()
            rows_add(self.work.at[far, 1, 0:64], 0, 64, self.work.at[far, 1, 0:64], self.ring_land.at[far, 0])
            to_right = self.copies.remote(self.work.at[far, 1], self.far_land.at[far, 0], self.right)
            self.ring[far][1].wait_recv()
            rows_add(self.work.at[far, 3, 64:128], 0, 64, self.work.at[far, 3, 64:128], self.ring_land.at[far, 1])
            to_left = self.copies.remote(self.work.at[far, 3], self.far_land.at[far, 1], self.left)
            self.final[far] = (to_right, to_left)

    def third(self):
        for far in range(2):
            for copy in self.final[far]:
                copy.wait_recv()
            rows_add(self.work.at[far, 0], 0, 128, self.work.at[far, 0], self.far_land.at[far, 0], self.far_land.at[far, 1])
            if far == 0:
                self.over = self.copies.remote(self.work.at[0, 0], self.y_land, self.across)

    def last(self, out):
        self.over.wait_recv()
        rows_add(out, 0, 128, self.work.at[1, 0], self.y_land)


def rows_add(out, first, rows, *terms):
    @pl.loop(0, rows // 16)
    def _(step):
        at = pl.ds(pl.multiple_of(step * 16, 16), 16)
        value = terms[0][at].astype(F32)
        for term in terms[1:]:
            value = value + term[at].astype(F32)
        out[at] = value.astype(out.dtype)


SCATTER_REMOTES, SCATTER_LOCALS = 8 + 4 + 4 + 1, 8
SCATTER_SCRATCH = [
    pltpu.VMEM((2, 4, 128, 1280), BF16),
    pltpu.VMEM((2, 4, 128, 1280), BF16),
    pltpu.VMEM((2, 2, 64, 1280), BF16),
    pltpu.VMEM((2, 2, 128, 1280), BF16),
    pltpu.VMEM((128, 1280), BF16),
]


ROW_PART = (16, 20)


def matrix_add(out, *terms):
    add_into(out, (), *terms, rows=ROW_PART)


def matrix_ring(copies, x, peers, flat, land, work=None):
    def part(chunk, half):
        return flat.at[half, pl.ds(pl.multiple_of(chunk * 320, 320), 320)]

    return RingSum(copies, x, peers[0], peers[1], part, land, work, matrix_add, resident=True if work is None else None)


def scatter_kernel(
    parts, rows_in, cots_in, act_in, back_in, early, d_shared, hidden_rows, gain, cot, w_out_in,
    gate_sum, up_out, down_out, first, d_mixed, d_hidden, d_attn, gain_term,
    a, b, c, d, e, rows, cots, act, back, gate, up, down, land, z_land, z_work, w_out, d_routed,
    send, recv, own, load_sem, keep_sem,
):
    where = place()
    x, y, z, core = where
    x_peers = [device((x + 1) % 4, y, z, core), device((x + 3) % 4, y, z, core)]
    loads = [
        pltpu.make_async_copy(src, dst, load_sem.at[i])
        for i, (src, dst) in enumerate(
            ((rows_in, rows), (back_in, back), (act_in.at[1], act), (cots_in.at[1], cots), (w_out_in, w_out))
        )
    ]
    for load in loads:
        load.start()
    greet(exp_peers(where) + x_peers)
    copies = Copies(send, recv, own)
    scatter = Scatter(copies, where, parts, a, b, c, d, e)
    hidden = act.shape[1]
    dense = RingSum(
        copies, z, device(x, y, (z + 1) % 4, core), device(x, y, (z + 3) % 4, core),
        lambda chunk, half: early.at[2 * chunk + half], z_land, z_work, add_blocks((4, 4)),
    )
    loads[0].wait()
    loads[1].wait()

    def term(dst, lanes):
        @pl.loop(0, 10)
        def _(index):
            expert = index // 5
            at = pl.ds(pl.multiple_of((index % 5) * 256, 256), 256)
            dst[expert, at] = dot_tn(rows[expert, :, at], back[expert, :, lanes]).astype(BF16)

    term(gate, slice(0, hidden))
    ring = matrix_ring(copies, x, x_peers, gate, land)
    ring.raw()
    scatter.first()
    term(up, slice(hidden, 2 * hidden))
    keep_up = pltpu.make_async_copy(up, up_out, keep_sem.at[0])
    keep_up.start()
    scatter.second()
    loads[2].wait()
    loads[3].wait()

    @pl.loop(0, hidden // 128)
    def _(index):
        at = pl.ds(pl.multiple_of(index * 128, 128), 128)
        down[at] = dot_tn(act[:, at], cots[...]).astype(BF16)

    keep_down = pltpu.make_async_copy(down, down_out, keep_sem.at[1])
    keep_down.start()
    dense.raw()
    dense.forward()
    ring.forward()
    scatter.third()
    scatter.last(d_routed)
    grad, term_sum = normed_back(hidden_rows[...], gain[...], d_shared[...] + d_routed[...])
    whole = cot[...].astype(F32) + grad
    d_hidden[...] = whole
    d_attn[...] = whole.astype(BF16)
    gain_term[...] = term_sum
    loads[4].wait()

    @pl.loop(0, 5)
    def _(index):
        value = dot_nt(d_attn[...], w_out[pl.ds(pl.multiple_of(index * 256, 256), 256)]).astype(BF16)
        d_mixed[2 * index] = value[:, :HEAD_DIM]
        d_mixed[2 * index + 1] = value[:, HEAD_DIM:]

    dense.finish([first.at[0], first.at[1]])
    ring.finish([gate_sum.at[0], gate_sum.at[1]])
    copies.drain()
    keep_up.wait()
    keep_down.wait()


def scatter_rows(parts, kept_rows, kept_cots, kept_act, kept_back, early, d_shared, hidden_rows, gain, cot, w_out, collective_id):
    width, hidden = kept_rows.shape[2], kept_act.shape[2]
    count = cot.shape[0]
    return pl.pallas_call(
        scatter_kernel,
        name="scatter_rows",
        out_shape=(
            jax.ShapeDtypeStruct((2, 320, hidden), BF16),
            jax.ShapeDtypeStruct((2, width, hidden), BF16),
            jax.ShapeDtypeStruct((hidden, width), BF16),
            jax.ShapeDtypeStruct((2, 4, 4, 80, 128), BF16),
            jax.ShapeDtypeStruct((10, count, HEAD_DIM), BF16),
            jax.ShapeDtypeStruct((count, width), F32),
            jax.ShapeDtypeStruct((count, width), BF16),
            jax.ShapeDtypeStruct((1, width), F32),
        ),
        in_specs=[ANYWHERE] * 6 + [VMEM] * 4 + [ANYWHERE],
        out_specs=(VMEM, ANYWHERE, ANYWHERE, VMEM, VMEM, VMEM, VMEM, VMEM),
        scratch_shapes=SCATTER_SCRATCH
        + [
            pltpu.VMEM(kept_rows.shape, BF16),
            pltpu.VMEM(kept_cots.shape[1:], BF16),
            pltpu.VMEM(kept_act.shape[1:], BF16),
            pltpu.VMEM(kept_back.shape, BF16),
            pltpu.VMEM((2, width, hidden), BF16),
            pltpu.VMEM((2, width, hidden), BF16),
            pltpu.VMEM((hidden, width), BF16),
            pltpu.VMEM((6, 320, hidden), BF16),
            pltpu.VMEM((6, 4, 4, 80, 128), BF16),
            pltpu.VMEM((4, 4, 4, 80, 128), BF16),
            pltpu.VMEM(w_out.shape, BF16),
            pltpu.VMEM((count, width), F32),
            pltpu.SemaphoreType.DMA((SCATTER_REMOTES + 12,)),
            pltpu.SemaphoreType.DMA((SCATTER_REMOTES + 12,)),
            pltpu.SemaphoreType.DMA((SCATTER_LOCALS + 4,)),
            pltpu.SemaphoreType.DMA((5,)),
            pltpu.SemaphoreType.DMA((2,)),
        ],
        compiler_params=params(collective_id),
        cost_estimate=cost(10**10, 10**8),
    )(
        parts, kept_rows, kept_cots, kept_act, kept_back, early.reshape(12, 4, 4, 80, 128),
        d_shared, hidden_rows, gain, cot, w_out,
    )


def ctx_device(ctx):
    return (ctx, lax.axis_index("exp"))


def owns_extra(ctx):
    return (ctx == EXTRA_HEAD[8]) | (ctx == EXTRA_HEAD[9])


def extra_head(ctx):
    return 8 + (ctx == EXTRA_HEAD[9]).astype(jnp.int32)


class Exchange:
    def __init__(self, send, recv, own):
        self.send, self.recv, self.own = send, recv, own
        self.ctx = lax.axis_index("ctx")

    def copy(self, src, dst, slot, d):
        return pltpu.make_async_remote_copy(
            src_ref=src,
            dst_ref=dst,
            send_sem=self.send.at[slot, d],
            recv_sem=self.recv.at[slot, d],
            device_id=ctx_device((self.ctx + d) % 8),
            device_id_type=MESH,
        )


def to_owners(exchange, block, land):
    ctx = exchange.ctx
    for d in range(1, 8):
        peer = (ctx + d) % 8
        exchange.copy(block(peer), land(0, ctx), 0, d).start()

        @pl.when(owns_extra(peer))
        def _():
            exchange.copy(block(extra_head(peer)), land(1, ctx), 1, d).start()

    mine = [pltpu.make_async_copy(block(ctx), land(0, ctx), exchange.own.at[0])]
    mine[0].start()
    extra = pltpu.make_async_copy(block(extra_head(ctx)), land(1, ctx), exchange.own.at[1])

    @pl.when(owns_extra(ctx))
    def _():
        extra.start()

    def arrived():
        mine[0].wait()
        for d in range(1, 8):
            exchange.copy(block(0), land(0, ctx), 0, d).wait_recv()

        @pl.when(owns_extra(ctx))
        def _():
            extra.wait()
            for d in range(1, 8):
                exchange.copy(block(0), land(1, ctx), 1, d).wait_recv()

    def sent():
        for d in range(1, 8):
            exchange.copy(block(0), land(0, ctx), 0, d).wait_send()

            @pl.when(owns_extra((ctx + d) % 8))
            def _():
                exchange.copy(block(0), land(1, ctx), 1, d).wait_send()

    return arrived, sent


class Home:
    def __init__(self, exchange, block, land):
        self.exchange, self.block, self.land = exchange, block, land
        self.ctx = exchange.ctx

    def head(self, slot):
        return self.ctx if slot == 0 else extra_head(self.ctx)

    def start(self, slot):
        for d in range(1, 8):
            self.exchange.copy(self.block(slot, (self.ctx + d) % 8), self.land(self.head(slot)), slot, d).start()
        self.mine(slot).start()

    def mine(self, slot):
        return pltpu.make_async_copy(
            self.block(slot, self.ctx), self.land(self.head(slot)), self.exchange.own.at[slot]
        )

    def finish(self):
        self.mine(0).wait()
        for d in range(1, 8):
            copy = self.exchange.copy(self.block(0, 0), self.land(0), 0, d)
            copy.wait_send()
            copy.wait_recv()

            @pl.when(owns_extra((self.ctx + 8 - d) % 8))
            def _():
                self.exchange.copy(self.block(1, 0), self.land(0), 1, d).wait_recv()

        @pl.when(owns_extra(self.ctx))
        def _():
            self.mine(1).wait()
            for d in range(1, 8):
                self.exchange.copy(self.block(1, 0), self.land(0), 1, d).wait_send()


def attend_kernel(qkv, length, cot, mixed, heads, cots, land, result, home, s1, r1, o1, s2, r2, o2, s3, r3, o3):
    where = place()
    ctx = lax.axis_index("ctx")
    greet([ctx_device((ctx + d) % 8) for d in range(1, 8)] + exp_peers(where))
    arrived, sent = to_owners(
        Exchange(s1, r1, o1), lambda head: qkv.at[head], lambda slot, c: land.at[slot, :, c]
    )
    copies = Copies(s3, r3, o3)
    gather = Gather(copies, where, cot, cots, 80)
    back = Home(Exchange(s2, r2, o2), lambda slot, c: result.at[slot, c], lambda head: home.at[head])
    keep = pltpu.make_async_copy(land, heads, o3.at[1])

    def run(slot, blocks):
        for block in blocks:
            width = (block + 1) * 128
            query = land[slot, 0, block]
            key = land[slot, 1, 0 : block + 1].reshape(width, HEAD_DIM)
            value = land[slot, 2, 0 : block + 1].reshape(width, HEAD_DIM)
            row = lax.broadcasted_iota(jnp.int32, (width, 128), 0)
            column = lax.broadcasted_iota(jnp.int32, (width, 128), 1) + block * 128
            scores = jnp.where(
                (row <= column) & (row < length[0]), dot_nt(key, query) * SCALE, -1e30
            )
            weights = jnp.exp(scores - jnp.max(scores, axis=0, keepdims=True))
            probs = weights * (1.0 / jnp.sum(weights, axis=0, keepdims=True))
            result[slot, block] = dot_tn(probs.astype(BF16), value).astype(BF16)

    arrived()
    run(0, range(8))
    back.start(0)
    gather.second()

    @pl.when(owns_extra(ctx))
    def _():
        run(1, range(8))
        back.start(1)

    gather.third()

    @pl.when(jnp.logical_not(owns_extra(ctx)))
    def _():
        land[1] = jnp.zeros_like(land[1])

    keep.start()
    gather.last()
    back.finish()
    for head in range(10):
        mixed[:, head * HEAD_DIM : (head + 1) * HEAD_DIM] = home[head]
    sent()
    keep.wait()
    copies.drain()


def exchange_semaphores():
    return [
        pltpu.SemaphoreType.DMA((2, 8)),
        pltpu.SemaphoreType.DMA((2, 8)),
        pltpu.SemaphoreType.DMA((2,)),
    ]


def attend(qkv, length, cot, collective_id):
    return pl.pallas_call(
        attend_kernel,
        name="attend",
        out_shape=(
            jax.ShapeDtypeStruct((128, 1280), BF16),
            jax.ShapeDtypeStruct((2, 3, 8, 128, HEAD_DIM), BF16),
            jax.ShapeDtypeStruct((16,) + cot.shape, BF16),
        ),
        in_specs=[ANYWHERE, SMEM, ANYWHERE],
        out_specs=(VMEM, ANYWHERE, ANYWHERE),
        scratch_shapes=[
            pltpu.VMEM((2, 3, 8, 128, HEAD_DIM), BF16),
            pltpu.VMEM((2, 8, 128, HEAD_DIM), BF16),
            pltpu.VMEM((10, 128, HEAD_DIM), BF16),
        ]
        + exchange_semaphores()
        + exchange_semaphores()
        + [
            pltpu.SemaphoreType.DMA((GATHER_REMOTES,)),
            pltpu.SemaphoreType.DMA((GATHER_REMOTES,)),
            pltpu.SemaphoreType.DMA((2,)),
        ],
        compiler_params=params(collective_id),
        cost_estimate=cost(10**9, 10**8),
    )(qkv, length, cot)


def attend_back_kernel(
    d_mixed, heads, length, cos, sin, parts, up, gate, early, d_attn, normed_one, mixed, tokens, gain, d_hidden,
    w_query_in, w_key_in, w_value_in, input_grad, gain_term, routed, up_sum, gate_out, second, late,
    land, kept, d_key, d_value, result, home, a, b, c, d, e, up_land, up_work, gate_other, z_land, z_work,
    pair_rows, d_qkv, pair_qkv, right, out_right, panels, weights, total,
    s1, r1, o1, s2, r2, o2, s3, r3, o3, load_sem, late_sem,
):
    where = place()
    x, y, z, core = where
    ctx = lax.axis_index("ctx")
    x_peers = [device((x + 1) % 4, y, z, core), device((x + 3) % 4, y, z, core)]
    loads = [
        pltpu.make_async_copy(src, dst, load_sem.at[i])
        for i, (src, dst) in enumerate(
            ((heads, kept), (w_query_in, weights.at[0]), (w_key_in, weights.at[1]), (w_value_in, weights.at[2]))
        )
    ]
    for load in loads:
        load.start()
    greet([ctx_device((ctx + step) % 8) for step in range(1, 8)] + exp_peers(where))
    arrived, sent = to_owners(
        Exchange(s1, r1, o1), lambda head: d_mixed.at[head], lambda slot, at: land.at[slot, at]
    )
    copies = Copies(s3, r3, o3)
    scatter = Scatter(copies, where, parts, a, b, c, d, e)
    back = Home(Exchange(s2, r2, o2), lambda slot, at: result.at[slot, :, at], lambda head: home.at[:, head])
    ring = matrix_ring(copies, x, x_peers, up, up_land, up_work)
    y_low = y % 2
    swap = copies.remote(
        gate.at[:, half_rows(1 - y_low, 160)], gate_other, device(x, (y // 2) * 2 + 1 - y_low, z, core)
    )
    dense = RingSum(
        copies, z, device(x, y, (z + 1) % 4, core), device(x, y, (z + 3) % 4, core),
        lambda chunk, half: early.at[8 + chunk, 2 * half : 2 * half + 2], z_land, z_work, add_blocks((2, 4)),
    )
    pair = device(x, y, z, 1 - core)
    pairs = [copies.remote(src, pair_rows.at[i], pair) for i, src in enumerate((normed_one, mixed, d_attn))]
    loads[0].wait()
    arrived()

    def run(slot):
        d_key[...] = jnp.zeros_like(d_key)
        d_value[...] = jnp.zeros_like(d_value)
        for block in range(8):
            width = (block + 1) * 128
            query, upstream = kept[slot, 0, block], land[slot, block]
            key = kept[slot, 1, 0 : block + 1].reshape(width, HEAD_DIM)
            value = kept[slot, 2, 0 : block + 1].reshape(width, HEAD_DIM)
            row = lax.broadcasted_iota(jnp.int32, (width, 128), 0)
            column = lax.broadcasted_iota(jnp.int32, (width, 128), 1) + block * 128
            scores = jnp.where(
                (row <= column) & (row < length[0]), dot_nt(key, query) * SCALE, -1e30
            )
            weight = jnp.exp(scores - jnp.max(scores, axis=0, keepdims=True))
            probs = weight * (1.0 / jnp.sum(weight, axis=0, keepdims=True))
            d_probs = dot_nt(value, upstream)
            delta = jnp.sum(probs * d_probs, axis=0, keepdims=True)
            d_scores = (probs * (d_probs - delta)).astype(BF16)
            rows = slice(block * 128, block * 128 + 128)
            d_query = dot_tn(d_scores, key) * SCALE
            result[slot, 0, block] = turned(d_query, cos[rows], sin[rows]).astype(BF16)
            d_key[0:width] += dot(d_scores, query)
            d_value[0:width] += dot(probs.astype(BF16), upstream)
        for block in range(8):
            rows = slice(block * 128, block * 128 + 128)
            result[slot, 1, block] = turned(d_key[rows] * SCALE, cos[rows], sin[rows]).astype(BF16)
            result[slot, 2, block] = d_value[rows].astype(BF16)
        back.start(slot)

    run(0)
    scatter.first()

    @pl.when(owns_extra(ctx))
    def _():
        run(1)

    ring.raw()
    scatter.second()
    dense.raw()
    dense.forward()
    ring.forward()
    scatter.third()
    back.finish()
    for head in range(10):
        for kind in range(3):
            at = kind * 1280 + head * HEAD_DIM
            d_qkv[:, at : at + HEAD_DIM] = home[kind, head]
    swap_qkv = copies.remote(d_qkv, pair_qkv, pair)
    for load in loads[1:]:
        load.wait()

    @pl.loop(0, 5)
    def _(index):
        at = pl.ds(pl.multiple_of(index * 256, 256), 256)
        value = dot_nt(d_qkv[:, 0:1280], weights[0, at])
        value += dot_nt(d_qkv[:, 1280:2560], weights[1, at])
        value += dot_nt(d_qkv[:, 2560:3840], weights[2, at])
        total[:, at] = value

    grad, term = normed_back(tokens[...].astype(F32), gain[...], total[...])
    input_grad[...] = d_hidden[...] + grad
    gain_term[...] = term

    for copy in pairs:
        copy.wait_recv()
    swap_qkv.wait_recv()
    at = pl.ds(pl.multiple_of(core * 1920, 128), 1920)
    right[0:128] = d_qkv[:, at]
    right[128:256] = pair_qkv[:, at]
    at = pl.ds(pl.multiple_of(core * 640, 128), 640)
    out_right[0:128] = d_attn[:, at]
    out_right[128:256] = pair_rows[2, :, at]

    def store(index):
        rows = pl.ds(pl.multiple_of(index * 256, 256), 256)
        return pltpu.make_async_copy(panels.at[index], late.at[:, rows], late_sem.at[index])

    @pl.loop(0, 5)
    def _(index):
        at = pl.ds(pl.multiple_of(index * 256, 256), 256)
        value = dot_tn(jnp.concatenate([normed_one[:, at], pair_rows[0, :, at]], axis=0), right[...])
        for panel in range(15):
            panels[index, panel] = value[:, panel * 128 : panel * 128 + 128].astype(BF16)
        value = dot_tn(jnp.concatenate([mixed[:, at], pair_rows[1, :, at]], axis=0), out_right[...])
        for panel in range(5):
            panels[index, 15 + panel] = value[:, panel * 128 : panel * 128 + 128].astype(BF16)
        store(index).start()

    scatter.last(routed)
    dense.finish([second.at[0:2], second.at[2:4]])
    swap.wait_recv()
    add_into(gate_out, (2,), gate.at[:, half_rows(y_low, 160)], gate_other, rows=(16, 10))
    ring.finish([up_sum.at[0], up_sum.at[1]])
    sent()
    copies.drain()
    for index in range(5):
        store(index).wait()


def attend_back(
    d_mixed, heads, length, cos, sin, parts, up, gate, early, d_attn, normed_one, mixed, tokens, gain, d_hidden,
    w_query, w_key, w_value, collective_id,
):
    rows, width = tokens.shape
    hidden = up.shape[2]
    return pl.pallas_call(
        attend_back_kernel,
        name="attend_back",
        out_shape=(
            jax.ShapeDtypeStruct((rows, width), F32),
            jax.ShapeDtypeStruct((1, width), F32),
            jax.ShapeDtypeStruct((rows, width), F32),
            jax.ShapeDtypeStruct((2, 320, hidden), BF16),
            jax.ShapeDtypeStruct((2, 160, hidden), F32),
            jax.ShapeDtypeStruct((4, 4, 80, 128), BF16),
            jax.ShapeDtypeStruct((20, width, 128), BF16),
        ),
        in_specs=[ANYWHERE, ANYWHERE, SMEM, VMEM, VMEM, ANYWHERE, ANYWHERE, VMEM, ANYWHERE] + [VMEM] * 6 + [ANYWHERE] * 3,
        out_specs=(VMEM,) * 6 + (ANYWHERE,),
        scratch_shapes=[
            pltpu.VMEM((2, 8, 128, HEAD_DIM), BF16),
            pltpu.VMEM((2, 3, 8, 128, HEAD_DIM), BF16),
            pltpu.VMEM((1024, HEAD_DIM), F32),
            pltpu.VMEM((1024, HEAD_DIM), F32),
            pltpu.VMEM((2, 3, 8, 128, HEAD_DIM), BF16),
            pltpu.VMEM((3, 10, 128, HEAD_DIM), BF16),
        ]
        + SCATTER_SCRATCH
        + [
            pltpu.VMEM((6, 320, hidden), BF16),
            pltpu.VMEM((4, 320, hidden), BF16),
            pltpu.VMEM((2, 160, hidden), BF16),
            pltpu.VMEM((6, 2, 4, 80, 128), BF16),
            pltpu.VMEM((4, 2, 4, 80, 128), BF16),
            pltpu.VMEM((3, rows, width), BF16),
            pltpu.VMEM((rows, 3 * width), BF16),
            pltpu.VMEM((rows, 3 * width), BF16),
            pltpu.VMEM((2 * rows, 1920), BF16),
            pltpu.VMEM((2 * rows, 640), BF16),
            pltpu.VMEM((5, 20, 256, 128), BF16),
            pltpu.VMEM((3, width, width), BF16),
            pltpu.VMEM((rows, width), F32),
        ]
        + exchange_semaphores()
        + exchange_semaphores()
        + [
            pltpu.SemaphoreType.DMA((SCATTER_REMOTES + 17,)),
            pltpu.SemaphoreType.DMA((SCATTER_REMOTES + 17,)),
            pltpu.SemaphoreType.DMA((SCATTER_LOCALS + 8,)),
            pltpu.SemaphoreType.DMA((4,)),
            pltpu.SemaphoreType.DMA((5,)),
        ],
        compiler_params=params(collective_id),
        cost_estimate=cost(10**9, 10**8),
    )(
        d_mixed, heads, length, cos, sin, parts, up, gate, early.reshape(12, 4, 4, 80, 128), d_attn, normed_one, mixed,
        tokens, gain, d_hidden, w_query, w_key, w_value,
    )


def after_kernel(mixed, w_out, tokens, gain, hidden, normed_two):
    step = pl.program_id(0)
    size = w_out.shape[1]
    at = pl.ds(pl.multiple_of(step * size, size), size)
    hidden[:, at] = tokens[:, at].astype(F32) + dot(mixed[...], w_out[...])

    @pl.when(step == pl.num_programs(0) - 1)
    def _():
        normed_two[...] = normed(hidden[...], gain[...]).astype(BF16)


def after(mixed, w_out, tokens, gain):
    rows, width = tokens.shape
    whole = pl.BlockSpec((rows, width), lambda h: (0, 0))
    return pl.pallas_call(
        after_kernel,
        name="after",
        grid=(5,),
        out_shape=(jax.ShapeDtypeStruct((rows, width), F32), jax.ShapeDtypeStruct((rows, width), BF16)),
        in_specs=[whole, pl.BlockSpec((width, 256), lambda h: (0, h)), whole, pl.BlockSpec((1, width), lambda h: (0, 0))],
        out_specs=(whole, whole),
        compiler_params=params(),
        cost_estimate=cost(2 * rows * width * width, 2 * width * width),
    )(mixed, w_out, tokens, gain)


def gated(gate, up):
    squash = 1.0 / (1.0 + jnp.exp(-gate))
    silu = gate * squash
    slope = squash * (1.0 + gate * (1.0 - squash))
    return silu, slope


SLOTS = 48
DEPTH = 4
SLOT_ROWS = 16 * SLOTS


def slot_lines(meta):
    member = jnp.where(meta[...].reshape(32, 128) > 0, 1.0, 0.0)
    before = lax.broadcasted_iota(jnp.int32, (128, 128), 0) < lax.broadcasted_iota(jnp.int32, (128, 128), 1)
    count = dot(member.astype(BF16), jnp.where(before, 1.0, 0.0).astype(BF16))
    return jnp.where(member > 0, count, -1.0)


def experts_kernel(
    meta, weight, rows, cots, gate_w, up_w, down_w, out, d_rows, kept_act, kept_back, down_sum,
    gate_up, down, slot_rows, slot_cots, slot_out, slot_back, lines, columns, act, back,
    out_buf, term, land, in_sem, out_sem, weight_sem, keep_sem, send, recv, own,
):
    hidden = down.shape[1]
    x, y, z, core = place()
    x_peers = [device((x + 1) % 4, y, z, core), device((x + 3) % 4, y, z, core)]

    def load(expert):
        return [
            pltpu.make_async_copy(gate_w.at[expert], gate_up.at[expert, :, 0:hidden], weight_sem.at[expert, 0]),
            pltpu.make_async_copy(up_w.at[expert], gate_up.at[expert, :, hidden : 2 * hidden], weight_sem.at[expert, 1]),
            pltpu.make_async_copy(down_w.at[expert], down.at[expert], weight_sem.at[expert, 2]),
        ]

    def fetch(expert):
        return [
            pltpu.make_async_copy(rows.at[expert], slot_rows.at[expert], in_sem.at[expert, 0]),
            pltpu.make_async_copy(cots.at[expert], slot_cots.at[expert], in_sem.at[expert, 1]),
        ]

    for expert in range(2):
        for copy in fetch(expert) + load(expert):
            copy.start()
    greet(x_peers)
    copies = Copies(send, recv, own)
    lines[...] = slot_lines(meta).reshape(16, 2, 128)
    columns[...] = jnp.concatenate([lines[...].reshape(32, 128), jnp.zeros((96, 128), F32)], axis=0).T
    keeps = [
        pltpu.make_async_copy(src, dst, keep_sem.at[i])
        for i, (src, dst) in enumerate(((act, kept_act), (back, kept_back)))
    ]

    def main(expert):
        for copy in fetch(expert) + load(expert):
            copy.wait()

        tile = 256

        @pl.loop(0, SLOT_ROWS // tile)
        def _(index):
            at = pl.ds(pl.multiple_of(index * tile, tile), tile)
            both = dot(slot_rows[expert, at], gate_up[expert])
            gate, up = both[:, :hidden], both[:, hidden:]
            silu, slope = gated(gate, up)
            activated = (silu * up).astype(BF16)
            act[expert, at] = activated
            produced = dot(activated, down[expert]).astype(BF16).astype(F32)
            slot_out[expert, at] = (produced * weight[expert, at][:, 0:1]).astype(BF16)
            d_act = dot_nt(slot_cots[expert, at], down[expert])
            back[expert, at, 0:hidden] = (d_act * up * slope).astype(BF16)
            back[expert, at, hidden : 2 * hidden] = (d_act * silu).astype(BF16)
            slot_back[expert, at] = dot_nt(back[expert, at], gate_up[expert]).astype(BF16)

    main(0)

    @pl.loop(0, hidden // 128)
    def _(index):
        at = pl.ds(pl.multiple_of(index * 128, 128), 128)
        term[at] = dot_tn(act[0, :, at], slot_cots[0]).astype(BF16)

    def part(chunk, half):
        return term.at[pl.ds(pl.multiple_of(chunk * 224 + half * 112, 112), 112)]

    def add(out, *terms):
        add_into(out, (), *terms, rows=(16, 7))

    ring = RingSum(copies, x, x_peers[0], x_peers[1], part, land, None, add, resident=True)
    ring.raw()
    main(1)
    ring.forward()
    keeps[0].start()
    keeps[1].start()

    def store(block):
        slot = block % DEPTH
        return [
            pltpu.make_async_copy(out_buf.at[slot, 0], out.at[block], out_sem.at[slot, 0]),
            pltpu.make_async_copy(out_buf.at[slot, 1], d_rows.at[block], out_sem.at[slot, 1]),
        ]

    lane = lax.broadcasted_iota(jnp.int32, (128, 2 * SLOTS), 1).astype(F32)
    for block in range(16):
        slot = block % DEPTH
        first, second = columns[:, 2 * block : 2 * block + 1], columns[:, 2 * block + 1 : 2 * block + 2]
        hit = ((lane < SLOTS) & (lane == first)) | ((lane >= SLOTS) & (lane - SLOTS == second))
        both = jnp.where(hit, 1.0, 0.0).astype(BF16)
        if block >= DEPTH:
            for copy in store(block - DEPTH):
                copy.wait()
        at = slice(block * SLOTS, (block + 1) * SLOTS)
        for index, source in enumerate((slot_out, slot_back)):
            value = jnp.concatenate([source[0, at], source[1, at]], axis=0)
            out_buf[slot, index] = dot(both, value).astype(BF16)
        for copy in store(block):
            copy.start()
    for block in range(16 - DEPTH, 16):
        for copy in store(block):
            copy.wait()
    ring.finish([down_sum.at[0:112], down_sum.at[112:224]])
    copies.drain()
    for copy in keeps:
        copy.wait()


def experts(meta, weight, rows, cots, gate_w, up_w, down_w, collective_id):
    width, hidden = gate_w.shape[1:]
    return pl.pallas_call(
        experts_kernel,
        name="experts",
        out_shape=(
            jax.ShapeDtypeStruct((16, 128, width), BF16),
            jax.ShapeDtypeStruct((16, 128, width), BF16),
            jax.ShapeDtypeStruct((2, SLOT_ROWS, hidden), BF16),
            jax.ShapeDtypeStruct((2, SLOT_ROWS, 2 * hidden), BF16),
            jax.ShapeDtypeStruct((hidden // 4, width), BF16),
        ),
        in_specs=[VMEM, VMEM] + [ANYWHERE] * 5,
        out_specs=[ANYWHERE] * 4 + [VMEM],
        scratch_shapes=[
            pltpu.VMEM((2, width, 2 * hidden), BF16),
            pltpu.VMEM((2, hidden, width), BF16),
            pltpu.VMEM((2, SLOT_ROWS, width), BF16),
            pltpu.VMEM((2, SLOT_ROWS, width), BF16),
            pltpu.VMEM((2, SLOT_ROWS, width), BF16),
            pltpu.VMEM((2, SLOT_ROWS, width), BF16),
            pltpu.VMEM((16, 2, 128), F32),
            pltpu.VMEM((128, 128), F32),
            pltpu.VMEM((2, SLOT_ROWS, hidden), BF16),
            pltpu.VMEM((2, SLOT_ROWS, 2 * hidden), BF16),
            pltpu.VMEM((DEPTH, 2, 128, width), BF16),
            pltpu.VMEM((hidden, width), BF16),
            pltpu.VMEM((6, hidden // 8, width), BF16),
            pltpu.SemaphoreType.DMA((2, 2)),
            pltpu.SemaphoreType.DMA((DEPTH, 2)),
            pltpu.SemaphoreType.DMA((2, 3)),
            pltpu.SemaphoreType.DMA((2,)),
            pltpu.SemaphoreType.DMA((6,)),
            pltpu.SemaphoreType.DMA((6,)),
            pltpu.SemaphoreType.DMA((1,)),
        ],
        compiler_params=params(collective_id),
        cost_estimate=cost(12 * 2 * SLOT_ROWS * width * hidden, 6 * 10**7),
    )(meta, weight, rows, cots, gate_w, up_w, down_w)


def with_weights(cot, routes, route_gates, row_live):
    routed = routes[:, :, None] == jnp.arange(32, dtype=jnp.int32)[None, None, :]
    live = jnp.where(row_live, 1.0, 0.0)
    table = jnp.sum(jnp.where(routed, route_gates[:, :, None], 0.0), axis=1) * live[:, None]
    table = table.T
    high = table.astype(BF16)
    low = (table - high.astype(F32)).astype(BF16)
    lines = jnp.stack([high, low]).reshape(4, 16, 128).transpose(1, 0, 2).reshape(16, 512)
    return jnp.concatenate([cot, jnp.pad(lines, ((0, 0), (0, 768)))], axis=0)


def read_weights(cots, exp):
    lines = cots[:, 128:144, :512].reshape(16, 16, 2, 2, 128).transpose(2, 0, 3, 1, 4).reshape(2, 16, 32, 128)
    mine = lax.dynamic_slice_in_dim(lines, exp * 2, 2, axis=2)
    return mine[0].astype(F32) + mine[1].astype(F32)


def local(
    tokens,
    lengths,
    routes,
    route_gates,
    attn_gain,
    w_query,
    w_key,
    w_value,
    w_out,
    ffn_gain,
    shared_gate,
    shared_up,
    shared_down,
    expert_gate,
    expert_up,
    expert_down,
    cotangent,
):
    resident, cot = tokens[0], cotangent[0]
    rows = resident.shape[0]
    attn_line, ffn_line = attn_gain[None], ffn_gain[None]
    ctx = lax.axis_index("ctx")
    positions = ctx * rows + jnp.arange(rows, dtype=jnp.int32)
    all_cos, all_sin = turn_tables(8 * rows)
    back_sin = jnp.asarray(-all_sin)
    all_cos, all_sin = jnp.asarray(all_cos), jnp.asarray(all_sin)
    cos = lax.dynamic_slice_in_dim(all_cos, ctx * rows, rows)
    sin = lax.dynamic_slice_in_dim(all_sin, ctx * rows, rows)
    sent_cot = with_weights(cot, routes[0], route_gates[0], positions < lengths[0])

    qkv, normed_one = project(resident, attn_line, w_query, w_key, w_value, cos, sin)
    mixed, heads, cots = attend(qkv, lengths, sent_cot, 1)
    hidden, normed_two = after(mixed, w_out, resident, ffn_line)
    meta = read_weights(cots, lax.axis_index("exp"))
    slot_rows, slot_cots, weight, act, d_gates, shared_out, d_shared = gather_rows(
        normed_two, cot, meta, cots, shared_gate, shared_up, shared_down, 2
    )
    parts, d_parts, kept_act, kept_back, down_one = experts(
        meta, weight, slot_rows, slot_cots, expert_gate, expert_up, expert_down, 5
    )
    padded = jnp.pad(act.reshape(rows, 128, 7), ((0, 0), (0, 0), (0, 3))).reshape(rows, 1280)
    early = dense_terms("early_terms", ((0, 7), (7, 12)), with_partner(normed_two, d_gates, padded, cot))
    gate_sum, up_term, down_term, first, d_mixed, d_hidden, d_attn, ffn_term = scatter_rows(
        d_parts, slot_rows, slot_cots, kept_act, kept_back, early, d_shared, hidden, ffn_line, cot, w_out, 3
    )
    input_grad, attn_term, routed, up_sum, expert_gate_grad, second, late = attend_back(
        d_mixed, heads, lengths, all_cos, back_sin, parts, up_term, gate_sum, early, d_attn, normed_one, mixed,
        resident, attn_line, d_hidden, w_query, w_key, w_value, 4,
    )
    block_out = hidden + shared_out + routed
    packed, expert_up_grad, expert_down_grad = sum_grads(
        late, first, second, gain_lines(attn_term[0], ffn_term[0]), up_sum, down_one, down_term
    )
    return (
        block_out[None],
        input_grad[None],
        *unpack_dense(packed),
        expert_gate_grad,
        expert_up_grad,
        expert_down_grad,
    )


def solution(mesh):
    in_specs = (
        P("exp", "ctx", None),
        P("exp"),
        P("exp", "ctx", None),
        P("exp", "ctx", None),
        P(),
        P(),
        P(),
        P(),
        P(),
        P(),
        P(),
        P(),
        P(),
        P("exp", None, None),
        P("exp", None, None),
        P("exp", None, None),
        P("exp", "ctx", None),
    )
    out_specs = (
        P("exp", "ctx", None),
        P("exp", "ctx", None),
        P(("ctx", "exp")),
        P(("ctx", "exp"), None),
        P(("ctx", "exp"), None),
        P(("ctx", "exp"), None),
        P(("ctx", "exp"), None),
        P(("ctx", "exp")),
        P(("ctx", "exp"), None),
        P(("ctx", "exp"), None),
        P(("ctx", "exp"), None),
        P("exp", "ctx", None),
        P("exp", "ctx", None),
        P("exp", "ctx", None),
    )
    return jax.shard_map(local, mesh=mesh, in_specs=in_specs, out_specs=out_specs, check_vma=False)
```

```python
import functools
import math

import jax
import jax.numpy as jnp
import numpy as np
from jax import lax
from jax.experimental import pallas as pl
from jax.experimental.pallas import tpu as pltpu
from jax.sharding import PartitionSpec as P

MESH = pl.DeviceIdType.MESH
HEAD_DIM = 128
VMEM_LIMIT = 60 * 2**20
F32, BF16 = jnp.float32, jnp.bfloat16


def place():
    ctx, exp = lax.axis_index("ctx"), lax.axis_index("exp")
    return ctx // 2, (exp // 8) * 2 + ctx % 2, (exp // 2) % 4, exp % 2


def device(x, y, z, core):
    return (x * 2 + y % 2, (y // 2) * 8 + z * 2 + core)


def greet(devices):
    barrier = pltpu.get_barrier_semaphore()
    for target in devices:
        pl.semaphore_signal(barrier, inc=1, device_id=target, device_id_type=MESH)
    pl.semaphore_wait(barrier, len(devices))


class Copies:
    def __init__(self, send, recv, own):
        self.send, self.recv, self.own = send, recv, own
        self.remotes, self.locals = 0, 0
        self.started = []

    def remote(self, src, dst, target):
        index = self.remotes
        self.remotes += 1
        copy = pltpu.make_async_remote_copy(
            src_ref=src,
            dst_ref=dst,
            send_sem=self.send.at[index],
            recv_sem=self.recv.at[index],
            device_id=target,
            device_id_type=MESH,
        )
        copy.start()
        self.started.append(copy)
        return copy

    def local(self, src, dst):
        index = self.locals
        self.locals += 1
        copy = pltpu.make_async_copy(src, dst, self.own.at[index])
        copy.start()
        return copy

    def drain(self):
        for copy in self.started:
            copy.wait_send()


def each(shape, body):
    @pl.loop(0, math.prod(shape))
    def _(step):
        index = []
        for size in reversed(shape):
            index.append(step % size)
            step = step // size
        body(tuple(reversed(index)))


def add_into(out, shape, *terms, rows=None):
    def body(index):
        total = terms[0][index].astype(F32)
        for term in terms[1:]:
            total = total + term[index].astype(F32)
        out[index] = total.astype(out.dtype)

    if rows is None:
        each(shape, body)
    else:
        step, count = rows
        each(shape + (count,), lambda i: body(i[:-1] + (pl.ds(pl.multiple_of(i[-1] * step, step), step),)))


class RingSum:
    def __init__(self, copies, me, right, left, part, land, work, add, resident=None):
        self.copies, self.right, self.left, self.land, self.work, self.add = copies, right, left, land, work, add
        self.part = part
        self.after, self.before, across = (me + 1) % 4, (me + 3) % 4, (me + 2) % 4
        self.one = copies.remote(part(across, 0), land.at[0], right)
        self.two = copies.remote(part(across, 1), land.at[1], left)
        sources = [part(self.after, 0), part(self.before, 1), part(me, 0), part(me, 1)]
        if resident is None:
            self.loads = [copies.local(source, work.at[i]) for i, source in enumerate(sources)]
            self.own = [work.at[i] for i in range(4)]
        else:
            self.loads = []
            self.own = sources

    def raw(self):
        self.three = self.copies.remote(self.part(self.after, 1), self.land.at[2], self.right)
        self.four = self.copies.remote(self.part(self.before, 0), self.land.at[4], self.left)

    def forward(self):
        for load in self.loads:
            load.wait()
        self.one.wait_recv()
        self.add(self.land.at[0], self.land.at[0], self.own[0])
        self.five = self.copies.remote(self.land.at[0], self.land.at[3], self.right)
        self.two.wait_recv()
        self.add(self.land.at[1], self.land.at[1], self.own[1])
        self.six = self.copies.remote(self.land.at[1], self.land.at[5], self.left)

    def finish(self, outs):
        for copy in (self.three, self.four, self.five, self.six):
            copy.wait_recv()
        self.add(outs[0], self.own[2], self.land.at[3], self.land.at[4])
        self.add(outs[1], self.own[3], self.land.at[2], self.land.at[5])


GRAD_REMOTES = 4 * 6 + 2 + 3 * 2 + 3 * 3 + 6 + 3 * 4 + 7
GRAD_LOCALS = 4 * 4


def add_blocks(shape):
    def add(out, *terms):
        add_into(out, shape, *terms)

    return add


def half_rows(which, size):
    return pl.ds(pl.multiple_of(which * size, size), size)


def order(y):
    return (y % 2) * 2 + y // 2


def grads_kernel(
    late, first, second, gains, up, down, dense_out, up_out, down_out,
    z_land, z_work, y_land, y_sum, x_land, u_land, u_work, v_land, v_sum, w_land,
    t_land, t_work, tz_land, t_sum, tx_land,
    gx_land, gx_sum, gy_land, total, stage, final_land, up_other, d_land, d_work, d_other, send, recv, own,
):
    x, y, z, core = place()
    y_half, y_low = y // 2, y % 2
    spot = z * 2 + core
    x_peers = [device((x + d) % 4, y, z, core) for d in (1, 2, 3)]
    y_peers = [device(x, (y + d) % 4, z, core) for d in (1, 2, 3)]
    z_peers = [device(x, y, (z + d) % 4, core) for d in (1, 2, 3)]
    spot_peers = [device(x, y, ((spot + d) % 8) // 2, (spot + d) % 2) for d in range(1, 8)]
    pair = device(x, y_half * 2 + 1 - y_low, z, core)
    greet(x_peers + y_peers + spot_peers)
    copies = Copies(send, recv, own)

    def direct(part, me, land, peers):
        return [copies.remote(part((me + d) % 4), land.at[d - 1], peers[d - 1]) for d in (1, 2, 3)]

    def arrived(arrivals):
        for copy in arrivals:
            copy.wait_recv()

    ring = RingSum(
        copies, z, z_peers[0], z_peers[2], lambda c, h: late.at[c, h], z_land, z_work, add_blocks((4, 4))
    )
    ring.raw()
    side = RingSum(
        copies, x, x_peers[0], x_peers[2], lambda c, h: late.at[2 * h : 2 * h + 2, 2, c],
        u_land, u_work, add_blocks((2, 4)),
    )
    gain_x = direct(lambda c: gains.at[c], x, gx_land, x_peers)
    tall = RingSum(
        copies, y, y_peers[0], y_peers[2], lambda c, h: late.at[2 * h : 2 * h + 2, 3, :, order(c)],
        t_land, t_work, add_blocks((2, 4)),
    )
    side.raw()
    tall.raw()

    def down_add(out, *terms):
        add_into(out, (), *terms, rows=(16, 7))

    downs = RingSum(
        copies, x, x_peers[0], x_peers[2],
        lambda c, h: down.at[half_rows(2 * c + h, 112)], d_land, d_work, down_add,
    )
    side.forward()
    tall.forward()
    x_copies = {0: direct(lambda c: first.at[:, c], x, x_land.at[0], x_peers)}
    y_copies = {1: direct(lambda c: second.at[:, :, order(c)], y, y_land.at[1], y_peers)}
    swap_up = copies.remote(up.at[1 - y_low], up_other, pair)
    downs.raw()
    ring.forward()
    arrived(gain_x)
    gx_sum[...] = gains[x] + gx_land[0] + gx_land[1] + gx_land[2]
    gain_y = direct(lambda c: gx_sum.at[order(c)], y, gy_land, y_peers)
    downs.forward()

    def start_x(t, mine):
        arrived(y_copies[t])
        add_into(y_sum.at[t], (2, 4), mine, y_land.at[t, 0], y_land.at[t, 1], y_land.at[t, 2])
        x_copies[t] = direct(lambda c: y_sum.at[t, :, c], x, x_land.at[t], x_peers)

    side.finish([u_work.at[2], u_work.at[3]])
    side_z = direct(lambda c: u_work.at[2 + c // 2, c % 2], z, v_land, z_peers)
    tall.finish([t_work.at[2], t_work.at[3]])
    tall_z = direct(lambda c: t_work.at[2 + c // 2, c % 2], z, tz_land, z_peers)
    start_x(1, second.at[:, :, order(y)])
    ring.finish([z_work.at[2], z_work.at[3]])
    y_copies[2] = direct(lambda c: z_work.at[2:4, :, order(c)], y, y_land.at[2], y_peers)
    arrived(side_z)
    add_into(v_sum, (4,), u_work.at[2 + z // 2, z % 2], v_land.at[0], v_land.at[1], v_land.at[2])
    side_y = direct(lambda c: v_sum.at[order(c)], y, w_land, y_peers)
    arrived(tall_z)
    add_into(t_sum, (4,), t_work.at[2 + z // 2, z % 2], tz_land.at[0], tz_land.at[1], tz_land.at[2])
    tall_x = direct(lambda c: t_sum.at[c], x, tx_land, x_peers)
    downs.finish([d_work.at[2], d_work.at[3]])
    swap_down = copies.remote(d_work.at[2 + 1 - y_low], d_other, pair)
    swap_up.wait_recv()
    add_into(up_out, (), up.at[y_low], up_other, rows=(16, 10))
    start_x(2, z_work.at[2:4, :, order(y)])

    def summed(panel, first_part, land, *index):
        value = first_part.astype(F32)
        for d in range(3):
            value = value + land[(d,) + index].astype(F32)
        total[panel, 0:80] = value
        total[panel, 80:96] = jnp.zeros((16, 128), F32)

    arrived(gain_y)
    lines = gx_sum[order(y)] + gy_land[0] + gy_land[1] + gy_land[2]
    arrived(side_y)
    summed(6, v_sum[order(y)], w_land)
    arrived(tall_x)
    summed(7, t_sum[x], tx_land)
    for t, panels in ((0, (0, 1)), (1, (2, 3)), (2, (4, 5))):
        arrived(x_copies[t])
        for half, panel in enumerate(panels):
            summed(panel, first[half, x] if t == 0 else y_sum[t, half, x], x_land.at[t], half)
    for j in range(8):
        for panel in range(8):
            stage[j, panel] = total[panel, 10 * j : 10 * j + 16]
        stage[j, 0, 10:11] = lines[j : j + 1]
    finals = [
        copies.remote(stage.at[(spot + d) % 8], final_land.at[d], spot_peers[d - 1]) for d in range(1, 8)
    ]
    swap_down.wait_recv()
    add_into(down_out, (), d_work.at[2 + y_low], d_other, rows=(16, 7))
    dense_out[spot] = stage[spot]
    for d, copy in enumerate(finals):
        copy.wait_recv()
        dense_out[(spot + 7 - d) % 8] = final_land[d + 1]
    copies.drain()


def sum_grads(late, first, second, gains, up, down):
    scratch = [
        pltpu.VMEM((6, 4, 4, 80, 128), BF16),
        pltpu.VMEM((4, 4, 4, 80, 128), BF16),
        pltpu.VMEM((3, 3, 2, 4, 80, 128), BF16),
        pltpu.VMEM((3, 2, 4, 80, 128), BF16),
        pltpu.VMEM((3, 3, 2, 80, 128), BF16),
        pltpu.VMEM((6, 2, 4, 80, 128), BF16),
        pltpu.VMEM((4, 2, 4, 80, 128), BF16),
        pltpu.VMEM((3, 4, 80, 128), BF16),
        pltpu.VMEM((4, 80, 128), BF16),
        pltpu.VMEM((3, 80, 128), BF16),
        pltpu.VMEM((6, 2, 4, 80, 128), BF16),
        pltpu.VMEM((4, 2, 4, 80, 128), BF16),
        pltpu.VMEM((3, 4, 80, 128), BF16),
        pltpu.VMEM((4, 80, 128), BF16),
        pltpu.VMEM((3, 80, 128), BF16),
        pltpu.VMEM((3, 4, 8, 128), F32),
        pltpu.VMEM((4, 8, 128), F32),
        pltpu.VMEM((3, 8, 128), F32),
        pltpu.VMEM((8, 96, 128), F32),
        pltpu.VMEM((8, 8, 16, 128), F32),
        pltpu.VMEM((8, 8, 16, 128), F32),
        pltpu.VMEM((160, 896), BF16),
        pltpu.VMEM((6, 112, 1280), BF16),
        pltpu.VMEM((4, 112, 1280), BF16),
        pltpu.VMEM((112, 1280), BF16),
        pltpu.SemaphoreType.DMA((GRAD_REMOTES,)),
        pltpu.SemaphoreType.DMA((GRAD_REMOTES,)),
        pltpu.SemaphoreType.DMA((GRAD_LOCALS,)),
    ]
    return pl.pallas_call(
        grads_kernel,
        name="sum_grads",
        out_shape=(
            jax.ShapeDtypeStruct((8, 8, 16, 128), F32),
            jax.ShapeDtypeStruct((160, 896), F32),
            jax.ShapeDtypeStruct((112, 1280), F32),
        ),
        in_specs=[ANYWHERE, VMEM, VMEM, VMEM, VMEM, ANYWHERE],
        out_specs=(VMEM,) * 3,
        scratch_shapes=scratch,
        compiler_params=params(0),
        cost_estimate=cost(10**8, 4 * 10**8),
    )(late.reshape(4, 4, 4, 4, 80, 128), first, second.reshape(2, 4, 4, 80, 128), gains, up, down)


def gain_lines(attn_term, ffn_term):
    both = jnp.concatenate([attn_term, ffn_term]).reshape(2, 16, 8, 10).transpose(1, 2, 0, 3).reshape(4, 4, 8, 20)
    return jnp.pad(both, ((0, 0), (0, 0), (0, 0), (0, 108)))


VMEM = pl.BlockSpec(memory_space=pltpu.VMEM)
ANYWHERE = pl.BlockSpec(memory_space=pl.ANY)
SMEM = pl.BlockSpec(memory_space=pltpu.SMEM)
EXTRA_HEAD = {8: 0, 9: 5}
SCALE = HEAD_DIM ** (-0.5)


def params(collective_id=None):
    if collective_id is None:
        return pltpu.CompilerParams(vmem_limit_bytes=VMEM_LIMIT)
    return pltpu.CompilerParams(
        collective_id=collective_id, has_side_effects=True, vmem_limit_bytes=VMEM_LIMIT
    )


def cost(flops, bytes_accessed):
    return pl.CostEstimate(flops=int(flops), bytes_accessed=int(bytes_accessed), transcendentals=0)


def dot(left, right):
    return jnp.dot(left, right, preferred_element_type=F32)


def dot_nt(left, right):
    return lax.dot_general(left, right, (((1,), (1,)), ((), ())), preferred_element_type=F32)


def dot_tn(left, right):
    return lax.dot_general(left, right, (((0,), (0,)), ((), ())), preferred_element_type=F32)


def normed(values, gain):
    return values * lax.rsqrt(jnp.mean(values * values, axis=-1, keepdims=True) + 1e-06) * gain


def normed_back(values, gain, upstream):
    factor = lax.rsqrt(jnp.mean(values * values, axis=-1, keepdims=True) + 1e-06)
    scaled = upstream * gain
    inner = jnp.mean(scaled * values, axis=-1, keepdims=True)
    term = jnp.sum(upstream * values * factor, axis=0, keepdims=True)
    return factor * scaled - values * factor * factor * factor * inner, term


def turned(values, cos, sin):
    return values * cos + pltpu.roll(values, HEAD_DIM // 2, 1) * sin


def turn_tables(count):
    half = HEAD_DIM // 2
    frequency = np.exp(np.arange(half, dtype=np.float32) * np.float32(-2.0 * math.log(10000.0) / HEAD_DIM))
    angle = np.arange(count, dtype=np.float32)[:, None] * frequency[None, :]
    cos, sin = np.cos(angle), np.sin(angle)
    return np.concatenate([cos, cos], axis=1), np.concatenate([-sin, sin], axis=1)


def project_kernel(tokens, gain, w_query, w_key, w_value, cos, sin, qkv, normed_one):
    @pl.when(pl.program_id(0) == 0)
    def _():
        normed_one[...] = normed(tokens[...].astype(F32), gain[...].reshape(1, -1)).astype(BF16)

    rows = normed_one[...]
    positions = pl.ds(pl.multiple_of(lax.axis_index("ctx") * 128, 128), 128)
    turn = cos[positions], sin[positions]
    query, key, value = dot(rows, w_query[...]), dot(rows, w_key[...]), dot(rows, w_value[...])
    for head in range(2):
        lanes = slice(head * HEAD_DIM, (head + 1) * HEAD_DIM)
        qkv[head, 0] = turned(query[:, lanes], *turn).astype(BF16)
        qkv[head, 1] = turned(key[:, lanes], *turn).astype(BF16)
        qkv[head, 2] = value[:, lanes].astype(BF16)


def project(tokens, gain, w_query, w_key, w_value, cos, sin):
    rows, width = tokens.shape
    whole = pl.BlockSpec((rows, width), lambda h: (0, 0))
    table = pl.BlockSpec(cos.shape, lambda h: (0, 0))
    columns = pl.BlockSpec((width, 2 * HEAD_DIM), lambda h: (0, h))
    return pl.pallas_call(
        project_kernel,
        name="project",
        grid=(5,),
        out_shape=(
            jax.ShapeDtypeStruct((10, 3, rows, HEAD_DIM), BF16),
            jax.ShapeDtypeStruct((rows, width), BF16),
        ),
        in_specs=[whole, pl.BlockSpec((width,), lambda h: (0,)), columns, columns, columns, table, table],
        out_specs=(pl.BlockSpec((2, 3, rows, HEAD_DIM), lambda h: (h, 0, 0, 0)), whole),
        compiler_params=params(),
        cost_estimate=cost(6 * rows * width * width, 6 * width * width),
    )(tokens, gain, w_query, w_key, w_value, cos, sin)


def rank(y_half, z, core):
    return y_half * 8 + z * 2 + core


class Gather:
    def __init__(self, copies, where, src, out, cut):
        x, y, z, core = where
        self.copies, self.out, self.cut = copies, out, cut
        self.y_half, self.z, self.core = y // 2, z, core
        self.pair = device(x, y, z, 1 - core)
        self.across = device(x, (y + 2) % 4, z, core)
        self.right, self.left = device(x, y, (z + 1) % 4, core), device(x, y, (z + 3) % 4, core)
        me = rank(self.y_half, z, core)
        self.mine = copies.local(src, out.at[me])
        self.over = copies.remote(src, out.at[me], self.across)
        self.to_right = copies.remote(src, out.at[me], self.right)
        self.to_left = copies.remote(src, out.at[me], self.left)
        self.pairs = [copies.remote(src, out.at[me], self.pair)]
        self.seen = 0

    def shard(self, other, dz):
        y_half = 1 - self.y_half if other else self.y_half
        return rank(y_half, (self.z + dz + 4) % 4, self.core)

    def half(self, index, which):
        rows = self.out.shape[1]
        return self.out.at[index, 0 : self.cut] if which == 0 else self.out.at[index, self.cut : rows]

    def send(self, ref, target):
        return self.copies.remote(ref, ref, target)

    def share(self, ref):
        self.pairs.append(self.send(ref, self.pair))

    def near(self):
        self.to_right.wait_recv()
        index = self.shard(False, -1)
        self.on_right = self.send(self.half(index, 0), self.right)
        self.share(self.out.at[index])
        self.to_left.wait_recv()
        index = self.shard(False, 1)
        self.on_left = self.send(self.half(index, 1), self.left)
        self.share(self.out.at[index])

    def far(self):
        self.over.wait_recv()
        index = self.shard(True, 0)
        self.far_right = self.send(self.out.at[index], self.right)
        self.far_left = self.send(self.out.at[index], self.left)
        self.share(self.out.at[index])

    def third(self):
        self.far_right.wait_recv()
        index = self.shard(True, -1)
        self.far_on_right = self.send(self.half(index, 0), self.right)
        self.share(self.out.at[index])
        self.far_left.wait_recv()
        index = self.shard(True, 1)
        self.far_on_left = self.send(self.half(index, 1), self.left)
        self.share(self.out.at[index])

    def pairs_arrived(self, count):
        for copy in self.pairs[self.seen : count]:
            copy.wait_recv()
        self.seen = count

    def last(self):
        for copies, other in (((self.on_right, self.on_left), False), ((self.far_on_right, self.far_on_left), True)):
            for which, copy in enumerate(copies):
                copy.wait_recv()
                self.share(self.half(self.shard(other, 2), which))
        self.pairs_arrived(len(self.pairs))


GATHER_REMOTES = 3 + 2 + 2 + 2 + 8 + 2


def exp_peers(where):
    x, y, z, core = where
    return [
        device(x, y, z, 1 - core),
        device(x, (y + 2) % 4, z, core),
        device(x, y, (z + 1) % 4, core),
        device(x, y, (z + 3) % 4, core),
    ]


def gather_kernel(
    rows, cot, cots, gate_w, up_w, down_w, spread,
    slot_rows, slot_cots, meta, weight, shared_out, d_shared, early,
    every, cots_in, gate, up, down, spread_in, filled_rows, filled_cots, lines, act, d_gates, pair_act, pair_gates,
    right, act_left, panels, send, recv, own, load_sem, keep_sem, early_sem,
):
    where = place()
    core, y_half = where[3], where[1] // 2
    me = lax.axis_index("exp")
    other = me + 1 - 2 * core
    loads = [
        pltpu.make_async_copy(src, dst, load_sem.at[i])
        for i, (src, dst) in enumerate(((gate_w, gate), (up_w, up), (down_w, down), (cots, cots_in), (spread, spread_in)))
    ]
    for load in loads:
        load.start()
    greet(exp_peers(where))
    copies = Copies(send, recv, own)
    gather = Gather(copies, where, rows, every, rows.shape[0] // 2)
    shared_out[...] = jnp.zeros_like(shared_out)
    d_shared[...] = jnp.zeros_like(d_shared)

    def shared(first, last):
        @pl.loop(first, last)
        def _(step):
            at = pl.ds(pl.multiple_of(step * 128, 128), 128)
            value = rows[...]
            gate_pre, up_pre = dot(value, gate[:, at]), dot(value, up[:, at])
            silu, slope = gated(gate_pre, up_pre)
            activated = (silu * up_pre).astype(BF16)
            act[:, at] = activated
            shared_out[...] += dot(activated, down[at])
            d_act = dot_nt(cot[...], down[at])
            gate_back = (d_act * up_pre * slope).astype(BF16)
            up_back = (d_act * silu).astype(BF16)
            d_gates[0, :, at] = gate_back
            d_gates[1, :, at] = up_back
            d_shared[...] += dot_nt(gate_back, gate[:, at]) + dot_nt(up_back, up[:, at])

    def hot(block):
        slot = lax.broadcasted_iota(jnp.int32, (SLOTS, 128), 0).astype(F32)
        return [jnp.where(slot == lines[block, e : e + 1], 1.0, 0.0) for e in range(2)]

    def fill(block, source, out, column=None):
        value = dot(jnp.concatenate(hot(block), axis=0).astype(BF16), source)
        if column is not None:
            value = value * column
        value = value.astype(BF16)
        at = pl.ds(pl.multiple_of(block * SLOTS, SLOTS), SLOTS)
        for expert in range(2):
            out[expert, at] = value[expert * SLOTS : (expert + 1) * SLOTS]

    def fill_cots(block):
        column = jnp.concatenate(
            [jnp.sum(one * meta[block, e : e + 1], axis=1, keepdims=True) for e, one in enumerate(hot(block))], axis=0
        )
        at = pl.ds(pl.multiple_of(block * SLOTS, SLOTS), SLOTS)
        for expert in range(2):
            weight[expert, at] = jnp.broadcast_to(column[expert * SLOTS : (expert + 1) * SLOTS], (SLOTS, 128))
        fill(block, cots_in[block, 0:128], filled_cots, column)

    def fill_rows(far, dz):
        own_block = gather.shard(far, dz)
        for block in (own_block, own_block + 1 - 2 * core):
            fill(block, every[block], filled_rows)

    for load in loads[:3]:
        load.wait()
    shared(0, 4)
    gather.near()
    gather.far()
    shared(4, 7)
    pair = device(where[0], where[1], where[2], 1 - core)
    from_pair = [copies.remote(act, pair_act, pair), copies.remote(d_gates.at[1 - core], pair_gates, pair)]
    loads[3].wait()

    @pl.loop(0, 16)
    def _(block):
        high = cots_in[block, 128:144, pl.ds(pl.multiple_of(y_half * 128, 128), 128)].astype(F32)
        low = cots_in[block, 128:144, pl.ds(pl.multiple_of(256 + y_half * 128, 128), 128)].astype(F32)
        line = lax.broadcasted_iota(jnp.int32, (16, 128), 0)
        for expert in range(2):
            mine = line == 2 * (me % 8) + expert
            meta[block, expert : expert + 1] = jnp.sum(jnp.where(mine, high + low, 0.0), axis=0, keepdims=True)

    lines[...] = slot_lines(meta).reshape(16, 2, 128)

    @pl.loop(0, 16, unroll=4)
    def _(block):
        fill_cots(block)

    gather.third()
    keep_cots = pltpu.make_async_copy(filled_cots, slot_cots, keep_sem.at[0])
    keep_cots.start()
    gather.pairs_arrived(4)
    for copy in from_pair:
        copy.wait_recv()
    loads[4].wait()
    right[0:128, 0:896] = d_gates[core]
    right[128:256, 0:896] = pair_gates[...]
    at = pl.ds(pl.multiple_of(core * 640, 128), 640)
    right[0:128, 896:1536] = cot[:, at]
    right[128:256, 896:1536] = cots_in[other, 0:128, at]
    act_left[...] = dot(jnp.concatenate([act[...], pair_act[...]], axis=0), spread_in[...]).astype(BF16)

    def store(index):
        return pltpu.make_async_copy(
            panels.at[index], early.at[:, pl.ds(pl.multiple_of(index * 256, 256), 256)], early_sem.at[index]
        )

    @pl.loop(0, 5)
    def _(index):
        at = pl.ds(pl.multiple_of(index * 256, 256), 256)
        value = dot_tn(jnp.concatenate([rows[:, at], every[other, :, at]], axis=0), right[:, 0:896])
        for panel in range(7):
            panels[index, panel] = value[:, panel * 128 : panel * 128 + 128].astype(BF16)
        value = dot_tn(act_left[:, at], right[:, 896:1536])
        for panel in range(5):
            panels[index, 7 + panel] = value[:, panel * 128 : panel * 128 + 128].astype(BF16)
        store(index).start()

    gather.mine.wait()
    for far, dz in ((False, 0), (False, -1), (False, 1), (True, 0)):
        fill_rows(far, dz)
    gather.pairs_arrived(6)
    for dz in (-1, 1):
        fill_rows(True, dz)
    gather.last()
    for far in (False, True):
        fill_rows(far, 2)
    keep_rows = pltpu.make_async_copy(filled_rows, slot_rows, keep_sem.at[1])
    keep_rows.start()
    copies.drain()
    keep_cots.wait()
    keep_rows.wait()
    for index in range(5):
        store(index).wait()


def gather_rows(rows, cot, cots, gate_w, up_w, down_w, collective_id):
    count, width = rows.shape
    hidden = gate_w.shape[1]
    spread = np.zeros((128, 7, 128, 10), np.float32)
    for group in range(128):
        spread[group, np.arange(7), group, np.arange(7)] = 1.0
    spread = jnp.asarray(spread.reshape(hidden, width), BF16)
    return pl.pallas_call(
        gather_kernel,
        name="gather_rows",
        out_shape=(
            jax.ShapeDtypeStruct((2, SLOT_ROWS, width), BF16),
            jax.ShapeDtypeStruct((2, SLOT_ROWS, width), BF16),
            jax.ShapeDtypeStruct((16, 2, 128), F32),
            jax.ShapeDtypeStruct((2, SLOT_ROWS, 128), F32),
            jax.ShapeDtypeStruct((count, width), F32),
            jax.ShapeDtypeStruct((count, width), F32),
            jax.ShapeDtypeStruct((12, width, 128), BF16),
        ),
        in_specs=[VMEM, VMEM] + [ANYWHERE] * 5,
        out_specs=(ANYWHERE, ANYWHERE) + (VMEM,) * 4 + (ANYWHERE,),
        scratch_shapes=[
            pltpu.VMEM((16, count, width), BF16),
            pltpu.VMEM(cots.shape, BF16),
            pltpu.VMEM(gate_w.shape, BF16),
            pltpu.VMEM(up_w.shape, BF16),
            pltpu.VMEM(down_w.shape, BF16),
            pltpu.VMEM(spread.shape, BF16),
            pltpu.VMEM((2, SLOT_ROWS, width), BF16),
            pltpu.VMEM((2, SLOT_ROWS, width), BF16),
            pltpu.VMEM((16, 2, 128), F32),
            pltpu.VMEM((count, hidden), BF16),
            pltpu.VMEM((2, count, hidden), BF16),
            pltpu.VMEM((count, hidden), BF16),
            pltpu.VMEM((count, hidden), BF16),
            pltpu.VMEM((2 * count, 1536), BF16),
            pltpu.VMEM((2 * count, width), BF16),
            pltpu.VMEM((5, 12, 256, 128), BF16),
            pltpu.SemaphoreType.DMA((GATHER_REMOTES + 2,)),
            pltpu.SemaphoreType.DMA((GATHER_REMOTES + 2,)),
            pltpu.SemaphoreType.DMA((1,)),
            pltpu.SemaphoreType.DMA((5,)),
            pltpu.SemaphoreType.DMA((2,)),
            pltpu.SemaphoreType.DMA((5,)),
        ],
        compiler_params=params(collective_id),
        cost_estimate=cost(10**9, 6 * 10**7),
    )(rows, cot, cots, gate_w, up_w, down_w, spread)


class Scatter:
    def __init__(self, copies, where, parts, pair_land, work, ring_land, far_land, y_land):
        x, y, z, core = where
        self.copies, self.work, self.pair_land = copies, work, pair_land
        self.ring_land, self.far_land, self.y_land = ring_land, far_land, y_land
        self.across = device(x, (y + 2) % 4, z, core)
        self.right, self.left = device(x, y, (z + 1) % 4, core), device(x, y, (z + 3) % 4, core)
        pair = device(x, y, z, 1 - core)
        self.pairs, self.loads = {}, {}
        for slot in ((0, 2), (1, 2), (0, 1), (0, 3), (1, 1), (1, 3), (0, 0), (1, 0)):
            y_half = 1 - y // 2 if slot[0] == 0 else y // 2
            at = (z + slot[1]) % 4
            self.pairs[slot] = copies.remote(parts.at[rank(y_half, at, 1 - core)], pair_land.at[slot], pair)
            self.loads[slot] = copies.local(parts.at[rank(y_half, at, core)], work.at[slot])

    def merge(self, slot):
        self.loads[slot].wait()
        self.pairs[slot].wait_recv()
        rows_add(self.work.at[slot], 0, 128, self.work.at[slot], self.pair_land.at[slot])

    def first(self):
        self.ring = {}
        for far in range(2):
            self.merge((far, 2))
            self.ring[far] = (
                self.copies.remote(self.work.at[far, 2, 0:64], self.ring_land.at[far, 0], self.right),
                self.copies.remote(self.work.at[far, 2, 64:128], self.ring_land.at[far, 1], self.left),
            )
        for far in range(2):
            self.merge((far, 1))
            self.merge((far, 3))
            self.merge((far, 0))

    def second(self):
        self.final = {}
        for far in range(2):
            self.ring[far][0].wait_recv()
            rows_add(self.work.at[far, 1, 0:64], 0, 64, self.work.at[far, 1, 0:64], self.ring_land.at[far, 0])
            to_right = self.copies.remote(self.work.at[far, 1], self.far_land.at[far, 0], self.right)
            self.ring[far][1].wait_recv()
            rows_add(self.work.at[far, 3, 64:128], 0, 64, self.work.at[far, 3, 64:128], self.ring_land.at[far, 1])
            to_left = self.copies.remote(self.work.at[far, 3], self.far_land.at[far, 1], self.left)
            self.final[far] = (to_right, to_left)

    def third(self):
        for far in range(2):
            for copy in self.final[far]:
                copy.wait_recv()
            rows_add(self.work.at[far, 0], 0, 128, self.work.at[far, 0], self.far_land.at[far, 0], self.far_land.at[far, 1])
            if far == 0:
                self.over = self.copies.remote(self.work.at[0, 0], self.y_land, self.across)

    def last(self, out):
        self.over.wait_recv()
        rows_add(out, 0, 128, self.work.at[1, 0], self.y_land)


def rows_add(out, first, rows, *terms):
    @pl.loop(0, rows // 16)
    def _(step):
        at = pl.ds(pl.multiple_of(step * 16, 16), 16)
        value = terms[0][at].astype(F32)
        for term in terms[1:]:
            value = value + term[at].astype(F32)
        out[at] = value.astype(out.dtype)


SCATTER_REMOTES, SCATTER_LOCALS = 8 + 4 + 4 + 1, 8
SCATTER_SCRATCH = [
    pltpu.VMEM((2, 4, 128, 1280), BF16),
    pltpu.VMEM((2, 4, 128, 1280), BF16),
    pltpu.VMEM((2, 2, 64, 1280), BF16),
    pltpu.VMEM((2, 2, 128, 1280), BF16),
    pltpu.VMEM((128, 1280), BF16),
]


def up_add(out, *terms):
    add_into(out, (), *terms, rows=(16, 10))


def scatter_kernel(
    parts, rows_in, cots_in, act_in, back_in, early, d_shared, hidden_rows, gain, cot, w_out_in, down_one,
    gate_sum, up_out, up_one, down_out, down_final, first, d_mixed, d_hidden, d_attn, gain_term,
    a, b, c, d, e, rows, cots, act, back, gate, up, down, land, z_land, z_work, w_out, d_routed, up_land, one_other,
    send, recv, own, load_sem, keep_sem,
):
    where = place()
    x, y, z, core = where
    x_peers = [device((x + 1) % 4, y, z, core), device((x + 3) % 4, y, z, core)]
    loads = [
        pltpu.make_async_copy(src, dst, load_sem.at[i])
        for i, (src, dst) in enumerate(
            ((rows_in, rows), (back_in, back), (act_in.at[1], act), (cots_in.at[1], cots), (w_out_in, w_out))
        )
    ]
    for load in loads:
        load.start()
    greet(exp_peers(where) + x_peers + [device(x, (y // 2) * 2 + 1 - y % 2, z, core)])
    copies = Copies(send, recv, own)
    scatter = Scatter(copies, where, parts, a, b, c, d, e)
    hidden = act.shape[1]
    dense = RingSum(
        copies, z, device(x, y, (z + 1) % 4, core), device(x, y, (z + 3) % 4, core),
        lambda chunk, half: early.at[2 * chunk + half], z_land, z_work, add_blocks((4, 4)),
    )
    loads[0].wait()
    loads[1].wait()

    y_low = y % 2
    pair = device(x, (y // 2) * 2 + 1 - y_low, z, core)

    def term(dst, lanes, first, last):
        @pl.loop(first, last)
        def _(index):
            expert = index // 5
            at = pl.ds(pl.multiple_of((index % 5) * 256, 256), 256)
            dst[expert, at] = dot_tn(rows[expert, :, at], back[expert, :, lanes]).astype(BF16)

    def up_rows(chunk, which):
        return pl.ds(pl.multiple_of(chunk * 320 + which * 160, 160), 160)

    swap_one = copies.remote(down_one.at[half_rows(1 - y_low, 112)], one_other, pair)

    def gate_ring(expert):
        return RingSum(
            copies, x, x_peers[0], x_peers[1], lambda chunk, half: gate.at[expert, half_rows(2 * chunk + half, 160)],
            land.at[expert], None, up_add, resident=True,
        )

    term(gate, slice(0, hidden), 0, 5)
    rings = [gate_ring(0)]
    rings[0].raw()
    term(up, slice(hidden, 2 * hidden), 5, 10)
    over = [copies.remote(up.at[1, up_rows(chunk, 1 - y_low)], up_land.at[chunk], pair) for chunk in range(4)]
    term(gate, slice(0, hidden), 5, 10)
    rings.append(gate_ring(1))
    rings[1].raw()
    scatter.first()
    rings[0].forward()
    term(up, slice(hidden, 2 * hidden), 0, 5)
    keep_up = pltpu.make_async_copy(up.at[0], up_out, keep_sem.at[0])
    keep_up.start()
    scatter.second()
    loads[2].wait()
    loads[3].wait()

    @pl.loop(0, hidden // 128)
    def _(index):
        at = pl.ds(pl.multiple_of(index * 128, 128), 128)
        down[at] = dot_tn(act[:, at], cots[...]).astype(BF16)

    keep_down = pltpu.make_async_copy(down, down_out, keep_sem.at[1])
    keep_down.start()
    dense.raw()
    dense.forward()
    rings[1].forward()
    scatter.third()
    scatter.last(d_routed)
    grad, term_sum = normed_back(hidden_rows[...], gain[...].reshape(1, -1), d_shared[...] + d_routed[...])
    whole = cot[...].astype(F32) + grad
    d_hidden[...] = whole
    d_attn[...] = whole.astype(BF16)
    gain_term[...] = term_sum
    loads[4].wait()

    @pl.loop(0, 5)
    def _(index):
        value = dot_nt(d_attn[...], w_out[pl.ds(pl.multiple_of(index * 256, 256), 256)]).astype(BF16)
        d_mixed[2 * index] = value[:, :HEAD_DIM]
        d_mixed[2 * index + 1] = value[:, HEAD_DIM:]

    dense.finish([first.at[0], first.at[1]])
    for chunk, copy in enumerate(over):
        copy.wait_recv()
        add_into(up_one.at[chunk], (), up.at[1, up_rows(chunk, y_low)], up_land.at[chunk], rows=(16, 10))
    for expert in range(2):
        rings[expert].finish([gate_sum.at[expert, 0:160], gate_sum.at[expert, 160:320]])
    swap_one.wait_recv()
    add_into(down_final, (), down_one.at[half_rows(y_low, 112)], one_other, rows=(16, 7))
    copies.drain()
    keep_up.wait()
    keep_down.wait()


def scatter_rows(parts, kept_rows, kept_cots, kept_act, kept_back, early, d_shared, hidden_rows, gain, cot, w_out, down_one, collective_id):
    width, hidden = kept_rows.shape[2], kept_act.shape[2]
    count = cot.shape[0]
    return pl.pallas_call(
        scatter_kernel,
        name="scatter_rows",
        out_shape=(
            jax.ShapeDtypeStruct((2, 320, hidden), BF16),
            jax.ShapeDtypeStruct((width, hidden), BF16),
            jax.ShapeDtypeStruct((4, 160, hidden), BF16),
            jax.ShapeDtypeStruct((hidden, width), BF16),
            jax.ShapeDtypeStruct((112, width), F32),
            jax.ShapeDtypeStruct((2, 4, 4, 80, 128), BF16),
            jax.ShapeDtypeStruct((10, count, HEAD_DIM), BF16),
            jax.ShapeDtypeStruct((count, width), F32),
            jax.ShapeDtypeStruct((count, width), BF16),
            jax.ShapeDtypeStruct((1, width), F32),
        ),
        in_specs=[ANYWHERE] * 6 + [VMEM] * 4 + [ANYWHERE, VMEM],
        out_specs=(VMEM, ANYWHERE, VMEM, ANYWHERE) + (VMEM,) * 6,
        scratch_shapes=SCATTER_SCRATCH
        + [
            pltpu.VMEM(kept_rows.shape, BF16),
            pltpu.VMEM(kept_cots.shape[1:], BF16),
            pltpu.VMEM(kept_act.shape[1:], BF16),
            pltpu.VMEM(kept_back.shape, BF16),
            pltpu.VMEM((2, width, hidden), BF16),
            pltpu.VMEM((2, width, hidden), BF16),
            pltpu.VMEM((hidden, width), BF16),
            pltpu.VMEM((2, 6, 160, hidden), BF16),
            pltpu.VMEM((6, 4, 4, 80, 128), BF16),
            pltpu.VMEM((4, 4, 4, 80, 128), BF16),
            pltpu.VMEM(w_out.shape, BF16),
            pltpu.VMEM((count, width), F32),
            pltpu.VMEM((4, 160, hidden), BF16),
            pltpu.VMEM((112, width), BF16),
            pltpu.SemaphoreType.DMA((SCATTER_REMOTES + 23,)),
            pltpu.SemaphoreType.DMA((SCATTER_REMOTES + 23,)),
            pltpu.SemaphoreType.DMA((SCATTER_LOCALS + 4,)),
            pltpu.SemaphoreType.DMA((5,)),
            pltpu.SemaphoreType.DMA((2,)),
        ],
        compiler_params=params(collective_id),
        cost_estimate=cost(10**10, 10**8),
    )(
        parts, kept_rows, kept_cots, kept_act, kept_back, early.reshape(12, 4, 4, 80, 128),
        d_shared, hidden_rows, gain, cot, w_out, down_one,
    )


def ctx_device(ctx):
    return (ctx, lax.axis_index("exp"))


def owns_extra(ctx):
    return (ctx == EXTRA_HEAD[8]) | (ctx == EXTRA_HEAD[9])


def extra_head(ctx):
    return 8 + (ctx == EXTRA_HEAD[9]).astype(jnp.int32)


class Exchange:
    def __init__(self, send, recv, own):
        self.send, self.recv, self.own = send, recv, own
        self.ctx = lax.axis_index("ctx")

    def copy(self, src, dst, slot, d):
        return pltpu.make_async_remote_copy(
            src_ref=src,
            dst_ref=dst,
            send_sem=self.send.at[slot, d],
            recv_sem=self.recv.at[slot, d],
            device_id=ctx_device((self.ctx + d) % 8),
            device_id_type=MESH,
        )


def to_owners(exchange, block, land):
    ctx = exchange.ctx
    for d in range(1, 8):
        peer = (ctx + d) % 8
        exchange.copy(block(peer), land(0, ctx), 0, d).start()

        @pl.when(owns_extra(peer))
        def _():
            exchange.copy(block(extra_head(peer)), land(1, ctx), 1, d).start()

    mine = [pltpu.make_async_copy(block(ctx), land(0, ctx), exchange.own.at[0])]
    mine[0].start()
    extra = pltpu.make_async_copy(block(extra_head(ctx)), land(1, ctx), exchange.own.at[1])

    @pl.when(owns_extra(ctx))
    def _():
        extra.start()

    def arrived():
        mine[0].wait()
        for d in range(1, 8):
            exchange.copy(block(0), land(0, ctx), 0, d).wait_recv()

        @pl.when(owns_extra(ctx))
        def _():
            extra.wait()
            for d in range(1, 8):
                exchange.copy(block(0), land(1, ctx), 1, d).wait_recv()

    def sent():
        for d in range(1, 8):
            exchange.copy(block(0), land(0, ctx), 0, d).wait_send()

            @pl.when(owns_extra((ctx + d) % 8))
            def _():
                exchange.copy(block(0), land(1, ctx), 1, d).wait_send()

    return arrived, sent


class Home:
    def __init__(self, exchange, block, land):
        self.exchange, self.block, self.land = exchange, block, land
        self.ctx = exchange.ctx

    def head(self, slot):
        return self.ctx if slot == 0 else extra_head(self.ctx)

    def start(self, slot):
        for d in range(1, 8):
            self.exchange.copy(self.block(slot, (self.ctx + d) % 8), self.land(self.head(slot)), slot, d).start()
        self.mine(slot).start()

    def mine(self, slot):
        return pltpu.make_async_copy(
            self.block(slot, self.ctx), self.land(self.head(slot)), self.exchange.own.at[slot]
        )

    def finish(self):
        self.mine(0).wait()
        for d in range(1, 8):
            copy = self.exchange.copy(self.block(0, 0), self.land(0), 0, d)
            copy.wait_send()
            copy.wait_recv()

            @pl.when(owns_extra((self.ctx + 8 - d) % 8))
            def _():
                self.exchange.copy(self.block(1, 0), self.land(0), 1, d).wait_recv()

        @pl.when(owns_extra(self.ctx))
        def _():
            self.mine(1).wait()
            for d in range(1, 8):
                self.exchange.copy(self.block(1, 0), self.land(0), 1, d).wait_send()


def attend_kernel(
    qkv, length, cot, w_out_in, tokens, gain, mixed, heads, cots, hidden, normed_two,
    land, result, home, w_out, s1, r1, o1, s2, r2, o2, s3, r3, o3, load_sem,
):
    load = pltpu.make_async_copy(w_out_in, w_out, load_sem)
    load.start()
    where = place()
    ctx = lax.axis_index("ctx")
    greet([ctx_device((ctx + d) % 8) for d in range(1, 8)] + exp_peers(where))
    arrived, sent = to_owners(
        Exchange(s1, r1, o1), lambda head: qkv.at[head], lambda slot, c: land.at[slot, :, c]
    )
    copies = Copies(s3, r3, o3)
    gather = Gather(copies, where, cot, cots, 80)
    back = Home(Exchange(s2, r2, o2), lambda slot, c: result.at[slot, c], lambda head: home.at[head])
    keep = pltpu.make_async_copy(land, heads, o3.at[1])

    def run(slot, blocks):
        for block in blocks:
            width = (block + 1) * 128
            query = land[slot, 0, block]
            key = land[slot, 1, 0 : block + 1].reshape(width, HEAD_DIM)
            value = land[slot, 2, 0 : block + 1].reshape(width, HEAD_DIM)
            row = lax.broadcasted_iota(jnp.int32, (width, 128), 0)
            column = lax.broadcasted_iota(jnp.int32, (width, 128), 1) + block * 128
            scores = jnp.where(
                (row <= column) & (row < length[0]), dot_nt(key, query) * SCALE, -1e30
            )
            weights = jnp.exp(scores - jnp.max(scores, axis=0, keepdims=True))
            probs = weights * (1.0 / jnp.sum(weights, axis=0, keepdims=True))
            result[slot, block] = dot_tn(probs.astype(BF16), value).astype(BF16)

    gather.near()
    gather.far()
    arrived()
    run(0, range(8))
    back.start(0)
    gather.third()
    gather.mine.wait()

    @pl.when(owns_extra(ctx))
    def _():
        run(1, range(8))
        back.start(1)

    @pl.when(jnp.logical_not(owns_extra(ctx)))
    def _():
        land[1] = jnp.zeros_like(land[1])

    keep.start()
    back.finish()
    for head in range(10):
        mixed[:, head * HEAD_DIM : (head + 1) * HEAD_DIM] = home[head]
    load.wait()

    @pl.loop(0, 5)
    def _(index):
        at = pl.ds(pl.multiple_of(index * 256, 256), 256)
        hidden[:, at] = tokens[:, at].astype(F32) + dot(mixed[...], w_out[:, at])

    normed_two[...] = normed(hidden[...], gain[...].reshape(1, -1)).astype(BF16)
    gather.last()
    sent()
    keep.wait()
    copies.drain()


def exchange_semaphores():
    return [
        pltpu.SemaphoreType.DMA((2, 8)),
        pltpu.SemaphoreType.DMA((2, 8)),
        pltpu.SemaphoreType.DMA((2,)),
    ]


def attend(qkv, length, cot, w_out, tokens, gain, collective_id):
    return pl.pallas_call(
        attend_kernel,
        name="attend",
        out_shape=(
            jax.ShapeDtypeStruct((128, 1280), BF16),
            jax.ShapeDtypeStruct((2, 3, 8, 128, HEAD_DIM), BF16),
            jax.ShapeDtypeStruct((16,) + cot.shape, BF16),
            jax.ShapeDtypeStruct(tokens.shape, F32),
            jax.ShapeDtypeStruct(tokens.shape, BF16),
        ),
        in_specs=[ANYWHERE, SMEM, ANYWHERE, ANYWHERE, VMEM, VMEM],
        out_specs=(VMEM, ANYWHERE, ANYWHERE, VMEM, VMEM),
        scratch_shapes=[
            pltpu.VMEM((2, 3, 8, 128, HEAD_DIM), BF16),
            pltpu.VMEM((2, 8, 128, HEAD_DIM), BF16),
            pltpu.VMEM((10, 128, HEAD_DIM), BF16),
            pltpu.VMEM(w_out.shape, BF16),
        ]
        + exchange_semaphores()
        + exchange_semaphores()
        + [
            pltpu.SemaphoreType.DMA((GATHER_REMOTES,)),
            pltpu.SemaphoreType.DMA((GATHER_REMOTES,)),
            pltpu.SemaphoreType.DMA((2,)),
            pltpu.SemaphoreType.DMA,
        ],
        compiler_params=params(collective_id),
        cost_estimate=cost(10**9, 10**8),
    )(qkv, length, cot, w_out, tokens, gain)


def attend_back_kernel(
    d_mixed, heads, length, cos, sin, parts, up, up_one, gate, early, first, d_attn, normed_one, mixed, tokens, gain, d_hidden,
    w_query_in, w_key_in, w_value_in, input_grad, gain_term, routed, up_sum, up_final, gate_out, first_sum, second, late,
    land, kept, d_key, d_value, result, home, a, b, c, d, e, up_land, up_work, one_land, gate_other, first_land,
    z_land, z_work,
    pair_rows, d_qkv, pair_qkv, right, out_right, panels, out_terms, out_land, weights, total,
    s1, r1, o1, s2, r2, o2, s3, r3, o3, load_sem, late_sem,
):
    where = place()
    x, y, z, core = where
    ctx = lax.axis_index("ctx")
    x_peers = [device((x + 1) % 4, y, z, core), device((x + 3) % 4, y, z, core)]
    loads = [
        pltpu.make_async_copy(src, dst, load_sem.at[i])
        for i, (src, dst) in enumerate(
            ((heads, kept), (w_query_in, weights.at[0]), (w_key_in, weights.at[1]), (w_value_in, weights.at[2]))
        )
    ]
    for load in loads:
        load.start()
    y_peers = [device(x, (y + step) % 4, z, core) for step in (1, 2, 3)]
    pair_peer = device(x, (y // 2) * 2 + 1 - y % 2, z, core)
    cross_peer = device(x, (y // 2) * 2 + 2 + 1 - y % 2 - 4 * (y // 2), z, core)
    greet([ctx_device((ctx + step) % 8) for step in range(1, 8)] + exp_peers(where) + [cross_peer])
    arrived, sent = to_owners(
        Exchange(s1, r1, o1), lambda head: d_mixed.at[head], lambda slot, at: land.at[slot, at]
    )
    copies = Copies(s3, r3, o3)
    scatter = Scatter(copies, where, parts, a, b, c, d, e)
    back = Home(Exchange(s2, r2, o2), lambda slot, at: result.at[slot, :, at], lambda head: home.at[:, head])
    y_low = y % 2

    def one_add(out, *terms):
        add_into(out, (), *terms, rows=(16, 5))

    ring_one = RingSum(
        copies, x, x_peers[0], x_peers[1], lambda chunk, half: up_one.at[chunk, 80 * half : 80 * half + 80],
        one_land, None, one_add, resident=True,
    )
    ring = RingSum(
        copies, x, x_peers[0], x_peers[1], lambda chunk, half: up.at[half_rows(2 * chunk + half, 160)],
        up_land, up_work, up_add,
    )
    swap = copies.remote(gate.at[:, half_rows(1 - y_low, 160)], gate_other, pair_peer)
    z_peers = [device(x, y, (z + 1) % 4, core), device(x, y, (z + 3) % 4, core)]

    def panel_add(out, *terms):
        add_into(out, (), *terms, rows=(80, 8))

    dense = RingSum(
        copies, z, z_peers[0], z_peers[1], lambda chunk, half: early.at[8 + chunk, 640 * half : 640 * half + 640],
        z_land, z_work, panel_add,
    )
    pair = device(x, y, z, 1 - core)
    pairs = [copies.remote(src, pair_rows.at[i], pair) for i, src in enumerate((normed_one, mixed, d_attn))]
    for copy in pairs:
        copy.wait_recv()
    at = pl.ds(pl.multiple_of(core * 640, 128), 640)
    out_right[0:128] = d_attn[:, at]
    out_right[128:256] = pair_rows[2, :, at]

    @pl.loop(0, 5)
    def _(index):
        at = pl.ds(pl.multiple_of(index * 256, 256), 256)
        value = dot_tn(jnp.concatenate([mixed[:, at], pair_rows[1, :, at]], axis=0), out_right[...])
        for panel in range(5):
            out_terms[panel, at] = value[:, panel * 128 : panel * 128 + 128].astype(BF16)

    store_out = pltpu.make_async_copy(out_terms.at[4], late.at[15], late_sem.at[5])
    store_out.start()
    loads[0].wait()
    arrived()

    def run(slot):
        d_key[...] = jnp.zeros_like(d_key)
        d_value[...] = jnp.zeros_like(d_value)
        for block in range(8):
            width = (block + 1) * 128
            query, upstream = kept[slot, 0, block], land[slot, block]
            key = kept[slot, 1, 0 : block + 1].reshape(width, HEAD_DIM)
            value = kept[slot, 2, 0 : block + 1].reshape(width, HEAD_DIM)
            row = lax.broadcasted_iota(jnp.int32, (width, 128), 0)
            column = lax.broadcasted_iota(jnp.int32, (width, 128), 1) + block * 128
            scores = jnp.where(
                (row <= column) & (row < length[0]), dot_nt(key, query) * SCALE, -1e30
            )
            weight = jnp.exp(scores - jnp.max(scores, axis=0, keepdims=True))
            probs = weight * (1.0 / jnp.sum(weight, axis=0, keepdims=True))
            d_probs = dot_nt(value, upstream)
            delta = jnp.sum(probs * d_probs, axis=0, keepdims=True)
            d_scores = (probs * (d_probs - delta)).astype(BF16)
            rows = slice(block * 128, block * 128 + 128)
            d_query = dot_tn(d_scores, key) * SCALE
            result[slot, 0, block] = turned(d_query, cos[rows], sin[rows]).astype(BF16)
            d_key[0:width] += dot(d_scores, query)
            d_value[0:width] += dot(probs.astype(BF16), upstream)
        for block in range(8):
            rows = slice(block * 128, block * 128 + 128)
            result[slot, 1, block] = turned(d_key[rows] * SCALE, cos[rows], sin[rows]).astype(BF16)
            result[slot, 2, block] = d_value[rows].astype(BF16)
        back.start(slot)

    run(0)
    scatter.first()

    @pl.when(owns_extra(ctx))
    def _():
        run(1)

    first_copies = [
        copies.remote(first.at[:, :, order((y + step) % 4)], first_land.at[step - 1], y_peers[step - 1])
        for step in (1, 2, 3)
    ]
    ring_one.raw()
    ring_one.forward()
    ring.raw()
    scatter.second()
    dense.raw()
    dense.forward()
    outs = RingSum(
        copies, z, z_peers[0], z_peers[1], lambda chunk, half: out_terms.at[chunk, 640 * half : 640 * half + 640],
        out_land, None, panel_add, resident=True,
    )
    outs.raw()
    ring.forward()
    scatter.third()
    back.finish()
    outs.forward()
    for head in range(10):
        for kind in range(3):
            at = kind * 1280 + head * HEAD_DIM
            d_qkv[:, at : at + HEAD_DIM] = home[kind, head]
    swap_qkv = copies.remote(d_qkv, pair_qkv, pair)
    for load in loads[1:]:
        load.wait()

    @pl.loop(0, 5)
    def _(index):
        at = pl.ds(pl.multiple_of(index * 256, 256), 256)
        value = dot_nt(d_qkv[:, 0:1280], weights[0, at])
        value += dot_nt(d_qkv[:, 1280:2560], weights[1, at])
        value += dot_nt(d_qkv[:, 2560:3840], weights[2, at])
        total[:, at] = value

    grad, term = normed_back(tokens[...].astype(F32), gain[...].reshape(1, -1), total[...])
    input_grad[...] = d_hidden[...] + grad
    gain_term[...] = term

    swap_qkv.wait_recv()
    at = pl.ds(pl.multiple_of(core * 1920, 128), 1920)
    right[0:128] = d_qkv[:, at]
    right[128:256] = pair_qkv[:, at]

    def store(index):
        rows = pl.ds(pl.multiple_of(index * 256, 256), 256)
        return pltpu.make_async_copy(panels.at[index], late.at[0:15, rows], late_sem.at[index])

    @pl.loop(0, 5)
    def _(index):
        at = pl.ds(pl.multiple_of(index * 256, 256), 256)
        value = dot_tn(jnp.concatenate([normed_one[:, at], pair_rows[0, :, at]], axis=0), right[...])
        for panel in range(15):
            panels[index, panel] = value[:, panel * 128 : panel * 128 + 128].astype(BF16)
        store(index).start()

    scatter.last(routed)
    dense.finish([second.at[0, 0:640], second.at[0, 640:1280]])
    outs.finish([second.at[1, 0:640], second.at[1, 640:1280]])
    swap.wait_recv()
    add_into(gate_out, (2,), gate.at[:, half_rows(y_low, 160)], gate_other, rows=(16, 10))
    for copy in first_copies:
        copy.wait_recv()
    add_into(first_sum, (2, 4), first.at[:, :, order(y)], first_land.at[0], first_land.at[1], first_land.at[2])
    ring_one.finish([up_final.at[0:80], up_final.at[80:160]])
    ring.finish([up_sum.at[0], up_sum.at[1]])
    sent()
    copies.drain()
    store_out.wait()
    for index in range(5):
        store(index).wait()


def attend_back(
    d_mixed, heads, length, cos, sin, parts, up, up_one, gate, early, first, d_attn, normed_one, mixed, tokens, gain, d_hidden,
    w_query, w_key, w_value, collective_id,
):
    rows, width = tokens.shape
    hidden = up.shape[1]
    return pl.pallas_call(
        attend_back_kernel,
        name="attend_back",
        out_shape=(
            jax.ShapeDtypeStruct((rows, width), F32),
            jax.ShapeDtypeStruct((1, width), F32),
            jax.ShapeDtypeStruct((rows, width), F32),
            jax.ShapeDtypeStruct((2, 160, hidden), BF16),
            jax.ShapeDtypeStruct((160, hidden), F32),
            jax.ShapeDtypeStruct((2, 160, hidden), F32),
            jax.ShapeDtypeStruct((2, 4, 80, 128), BF16),
            jax.ShapeDtypeStruct((2, width, 128), BF16),
            jax.ShapeDtypeStruct((16, width, 128), BF16),
        ),
        in_specs=[ANYWHERE, ANYWHERE, SMEM, VMEM, VMEM, ANYWHERE, ANYWHERE, VMEM, VMEM, ANYWHERE, VMEM]
        + [VMEM] * 6
        + [ANYWHERE] * 3,
        out_specs=(VMEM,) * 8 + (ANYWHERE,),
        scratch_shapes=[
            pltpu.VMEM((2, 8, 128, HEAD_DIM), BF16),
            pltpu.VMEM((2, 3, 8, 128, HEAD_DIM), BF16),
            pltpu.VMEM((1024, HEAD_DIM), F32),
            pltpu.VMEM((1024, HEAD_DIM), F32),
            pltpu.VMEM((2, 3, 8, 128, HEAD_DIM), BF16),
            pltpu.VMEM((3, 10, 128, HEAD_DIM), BF16),
        ]
        + SCATTER_SCRATCH
        + [
            pltpu.VMEM((6, 160, hidden), BF16),
            pltpu.VMEM((4, 160, hidden), BF16),
            pltpu.VMEM((6, 80, hidden), BF16),
            pltpu.VMEM((2, 160, hidden), BF16),
            pltpu.VMEM((3, 2, 4, 80, 128), BF16),
            pltpu.VMEM((6, width // 2, 128), BF16),
            pltpu.VMEM((4, width // 2, 128), BF16),
            pltpu.VMEM((3, rows, width), BF16),
            pltpu.VMEM((rows, 3 * width), BF16),
            pltpu.VMEM((rows, 3 * width), BF16),
            pltpu.VMEM((2 * rows, 1920), BF16),
            pltpu.VMEM((2 * rows, 640), BF16),
            pltpu.VMEM((5, 15, 256, 128), BF16),
            pltpu.VMEM((5, width, 128), BF16),
            pltpu.VMEM((6, width // 2, 128), BF16),
            pltpu.VMEM((3, width, width), BF16),
            pltpu.VMEM((rows, width), F32),
        ]
        + exchange_semaphores()
        + exchange_semaphores()
        + [
            pltpu.SemaphoreType.DMA((SCATTER_REMOTES + 32,)),
            pltpu.SemaphoreType.DMA((SCATTER_REMOTES + 32,)),
            pltpu.SemaphoreType.DMA((SCATTER_LOCALS + 8,)),
            pltpu.SemaphoreType.DMA((4,)),
            pltpu.SemaphoreType.DMA((6,)),
        ],
        compiler_params=params(collective_id),
        cost_estimate=cost(10**9, 10**8),
    )(
        d_mixed, heads, length, cos, sin, parts, up, up_one, gate, early, first, d_attn, normed_one, mixed,
        tokens, gain, d_hidden, w_query, w_key, w_value,
    )


def gated(gate, up):
    squash = 1.0 / (1.0 + jnp.exp(-gate))
    silu = gate * squash
    slope = squash * (1.0 + gate * (1.0 - squash))
    return silu, slope


SLOTS = 48
DEPTH = 4
SLOT_ROWS = 16 * SLOTS


def slot_lines(meta):
    member = jnp.where(meta[...].reshape(32, 128) > 0, 1.0, 0.0)
    before = lax.broadcasted_iota(jnp.int32, (128, 128), 0) < lax.broadcasted_iota(jnp.int32, (128, 128), 1)
    count = dot(member.astype(BF16), jnp.where(before, 1.0, 0.0).astype(BF16))
    return jnp.where(member > 0, count, -1.0)


def experts_kernel(
    meta, weight, rows, cots, gate_w, up_w, down_w, out, d_rows, kept_act, kept_back, down_sum,
    gate_up, down, slot_rows, slot_cots, slot_out, slot_back, lines, columns, act, back,
    out_buf, term, land, in_sem, out_sem, weight_sem, keep_sem, send, recv, own,
):
    hidden = down.shape[1]
    x, y, z, core = place()
    x_peers = [device((x + 1) % 4, y, z, core), device((x + 3) % 4, y, z, core)]

    def load(expert):
        return [
            pltpu.make_async_copy(gate_w.at[expert], gate_up.at[expert, :, 0:hidden], weight_sem.at[expert, 0]),
            pltpu.make_async_copy(up_w.at[expert], gate_up.at[expert, :, hidden : 2 * hidden], weight_sem.at[expert, 1]),
            pltpu.make_async_copy(down_w.at[expert], down.at[expert], weight_sem.at[expert, 2]),
        ]

    def fetch(expert):
        return [
            pltpu.make_async_copy(rows.at[expert], slot_rows.at[expert], in_sem.at[expert, 0]),
            pltpu.make_async_copy(cots.at[expert], slot_cots.at[expert], in_sem.at[expert, 1]),
        ]

    for expert in range(2):
        for copy in fetch(expert) + load(expert):
            copy.start()
    greet(x_peers)
    copies = Copies(send, recv, own)
    lines[...] = slot_lines(meta).reshape(16, 2, 128)
    columns[...] = jnp.concatenate([lines[...].reshape(32, 128), jnp.zeros((96, 128), F32)], axis=0).T
    keeps = [
        pltpu.make_async_copy(src, dst, keep_sem.at[i])
        for i, (src, dst) in enumerate(((act, kept_act), (back, kept_back)))
    ]

    def main(expert):
        for copy in fetch(expert) + load(expert):
            copy.wait()

        tile = 256

        @pl.loop(0, SLOT_ROWS // tile)
        def _(index):
            at = pl.ds(pl.multiple_of(index * tile, tile), tile)
            both = dot(slot_rows[expert, at], gate_up[expert])
            gate, up = both[:, :hidden], both[:, hidden:]
            silu, slope = gated(gate, up)
            activated = (silu * up).astype(BF16)
            act[expert, at] = activated
            produced = dot(activated, down[expert]).astype(BF16).astype(F32)
            slot_out[expert, at] = (produced * weight[expert, at][:, 0:1]).astype(BF16)
            d_act = dot_nt(slot_cots[expert, at], down[expert])
            back[expert, at, 0:hidden] = (d_act * up * slope).astype(BF16)
            back[expert, at, hidden : 2 * hidden] = (d_act * silu).astype(BF16)
            slot_back[expert, at] = dot_nt(back[expert, at], gate_up[expert]).astype(BF16)

    main(0)

    @pl.loop(0, hidden // 128)
    def _(index):
        at = pl.ds(pl.multiple_of(index * 128, 128), 128)
        term[at] = dot_tn(act[0, :, at], slot_cots[0]).astype(BF16)

    def part(chunk, half):
        return term.at[pl.ds(pl.multiple_of(chunk * 224 + half * 112, 112), 112)]

    def add(out, *terms):
        add_into(out, (), *terms, rows=(16, 7))

    ring = RingSum(copies, x, x_peers[0], x_peers[1], part, land, None, add, resident=True)
    ring.raw()
    main(1)
    ring.forward()
    keeps[0].start()
    keeps[1].start()

    def store(block):
        slot = block % DEPTH
        return [
            pltpu.make_async_copy(out_buf.at[slot, 0], out.at[block], out_sem.at[slot, 0]),
            pltpu.make_async_copy(out_buf.at[slot, 1], d_rows.at[block], out_sem.at[slot, 1]),
        ]

    lane = lax.broadcasted_iota(jnp.int32, (128, 2 * SLOTS), 1).astype(F32)
    for block in range(16):
        slot = block % DEPTH
        first, second = columns[:, 2 * block : 2 * block + 1], columns[:, 2 * block + 1 : 2 * block + 2]
        hit = ((lane < SLOTS) & (lane == first)) | ((lane >= SLOTS) & (lane - SLOTS == second))
        both = jnp.where(hit, 1.0, 0.0).astype(BF16)
        if block >= DEPTH:
            for copy in store(block - DEPTH):
                copy.wait()
        at = slice(block * SLOTS, (block + 1) * SLOTS)
        for index, source in enumerate((slot_out, slot_back)):
            value = jnp.concatenate([source[0, at], source[1, at]], axis=0)
            out_buf[slot, index] = dot(both, value).astype(BF16)
        for copy in store(block):
            copy.start()
    for block in range(16 - DEPTH, 16):
        for copy in store(block):
            copy.wait()
    ring.finish([down_sum.at[0:112], down_sum.at[112:224]])
    copies.drain()
    for copy in keeps:
        copy.wait()


def experts(meta, weight, rows, cots, gate_w, up_w, down_w, collective_id):
    width, hidden = gate_w.shape[1:]
    return pl.pallas_call(
        experts_kernel,
        name="experts",
        out_shape=(
            jax.ShapeDtypeStruct((16, 128, width), BF16),
            jax.ShapeDtypeStruct((16, 128, width), BF16),
            jax.ShapeDtypeStruct((2, SLOT_ROWS, hidden), BF16),
            jax.ShapeDtypeStruct((2, SLOT_ROWS, 2 * hidden), BF16),
            jax.ShapeDtypeStruct((hidden // 4, width), BF16),
        ),
        in_specs=[VMEM, VMEM] + [ANYWHERE] * 5,
        out_specs=[ANYWHERE] * 4 + [VMEM],
        scratch_shapes=[
            pltpu.VMEM((2, width, 2 * hidden), BF16),
            pltpu.VMEM((2, hidden, width), BF16),
            pltpu.VMEM((2, SLOT_ROWS, width), BF16),
            pltpu.VMEM((2, SLOT_ROWS, width), BF16),
            pltpu.VMEM((2, SLOT_ROWS, width), BF16),
            pltpu.VMEM((2, SLOT_ROWS, width), BF16),
            pltpu.VMEM((16, 2, 128), F32),
            pltpu.VMEM((128, 128), F32),
            pltpu.VMEM((2, SLOT_ROWS, hidden), BF16),
            pltpu.VMEM((2, SLOT_ROWS, 2 * hidden), BF16),
            pltpu.VMEM((DEPTH, 2, 128, width), BF16),
            pltpu.VMEM((hidden, width), BF16),
            pltpu.VMEM((6, hidden // 8, width), BF16),
            pltpu.SemaphoreType.DMA((2, 2)),
            pltpu.SemaphoreType.DMA((DEPTH, 2)),
            pltpu.SemaphoreType.DMA((2, 3)),
            pltpu.SemaphoreType.DMA((2,)),
            pltpu.SemaphoreType.DMA((6,)),
            pltpu.SemaphoreType.DMA((6,)),
            pltpu.SemaphoreType.DMA((1,)),
        ],
        compiler_params=params(collective_id),
        cost_estimate=cost(12 * 2 * SLOT_ROWS * width * hidden, 6 * 10**7),
    )(meta, weight, rows, cots, gate_w, up_w, down_w)


def finish_kernel(
    packed, gate, up_zero, up_one, down_zero, down_one, grad, hidden, shared_out, routed,
    block_out, input_grad, attn_gain, query, key, value, out, ffn_gain, s_gate, s_up, s_down, gate_grad, up_grad, down_grad,
):
    block_out[...] = hidden[...] + shared_out[...] + routed[...]
    input_grad[...] = grad[...]
    gate_grad[...] = gate[...]
    up_grad[0] = up_zero[...]
    up_grad[1] = up_one[...]
    down_grad[0] = down_zero[...]
    down_grad[1] = down_one[...]
    gains = packed[0, 0, 10:11]
    for source in range(1, 8):
        gains = gains + packed[source, 0, 10:11]
    attn_gain[...] = gains[:, 0:10]
    ffn_gain[...] = gains[:, 10:20]
    for core in range(2):
        for panel in range(20):
            if panel < 15:
                part = packed[2 * (panel // 4) + core, 4 + panel % 4, 0:10]
                at = core * 1920 + panel * 128
                (query, key, value)[at // 1280][:, at % 1280 : at % 1280 + 128] = part
            else:
                part = packed[2 * (panel - 15) + core, 3, 0:10] if panel < 19 else packed[6 + core, 7, 0:10]
                at = core * 640 + (panel - 15) * 128
                out[:, at : at + 128] = part
        for panel in range(12):
            where = (panel // 2, panel % 2) if panel < 8 else (panel - 8, 2)
            part = packed[2 * where[0] + core, where[1], 0:10]
            if panel < 7:
                (s_gate, s_up)[core][:, panel * 128 : panel * 128 + 128] = part
            else:
                at = core * 640 + (panel - 7) * 128
                s_down[:, at : at + 128] = part[0:7]


def finish(packed, *values):
    def shape(*dims):
        return jax.ShapeDtypeStruct(dims, F32)

    return pl.pallas_call(
        finish_kernel,
        name="finish",
        out_shape=(
            shape(128, 1280), shape(128, 1280), shape(1, 10),
            shape(10, 1280), shape(10, 1280), shape(10, 1280), shape(10, 1280), shape(1, 10),
            shape(10, 896), shape(10, 896), shape(7, 1280),
            shape(2, 160, 896), shape(2, 160, 896), shape(2, 112, 1280),
        ),
        in_specs=[VMEM] * 10,
        out_specs=(VMEM,) * 14,
        compiler_params=params(),
        cost_estimate=cost(10**7, 12 * 10**6),
    )(packed, *values)


def with_weights(cot, routes, route_gates, row_live):
    routed = routes[:, :, None] == jnp.arange(32, dtype=jnp.int32)[None, None, :]
    live = jnp.where(row_live, 1.0, 0.0)
    table = jnp.sum(jnp.where(routed, route_gates[:, :, None], 0.0), axis=1) * live[:, None]
    table = table.T
    high = table.astype(BF16)
    low = (table - high.astype(F32)).astype(BF16)
    lines = jnp.stack([high, low]).reshape(4, 16, 128).transpose(1, 0, 2).reshape(16, 512)
    return jnp.concatenate([cot, jnp.pad(lines, ((0, 0), (0, 768)))], axis=0)


def local(
    tokens,
    lengths,
    routes,
    route_gates,
    attn_gain,
    w_query,
    w_key,
    w_value,
    w_out,
    ffn_gain,
    shared_gate,
    shared_up,
    shared_down,
    expert_gate,
    expert_up,
    expert_down,
    cotangent,
):
    resident, cot = tokens[0], cotangent[0]
    rows = resident.shape[0]
    ctx = lax.axis_index("ctx")
    positions = ctx * rows + jnp.arange(rows, dtype=jnp.int32)
    all_cos, all_sin = turn_tables(8 * rows)
    back_sin = jnp.asarray(-all_sin)
    all_cos, all_sin = jnp.asarray(all_cos), jnp.asarray(all_sin)
    sent_cot = with_weights(cot, routes[0], route_gates[0], positions < lengths[0])

    qkv, normed_one = project(resident, attn_gain, w_query, w_key, w_value, all_cos, all_sin)
    mixed, heads, cots, hidden, normed_two = attend(qkv, lengths, sent_cot, w_out, resident, ffn_gain, 1)
    slot_rows, slot_cots, meta, weight, shared_out, d_shared, early = gather_rows(
        normed_two, cot, cots, shared_gate, shared_up, shared_down, 2
    )
    parts, d_parts, kept_act, kept_back, down_one = experts(
        meta, weight, slot_rows, slot_cots, expert_gate, expert_up, expert_down, 5
    )
    gate_sum, up_term, up_one, down_term, down_zero, first, d_mixed, d_hidden, d_attn, ffn_term = scatter_rows(
        d_parts, slot_rows, slot_cots, kept_act, kept_back, early, d_shared, hidden, ffn_gain, cot, w_out, down_one, 3
    )
    grad, attn_term, routed, up_sum, up_last, gate_grad, first_sum, second, late = attend_back(
        d_mixed, heads, lengths, all_cos, back_sin, parts, up_term, up_one, gate_sum, early, first, d_attn, normed_one,
        mixed, resident, attn_gain, d_hidden, w_query, w_key, w_value, 4,
    )
    packed, up_first, down_last = sum_grads(
        late, first_sum, second, gain_lines(attn_term[0], ffn_term[0]), up_sum, down_term
    )
    outs = finish(
        packed, gate_grad, up_first, up_last, down_zero, down_last, grad, hidden, shared_out, routed
    )
    return (outs[0][None], outs[1][None], outs[2][0], *outs[3:7], outs[7][0], *outs[8:])


def solution(mesh):
    in_specs = (
        P("exp", "ctx", None),
        P("exp"),
        P("exp", "ctx", None),
        P("exp", "ctx", None),
        P(),
        P(),
        P(),
        P(),
        P(),
        P(),
        P(),
        P(),
        P(),
        P("exp", None, None),
        P("exp", None, None),
        P("exp", None, None),
        P("exp", "ctx", None),
    )
    out_specs = (
        P("exp", "ctx", None),
        P("exp", "ctx", None),
        P(("ctx", "exp")),
        P(("ctx", "exp"), None),
        P(("ctx", "exp"), None),
        P(("ctx", "exp"), None),
        P(("ctx", "exp"), None),
        P(("ctx", "exp")),
        P(("ctx", "exp"), None),
        P(("ctx", "exp"), None),
        P(("ctx", "exp"), None),
        P("exp", "ctx", None),
        P("exp", "ctx", None),
        P("exp", "ctx", None),
    )
    return jax.shard_map(local, mesh=mesh, in_specs=in_specs, out_specs=out_specs, check_vma=False)
```

```python
import functools
import math

import jax
import jax.numpy as jnp
import numpy as np
from jax import lax
from jax.experimental import pallas as pl
from jax.experimental.pallas import tpu as pltpu
from jax.sharding import PartitionSpec as P

MESH = pl.DeviceIdType.MESH
HEAD_DIM = 128
VMEM_LIMIT = 60 * 2**20
F32, BF16 = jnp.float32, jnp.bfloat16


def place():
    ctx, exp = lax.axis_index("ctx"), lax.axis_index("exp")
    return ctx // 2, (exp // 8) * 2 + ctx % 2, (exp // 2) % 4, exp % 2


def device(x, y, z, core):
    return (x * 2 + y % 2, (y // 2) * 8 + z * 2 + core)


def greet(devices):
    barrier = pltpu.get_barrier_semaphore()
    for target in devices:
        pl.semaphore_signal(barrier, inc=1, device_id=target, device_id_type=MESH)
    pl.semaphore_wait(barrier, len(devices))


class Copies:
    def __init__(self, send, recv, own):
        self.send, self.recv, self.own = send, recv, own
        self.remotes, self.locals = 0, 0
        self.started = []

    def remote(self, src, dst, target):
        index = self.remotes
        self.remotes += 1
        copy = pltpu.make_async_remote_copy(
            src_ref=src,
            dst_ref=dst,
            send_sem=self.send.at[index],
            recv_sem=self.recv.at[index],
            device_id=target,
            device_id_type=MESH,
        )
        copy.start()
        self.started.append(copy)
        return copy

    def local(self, src, dst):
        index = self.locals
        self.locals += 1
        copy = pltpu.make_async_copy(src, dst, self.own.at[index])
        copy.start()
        return copy

    def drain(self):
        for copy in self.started:
            copy.wait_send()


def each(shape, body):
    @pl.loop(0, math.prod(shape))
    def _(step):
        index = []
        for size in reversed(shape):
            index.append(step % size)
            step = step // size
        body(tuple(reversed(index)))


def add_into(out, shape, *terms, rows=None):
    def body(index):
        total = terms[0][index].astype(F32)
        for term in terms[1:]:
            total = total + term[index].astype(F32)
        out[index] = total.astype(out.dtype)

    if rows is None:
        each(shape, body)
    else:
        step, count = rows
        each(shape + (count,), lambda i: body(i[:-1] + (pl.ds(pl.multiple_of(i[-1] * step, step), step),)))


class RingSum:
    def __init__(self, copies, me, right, left, part, land, work, add, resident=None):
        self.copies, self.right, self.left, self.land, self.work, self.add = copies, right, left, land, work, add
        self.part = part
        self.after, self.before, across = (me + 1) % 4, (me + 3) % 4, (me + 2) % 4
        self.one = copies.remote(part(across, 0), land.at[0], right)
        self.two = copies.remote(part(across, 1), land.at[1], left)
        sources = [part(self.after, 0), part(self.before, 1), part(me, 0), part(me, 1)]
        if resident is None:
            self.loads = [copies.local(source, work.at[i]) for i, source in enumerate(sources)]
            self.own = [work.at[i] for i in range(4)]
        else:
            self.loads = []
            self.own = sources

    def raw(self):
        self.three = self.copies.remote(self.part(self.after, 1), self.land.at[2], self.right)
        self.four = self.copies.remote(self.part(self.before, 0), self.land.at[4], self.left)

    def forward(self):
        for load in self.loads:
            load.wait()
        self.one.wait_recv()
        self.add(self.land.at[0], self.land.at[0], self.own[0])
        self.five = self.copies.remote(self.land.at[0], self.land.at[3], self.right)
        self.two.wait_recv()
        self.add(self.land.at[1], self.land.at[1], self.own[1])
        self.six = self.copies.remote(self.land.at[1], self.land.at[5], self.left)

    def finish(self, outs):
        for copy in (self.three, self.four, self.five, self.six):
            copy.wait_recv()
        self.add(outs[0], self.own[2], self.land.at[3], self.land.at[4])
        self.add(outs[1], self.own[3], self.land.at[2], self.land.at[5])


GRAD_REMOTES = 4 * 6 + 2 + 3 * 2 + 3 * 3 + 6 + 3 * 4 + 7
GRAD_LOCALS = 4 * 4


def add_blocks(shape):
    def add(out, *terms):
        add_into(out, shape, *terms)

    return add


def half_rows(which, size):
    return pl.ds(pl.multiple_of(which * size, size), size)


def order(y):
    return (y % 2) * 2 + y // 2


def grads_kernel(
    late, first, second, gains, up, down, dense_out, up_out, down_out,
    z_land, z_work, f_land, y_land, y_sum, x_land, u_land, u_work, v_land, v_sum, w_land,
    t_land, t_work, tz_land, t_sum, tx_land,
    gx_land, gx_sum, gy_land, total, stage, final_land, up_other, d_land, d_work, d_other, send, recv, own,
):
    x, y, z, core = place()
    y_half, y_low = y // 2, y % 2
    spot = z * 2 + core
    x_peers = [device((x + d) % 4, y, z, core) for d in (1, 2, 3)]
    y_peers = [device(x, (y + d) % 4, z, core) for d in (1, 2, 3)]
    z_peers = [device(x, y, (z + d) % 4, core) for d in (1, 2, 3)]
    spot_peers = [device(x, y, ((spot + d) % 8) // 2, (spot + d) % 2) for d in range(1, 8)]
    pair = device(x, y_half * 2 + 1 - y_low, z, core)
    greet(x_peers + y_peers + spot_peers)
    copies = Copies(send, recv, own)

    def direct(part, me, land, peers):
        return [copies.remote(part((me + d) % 4), land.at[d - 1], peers[d - 1]) for d in (1, 2, 3)]

    def arrived(arrivals):
        for copy in arrivals:
            copy.wait_recv()

    ring = RingSum(
        copies, z, z_peers[0], z_peers[2], lambda c, h: late.at[c, h], z_land, z_work, add_blocks((4, 4))
    )
    ring.raw()
    side = RingSum(
        copies, x, x_peers[0], x_peers[2], lambda c, h: late.at[2 * h : 2 * h + 2, 2, c],
        u_land, u_work, add_blocks((2, 4)),
    )
    gain_x = direct(lambda c: gains.at[c], x, gx_land, x_peers)
    tall = RingSum(
        copies, y, y_peers[0], y_peers[2], lambda c, h: late.at[2 * h : 2 * h + 2, 3, :, order(c)],
        t_land, t_work, add_blocks((2, 4)),
    )
    side.raw()
    tall.raw()

    def down_add(out, *terms):
        add_into(out, (), *terms, rows=(16, 7))

    downs = RingSum(
        copies, x, x_peers[0], x_peers[2],
        lambda c, h: down.at[half_rows(2 * c + h, 112)], d_land, d_work, down_add,
    )
    side.forward()
    tall.forward()
    x_copies = {0: direct(lambda c: first.at[:, c], x, f_land, x_peers)}
    y_copies = {1: direct(lambda c: second.at[:, :, order(c)], y, y_land.at[1, :, 0:1], y_peers)}
    swap_up = copies.remote(up.at[1 - y_low], up_other, pair)
    downs.raw()
    ring.forward()
    arrived(gain_x)
    gx_sum[...] = gains[x] + gx_land[0] + gx_land[1] + gx_land[2]
    gain_y = direct(lambda c: gx_sum.at[order(c)], y, gy_land, y_peers)
    downs.forward()

    def start_x(t, mine, panels):
        arrived(y_copies[t])
        lands = [y_land.at[t, d, 0:panels] for d in range(3)]
        add_into(y_sum.at[t], (panels, 4), mine, *lands)
        x_copies[t] = direct(lambda c: y_sum.at[t, 0:panels, c], x, x_land.at[t, :, 0:panels], x_peers)

    side.finish([u_work.at[2], u_work.at[3]])
    side_z = direct(lambda c: u_work.at[2 + c // 2, c % 2], z, v_land, z_peers)
    tall.finish([t_work.at[2], t_work.at[3]])
    tall_z = direct(lambda c: t_work.at[2 + c // 2, c % 2], z, tz_land, z_peers)
    start_x(1, second.at[:, :, order(y)], 1)
    ring.finish([z_work.at[2], z_work.at[3]])
    y_copies[2] = direct(lambda c: z_work.at[2:4, :, order(c)], y, y_land.at[2], y_peers)
    arrived(side_z)
    add_into(v_sum, (4,), u_work.at[2 + z // 2, z % 2], v_land.at[0], v_land.at[1], v_land.at[2])
    side_y = direct(lambda c: v_sum.at[order(c)], y, w_land, y_peers)
    arrived(tall_z)
    add_into(t_sum, (4,), t_work.at[2 + z // 2, z % 2], tz_land.at[0], tz_land.at[1], tz_land.at[2])
    tall_x = direct(lambda c: t_sum.at[c], x, tx_land, x_peers)
    downs.finish([d_work.at[2], d_work.at[3]])
    swap_down = copies.remote(d_work.at[2 + 1 - y_low], d_other, pair)
    swap_up.wait_recv()
    add_into(up_out, (), up.at[y_low], up_other, rows=(16, 10))
    start_x(2, z_work.at[2:4, :, order(y)], 2)

    def summed(panel, first_part, land, *index):
        value = first_part.astype(F32)
        for d in range(3):
            value = value + land[(d,) + index].astype(F32)
        total[panel, 0:80] = value
        total[panel, 80:96] = jnp.zeros((16, 128), F32)

    arrived(gain_y)
    lines = gx_sum[order(y)] + gy_land[0] + gy_land[1] + gy_land[2]
    arrived(side_y)
    summed(6, v_sum[order(y)], w_land)
    arrived(tall_x)
    summed(7, t_sum[x], tx_land)
    arrived(x_copies[0])
    for panel in range(3):
        summed(panel, first[panel, x], f_land, panel)
    for t, panels in ((1, (3,)), (2, (4, 5))):
        arrived(x_copies[t])
        for half, panel in enumerate(panels):
            summed(panel, y_sum[t, half, x], x_land.at[t], half)
    for j in range(8):
        for panel in range(8):
            stage[j, panel] = total[panel, 10 * j : 10 * j + 16]
        stage[j, 0, 10:11] = lines[j : j + 1]
    finals = [
        copies.remote(stage.at[(spot + d) % 8], final_land.at[d], spot_peers[d - 1]) for d in range(1, 8)
    ]
    swap_down.wait_recv()
    add_into(down_out, (), d_work.at[2 + y_low], d_other, rows=(16, 7))
    dense_out[spot] = stage[spot]
    for d, copy in enumerate(finals):
        copy.wait_recv()
        dense_out[(spot + 7 - d) % 8] = final_land[d + 1]
    copies.drain()


def sum_grads(late, first, second, gains, up, down):
    scratch = [
        pltpu.VMEM((6, 4, 4, 80, 128), BF16),
        pltpu.VMEM((4, 4, 4, 80, 128), BF16),
        pltpu.VMEM((3, 3, 80, 128), BF16),
        pltpu.VMEM((3, 3, 2, 4, 80, 128), BF16),
        pltpu.VMEM((3, 2, 4, 80, 128), BF16),
        pltpu.VMEM((3, 3, 2, 80, 128), BF16),
        pltpu.VMEM((6, 2, 4, 80, 128), BF16),
        pltpu.VMEM((4, 2, 4, 80, 128), BF16),
        pltpu.VMEM((3, 4, 80, 128), BF16),
        pltpu.VMEM((4, 80, 128), BF16),
        pltpu.VMEM((3, 80, 128), BF16),
        pltpu.VMEM((6, 2, 4, 80, 128), BF16),
        pltpu.VMEM((4, 2, 4, 80, 128), BF16),
        pltpu.VMEM((3, 4, 80, 128), BF16),
        pltpu.VMEM((4, 80, 128), BF16),
        pltpu.VMEM((3, 80, 128), BF16),
        pltpu.VMEM((3, 4, 8, 128), F32),
        pltpu.VMEM((4, 8, 128), F32),
        pltpu.VMEM((3, 8, 128), F32),
        pltpu.VMEM((8, 96, 128), F32),
        pltpu.VMEM((8, 8, 16, 128), F32),
        pltpu.VMEM((8, 8, 16, 128), F32),
        pltpu.VMEM((160, 896), BF16),
        pltpu.VMEM((6, 112, 1280), BF16),
        pltpu.VMEM((4, 112, 1280), BF16),
        pltpu.VMEM((112, 1280), BF16),
        pltpu.SemaphoreType.DMA((GRAD_REMOTES,)),
        pltpu.SemaphoreType.DMA((GRAD_REMOTES,)),
        pltpu.SemaphoreType.DMA((GRAD_LOCALS,)),
    ]
    return pl.pallas_call(
        grads_kernel,
        name="sum_grads",
        out_shape=(
            jax.ShapeDtypeStruct((8, 8, 16, 128), F32),
            jax.ShapeDtypeStruct((160, 896), F32),
            jax.ShapeDtypeStruct((112, 1280), F32),
        ),
        in_specs=[ANYWHERE, VMEM, VMEM, VMEM, VMEM, ANYWHERE],
        out_specs=(VMEM,) * 3,
        scratch_shapes=scratch,
        compiler_params=params(0),
        cost_estimate=cost(10**8, 4 * 10**8),
    )(late.reshape(4, 4, 4, 4, 80, 128), first, second.reshape(1, 4, 4, 80, 128), gains, up, down)


def gain_lines(attn_term, ffn_term):
    both = jnp.concatenate([attn_term, ffn_term]).reshape(2, 16, 8, 10).transpose(1, 2, 0, 3).reshape(4, 4, 8, 20)
    return jnp.pad(both, ((0, 0), (0, 0), (0, 0), (0, 108)))


VMEM = pl.BlockSpec(memory_space=pltpu.VMEM)
ANYWHERE = pl.BlockSpec(memory_space=pl.ANY)
SMEM = pl.BlockSpec(memory_space=pltpu.SMEM)
SCALE = HEAD_DIM ** (-0.5)


def params(collective_id=None):
    if collective_id is None:
        return pltpu.CompilerParams(vmem_limit_bytes=VMEM_LIMIT)
    return pltpu.CompilerParams(
        collective_id=collective_id, has_side_effects=True, vmem_limit_bytes=VMEM_LIMIT
    )


def cost(flops, bytes_accessed):
    return pl.CostEstimate(flops=int(flops), bytes_accessed=int(bytes_accessed), transcendentals=0)


def dot(left, right):
    return jnp.dot(left, right, preferred_element_type=F32)


def dot_nt(left, right):
    return lax.dot_general(left, right, (((1,), (1,)), ((), ())), preferred_element_type=F32)


def dot_tn(left, right):
    return lax.dot_general(left, right, (((0,), (0,)), ((), ())), preferred_element_type=F32)


def normed(values, gain):
    return values * lax.rsqrt(jnp.mean(values * values, axis=-1, keepdims=True) + 1e-06) * gain


def normed_back(values, gain, upstream):
    factor = lax.rsqrt(jnp.mean(values * values, axis=-1, keepdims=True) + 1e-06)
    scaled = upstream * gain
    inner = jnp.mean(scaled * values, axis=-1, keepdims=True)
    term = jnp.sum(upstream * values * factor, axis=0, keepdims=True)
    return factor * scaled - values * factor * factor * factor * inner, term


def turned(values, cos, sin):
    return values * cos + pltpu.roll(values, HEAD_DIM // 2, 1) * sin


def turn_tables(count):
    half = HEAD_DIM // 2
    frequency = np.exp(np.arange(half, dtype=np.float32) * np.float32(-2.0 * math.log(10000.0) / HEAD_DIM))
    angle = np.arange(count, dtype=np.float32)[:, None] * frequency[None, :]
    cos, sin = np.cos(angle), np.sin(angle)
    return np.concatenate([cos, cos], axis=1), np.concatenate([-sin, sin], axis=1)


def rank(y_half, z, core):
    return y_half * 8 + z * 2 + core


class Gather:
    def __init__(self, copies, where, src, out, cut, far, far_cut):
        x, y, z, core = where
        self.copies, self.out, self.cut, self.far_rows, self.far_cut = copies, out, cut, far, far_cut
        self.rows = out.shape[1]
        self.split = far < self.rows
        self.y_half, self.z, self.core = y // 2, z, core
        self.pair = device(x, y, z, 1 - core)
        self.across = device(x, (y + 2) % 4, z, core)
        self.right, self.left = device(x, y, (z + 1) % 4, core), device(x, y, (z + 3) % 4, core)
        me = rank(self.y_half, z, core)
        self.mine = copies.local(src, out.at[me])
        self.over = copies.remote(src, out.at[me], self.across)
        self.to_right = copies.remote(src, out.at[me], self.right)
        self.to_left = copies.remote(src, out.at[me], self.left)
        self.pairs = [copies.remote(src, out.at[me], self.pair)]
        self.seen = 0

    def shard(self, other, dz):
        y_half = 1 - self.y_half if other else self.y_half
        return rank(y_half, (self.z + dz + 4) % 4, self.core)

    def send(self, ref, target):
        return self.copies.remote(ref, ref, target)

    def share(self, ref):
        self.pairs.append(self.send(ref, self.pair))

    def near(self):
        self.to_right.wait_recv()
        index = self.shard(False, -1)
        self.on_right = self.send(self.out.at[index, 0 : self.cut], self.right)
        if self.split:
            self.side_before = self.send(self.out.at[index, self.far_rows : self.rows], self.across)
        self.share(self.out.at[index])
        self.to_left.wait_recv()
        index = self.shard(False, 1)
        self.on_left = self.send(self.out.at[index, self.cut : self.rows], self.left)
        if self.split:
            self.side_after = self.send(self.out.at[index, self.far_rows : self.rows], self.across)
        self.share(self.out.at[index])

    def far(self):
        self.over.wait_recv()
        index = self.shard(True, 0)
        self.far_right = self.send(self.out.at[index, 0 : self.far_rows], self.right)
        self.far_left = self.send(self.out.at[index, 0 : self.far_rows], self.left)
        self.share(self.out.at[index])

    def middle(self):
        index = self.shard(False, 2)
        self.on_right.wait_recv()
        self.share(self.out.at[index, 0 : self.cut])
        self.on_left.wait_recv()
        if self.split:
            self.side_middle = self.send(self.out.at[index, self.far_rows : self.rows], self.across)
        self.share(self.out.at[index, self.cut : self.rows])

    def third(self):
        self.far_right.wait_recv()
        index = self.shard(True, -1)
        self.far_on_right = self.send(self.out.at[index, 0 : self.far_cut], self.right)
        self.share(self.out.at[index, 0 : self.far_rows])
        self.far_left.wait_recv()
        index = self.shard(True, 1)
        self.far_on_left = self.send(self.out.at[index, self.far_cut : self.far_rows], self.left)
        self.share(self.out.at[index, 0 : self.far_rows])

    def sides(self):
        for copy, dz in ((self.side_before, -1), (self.side_after, 1)):
            copy.wait_recv()
            self.share(self.out.at[self.shard(True, dz), self.far_rows : self.rows])

    def pairs_arrived(self, count):
        for copy in self.pairs[self.seen : count]:
            copy.wait_recv()
        self.seen = count

    def last(self):
        index = self.shard(True, 2)
        self.far_on_right.wait_recv()
        self.share(self.out.at[index, 0 : self.far_cut])
        self.far_on_left.wait_recv()
        self.share(self.out.at[index, self.far_cut : self.far_rows])
        if self.split:
            self.side_middle.wait_recv()
            self.share(self.out.at[index, self.far_rows : self.rows])
        self.pairs_arrived(len(self.pairs))


GATHER_REMOTES = 3 + 2 + 2 + 2 + 8 + 2


def exp_peers(where):
    x, y, z, core = where
    return [
        device(x, y, z, 1 - core),
        device(x, (y + 2) % 4, z, core),
        device(x, y, (z + 1) % 4, core),
        device(x, y, (z + 3) % 4, core),
    ]


def gather_kernel(
    rows, cot, cots, gate_w, up_w, down_w, spread,
    slot_rows, slot_cots, meta, weight, shared_out, d_shared, early,
    every, cots_in, gate, up, down, spread_in, filled_rows, filled_cots, lines, act, d_gates, pair_act, pair_gates,
    right, act_left, panels, send, recv, own, load_sem, keep_sem, early_sem,
):
    where = place()
    core, y_half = where[3], where[1] // 2
    me = lax.axis_index("exp")
    other = me + 1 - 2 * core
    loads = [
        pltpu.make_async_copy(src, dst, load_sem.at[i])
        for i, (src, dst) in enumerate(((gate_w, gate), (up_w, up), (down_w, down), (cots, cots_in), (spread, spread_in)))
    ]
    for load in loads:
        load.start()
    greet(exp_peers(where))
    copies = Copies(send, recv, own)
    gather = Gather(copies, where, rows, every, 64, 80, 48)
    shared_out[...] = jnp.zeros_like(shared_out)
    d_shared[...] = jnp.zeros_like(d_shared)

    def shared(first, last):
        @pl.loop(first, last)
        def _(step):
            at = pl.ds(pl.multiple_of(step * 128, 128), 128)
            value = rows[...]
            gate_pre, up_pre = dot(value, gate[:, at]), dot(value, up[:, at])
            silu, slope = gated(gate_pre, up_pre)
            activated = (silu * up_pre).astype(BF16)
            act[:, at] = activated
            shared_out[...] += dot(activated, down[at])
            d_act = dot_nt(cot[...], down[at])
            gate_back = (d_act * up_pre * slope).astype(BF16)
            up_back = (d_act * silu).astype(BF16)
            d_gates[0, :, at] = gate_back
            d_gates[1, :, at] = up_back
            d_shared[...] += dot_nt(gate_back, gate[:, at]) + dot_nt(up_back, up[:, at])

    def hot(block):
        slot = lax.broadcasted_iota(jnp.int32, (SLOTS, 128), 0).astype(F32)
        return [jnp.where(slot == lines[block, e : e + 1], 1.0, 0.0) for e in range(2)]

    def fill(block, source, out, column=None):
        value = dot(jnp.concatenate(hot(block), axis=0).astype(BF16), source)
        if column is not None:
            value = value * column
        value = value.astype(BF16)
        at = pl.ds(pl.multiple_of(block * SLOTS, SLOTS), SLOTS)
        for expert in range(2):
            out[expert, at] = value[expert * SLOTS : (expert + 1) * SLOTS]

    def fill_cots(block):
        column = jnp.concatenate(
            [jnp.sum(one * meta[block, e : e + 1], axis=1, keepdims=True) for e, one in enumerate(hot(block))], axis=0
        )
        at = pl.ds(pl.multiple_of(block * SLOTS, SLOTS), SLOTS)
        for expert in range(2):
            weight[expert, at] = jnp.broadcast_to(column[expert * SLOTS : (expert + 1) * SLOTS], (SLOTS, 128))
        fill(block, cots_in[block, 0:128], filled_cots, column)

    def fill_rows(far, dz):
        own_block = gather.shard(far, dz)
        for block in (own_block, own_block + 1 - 2 * core):
            fill(block, every[block], filled_rows)

    for load in loads[:3]:
        load.wait()
    shared(0, 4)
    gather.near()
    gather.far()
    shared(4, 7)
    pair = device(where[0], where[1], where[2], 1 - core)
    from_pair = [copies.remote(act, pair_act, pair), copies.remote(d_gates.at[1 - core], pair_gates, pair)]
    gather.middle()
    loads[3].wait()

    @pl.loop(0, 16)
    def _(block):
        high = cots_in[block, 128:144, pl.ds(pl.multiple_of(y_half * 128, 128), 128)].astype(F32)
        low = cots_in[block, 128:144, pl.ds(pl.multiple_of(256 + y_half * 128, 128), 128)].astype(F32)
        line = lax.broadcasted_iota(jnp.int32, (16, 128), 0)
        for expert in range(2):
            mine = line == 2 * (me % 8) + expert
            meta[block, expert : expert + 1] = jnp.sum(jnp.where(mine, high + low, 0.0), axis=0, keepdims=True)

    lines[...] = slot_lines(meta).reshape(16, 2, 128)

    @pl.loop(0, 16, unroll=4)
    def _(block):
        fill_cots(block)

    gather.third()
    keep_cots = pltpu.make_async_copy(filled_cots, slot_cots, keep_sem.at[0])
    keep_cots.start()
    gather.pairs_arrived(4)
    for copy in from_pair:
        copy.wait_recv()
    loads[4].wait()
    right[0:128, 0:896] = d_gates[core]
    right[128:256, 0:896] = pair_gates[...]
    at = pl.ds(pl.multiple_of(core * 640, 128), 640)
    right[0:128, 896:1536] = cot[:, at]
    right[128:256, 896:1536] = cots_in[other, 0:128, at]
    act_left[...] = dot(jnp.concatenate([act[...], pair_act[...]], axis=0), spread_in[...]).astype(BF16)

    def store(index):
        return pltpu.make_async_copy(
            panels.at[index], early.at[:, pl.ds(pl.multiple_of(index * 256, 256), 256)], early_sem.at[index]
        )

    @pl.loop(0, 5)
    def _(index):
        at = pl.ds(pl.multiple_of(index * 256, 256), 256)
        value = dot_tn(jnp.concatenate([rows[:, at], every[other, :, at]], axis=0), right[:, 0:896])
        for panel in range(7):
            panels[index, panel] = value[:, panel * 128 : panel * 128 + 128].astype(BF16)
        value = dot_tn(act_left[:, at], right[:, 896:1536])
        for panel in range(5):
            panels[index, 7 + panel] = value[:, panel * 128 : panel * 128 + 128].astype(BF16)
        store(index).start()

    gather.mine.wait()
    gather.sides()
    gather.pairs_arrived(6)
    for far, dz in ((False, 0), (False, -1), (False, 1), (True, 0), (False, 2)):
        fill_rows(far, dz)
    gather.pairs_arrived(10)
    for dz in (-1, 1):
        fill_rows(True, dz)
    gather.last()
    fill_rows(True, 2)
    keep_rows = pltpu.make_async_copy(filled_rows, slot_rows, keep_sem.at[1])
    keep_rows.start()
    copies.drain()
    keep_cots.wait()
    keep_rows.wait()
    for index in range(5):
        store(index).wait()


def gather_rows(rows, cot, cots, gate_w, up_w, down_w, collective_id):
    count, width = rows.shape
    hidden = gate_w.shape[1]
    spread = np.zeros((128, 7, 128, 10), np.float32)
    for group in range(128):
        spread[group, np.arange(7), group, np.arange(7)] = 1.0
    spread = jnp.asarray(spread.reshape(hidden, width), BF16)
    return pl.pallas_call(
        gather_kernel,
        name="gather_rows",
        out_shape=(
            jax.ShapeDtypeStruct((2, SLOT_ROWS, width), BF16),
            jax.ShapeDtypeStruct((2, SLOT_ROWS, width), BF16),
            jax.ShapeDtypeStruct((16, 2, 128), F32),
            jax.ShapeDtypeStruct((2, SLOT_ROWS, 128), F32),
            jax.ShapeDtypeStruct((count, width), F32),
            jax.ShapeDtypeStruct((count, width), F32),
            jax.ShapeDtypeStruct((12, width, 128), BF16),
        ),
        in_specs=[VMEM, VMEM] + [ANYWHERE] * 5,
        out_specs=(ANYWHERE, ANYWHERE) + (VMEM,) * 4 + (ANYWHERE,),
        scratch_shapes=[
            pltpu.VMEM((16, count, width), BF16),
            pltpu.VMEM(cots.shape, BF16),
            pltpu.VMEM(gate_w.shape, BF16),
            pltpu.VMEM(up_w.shape, BF16),
            pltpu.VMEM(down_w.shape, BF16),
            pltpu.VMEM(spread.shape, BF16),
            pltpu.VMEM((2, SLOT_ROWS, width), BF16),
            pltpu.VMEM((2, SLOT_ROWS, width), BF16),
            pltpu.VMEM((16, 2, 128), F32),
            pltpu.VMEM((count, hidden), BF16),
            pltpu.VMEM((2, count, hidden), BF16),
            pltpu.VMEM((count, hidden), BF16),
            pltpu.VMEM((count, hidden), BF16),
            pltpu.VMEM((2 * count, 1536), BF16),
            pltpu.VMEM((2 * count, width), BF16),
            pltpu.VMEM((5, 12, 256, 128), BF16),
            pltpu.SemaphoreType.DMA((GATHER_REMOTES + 8,)),
            pltpu.SemaphoreType.DMA((GATHER_REMOTES + 8,)),
            pltpu.SemaphoreType.DMA((1,)),
            pltpu.SemaphoreType.DMA((5,)),
            pltpu.SemaphoreType.DMA((2,)),
            pltpu.SemaphoreType.DMA((5,)),
        ],
        compiler_params=params(collective_id),
        cost_estimate=cost(10**9, 6 * 10**7),
    )(rows, cot, cots, gate_w, up_w, down_w, spread)


class Scatter:
    def __init__(self, copies, where, parts, pair_land, work, ring_land, far_land, y_land):
        x, y, z, core = where
        self.copies, self.work, self.pair_land = copies, work, pair_land
        self.ring_land, self.far_land, self.y_land = ring_land, far_land, y_land
        self.across = device(x, (y + 2) % 4, z, core)
        self.right, self.left = device(x, y, (z + 1) % 4, core), device(x, y, (z + 3) % 4, core)
        pair = device(x, y, z, 1 - core)
        self.pairs, self.loads = {}, {}
        for slot in ((0, 2), (1, 2), (0, 1), (0, 3), (1, 1), (1, 3), (0, 0), (1, 0)):
            y_half = 1 - y // 2 if slot[0] == 0 else y // 2
            at = (z + slot[1]) % 4
            self.pairs[slot] = copies.remote(parts.at[rank(y_half, at, 1 - core)], pair_land.at[slot], pair)
            self.loads[slot] = copies.local(parts.at[rank(y_half, at, core)], work.at[slot])

    def merge(self, slot):
        self.loads[slot].wait()
        self.pairs[slot].wait_recv()
        rows_add(self.work.at[slot], 0, 128, self.work.at[slot], self.pair_land.at[slot])

    def first(self):
        self.ring = {}
        for far in range(2):
            self.merge((far, 2))
            self.ring[far] = (
                self.copies.remote(self.work.at[far, 2, 0:64], self.ring_land.at[far, 0], self.right),
                self.copies.remote(self.work.at[far, 2, 64:128], self.ring_land.at[far, 1], self.left),
            )

    def merge_rest(self):
        for far in range(2):
            self.merge((far, 1))
            self.merge((far, 3))
            self.merge((far, 0))

    def second(self):
        self.final = {}
        for far in range(2):
            self.ring[far][0].wait_recv()
            rows_add(self.work.at[far, 1, 0:64], 0, 64, self.work.at[far, 1, 0:64], self.ring_land.at[far, 0])
            to_right = self.copies.remote(self.work.at[far, 1], self.far_land.at[far, 0], self.right)
            self.ring[far][1].wait_recv()
            rows_add(self.work.at[far, 3, 64:128], 0, 64, self.work.at[far, 3, 64:128], self.ring_land.at[far, 1])
            to_left = self.copies.remote(self.work.at[far, 3], self.far_land.at[far, 1], self.left)
            self.final[far] = (to_right, to_left)

    def third(self):
        for far in range(2):
            for copy in self.final[far]:
                copy.wait_recv()
            rows_add(self.work.at[far, 0], 0, 128, self.work.at[far, 0], self.far_land.at[far, 0], self.far_land.at[far, 1])
            if far == 0:
                self.over = self.copies.remote(self.work.at[0, 0], self.y_land, self.across)

    def last(self, out):
        self.over.wait_recv()
        rows_add(out, 0, 128, self.work.at[1, 0], self.y_land)


def rows_add(out, first, rows, *terms):
    @pl.loop(0, rows // 16)
    def _(step):
        at = pl.ds(pl.multiple_of(step * 16, 16), 16)
        value = terms[0][at].astype(F32)
        for term in terms[1:]:
            value = value + term[at].astype(F32)
        out[at] = value.astype(out.dtype)


SCATTER_REMOTES, SCATTER_LOCALS = 8 + 4 + 4 + 1, 8
SCATTER_SCRATCH = [
    pltpu.VMEM((2, 4, 128, 1280), BF16),
    pltpu.VMEM((2, 4, 128, 1280), BF16),
    pltpu.VMEM((2, 2, 64, 1280), BF16),
    pltpu.VMEM((2, 2, 128, 1280), BF16),
    pltpu.VMEM((128, 1280), BF16),
]


def up_add(out, *terms):
    add_into(out, (), *terms, rows=(16, 10))


def scatter_kernel(
    parts, rows_in, cots_in, act_in, back_in, d_shared, hidden_rows, gain, cot, w_out_in, down_one,
    gate_sum, up_out, up_one, down_out, down_final, d_mixed, d_hidden, d_attn, gain_term,
    a, b, c, d, e, rows, cots, act, back, gate, up, down, land, w_out, d_routed, up_land, one_other,
    send, recv, own, load_sem, keep_sem,
):
    where = place()
    x, y, z, core = where
    x_peers = [device((x + 1) % 4, y, z, core), device((x + 3) % 4, y, z, core)]
    loads = [
        pltpu.make_async_copy(src, dst, load_sem.at[i])
        for i, (src, dst) in enumerate(
            (
                (rows_in.at[0], rows.at[0]), (back_in.at[0], back.at[0]), (rows_in.at[1], rows.at[1]),
                (back_in.at[1], back.at[1]), (act_in.at[1], act), (cots_in.at[1], cots), (w_out_in, w_out),
            )
        )
    ]
    for load in loads:
        load.start()
    greet(exp_peers(where) + x_peers + [device(x, (y // 2) * 2 + 1 - y % 2, z, core)])
    copies = Copies(send, recv, own)
    scatter = Scatter(copies, where, parts, a, b, c, d, e)
    hidden = act.shape[1]
    loads[0].wait()
    loads[1].wait()

    y_low = y % 2
    pair = device(x, (y // 2) * 2 + 1 - y_low, z, core)

    def term(dst, lanes, first, last):
        @pl.loop(first, last)
        def _(index):
            expert = index // 5
            at = pl.ds(pl.multiple_of((index % 5) * 256, 256), 256)
            dst[expert, at] = dot_tn(rows[expert, :, at], back[expert, :, lanes]).astype(BF16)

    def up_rows(chunk, which):
        return pl.ds(pl.multiple_of(chunk * 320 + which * 160, 160), 160)

    swap_one = copies.remote(down_one.at[half_rows(1 - y_low, 112)], one_other, pair)

    def gate_ring(expert):
        return RingSum(
            copies, x, x_peers[0], x_peers[1], lambda chunk, half: gate.at[expert, half_rows(2 * chunk + half, 160)],
            land.at[expert], None, up_add, resident=True,
        )

    term(gate, slice(0, hidden), 0, 5)
    rings = [gate_ring(0)]
    rings[0].raw()
    scatter.first()
    scatter.merge_rest()
    loads[2].wait()
    loads[3].wait()
    term(up, slice(hidden, 2 * hidden), 5, 10)
    over = [copies.remote(up.at[1, up_rows(chunk, 1 - y_low)], up_land.at[chunk], pair) for chunk in range(4)]
    term(gate, slice(0, hidden), 5, 10)
    rings.append(gate_ring(1))
    rings[1].raw()
    scatter.second()
    rings[0].forward()
    term(up, slice(hidden, 2 * hidden), 0, 5)
    keep_up = pltpu.make_async_copy(up.at[0], up_out, keep_sem.at[0])
    keep_up.start()
    loads[4].wait()
    loads[5].wait()

    @pl.loop(0, hidden // 128)
    def _(index):
        at = pl.ds(pl.multiple_of(index * 128, 128), 128)
        down[at] = dot_tn(act[:, at], cots[...]).astype(BF16)

    keep_down = pltpu.make_async_copy(down, down_out, keep_sem.at[1])
    keep_down.start()
    rings[1].forward()
    scatter.third()
    scatter.last(d_routed)
    grad, term_sum = normed_back(hidden_rows[...], gain[...].reshape(1, -1), d_shared[...] + d_routed[...])
    whole = cot[...].astype(F32) + grad
    d_hidden[...] = whole
    d_attn[...] = whole.astype(BF16)
    gain_term[...] = term_sum
    loads[6].wait()

    @pl.loop(0, 5)
    def _(index):
        value = dot_nt(d_attn[...], w_out[pl.ds(pl.multiple_of(index * 256, 256), 256)]).astype(BF16)
        d_mixed[2 * index] = value[:, :HEAD_DIM]
        d_mixed[2 * index + 1] = value[:, HEAD_DIM:]

    for chunk, copy in enumerate(over):
        copy.wait_recv()
        add_into(up_one.at[chunk], (), up.at[1, up_rows(chunk, y_low)], up_land.at[chunk], rows=(16, 10))
    for expert in range(2):
        rings[expert].finish([gate_sum.at[expert, 0:160], gate_sum.at[expert, 160:320]])
    swap_one.wait_recv()
    add_into(down_final, (), down_one.at[half_rows(y_low, 112)], one_other, rows=(16, 7))
    copies.drain()
    keep_up.wait()
    keep_down.wait()


def scatter_rows(parts, kept_rows, kept_cots, kept_act, kept_back, d_shared, hidden_rows, gain, cot, w_out, down_one, collective_id):
    width, hidden = kept_rows.shape[2], kept_act.shape[2]
    count = cot.shape[0]
    return pl.pallas_call(
        scatter_kernel,
        name="scatter_rows",
        out_shape=(
            jax.ShapeDtypeStruct((2, 320, hidden), BF16),
            jax.ShapeDtypeStruct((width, hidden), BF16),
            jax.ShapeDtypeStruct((4, 160, hidden), BF16),
            jax.ShapeDtypeStruct((hidden, width), BF16),
            jax.ShapeDtypeStruct((112, width), F32),
            jax.ShapeDtypeStruct((10, count, HEAD_DIM), BF16),
            jax.ShapeDtypeStruct((count, width), F32),
            jax.ShapeDtypeStruct((count, width), BF16),
            jax.ShapeDtypeStruct((1, width), F32),
        ),
        in_specs=[ANYWHERE] * 5 + [VMEM] * 4 + [ANYWHERE, VMEM],
        out_specs=(VMEM, ANYWHERE, VMEM, ANYWHERE) + (VMEM,) * 5,
        scratch_shapes=SCATTER_SCRATCH
        + [
            pltpu.VMEM(kept_rows.shape, BF16),
            pltpu.VMEM(kept_cots.shape[1:], BF16),
            pltpu.VMEM(kept_act.shape[1:], BF16),
            pltpu.VMEM(kept_back.shape, BF16),
            pltpu.VMEM((2, width, hidden), BF16),
            pltpu.VMEM((2, width, hidden), BF16),
            pltpu.VMEM((hidden, width), BF16),
            pltpu.VMEM((2, 6, 160, hidden), BF16),
            pltpu.VMEM(w_out.shape, BF16),
            pltpu.VMEM((count, width), F32),
            pltpu.VMEM((4, 160, hidden), BF16),
            pltpu.VMEM((112, width), BF16),
            pltpu.SemaphoreType.DMA((SCATTER_REMOTES + 17,)),
            pltpu.SemaphoreType.DMA((SCATTER_REMOTES + 17,)),
            pltpu.SemaphoreType.DMA((SCATTER_LOCALS,)),
            pltpu.SemaphoreType.DMA((7,)),
            pltpu.SemaphoreType.DMA((2,)),
        ],
        compiler_params=params(collective_id),
        cost_estimate=cost(10**10, 10**8),
    )(
        parts, kept_rows, kept_cots, kept_act, kept_back,
        d_shared, hidden_rows, gain, cot, w_out, down_one,
    )


def ctx_device(ctx):
    return (ctx, lax.axis_index("exp"))


def extra_owner(head):
    core = lax.axis_index("exp") % 2
    return 3 * core if head == 8 else 5 + core


def owns_extra(ctx):
    return (ctx == extra_owner(8)) | (ctx == extra_owner(9))


def extra_head(ctx):
    return 8 + (ctx == extra_owner(9)).astype(jnp.int32)


class Exchange:
    def __init__(self, send, recv, own):
        self.send, self.recv, self.own = send, recv, own
        self.ctx = lax.axis_index("ctx")

    def copy(self, src, dst, slot, d):
        return pltpu.make_async_remote_copy(
            src_ref=src,
            dst_ref=dst,
            send_sem=self.send.at[slot, d],
            recv_sem=self.recv.at[slot, d],
            device_id=ctx_device((self.ctx + d) % 8),
            device_id_type=MESH,
        )


class ToOwners:
    def __init__(self, exchange, block, land):
        self.exchange, self.block, self.land, self.ctx = exchange, block, land, exchange.ctx

    def mine(self, slot, head):
        return pltpu.make_async_copy(self.block(head), self.land(slot, self.ctx), self.exchange.own.at[slot])

    def start(self, head):
        slot, owner = (0, head) if head < 8 else (1, extra_owner(head))
        d = (owner + 8 - self.ctx) % 8

        @pl.when(d == 0)
        def _():
            self.mine(slot, head).start()

        @pl.when(d != 0)
        def _():
            self.exchange.copy(self.block(head), self.land(slot, self.ctx), slot, d).start()

    def any(self, slot, d):
        return self.exchange.copy(self.block(0), self.land(slot, self.ctx), slot, d)

    def arrived(self):
        self.mine(0, 0).wait()
        for d in range(1, 8):
            self.any(0, d).wait_recv()

        @pl.when(owns_extra(self.ctx))
        def _():
            self.mine(1, 0).wait()
            for d in range(1, 8):
                self.any(1, d).wait_recv()

    def sent(self):
        for d in range(1, 8):
            self.any(0, d).wait_send()

            @pl.when(owns_extra((self.ctx + d) % 8))
            def _():
                self.any(1, d).wait_send()


class Home:
    def __init__(self, exchange, block, land):
        self.exchange, self.block, self.land = exchange, block, land
        self.ctx = exchange.ctx

    def head(self, slot):
        return self.ctx if slot == 0 else extra_head(self.ctx)

    def start(self, slot):
        for d in range(1, 8):
            self.exchange.copy(self.block(slot, (self.ctx + d) % 8), self.land(self.head(slot)), slot, d).start()
        self.mine(slot).start()

    def mine(self, slot):
        return pltpu.make_async_copy(
            self.block(slot, self.ctx), self.land(self.head(slot)), self.exchange.own.at[slot]
        )

    def finish(self):
        self.mine(0).wait()
        for d in range(1, 8):
            copy = self.exchange.copy(self.block(0, 0), self.land(0), 0, d)
            copy.wait_send()
            copy.wait_recv()

            @pl.when(owns_extra((self.ctx + 8 - d) % 8))
            def _():
                self.exchange.copy(self.block(1, 0), self.land(0), 1, d).wait_recv()

        @pl.when(owns_extra(self.ctx))
        def _():
            self.mine(1).wait()
            for d in range(1, 8):
                self.exchange.copy(self.block(1, 0), self.land(0), 1, d).wait_send()


def attend_kernel(
    length, cot, routes, route_gates, w_query, w_key, w_value, w_out_in, tokens, attn_gain, ffn_gain, cos, sin,
    normed_one, mixed, heads, cots, hidden, normed_two,
    sent_cot, qkv, weights, land, result, home, w_out, s1, r1, o1, s2, r2, o2, s3, r3, o3, load_sem, weight_sem,
):
    def fetch(index):
        return [
            pltpu.make_async_copy(source.at[:, 256 * index : 256 * index + 256], weights.at[index, kind], weight_sem.at[index, kind])
            for kind, source in enumerate((w_query, w_key, w_value))
        ]

    pairs_of_heads = (4, 0, 1, 2, 3)
    for index in pairs_of_heads:
        for copy in fetch(index):
            copy.start()
    load = pltpu.make_async_copy(w_out_in, w_out, load_sem)
    load.start()
    where = place()
    ctx = lax.axis_index("ctx")
    greet([ctx_device((ctx + d) % 8) for d in range(1, 8)] + exp_peers(where))
    copies = Copies(s3, r3, o3)
    lane = lax.broadcasted_iota(jnp.int32, (128, 128), 1)
    table = jnp.zeros((128, 128), F32)
    for choice in range(routes.shape[1]):
        table += jnp.where(lane == routes[:, choice : choice + 1], route_gates[:, choice : choice + 1], 0.0)
    row = lax.broadcasted_iota(jnp.int32, (128, 128), 0) + ctx * 128
    table = jnp.where(row < length[0], table, 0.0).T
    high = table.astype(BF16)
    low = (table - high.astype(F32)).astype(BF16)
    sent_cot[0:128] = cot[...]
    sent_cot[128:144] = jnp.zeros((16, cot.shape[1]), BF16)
    for index, part in enumerate((high[0:16], high[16:32], low[0:16], low[16:32])):
        sent_cot[128:144, index * 128 : index * 128 + 128] = part
    gather = Gather(copies, where, sent_cot, cots, 80, 144, 80)
    owners = ToOwners(Exchange(s1, r1, o1), lambda head: qkv.at[head], lambda slot, c: land.at[slot, :, c])
    normed_one[...] = normed(tokens[...].astype(F32), attn_gain[...].reshape(1, -1)).astype(BF16)
    positions = pl.ds(pl.multiple_of(ctx * 128, 128), 128)
    for index in pairs_of_heads:
        for copy in fetch(index):
            copy.wait()
        parts = [dot(normed_one[...], weights[index, kind]) for kind in range(3)]
        for half in range(2):
            head, lanes = 2 * index + half, slice(half * HEAD_DIM, (half + 1) * HEAD_DIM)
            qkv[head, 0] = turned(parts[0][:, lanes], cos[positions], sin[positions]).astype(BF16)
            qkv[head, 1] = turned(parts[1][:, lanes], cos[positions], sin[positions]).astype(BF16)
            qkv[head, 2] = parts[2][:, lanes].astype(BF16)
            owners.start(head)
    back = Home(Exchange(s2, r2, o2), lambda slot, c: result.at[slot, c], lambda head: home.at[head])
    keep = pltpu.make_async_copy(land, heads, o3.at[1])

    def run(slot, blocks):
        for block in blocks:
            width = (block + 1) * 128
            query = land[slot, 0, block]
            key = land[slot, 1, 0 : block + 1].reshape(width, HEAD_DIM)
            value = land[slot, 2, 0 : block + 1].reshape(width, HEAD_DIM)
            row = lax.broadcasted_iota(jnp.int32, (width, 128), 0)
            column = lax.broadcasted_iota(jnp.int32, (width, 128), 1) + block * 128
            scores = jnp.where(
                (row <= column) & (row < length[0]), dot_nt(key, query) * SCALE, -1e30
            )
            weights = jnp.exp(scores - jnp.max(scores, axis=0, keepdims=True))
            probs = weights * (1.0 / jnp.sum(weights, axis=0, keepdims=True))
            result[slot, block] = dot_tn(probs.astype(BF16), value).astype(BF16)

    gather.near()
    gather.far()
    owners.arrived()
    run(0, range(8))
    back.start(0)

    @pl.when(owns_extra(ctx))
    def _():
        run(1, range(8))
        back.start(1)

    @pl.when(jnp.logical_not(owns_extra(ctx)))
    def _():
        land[1] = jnp.zeros_like(land[1])

    keep.start()
    gather.middle()
    gather.third()
    gather.mine.wait()
    back.finish()
    for head in range(10):
        mixed[:, head * HEAD_DIM : (head + 1) * HEAD_DIM] = home[head]
    load.wait()

    @pl.loop(0, 5)
    def _(index):
        at = pl.ds(pl.multiple_of(index * 256, 256), 256)
        hidden[:, at] = tokens[:, at].astype(F32) + dot(mixed[...], w_out[:, at])

    normed_two[...] = normed(hidden[...], ffn_gain[...].reshape(1, -1)).astype(BF16)
    gather.last()
    owners.sent()
    keep.wait()
    copies.drain()


def exchange_semaphores():
    return [
        pltpu.SemaphoreType.DMA((2, 8)),
        pltpu.SemaphoreType.DMA((2, 8)),
        pltpu.SemaphoreType.DMA((2,)),
    ]


def attend(length, cot, routes, route_gates, w_query, w_key, w_value, w_out, tokens, attn_gain, ffn_gain, cos, sin, collective_id):
    rows, width = tokens.shape
    return pl.pallas_call(
        attend_kernel,
        name="attend",
        out_shape=(
            jax.ShapeDtypeStruct((rows, width), BF16),
            jax.ShapeDtypeStruct((rows, width), BF16),
            jax.ShapeDtypeStruct((2, 3, 8, rows, HEAD_DIM), BF16),
            jax.ShapeDtypeStruct((16, rows + 16, width), BF16),
            jax.ShapeDtypeStruct((rows, width), F32),
            jax.ShapeDtypeStruct((rows, width), BF16),
        ),
        in_specs=[SMEM] + [VMEM] * 3 + [ANYWHERE] * 4 + [VMEM] * 5,
        out_specs=(VMEM, VMEM, ANYWHERE, ANYWHERE, VMEM, VMEM),
        scratch_shapes=[
            pltpu.VMEM((rows + 16, width), BF16),
            pltpu.VMEM((10, 3, rows, HEAD_DIM), BF16),
            pltpu.VMEM((5, 3, width, 256), BF16),
            pltpu.VMEM((2, 3, 8, rows, HEAD_DIM), BF16),
            pltpu.VMEM((2, 8, rows, HEAD_DIM), BF16),
            pltpu.VMEM((10, rows, HEAD_DIM), BF16),
            pltpu.VMEM(w_out.shape, BF16),
        ]
        + exchange_semaphores()
        + exchange_semaphores()
        + [
            pltpu.SemaphoreType.DMA((GATHER_REMOTES,)),
            pltpu.SemaphoreType.DMA((GATHER_REMOTES,)),
            pltpu.SemaphoreType.DMA((2,)),
            pltpu.SemaphoreType.DMA,
            pltpu.SemaphoreType.DMA((5, 3)),
        ],
        compiler_params=params(collective_id),
        cost_estimate=cost(10**9, 10**8),
    )(length, cot, routes, route_gates, w_query, w_key, w_value, w_out, tokens, attn_gain, ffn_gain, cos, sin)


def attend_back_kernel(
    d_mixed, heads, length, cos, sin, parts, up, up_one, gate, first, d_attn, normed_one, mixed, tokens, gain, d_hidden,
    w_query_in, w_key_in, w_value_in, input_grad, gain_term, routed, up_sum, up_final, gate_out, first_sum, second, late,
    land, kept, d_key, d_value, result, home, a, b, c, d, e, up_land, up_work, one_land, gate_other, first_land,
    pair_rows, d_qkv, pair_qkv, right, out_right, panels, out_terms, out_land, weights, total,
    s1, r1, o1, s2, r2, o2, s3, r3, o3, load_sem, late_sem,
):
    where = place()
    x, y, z, core = where
    ctx = lax.axis_index("ctx")
    x_peers = [device((x + 1) % 4, y, z, core), device((x + 3) % 4, y, z, core)]
    loads = [
        pltpu.make_async_copy(src, dst, load_sem.at[i])
        for i, (src, dst) in enumerate(
            ((heads, kept), (w_query_in, weights.at[0]), (w_key_in, weights.at[1]), (w_value_in, weights.at[2]))
        )
    ]
    for load in loads:
        load.start()
    y_peers = [device(x, (y + step) % 4, z, core) for step in (1, 2, 3)]
    pair_peer = device(x, (y // 2) * 2 + 1 - y % 2, z, core)
    cross_peer = device(x, (y // 2) * 2 + 2 + 1 - y % 2 - 4 * (y // 2), z, core)
    greet([ctx_device((ctx + step) % 8) for step in range(1, 8)] + exp_peers(where) + [cross_peer])
    owners = ToOwners(Exchange(s1, r1, o1), lambda head: d_mixed.at[head], lambda slot, at: land.at[slot, at])
    for head in (8, 9, 0, 1, 2, 3, 4, 5, 6, 7):
        owners.start(head)
    copies = Copies(s3, r3, o3)
    scatter = Scatter(copies, where, parts, a, b, c, d, e)
    back = Home(Exchange(s2, r2, o2), lambda slot, at: result.at[slot, :, at], lambda head: home.at[:, head])
    y_low = y % 2

    def one_add(out, *terms):
        add_into(out, (), *terms, rows=(16, 5))

    ring_one = RingSum(
        copies, x, x_peers[0], x_peers[1], lambda chunk, half: up_one.at[chunk, 80 * half : 80 * half + 80],
        one_land, None, one_add, resident=True,
    )
    ring = RingSum(
        copies, x, x_peers[0], x_peers[1], lambda chunk, half: up.at[half_rows(2 * chunk + half, 160)],
        up_land, up_work, up_add,
    )
    swap = copies.remote(gate.at[:, half_rows(1 - y_low, 160)], gate_other, pair_peer)
    z_peers = [device(x, y, (z + 1) % 4, core), device(x, y, (z + 3) % 4, core)]

    def panel_add(out, *terms):
        add_into(out, (), *terms, rows=(80, 8))

    pair = device(x, y, z, 1 - core)
    pairs = [copies.remote(src, pair_rows.at[i], pair) for i, src in enumerate((normed_one, mixed, d_attn))]
    for copy in pairs:
        copy.wait_recv()
    at = pl.ds(pl.multiple_of(core * 640, 128), 640)
    out_right[0:128] = d_attn[:, at]
    out_right[128:256] = pair_rows[2, :, at]

    @pl.loop(0, 5)
    def _(index):
        at = pl.ds(pl.multiple_of(index * 256, 256), 256)
        value = dot_tn(jnp.concatenate([mixed[:, at], pair_rows[1, :, at]], axis=0), out_right[...])
        for panel in range(5):
            out_terms[panel, at] = value[:, panel * 128 : panel * 128 + 128].astype(BF16)

    store_out = pltpu.make_async_copy(out_terms.at[4], late.at[15], late_sem.at[5])
    store_out.start()
    scatter.first()
    loads[0].wait()
    owners.arrived()

    def run(slot):
        d_key[...] = jnp.zeros_like(d_key)
        d_value[...] = jnp.zeros_like(d_value)
        for block in range(8):
            width = (block + 1) * 128
            query, upstream = kept[slot, 0, block], land[slot, block]
            key = kept[slot, 1, 0 : block + 1].reshape(width, HEAD_DIM)
            value = kept[slot, 2, 0 : block + 1].reshape(width, HEAD_DIM)
            row = lax.broadcasted_iota(jnp.int32, (width, 128), 0)
            column = lax.broadcasted_iota(jnp.int32, (width, 128), 1) + block * 128
            scores = jnp.where(
                (row <= column) & (row < length[0]), dot_nt(key, query) * SCALE, -1e30
            )
            weight = jnp.exp(scores - jnp.max(scores, axis=0, keepdims=True))
            probs = weight * (1.0 / jnp.sum(weight, axis=0, keepdims=True))
            d_probs = dot_nt(value, upstream)
            delta = jnp.sum(probs * d_probs, axis=0, keepdims=True)
            d_scores = (probs * (d_probs - delta)).astype(BF16)
            rows = slice(block * 128, block * 128 + 128)
            d_query = dot_tn(d_scores, key) * SCALE
            result[slot, 0, block] = turned(d_query, cos[rows], sin[rows]).astype(BF16)
            d_key[0:width] += dot(d_scores, query)
            d_value[0:width] += dot(probs.astype(BF16), upstream)
        for block in range(8):
            rows = slice(block * 128, block * 128 + 128)
            result[slot, 1, block] = turned(d_key[rows] * SCALE, cos[rows], sin[rows]).astype(BF16)
            result[slot, 2, block] = d_value[rows].astype(BF16)
        back.start(slot)

    run(0)
    scatter.merge_rest()
    scatter.second()

    @pl.when(owns_extra(ctx))
    def _():
        run(1)

    first_copies = [
        copies.remote(first.at[:, :, order((y + step) % 4)], first_land.at[step - 1], y_peers[step - 1])
        for step in (1, 2, 3)
    ]
    ring_one.raw()
    ring_one.forward()
    ring.raw()
    outs = RingSum(
        copies, z, z_peers[0], z_peers[1], lambda chunk, half: out_terms.at[chunk, 640 * half : 640 * half + 640],
        out_land, None, panel_add, resident=True,
    )
    outs.raw()
    ring.forward()
    scatter.third()
    back.finish()
    outs.forward()
    for head in range(10):
        for kind in range(3):
            at = kind * 1280 + head * HEAD_DIM
            d_qkv[:, at : at + HEAD_DIM] = home[kind, head]
    swap_qkv = copies.remote(d_qkv, pair_qkv, pair)
    for load in loads[1:]:
        load.wait()

    @pl.loop(0, 5)
    def _(index):
        at = pl.ds(pl.multiple_of(index * 256, 256), 256)
        value = dot_nt(d_qkv[:, 0:1280], weights[0, at])
        value += dot_nt(d_qkv[:, 1280:2560], weights[1, at])
        value += dot_nt(d_qkv[:, 2560:3840], weights[2, at])
        total[:, at] = value

    grad, term = normed_back(tokens[...].astype(F32), gain[...].reshape(1, -1), total[...])
    input_grad[...] = d_hidden[...] + grad
    gain_term[...] = term

    swap_qkv.wait_recv()
    at = pl.ds(pl.multiple_of(core * 1920, 128), 1920)
    right[0:128] = d_qkv[:, at]
    right[128:256] = pair_qkv[:, at]

    def store(index):
        rows = pl.ds(pl.multiple_of(index * 256, 256), 256)
        return pltpu.make_async_copy(panels.at[index], late.at[0:15, rows], late_sem.at[index])

    @pl.loop(0, 5)
    def _(index):
        at = pl.ds(pl.multiple_of(index * 256, 256), 256)
        value = dot_tn(jnp.concatenate([normed_one[:, at], pair_rows[0, :, at]], axis=0), right[...])
        for panel in range(15):
            panels[index, panel] = value[:, panel * 128 : panel * 128 + 128].astype(BF16)
        store(index).start()

    scatter.last(routed)
    outs.finish([second.at[0:640], second.at[640:1280]])
    swap.wait_recv()
    add_into(gate_out, (2,), gate.at[:, half_rows(y_low, 160)], gate_other, rows=(16, 10))
    for copy in first_copies:
        copy.wait_recv()
    add_into(first_sum, (3, 4), first.at[:, :, order(y)], first_land.at[0], first_land.at[1], first_land.at[2])
    ring_one.finish([up_final.at[0:80], up_final.at[80:160]])
    ring.finish([up_sum.at[0], up_sum.at[1]])
    owners.sent()
    copies.drain()
    store_out.wait()
    for index in range(5):
        store(index).wait()


def attend_back(
    d_mixed, heads, length, cos, sin, parts, up, up_one, gate, first, d_attn, normed_one, mixed, tokens, gain, d_hidden,
    w_query, w_key, w_value, collective_id,
):
    rows, width = tokens.shape
    hidden = up.shape[1]
    return pl.pallas_call(
        attend_back_kernel,
        name="attend_back",
        out_shape=(
            jax.ShapeDtypeStruct((rows, width), F32),
            jax.ShapeDtypeStruct((1, width), F32),
            jax.ShapeDtypeStruct((rows, width), F32),
            jax.ShapeDtypeStruct((2, 160, hidden), BF16),
            jax.ShapeDtypeStruct((160, hidden), F32),
            jax.ShapeDtypeStruct((2, 160, hidden), F32),
            jax.ShapeDtypeStruct((3, 4, 80, 128), BF16),
            jax.ShapeDtypeStruct((width, 128), BF16),
            jax.ShapeDtypeStruct((16, width, 128), BF16),
        ),
        in_specs=[ANYWHERE, ANYWHERE, SMEM, VMEM, VMEM, ANYWHERE, ANYWHERE, VMEM, VMEM, VMEM]
        + [VMEM] * 6
        + [ANYWHERE] * 3,
        out_specs=(VMEM,) * 8 + (ANYWHERE,),
        scratch_shapes=[
            pltpu.VMEM((2, 8, 128, HEAD_DIM), BF16),
            pltpu.VMEM((2, 3, 8, 128, HEAD_DIM), BF16),
            pltpu.VMEM((1024, HEAD_DIM), F32),
            pltpu.VMEM((1024, HEAD_DIM), F32),
            pltpu.VMEM((2, 3, 8, 128, HEAD_DIM), BF16),
            pltpu.VMEM((3, 10, 128, HEAD_DIM), BF16),
        ]
        + SCATTER_SCRATCH
        + [
            pltpu.VMEM((6, 160, hidden), BF16),
            pltpu.VMEM((4, 160, hidden), BF16),
            pltpu.VMEM((6, 80, hidden), BF16),
            pltpu.VMEM((2, 160, hidden), BF16),
            pltpu.VMEM((3, 3, 4, 80, 128), BF16),
            pltpu.VMEM((3, rows, width), BF16),
            pltpu.VMEM((rows, 3 * width), BF16),
            pltpu.VMEM((rows, 3 * width), BF16),
            pltpu.VMEM((2 * rows, 1920), BF16),
            pltpu.VMEM((2 * rows, 640), BF16),
            pltpu.VMEM((5, 15, 256, 128), BF16),
            pltpu.VMEM((5, width, 128), BF16),
            pltpu.VMEM((6, width // 2, 128), BF16),
            pltpu.VMEM((3, width, width), BF16),
            pltpu.VMEM((rows, width), F32),
        ]
        + exchange_semaphores()
        + exchange_semaphores()
        + [
            pltpu.SemaphoreType.DMA((SCATTER_REMOTES + 26,)),
            pltpu.SemaphoreType.DMA((SCATTER_REMOTES + 26,)),
            pltpu.SemaphoreType.DMA((SCATTER_LOCALS + 4,)),
            pltpu.SemaphoreType.DMA((4,)),
            pltpu.SemaphoreType.DMA((6,)),
        ],
        compiler_params=params(collective_id),
        cost_estimate=cost(10**9, 10**8),
    )(
        d_mixed, heads, length, cos, sin, parts, up, up_one, gate, first, d_attn, normed_one, mixed,
        tokens, gain, d_hidden, w_query, w_key, w_value,
    )


def gated(gate, up):
    squash = 1.0 / (1.0 + jnp.exp(-gate))
    silu = gate * squash
    slope = squash * (1.0 + gate * (1.0 - squash))
    return silu, slope


SLOTS = 48
DEPTH = 4
SLOT_ROWS = 16 * SLOTS


def slot_lines(meta):
    member = jnp.where(meta[...].reshape(32, 128) > 0, 1.0, 0.0)
    before = lax.broadcasted_iota(jnp.int32, (128, 128), 0) < lax.broadcasted_iota(jnp.int32, (128, 128), 1)
    count = dot(member.astype(BF16), jnp.where(before, 1.0, 0.0).astype(BF16))
    return jnp.where(member > 0, count, -1.0)


def experts_kernel(
    meta, weight, rows, cots, gate_w, up_w, down_w, early, out, d_rows, kept_act, kept_back, down_sum, first_sum,
    gate_up, down, slot_rows, slot_cots, slot_out, slot_back, lines, columns, act, back,
    out_buf, term, land, z_land, z_work, in_sem, out_sem, weight_sem, keep_sem, send, recv, own,
):
    hidden = down.shape[1]
    x, y, z, core = place()
    x_peers = [device((x + 1) % 4, y, z, core), device((x + 3) % 4, y, z, core)]

    def load(expert):
        return [
            pltpu.make_async_copy(gate_w.at[expert], gate_up.at[expert, :, 0:hidden], weight_sem.at[expert, 0]),
            pltpu.make_async_copy(up_w.at[expert], gate_up.at[expert, :, hidden : 2 * hidden], weight_sem.at[expert, 1]),
            pltpu.make_async_copy(down_w.at[expert], down.at[expert], weight_sem.at[expert, 2]),
        ]

    def fetch(expert):
        return [
            pltpu.make_async_copy(rows.at[expert], slot_rows.at[expert], in_sem.at[expert, 0]),
            pltpu.make_async_copy(cots.at[expert], slot_cots.at[expert], in_sem.at[expert, 1]),
        ]

    for copy in fetch(0) + load(0):
        copy.start()
    z_peers = [device(x, y, (z + 1) % 4, core), device(x, y, (z + 3) % 4, core)]
    greet(x_peers + z_peers)
    copies = Copies(send, recv, own)

    def panel_add(out, *terms):
        add_into(out, (), *terms, rows=(80, 8))

    dense = [
        RingSum(
            copies, z, z_peers[0], z_peers[1],
            lambda chunk, half, panel=panel: early.at[
                2 * chunk + panel if panel < 2 else 8 + chunk, 640 * half : 640 * half + 640
            ],
            z_land.at[panel], z_work.at[panel], panel_add,
        )
        for panel in range(3)
    ]
    for panel in dense:
        panel.raw()
    lines[...] = slot_lines(meta).reshape(16, 2, 128)
    columns[...] = jnp.concatenate([lines[...].reshape(32, 128), jnp.zeros((96, 128), F32)], axis=0).T
    def keep(expert):
        return [
            pltpu.make_async_copy(act.at[expert], kept_act.at[expert], keep_sem.at[expert, 0]),
            pltpu.make_async_copy(back.at[expert], kept_back.at[expert], keep_sem.at[expert, 1]),
        ]

    def main(expert):
        for copy in fetch(expert) + load(expert):
            copy.wait()
        if expert == 0:
            for copy in fetch(1) + load(1):
                copy.start()

        tile = 256

        @pl.loop(0, SLOT_ROWS // tile)
        def _(index):
            at = pl.ds(pl.multiple_of(index * tile, tile), tile)
            both = dot(slot_rows[expert, at], gate_up[expert])
            gate, up = both[:, :hidden], both[:, hidden:]
            silu, slope = gated(gate, up)
            activated = (silu * up).astype(BF16)
            act[expert, at] = activated
            produced = dot(activated, down[expert]).astype(BF16).astype(F32)
            slot_out[expert, at] = (produced * weight[expert, at][:, 0:1]).astype(BF16)
            d_act = dot_nt(slot_cots[expert, at], down[expert])
            back[expert, at, 0:hidden] = (d_act * up * slope).astype(BF16)
            back[expert, at, hidden : 2 * hidden] = (d_act * silu).astype(BF16)
            slot_back[expert, at] = dot_nt(back[expert, at], gate_up[expert]).astype(BF16)

    main(0)
    for copy in keep(0):
        copy.start()

    @pl.loop(0, hidden // 128)
    def _(index):
        at = pl.ds(pl.multiple_of(index * 128, 128), 128)
        term[at] = dot_tn(act[0, :, at], slot_cots[0]).astype(BF16)

    def part(chunk, half):
        return term.at[pl.ds(pl.multiple_of(chunk * 224 + half * 112, 112), 112)]

    def add(out, *terms):
        add_into(out, (), *terms, rows=(16, 7))

    ring = RingSum(copies, x, x_peers[0], x_peers[1], part, land, None, add, resident=True)
    ring.raw()
    for panel in dense:
        panel.forward()
    main(1)
    ring.forward()
    for copy in keep(1):
        copy.start()

    def store(block):
        slot = block % DEPTH
        return [
            pltpu.make_async_copy(out_buf.at[slot, 0], out.at[block], out_sem.at[slot, 0]),
            pltpu.make_async_copy(out_buf.at[slot, 1], d_rows.at[block], out_sem.at[slot, 1]),
        ]

    lane = lax.broadcasted_iota(jnp.int32, (128, 2 * SLOTS), 1).astype(F32)
    for block in range(16):
        slot = block % DEPTH
        first, second = columns[:, 2 * block : 2 * block + 1], columns[:, 2 * block + 1 : 2 * block + 2]
        hit = ((lane < SLOTS) & (lane == first)) | ((lane >= SLOTS) & (lane - SLOTS == second))
        both = jnp.where(hit, 1.0, 0.0).astype(BF16)
        if block >= DEPTH:
            for copy in store(block - DEPTH):
                copy.wait()
        at = slice(block * SLOTS, (block + 1) * SLOTS)
        for index, source in enumerate((slot_out, slot_back)):
            value = jnp.concatenate([source[0, at], source[1, at]], axis=0)
            out_buf[slot, index] = dot(both, value).astype(BF16)
        for copy in store(block):
            copy.start()
    for block in range(16 - DEPTH, 16):
        for copy in store(block):
            copy.wait()
    for panel in range(3):
        dense[panel].finish([first_sum.at[panel, 0:640], first_sum.at[panel, 640:1280]])
    ring.finish([down_sum.at[0:112], down_sum.at[112:224]])
    copies.drain()
    for copy in keep(0) + keep(1):
        copy.wait()


def experts(meta, weight, rows, cots, gate_w, up_w, down_w, early, collective_id):
    width, hidden = gate_w.shape[1:]
    return pl.pallas_call(
        experts_kernel,
        name="experts",
        out_shape=(
            jax.ShapeDtypeStruct((16, 128, width), BF16),
            jax.ShapeDtypeStruct((16, 128, width), BF16),
            jax.ShapeDtypeStruct((2, SLOT_ROWS, hidden), BF16),
            jax.ShapeDtypeStruct((2, SLOT_ROWS, 2 * hidden), BF16),
            jax.ShapeDtypeStruct((hidden // 4, width), BF16),
            jax.ShapeDtypeStruct((3, width, 128), BF16),
        ),
        in_specs=[VMEM, VMEM] + [ANYWHERE] * 6,
        out_specs=[ANYWHERE] * 4 + [VMEM, VMEM],
        scratch_shapes=[
            pltpu.VMEM((2, width, 2 * hidden), BF16),
            pltpu.VMEM((2, hidden, width), BF16),
            pltpu.VMEM((2, SLOT_ROWS, width), BF16),
            pltpu.VMEM((2, SLOT_ROWS, width), BF16),
            pltpu.VMEM((2, SLOT_ROWS, width), BF16),
            pltpu.VMEM((2, SLOT_ROWS, width), BF16),
            pltpu.VMEM((16, 2, 128), F32),
            pltpu.VMEM((128, 128), F32),
            pltpu.VMEM((2, SLOT_ROWS, hidden), BF16),
            pltpu.VMEM((2, SLOT_ROWS, 2 * hidden), BF16),
            pltpu.VMEM((DEPTH, 2, 128, width), BF16),
            pltpu.VMEM((hidden, width), BF16),
            pltpu.VMEM((6, hidden // 8, width), BF16),
            pltpu.VMEM((3, 6, width // 2, 128), BF16),
            pltpu.VMEM((3, 4, width // 2, 128), BF16),
            pltpu.SemaphoreType.DMA((2, 2)),
            pltpu.SemaphoreType.DMA((DEPTH, 2)),
            pltpu.SemaphoreType.DMA((2, 3)),
            pltpu.SemaphoreType.DMA((2, 2)),
            pltpu.SemaphoreType.DMA((24,)),
            pltpu.SemaphoreType.DMA((24,)),
            pltpu.SemaphoreType.DMA((12,)),
        ],
        compiler_params=params(collective_id),
        cost_estimate=cost(12 * 2 * SLOT_ROWS * width * hidden, 6 * 10**7),
    )(meta, weight, rows, cots, gate_w, up_w, down_w, early)


def finish_kernel(
    packed, hidden, shared_out, routed, gate, up_zero, up_one, down_zero, down_one, grad,
    block_out, input_grad, attn_gain, query, key, value, out, ffn_gain, s_gate, s_up, s_down, gate_grad, up_grad, down_grad,
):
    input_grad[...] = grad[...]
    gate_grad[...] = gate[...]
    up_grad[0] = up_zero[...]
    up_grad[1] = up_one[...]
    down_grad[0] = down_zero[...]
    down_grad[1] = down_one[...]
    block_out[...] = hidden[...] + shared_out[...] + routed[...]
    gains = packed[0, 0, 10:11]
    for source in range(1, 8):
        gains = gains + packed[source, 0, 10:11]
    attn_gain[...] = gains[:, 0:10]
    ffn_gain[...] = gains[:, 10:20]
    for core in range(2):
        for panel in range(20):
            if panel < 15:
                part = packed[2 * (panel // 4) + core, 4 + panel % 4, 0:10]
                at = core * 1920 + panel * 128
                (query, key, value)[at // 1280][:, at % 1280 : at % 1280 + 128] = part
            else:
                part = packed[2 * (panel - 15) + core, 3, 0:10] if panel < 19 else packed[6 + core, 7, 0:10]
                at = core * 640 + (panel - 15) * 128
                out[:, at : at + 128] = part
        for panel in range(12):
            where = (panel // 2, panel % 2) if panel < 8 else (panel - 8, 2)
            part = packed[2 * where[0] + core, where[1], 0:10]
            if panel < 7:
                (s_gate, s_up)[core][:, panel * 128 : panel * 128 + 128] = part
            else:
                at = core * 640 + (panel - 7) * 128
                s_down[:, at : at + 128] = part[0:7]


def finish(packed, *values):
    def shape(*dims):
        return jax.ShapeDtypeStruct(dims, F32)

    return pl.pallas_call(
        finish_kernel,
        name="finish",
        out_shape=(
            shape(128, 1280), shape(128, 1280), shape(1, 10),
            shape(10, 1280), shape(10, 1280), shape(10, 1280), shape(10, 1280), shape(1, 10),
            shape(10, 896), shape(10, 896), shape(7, 1280),
            shape(2, 160, 896), shape(2, 160, 896), shape(2, 112, 1280),
        ),
        in_specs=[VMEM] * 10,
        out_specs=(VMEM,) * 14,
        compiler_params=params(),
        cost_estimate=cost(10**7, 12 * 10**6),
    )(packed, *values)


def local(
    tokens,
    lengths,
    routes,
    route_gates,
    attn_gain,
    w_query,
    w_key,
    w_value,
    w_out,
    ffn_gain,
    shared_gate,
    shared_up,
    shared_down,
    expert_gate,
    expert_up,
    expert_down,
    cotangent,
):
    resident, cot = tokens[0], cotangent[0]
    rows = resident.shape[0]
    all_cos, all_sin = turn_tables(8 * rows)
    back_sin = jnp.asarray(-all_sin)
    all_cos, all_sin = jnp.asarray(all_cos), jnp.asarray(all_sin)
    normed_one, mixed, heads, cots, hidden, normed_two = attend(
        lengths, cot, routes[0], route_gates[0], w_query, w_key, w_value, w_out, resident, attn_gain, ffn_gain, all_cos, all_sin, 1
    )
    slot_rows, slot_cots, meta, weight, shared_out, d_shared, early = gather_rows(
        normed_two, cot, cots, shared_gate, shared_up, shared_down, 2
    )
    parts, d_parts, kept_act, kept_back, down_one, first = experts(
        meta, weight, slot_rows, slot_cots, expert_gate, expert_up, expert_down, early, 5
    )
    first = first.reshape(3, 4, 4, 80, 128)
    gate_sum, up_term, up_one, down_term, down_zero, d_mixed, d_hidden, d_attn, ffn_term = scatter_rows(
        d_parts, slot_rows, slot_cots, kept_act, kept_back, d_shared, hidden, ffn_gain, cot, w_out, down_one, 3
    )
    grad, attn_term, routed, up_sum, up_last, gate_grad, first_sum, second, late = attend_back(
        d_mixed, heads, lengths, all_cos, back_sin, parts, up_term, up_one, gate_sum, first, d_attn, normed_one,
        mixed, resident, attn_gain, d_hidden, w_query, w_key, w_value, 4,
    )
    packed, up_first, down_last = sum_grads(
        late, first_sum, second, gain_lines(attn_term[0], ffn_term[0]), up_sum, down_term
    )
    outs = finish(
        packed, hidden, shared_out, routed, gate_grad, up_first, up_last, down_zero, down_last, grad
    )
    return (outs[0][None], outs[1][None], outs[2][0], *outs[3:7], outs[7][0], *outs[8:])


def solution(mesh):
    in_specs = (
        P("exp", "ctx", None),
        P("exp"),
        P("exp", "ctx", None),
        P("exp", "ctx", None),
        P(),
        P(),
        P(),
        P(),
        P(),
        P(),
        P(),
        P(),
        P(),
        P("exp", None, None),
        P("exp", None, None),
        P("exp", None, None),
        P("exp", "ctx", None),
    )
    out_specs = (
        P("exp", "ctx", None),
        P("exp", "ctx", None),
        P(("ctx", "exp")),
        P(("ctx", "exp"), None),
        P(("ctx", "exp"), None),
        P(("ctx", "exp"), None),
        P(("ctx", "exp"), None),
        P(("ctx", "exp")),
        P(("ctx", "exp"), None),
        P(("ctx", "exp"), None),
        P(("ctx", "exp"), None),
        P("exp", "ctx", None),
        P("exp", "ctx", None),
        P("exp", "ctx", None),
    )
    return jax.shard_map(local, mesh=mesh, in_specs=in_specs, out_specs=out_specs, check_vma=False)
```

```python
import functools
import math

import jax
import jax.numpy as jnp
import numpy as np
from jax import lax
from jax.experimental import pallas as pl
from jax.experimental.pallas import tpu as pltpu
from jax.sharding import PartitionSpec as P

MESH = pl.DeviceIdType.MESH
HEAD_DIM = 128
VMEM_LIMIT = 60 * 2**20
F32, BF16 = jnp.float32, jnp.bfloat16


def place():
    ctx, exp = lax.axis_index("ctx"), lax.axis_index("exp")
    return ctx // 2, (exp // 8) * 2 + ctx % 2, (exp // 2) % 4, exp % 2


def device(x, y, z, core):
    return (x * 2 + y % 2, (y // 2) * 8 + z * 2 + core)


def greet(devices):
    barrier = pltpu.get_barrier_semaphore()
    for target in devices:
        pl.semaphore_signal(barrier, inc=1, device_id=target, device_id_type=MESH)
    pl.semaphore_wait(barrier, len(devices))


class Copies:
    def __init__(self, send, recv, own):
        self.send, self.recv, self.own = send, recv, own
        self.remotes, self.locals = 0, 0
        self.started = []

    def remote(self, src, dst, target):
        index = self.remotes
        self.remotes += 1
        copy = pltpu.make_async_remote_copy(
            src_ref=src,
            dst_ref=dst,
            send_sem=self.send.at[index],
            recv_sem=self.recv.at[index],
            device_id=target,
            device_id_type=MESH,
        )
        copy.start()
        self.started.append(copy)
        return copy

    def local(self, src, dst):
        index = self.locals
        self.locals += 1
        copy = pltpu.make_async_copy(src, dst, self.own.at[index])
        copy.start()
        return copy

    def drain(self):
        for copy in self.started:
            copy.wait_send()


def each(shape, body):
    @pl.loop(0, math.prod(shape))
    def _(step):
        index = []
        for size in reversed(shape):
            index.append(step % size)
            step = step // size
        body(tuple(reversed(index)))


def add_into(out, shape, *terms, rows=None):
    def body(index):
        total = terms[0][index].astype(F32)
        for term in terms[1:]:
            total = total + term[index].astype(F32)
        out[index] = total.astype(out.dtype)

    if rows is None:
        each(shape, body)
    else:
        step, count = rows
        each(shape + (count,), lambda i: body(i[:-1] + (pl.ds(pl.multiple_of(i[-1] * step, step), step),)))


class RingSum:
    def __init__(self, copies, me, right, left, part, land, work, add, resident=None):
        self.copies, self.right, self.left, self.land, self.work, self.add = copies, right, left, land, work, add
        self.part = part
        self.after, self.before, across = (me + 1) % 4, (me + 3) % 4, (me + 2) % 4
        self.one = copies.remote(part(across, 0), land.at[0], right)
        self.two = copies.remote(part(across, 1), land.at[1], left)
        sources = [part(self.after, 0), part(self.before, 1), part(me, 0), part(me, 1)]
        if resident is None:
            self.loads = [copies.local(source, work.at[i]) for i, source in enumerate(sources)]
            self.own = [work.at[i] for i in range(4)]
        else:
            self.loads = []
            self.own = sources

    def raw(self):
        self.three = self.copies.remote(self.part(self.after, 1), self.land.at[2], self.right)
        self.four = self.copies.remote(self.part(self.before, 0), self.land.at[4], self.left)

    def forward(self):
        for load in self.loads:
            load.wait()
        self.one.wait_recv()
        self.add(self.land.at[0], self.land.at[0], self.own[0])
        self.five = self.copies.remote(self.land.at[0], self.land.at[3], self.right)
        self.two.wait_recv()
        self.add(self.land.at[1], self.land.at[1], self.own[1])
        self.six = self.copies.remote(self.land.at[1], self.land.at[5], self.left)

    def finish(self, outs):
        for copy in (self.three, self.four, self.five, self.six):
            copy.wait_recv()
        self.add(outs[0], self.own[2], self.land.at[3], self.land.at[4])
        self.add(outs[1], self.own[3], self.land.at[2], self.land.at[5])


GRAD_REMOTES = 5 * 6 + 2 + 3 * 3 + 3 * 4 + 6 + 3 * 4 + 7


def add_blocks(shape):
    def add(out, *terms):
        add_into(out, shape, *terms)

    return add


def half_rows(which, size):
    return pl.ds(pl.multiple_of(which * size, size), size)


def order(y):
    return (y % 2) * 2 + y // 2


VMEM = pl.BlockSpec(memory_space=pltpu.VMEM)
ANYWHERE = pl.BlockSpec(memory_space=pl.ANY)
SMEM = pl.BlockSpec(memory_space=pltpu.SMEM)
SCALE = HEAD_DIM ** (-0.5)


def params(collective_id=None):
    if collective_id is None:
        return pltpu.CompilerParams(vmem_limit_bytes=VMEM_LIMIT)
    return pltpu.CompilerParams(
        collective_id=collective_id, has_side_effects=True, vmem_limit_bytes=VMEM_LIMIT
    )


def cost(flops, bytes_accessed):
    return pl.CostEstimate(flops=int(flops), bytes_accessed=int(bytes_accessed), transcendentals=0)


def dot(left, right):
    return jnp.dot(left, right, preferred_element_type=F32)


def dot_nt(left, right):
    return lax.dot_general(left, right, (((1,), (1,)), ((), ())), preferred_element_type=F32)


def dot_tn(left, right):
    return lax.dot_general(left, right, (((0,), (0,)), ((), ())), preferred_element_type=F32)


def normed(values, gain):
    return values * lax.rsqrt(jnp.mean(values * values, axis=-1, keepdims=True) + 1e-06) * gain


def normed_back(values, gain, upstream):
    factor = lax.rsqrt(jnp.mean(values * values, axis=-1, keepdims=True) + 1e-06)
    scaled = upstream * gain
    inner = jnp.mean(scaled * values, axis=-1, keepdims=True)
    term = jnp.sum(upstream * values * factor, axis=0, keepdims=True)
    return factor * scaled - values * factor * factor * factor * inner, term


def turned(values, cos, sin):
    return values * cos + pltpu.roll(values, HEAD_DIM // 2, 1) * sin


def turn_tables(count):
    half = HEAD_DIM // 2
    frequency = np.exp(np.arange(half, dtype=np.float32) * np.float32(-2.0 * math.log(10000.0) / HEAD_DIM))
    angle = np.arange(count, dtype=np.float32)[:, None] * frequency[None, :]
    cos, sin = np.cos(angle), np.sin(angle)
    return np.concatenate([cos, cos], axis=1), np.concatenate([-sin, sin], axis=1)


def rank(y_half, z, core):
    return y_half * 8 + z * 2 + core


class Gather:
    def __init__(self, copies, where, src, out, cut, far, far_cut):
        x, y, z, core = where
        self.copies, self.out, self.cut, self.far_rows, self.far_cut = copies, out, cut, far, far_cut
        self.rows = out.shape[1]
        self.split = far < self.rows
        self.y_half, self.z, self.core = y // 2, z, core
        self.pair = device(x, y, z, 1 - core)
        self.across = device(x, (y + 2) % 4, z, core)
        self.right, self.left = device(x, y, (z + 1) % 4, core), device(x, y, (z + 3) % 4, core)
        me = rank(self.y_half, z, core)
        self.mine = copies.local(src, out.at[me])
        self.over = copies.remote(src, out.at[me], self.across)
        self.to_right = copies.remote(src, out.at[me], self.right)
        self.to_left = copies.remote(src, out.at[me], self.left)
        self.pairs = [copies.remote(src, out.at[me], self.pair)]
        self.seen = 0

    def shard(self, other, dz):
        y_half = 1 - self.y_half if other else self.y_half
        return rank(y_half, (self.z + dz + 4) % 4, self.core)

    def send(self, ref, target):
        return self.copies.remote(ref, ref, target)

    def share(self, ref):
        self.pairs.append(self.send(ref, self.pair))

    def near(self):
        self.to_right.wait_recv()
        index = self.shard(False, -1)
        self.on_right = self.send(self.out.at[index, 0 : self.cut], self.right)
        if self.split:
            self.side_before = self.send(self.out.at[index, self.far_rows : self.rows], self.across)
        self.share(self.out.at[index])
        self.to_left.wait_recv()
        index = self.shard(False, 1)
        self.on_left = self.send(self.out.at[index, self.cut : self.rows], self.left)
        if self.split:
            self.side_after = self.send(self.out.at[index, self.far_rows : self.rows], self.across)
        self.share(self.out.at[index])

    def far(self):
        self.over.wait_recv()
        index = self.shard(True, 0)
        self.far_right = self.send(self.out.at[index, 0 : self.far_rows], self.right)
        self.far_left = self.send(self.out.at[index, 0 : self.far_rows], self.left)
        self.share(self.out.at[index])

    def middle(self):
        index = self.shard(False, 2)
        self.on_right.wait_recv()
        self.share(self.out.at[index, 0 : self.cut])
        self.on_left.wait_recv()
        if self.split:
            self.side_middle = self.send(self.out.at[index, self.far_rows : self.rows], self.across)
        self.share(self.out.at[index, self.cut : self.rows])

    def third(self):
        self.far_right.wait_recv()
        index = self.shard(True, -1)
        self.far_on_right = self.send(self.out.at[index, 0 : self.far_cut], self.right)
        self.share(self.out.at[index, 0 : self.far_rows])
        self.far_left.wait_recv()
        index = self.shard(True, 1)
        self.far_on_left = self.send(self.out.at[index, self.far_cut : self.far_rows], self.left)
        self.share(self.out.at[index, 0 : self.far_rows])

    def sides(self):
        for copy, dz in ((self.side_before, -1), (self.side_after, 1)):
            copy.wait_recv()
            self.share(self.out.at[self.shard(True, dz), self.far_rows : self.rows])

    def pairs_arrived(self, count):
        for copy in self.pairs[self.seen : count]:
            copy.wait_recv()
        self.seen = count

    def last(self):
        index = self.shard(True, 2)
        self.far_on_right.wait_recv()
        self.share(self.out.at[index, 0 : self.far_cut])
        self.far_on_left.wait_recv()
        self.share(self.out.at[index, self.far_cut : self.far_rows])
        if self.split:
            self.side_middle.wait_recv()
            self.share(self.out.at[index, self.far_rows : self.rows])
        self.pairs_arrived(len(self.pairs))


GATHER_REMOTES = 3 + 2 + 2 + 2 + 8 + 2


def exp_peers(where):
    x, y, z, core = where
    return [
        device(x, y, z, 1 - core),
        device(x, (y + 2) % 4, z, core),
        device(x, y, (z + 1) % 4, core),
        device(x, y, (z + 3) % 4, core),
    ]


def gather_kernel(
    rows, cot, cots, gate_w, up_w, down_w, spread,
    slot_rows, slot_cots, meta, weight, shared_out, d_shared, early,
    every, cots_in, gate, up, down, spread_in, filled_rows, filled_cots, lines, act, d_gates, pair_act, pair_gates,
    right, act_left, panels, send, recv, own, load_sem, keep_sem, early_sem,
):
    where = place()
    core, y_half = where[3], where[1] // 2
    me = lax.axis_index("exp")
    other = me + 1 - 2 * core
    loads = [
        pltpu.make_async_copy(src, dst, load_sem.at[i])
        for i, (src, dst) in enumerate(((gate_w, gate), (up_w, up), (down_w, down), (cots, cots_in), (spread, spread_in)))
    ]
    for load in loads:
        load.start()
    greet(exp_peers(where))
    copies = Copies(send, recv, own)
    gather = Gather(copies, where, rows, every, 64, 80, 48)
    shared_out[...] = jnp.zeros_like(shared_out)
    d_shared[...] = jnp.zeros_like(d_shared)

    def shared(first, last):
        @pl.loop(first, last)
        def _(step):
            at = pl.ds(pl.multiple_of(step * 128, 128), 128)
            value = rows[...]
            gate_pre, up_pre = dot(value, gate[:, at]), dot(value, up[:, at])
            silu, slope = gated(gate_pre, up_pre)
            activated = (silu * up_pre).astype(BF16)
            act[:, at] = activated
            shared_out[...] += dot(activated, down[at])
            d_act = dot_nt(cot[...], down[at])
            gate_back = (d_act * up_pre * slope).astype(BF16)
            up_back = (d_act * silu).astype(BF16)
            d_gates[0, :, at] = gate_back
            d_gates[1, :, at] = up_back
            d_shared[...] += dot_nt(gate_back, gate[:, at]) + dot_nt(up_back, up[:, at])

    def hot(block):
        slot = lax.broadcasted_iota(jnp.int32, (SLOTS, 128), 0).astype(F32)
        return [jnp.where(slot == lines[block, e : e + 1], 1.0, 0.0) for e in range(2)]

    def fill(block, source, out, column=None):
        value = dot(jnp.concatenate(hot(block), axis=0).astype(BF16), source)
        if column is not None:
            value = value * column
        value = value.astype(BF16)
        at = pl.ds(pl.multiple_of(block * SLOTS, SLOTS), SLOTS)
        for expert in range(2):
            out[expert, at] = value[expert * SLOTS : (expert + 1) * SLOTS]

    def fill_cots(block):
        column = jnp.concatenate(
            [jnp.sum(one * meta[block, e : e + 1], axis=1, keepdims=True) for e, one in enumerate(hot(block))], axis=0
        )
        at = pl.ds(pl.multiple_of(block * SLOTS, SLOTS), SLOTS)
        for expert in range(2):
            weight[expert, at] = jnp.broadcast_to(column[expert * SLOTS : (expert + 1) * SLOTS], (SLOTS, 128))
        fill(block, cots_in[block, 0:128], filled_cots, column)

    def fill_rows(far, dz):
        own_block = gather.shard(far, dz)
        for block in (own_block, own_block + 1 - 2 * core):
            fill(block, every[block], filled_rows)

    for load in loads[:3]:
        load.wait()
    shared(0, 4)
    gather.near()
    gather.far()
    shared(4, 7)
    pair = device(where[0], where[1], where[2], 1 - core)
    from_pair = [copies.remote(act, pair_act, pair), copies.remote(d_gates.at[1 - core], pair_gates, pair)]
    gather.middle()
    loads[3].wait()

    @pl.loop(0, 16)
    def _(block):
        high = cots_in[block, 128:144, pl.ds(pl.multiple_of(y_half * 128, 128), 128)].astype(F32)
        low = cots_in[block, 128:144, pl.ds(pl.multiple_of(256 + y_half * 128, 128), 128)].astype(F32)
        line = lax.broadcasted_iota(jnp.int32, (16, 128), 0)
        for expert in range(2):
            mine = line == 2 * (me % 8) + expert
            meta[block, expert : expert + 1] = jnp.sum(jnp.where(mine, high + low, 0.0), axis=0, keepdims=True)

    lines[...] = slot_lines(meta).reshape(16, 2, 128)

    @pl.loop(0, 16, unroll=4)
    def _(block):
        fill_cots(block)

    gather.third()
    keep_cots = pltpu.make_async_copy(filled_cots, slot_cots, keep_sem.at[0])
    keep_cots.start()
    gather.pairs_arrived(4)
    for copy in from_pair:
        copy.wait_recv()
    loads[4].wait()
    right[0:128, 0:896] = d_gates[core]
    right[128:256, 0:896] = pair_gates[...]
    at = pl.ds(pl.multiple_of(core * 640, 128), 640)
    right[0:128, 896:1536] = cot[:, at]
    right[128:256, 896:1536] = cots_in[other, 0:128, at]
    act_left[...] = dot(jnp.concatenate([act[...], pair_act[...]], axis=0), spread_in[...]).astype(BF16)

    def store(index):
        return pltpu.make_async_copy(
            panels.at[index], early.at[:, pl.ds(pl.multiple_of(index * 256, 256), 256)], early_sem.at[index]
        )

    @pl.loop(0, 5)
    def _(index):
        at = pl.ds(pl.multiple_of(index * 256, 256), 256)
        value = dot_tn(jnp.concatenate([rows[:, at], every[other, :, at]], axis=0), right[:, 0:896])
        for panel in range(7):
            panels[index, panel] = value[:, panel * 128 : panel * 128 + 128].astype(BF16)
        value = dot_tn(act_left[:, at], right[:, 896:1536])
        for panel in range(5):
            panels[index, 7 + panel] = value[:, panel * 128 : panel * 128 + 128].astype(BF16)
        store(index).start()

    gather.mine.wait()
    gather.sides()
    gather.pairs_arrived(6)
    for far, dz in ((False, 0), (False, -1), (False, 1), (True, 0), (False, 2)):
        fill_rows(far, dz)
    gather.pairs_arrived(10)
    for dz in (-1, 1):
        fill_rows(True, dz)
    gather.last()
    fill_rows(True, 2)
    keep_rows = pltpu.make_async_copy(filled_rows, slot_rows, keep_sem.at[1])
    keep_rows.start()
    copies.drain()
    keep_cots.wait()
    keep_rows.wait()
    for index in range(5):
        store(index).wait()


def gather_rows(rows, cot, cots, gate_w, up_w, down_w, collective_id):
    count, width = rows.shape
    hidden = gate_w.shape[1]
    spread = np.zeros((128, 7, 128, 10), np.float32)
    for group in range(128):
        spread[group, np.arange(7), group, np.arange(7)] = 1.0
    spread = jnp.asarray(spread.reshape(hidden, width), BF16)
    return pl.pallas_call(
        gather_kernel,
        name="gather_rows",
        out_shape=(
            jax.ShapeDtypeStruct((2, SLOT_ROWS, width), BF16),
            jax.ShapeDtypeStruct((2, SLOT_ROWS, width), BF16),
            jax.ShapeDtypeStruct((16, 2, 128), F32),
            jax.ShapeDtypeStruct((2, SLOT_ROWS, 128), F32),
            jax.ShapeDtypeStruct((count, width), F32),
            jax.ShapeDtypeStruct((count, width), F32),
            jax.ShapeDtypeStruct((12, width, 128), BF16),
        ),
        in_specs=[VMEM, VMEM] + [ANYWHERE] * 5,
        out_specs=(ANYWHERE, ANYWHERE) + (VMEM,) * 4 + (ANYWHERE,),
        scratch_shapes=[
            pltpu.VMEM((16, count, width), BF16),
            pltpu.VMEM(cots.shape, BF16),
            pltpu.VMEM(gate_w.shape, BF16),
            pltpu.VMEM(up_w.shape, BF16),
            pltpu.VMEM(down_w.shape, BF16),
            pltpu.VMEM(spread.shape, BF16),
            pltpu.VMEM((2, SLOT_ROWS, width), BF16),
            pltpu.VMEM((2, SLOT_ROWS, width), BF16),
            pltpu.VMEM((16, 2, 128), F32),
            pltpu.VMEM((count, hidden), BF16),
            pltpu.VMEM((2, count, hidden), BF16),
            pltpu.VMEM((count, hidden), BF16),
            pltpu.VMEM((count, hidden), BF16),
            pltpu.VMEM((2 * count, 1536), BF16),
            pltpu.VMEM((2 * count, width), BF16),
            pltpu.VMEM((5, 12, 256, 128), BF16),
            pltpu.SemaphoreType.DMA((GATHER_REMOTES + 8,)),
            pltpu.SemaphoreType.DMA((GATHER_REMOTES + 8,)),
            pltpu.SemaphoreType.DMA((1,)),
            pltpu.SemaphoreType.DMA((5,)),
            pltpu.SemaphoreType.DMA((2,)),
            pltpu.SemaphoreType.DMA((5,)),
        ],
        compiler_params=params(collective_id),
        cost_estimate=cost(10**9, 6 * 10**7),
    )(rows, cot, cots, gate_w, up_w, down_w, spread)


class Scatter:
    def __init__(self, copies, where, parts, pair_land, work, ring_land, far_land, y_land):
        x, y, z, core = where
        self.copies, self.work, self.pair_land = copies, work, pair_land
        self.ring_land, self.far_land, self.y_land = ring_land, far_land, y_land
        self.across = device(x, (y + 2) % 4, z, core)
        self.right, self.left = device(x, y, (z + 1) % 4, core), device(x, y, (z + 3) % 4, core)
        pair = device(x, y, z, 1 - core)
        self.pairs, self.loads = {}, {}
        for slot in ((0, 2), (1, 2), (0, 1), (0, 3), (1, 1), (1, 3), (0, 0), (1, 0)):
            y_half = 1 - y // 2 if slot[0] == 0 else y // 2
            at = (z + slot[1]) % 4
            self.pairs[slot] = copies.remote(parts.at[rank(y_half, at, 1 - core)], pair_land.at[slot], pair)
            self.loads[slot] = copies.local(parts.at[rank(y_half, at, core)], work.at[slot])

    def merge(self, slot):
        self.loads[slot].wait()
        self.pairs[slot].wait_recv()
        rows_add(self.work.at[slot], 0, 128, self.work.at[slot], self.pair_land.at[slot])

    def first(self):
        self.ring = {}
        for far in range(2):
            self.merge((far, 2))
            self.ring[far] = (
                self.copies.remote(self.work.at[far, 2, 0:64], self.ring_land.at[far, 0], self.right),
                self.copies.remote(self.work.at[far, 2, 64:128], self.ring_land.at[far, 1], self.left),
            )

    def merge_rest(self):
        for far in range(2):
            self.merge((far, 1))
            self.merge((far, 3))
            self.merge((far, 0))

    def second(self):
        self.final = {}
        for far in range(2):
            self.ring[far][0].wait_recv()
            rows_add(self.work.at[far, 1, 0:64], 0, 64, self.work.at[far, 1, 0:64], self.ring_land.at[far, 0])
            to_right = self.copies.remote(self.work.at[far, 1], self.far_land.at[far, 0], self.right)
            self.ring[far][1].wait_recv()
            rows_add(self.work.at[far, 3, 64:128], 0, 64, self.work.at[far, 3, 64:128], self.ring_land.at[far, 1])
            to_left = self.copies.remote(self.work.at[far, 3], self.far_land.at[far, 1], self.left)
            self.final[far] = (to_right, to_left)

    def third(self):
        for far in range(2):
            for copy in self.final[far]:
                copy.wait_recv()
            rows_add(self.work.at[far, 0], 0, 128, self.work.at[far, 0], self.far_land.at[far, 0], self.far_land.at[far, 1])
            if far == 0:
                self.over = self.copies.remote(self.work.at[0, 0], self.y_land, self.across)

    def last(self, out):
        self.over.wait_recv()
        rows_add(out, 0, 128, self.work.at[1, 0], self.y_land)


def rows_add(out, first, rows, *terms):
    @pl.loop(0, rows // 16)
    def _(step):
        at = pl.ds(pl.multiple_of(step * 16, 16), 16)
        value = terms[0][at].astype(F32)
        for term in terms[1:]:
            value = value + term[at].astype(F32)
        out[at] = value.astype(out.dtype)


SCATTER_REMOTES, SCATTER_LOCALS = 8 + 4 + 4 + 1, 8
SCATTER_SCRATCH = [
    pltpu.VMEM((2, 4, 128, 1280), BF16),
    pltpu.VMEM((2, 4, 128, 1280), BF16),
    pltpu.VMEM((2, 2, 64, 1280), BF16),
    pltpu.VMEM((2, 2, 128, 1280), BF16),
    pltpu.VMEM((128, 1280), BF16),
]


def up_add(out, *terms):
    add_into(out, (), *terms, rows=(16, 10))


def scatter_kernel(
    parts, rows_in, cots_in, act_in, back_in, d_shared, hidden_rows, gain, cot, w_out_in, down_one,
    gate_sum, up_out, up_one, down_out, down_final, d_mixed, d_hidden, d_attn, gain_term,
    a, b, c, d, e, rows, cots, act, back, gate, up, down, land, w_out, d_routed, up_land, one_other,
    send, recv, own, load_sem, keep_sem,
):
    where = place()
    x, y, z, core = where
    x_peers = [device((x + 1) % 4, y, z, core), device((x + 3) % 4, y, z, core)]
    loads = [
        pltpu.make_async_copy(src, dst, load_sem.at[i])
        for i, (src, dst) in enumerate(
            (
                (rows_in.at[0], rows.at[0]), (back_in.at[0], back.at[0]), (rows_in.at[1], rows.at[1]),
                (back_in.at[1], back.at[1]), (act_in.at[1], act), (cots_in.at[1], cots), (w_out_in, w_out),
            )
        )
    ]
    for load in loads:
        load.start()
    greet(exp_peers(where) + x_peers + [device(x, (y // 2) * 2 + 1 - y % 2, z, core)])
    copies = Copies(send, recv, own)
    scatter = Scatter(copies, where, parts, a, b, c, d, e)
    hidden = act.shape[1]
    loads[0].wait()
    loads[1].wait()

    y_low = y % 2
    pair = device(x, (y // 2) * 2 + 1 - y_low, z, core)

    def term(dst, lanes, first, last):
        @pl.loop(first, last)
        def _(index):
            expert = index // 5
            at = pl.ds(pl.multiple_of((index % 5) * 256, 256), 256)
            dst[expert, at] = dot_tn(rows[expert, :, at], back[expert, :, lanes]).astype(BF16)

    def up_rows(chunk, which):
        return pl.ds(pl.multiple_of(chunk * 320 + which * 160, 160), 160)

    swap_one = copies.remote(down_one.at[half_rows(1 - y_low, 112)], one_other, pair)

    def gate_ring(expert):
        return RingSum(
            copies, x, x_peers[0], x_peers[1], lambda chunk, half: gate.at[expert, half_rows(2 * chunk + half, 160)],
            land.at[expert], None, up_add, resident=True,
        )

    term(gate, slice(0, hidden), 0, 5)
    rings = [gate_ring(0)]
    rings[0].raw()
    scatter.first()
    scatter.merge_rest()
    loads[2].wait()
    loads[3].wait()
    term(up, slice(hidden, 2 * hidden), 5, 10)
    over = [copies.remote(up.at[1, up_rows(chunk, 1 - y_low)], up_land.at[chunk], pair) for chunk in range(4)]
    term(gate, slice(0, hidden), 5, 10)
    rings.append(gate_ring(1))
    rings[1].raw()
    scatter.second()
    rings[0].forward()
    term(up, slice(hidden, 2 * hidden), 0, 5)
    keep_up = pltpu.make_async_copy(up.at[0], up_out, keep_sem.at[0])
    keep_up.start()
    loads[4].wait()
    loads[5].wait()

    @pl.loop(0, hidden // 128)
    def _(index):
        at = pl.ds(pl.multiple_of(index * 128, 128), 128)
        down[at] = dot_tn(act[:, at], cots[...]).astype(BF16)

    keep_down = pltpu.make_async_copy(down, down_out, keep_sem.at[1])
    keep_down.start()
    rings[1].forward()
    scatter.third()
    scatter.last(d_routed)
    grad, term_sum = normed_back(hidden_rows[...], gain[...].reshape(1, -1), d_shared[...] + d_routed[...])
    whole = cot[...].astype(F32) + grad
    d_hidden[...] = whole
    d_attn[...] = whole.astype(BF16)
    gain_term[...] = term_sum
    loads[6].wait()

    @pl.loop(0, 5)
    def _(index):
        value = dot_nt(d_attn[...], w_out[pl.ds(pl.multiple_of(index * 256, 256), 256)]).astype(BF16)
        d_mixed[2 * index] = value[:, :HEAD_DIM]
        d_mixed[2 * index + 1] = value[:, HEAD_DIM:]

    for chunk, copy in enumerate(over):
        copy.wait_recv()
        add_into(up_one.at[chunk], (), up.at[1, up_rows(chunk, y_low)], up_land.at[chunk], rows=(16, 10))
    for expert in range(2):
        rings[expert].finish([gate_sum.at[expert, 0:160], gate_sum.at[expert, 160:320]])
    swap_one.wait_recv()
    add_into(down_final, (), down_one.at[half_rows(y_low, 112)], one_other, rows=(16, 7))
    copies.drain()
    keep_up.wait()
    keep_down.wait()


def scatter_rows(parts, kept_rows, kept_cots, kept_act, kept_back, d_shared, hidden_rows, gain, cot, w_out, down_one, collective_id):
    width, hidden = kept_rows.shape[2], kept_act.shape[2]
    count = cot.shape[0]
    return pl.pallas_call(
        scatter_kernel,
        name="scatter_rows",
        out_shape=(
            jax.ShapeDtypeStruct((2, 320, hidden), BF16),
            jax.ShapeDtypeStruct((width, hidden), BF16),
            jax.ShapeDtypeStruct((4, 160, hidden), BF16),
            jax.ShapeDtypeStruct((hidden, width), BF16),
            jax.ShapeDtypeStruct((112, width), F32),
            jax.ShapeDtypeStruct((10, count, HEAD_DIM), BF16),
            jax.ShapeDtypeStruct((count, width), F32),
            jax.ShapeDtypeStruct((count, width), BF16),
            jax.ShapeDtypeStruct((1, width), F32),
        ),
        in_specs=[ANYWHERE] * 5 + [VMEM] * 4 + [ANYWHERE, VMEM],
        out_specs=(VMEM, ANYWHERE, VMEM, ANYWHERE) + (VMEM,) * 5,
        scratch_shapes=SCATTER_SCRATCH
        + [
            pltpu.VMEM(kept_rows.shape, BF16),
            pltpu.VMEM(kept_cots.shape[1:], BF16),
            pltpu.VMEM(kept_act.shape[1:], BF16),
            pltpu.VMEM(kept_back.shape, BF16),
            pltpu.VMEM((2, width, hidden), BF16),
            pltpu.VMEM((2, width, hidden), BF16),
            pltpu.VMEM((hidden, width), BF16),
            pltpu.VMEM((2, 6, 160, hidden), BF16),
            pltpu.VMEM(w_out.shape, BF16),
            pltpu.VMEM((count, width), F32),
            pltpu.VMEM((4, 160, hidden), BF16),
            pltpu.VMEM((112, width), BF16),
            pltpu.SemaphoreType.DMA((SCATTER_REMOTES + 17,)),
            pltpu.SemaphoreType.DMA((SCATTER_REMOTES + 17,)),
            pltpu.SemaphoreType.DMA((SCATTER_LOCALS,)),
            pltpu.SemaphoreType.DMA((7,)),
            pltpu.SemaphoreType.DMA((2,)),
        ],
        compiler_params=params(collective_id),
        cost_estimate=cost(10**10, 10**8),
    )(
        parts, kept_rows, kept_cots, kept_act, kept_back,
        d_shared, hidden_rows, gain, cot, w_out, down_one,
    )


def ctx_device(ctx):
    return (ctx, lax.axis_index("exp"))


def extra_owner(head):
    core = lax.axis_index("exp") % 2
    return 3 * core if head == 8 else 5 + core


def owns_extra(ctx):
    return (ctx == extra_owner(8)) | (ctx == extra_owner(9))


def extra_head(ctx):
    return 8 + (ctx == extra_owner(9)).astype(jnp.int32)


class Exchange:
    def __init__(self, send, recv, own):
        self.send, self.recv, self.own = send, recv, own
        self.ctx = lax.axis_index("ctx")

    def copy(self, src, dst, slot, d):
        return pltpu.make_async_remote_copy(
            src_ref=src,
            dst_ref=dst,
            send_sem=self.send.at[slot, d],
            recv_sem=self.recv.at[slot, d],
            device_id=ctx_device((self.ctx + d) % 8),
            device_id_type=MESH,
        )


class ToOwners:
    def __init__(self, exchange, block, land):
        self.exchange, self.block, self.land, self.ctx = exchange, block, land, exchange.ctx

    def mine(self, slot, head):
        return pltpu.make_async_copy(self.block(head), self.land(slot, self.ctx), self.exchange.own.at[slot])

    def start(self, head):
        slot, owner = (0, head) if head < 8 else (1, extra_owner(head))
        d = (owner + 8 - self.ctx) % 8

        @pl.when(d == 0)
        def _():
            self.mine(slot, head).start()

        @pl.when(d != 0)
        def _():
            self.exchange.copy(self.block(head), self.land(slot, self.ctx), slot, d).start()

    def any(self, slot, d):
        return self.exchange.copy(self.block(0), self.land(slot, self.ctx), slot, d)

    def arrived(self):
        self.mine(0, 0).wait()
        for d in range(1, 8):
            self.any(0, d).wait_recv()

        @pl.when(owns_extra(self.ctx))
        def _():
            self.mine(1, 0).wait()
            for d in range(1, 8):
                self.any(1, d).wait_recv()

    def sent(self):
        for d in range(1, 8):
            self.any(0, d).wait_send()

            @pl.when(owns_extra((self.ctx + d) % 8))
            def _():
                self.any(1, d).wait_send()


class Home:
    def __init__(self, exchange, block, land):
        self.exchange, self.block, self.land = exchange, block, land
        self.ctx = exchange.ctx

    def head(self, slot):
        return self.ctx if slot == 0 else extra_head(self.ctx)

    def start(self, slot):
        for d in range(1, 8):
            self.exchange.copy(self.block(slot, (self.ctx + d) % 8), self.land(self.head(slot)), slot, d).start()
        self.mine(slot).start()

    def mine(self, slot):
        return pltpu.make_async_copy(
            self.block(slot, self.ctx), self.land(self.head(slot)), self.exchange.own.at[slot]
        )

    def finish(self):
        self.mine(0).wait()
        for d in range(1, 8):
            copy = self.exchange.copy(self.block(0, 0), self.land(0), 0, d)
            copy.wait_send()
            copy.wait_recv()

            @pl.when(owns_extra((self.ctx + 8 - d) % 8))
            def _():
                self.exchange.copy(self.block(1, 0), self.land(0), 1, d).wait_recv()

        @pl.when(owns_extra(self.ctx))
        def _():
            self.mine(1).wait()
            for d in range(1, 8):
                self.exchange.copy(self.block(1, 0), self.land(0), 1, d).wait_send()


def attend_kernel(
    length, cot, routes, route_gates, w_query, w_key, w_value, w_out_in, tokens, attn_gain, ffn_gain, cos, sin,
    normed_one, mixed, heads, cots, hidden, normed_two,
    sent_cot, qkv, weights, land, result, home, w_out, s1, r1, o1, s2, r2, o2, s3, r3, o3, load_sem, weight_sem,
):
    def fetch(index):
        return [
            pltpu.make_async_copy(source.at[:, 256 * index : 256 * index + 256], weights.at[index, kind], weight_sem.at[index, kind])
            for kind, source in enumerate((w_query, w_key, w_value))
        ]

    pairs_of_heads = (4, 0, 1, 2, 3)
    for index in pairs_of_heads:
        for copy in fetch(index):
            copy.start()
    load = pltpu.make_async_copy(w_out_in, w_out, load_sem)
    load.start()
    where = place()
    ctx = lax.axis_index("ctx")
    greet([ctx_device((ctx + d) % 8) for d in range(1, 8)] + exp_peers(where))
    copies = Copies(s3, r3, o3)
    expert = lax.broadcasted_iota(jnp.int32, (32, 128), 0)
    table = jnp.zeros((32, 128), F32)
    for choice in range(routes.shape[0]):
        table += jnp.where(expert == routes[choice : choice + 1], route_gates[choice : choice + 1], 0.0)
    position = lax.broadcasted_iota(jnp.int32, (32, 128), 1) + ctx * 128
    table = jnp.where(position < length[0], table, 0.0)
    high = table.astype(BF16)
    low = (table - high.astype(F32)).astype(BF16)
    sent_cot[0:128] = cot[...]
    sent_cot[128:144] = jnp.zeros((16, cot.shape[1]), BF16)
    for index, part in enumerate((high[0:16], high[16:32], low[0:16], low[16:32])):
        sent_cot[128:144, index * 128 : index * 128 + 128] = part
    gather = Gather(copies, where, sent_cot, cots, 80, 144, 80)
    owners = ToOwners(Exchange(s1, r1, o1), lambda head: qkv.at[head], lambda slot, c: land.at[slot, :, c])
    normed_one[...] = normed(tokens[...].astype(F32), attn_gain[...].reshape(1, -1)).astype(BF16)
    positions = pl.ds(pl.multiple_of(ctx * 128, 128), 128)
    for index in pairs_of_heads:
        for copy in fetch(index):
            copy.wait()
        parts = [dot(normed_one[...], weights[index, kind]) for kind in range(3)]
        for half in range(2):
            head, lanes = 2 * index + half, slice(half * HEAD_DIM, (half + 1) * HEAD_DIM)
            qkv[head, 0] = turned(parts[0][:, lanes], cos[positions], sin[positions]).astype(BF16)
            qkv[head, 1] = turned(parts[1][:, lanes], cos[positions], sin[positions]).astype(BF16)
            qkv[head, 2] = parts[2][:, lanes].astype(BF16)
            owners.start(head)
    back = Home(Exchange(s2, r2, o2), lambda slot, c: result.at[slot, c], lambda head: home.at[head])
    keep = pltpu.make_async_copy(land, heads, o3.at[1])

    def run(slot, blocks):
        for block in blocks:
            width = (block + 1) * 128
            query = land[slot, 0, block]
            key = land[slot, 1, 0 : block + 1].reshape(width, HEAD_DIM)
            value = land[slot, 2, 0 : block + 1].reshape(width, HEAD_DIM)
            row = lax.broadcasted_iota(jnp.int32, (width, 128), 0)
            column = lax.broadcasted_iota(jnp.int32, (width, 128), 1) + block * 128
            scores = jnp.where(
                (row <= column) & (row < length[0]), dot_nt(key, query) * SCALE, -1e30
            )
            weights = jnp.exp(scores - jnp.max(scores, axis=0, keepdims=True))
            probs = weights * (1.0 / jnp.sum(weights, axis=0, keepdims=True))
            result[slot, block] = dot_tn(probs.astype(BF16), value).astype(BF16)

    gather.near()
    gather.far()
    owners.arrived()
    run(0, range(8))
    back.start(0)

    @pl.when(owns_extra(ctx))
    def _():
        run(1, range(8))
        back.start(1)

    @pl.when(jnp.logical_not(owns_extra(ctx)))
    def _():
        land[1] = jnp.zeros_like(land[1])

    keep.start()
    gather.middle()
    gather.third()
    gather.mine.wait()
    back.finish()
    for head in range(10):
        mixed[:, head * HEAD_DIM : (head + 1) * HEAD_DIM] = home[head]
    load.wait()

    @pl.loop(0, 5)
    def _(index):
        at = pl.ds(pl.multiple_of(index * 256, 256), 256)
        hidden[:, at] = tokens[:, at].astype(F32) + dot(mixed[...], w_out[:, at])

    normed_two[...] = normed(hidden[...], ffn_gain[...].reshape(1, -1)).astype(BF16)
    gather.last()
    owners.sent()
    keep.wait()
    copies.drain()


def exchange_semaphores():
    return [
        pltpu.SemaphoreType.DMA((2, 8)),
        pltpu.SemaphoreType.DMA((2, 8)),
        pltpu.SemaphoreType.DMA((2,)),
    ]


def attend(length, cot, routes, route_gates, w_query, w_key, w_value, w_out, tokens, attn_gain, ffn_gain, cos, sin, collective_id):
    rows, width = tokens.shape
    return pl.pallas_call(
        attend_kernel,
        name="attend",
        out_shape=(
            jax.ShapeDtypeStruct((rows, width), BF16),
            jax.ShapeDtypeStruct((rows, width), BF16),
            jax.ShapeDtypeStruct((2, 3, 8, rows, HEAD_DIM), BF16),
            jax.ShapeDtypeStruct((16, rows + 16, width), BF16),
            jax.ShapeDtypeStruct((rows, width), F32),
            jax.ShapeDtypeStruct((rows, width), BF16),
        ),
        in_specs=[SMEM] + [VMEM] * 3 + [ANYWHERE] * 4 + [VMEM] * 5,
        out_specs=(VMEM, VMEM, ANYWHERE, ANYWHERE, VMEM, VMEM),
        scratch_shapes=[
            pltpu.VMEM((rows + 16, width), BF16),
            pltpu.VMEM((10, 3, rows, HEAD_DIM), BF16),
            pltpu.VMEM((5, 3, width, 256), BF16),
            pltpu.VMEM((2, 3, 8, rows, HEAD_DIM), BF16),
            pltpu.VMEM((2, 8, rows, HEAD_DIM), BF16),
            pltpu.VMEM((10, rows, HEAD_DIM), BF16),
            pltpu.VMEM(w_out.shape, BF16),
        ]
        + exchange_semaphores()
        + exchange_semaphores()
        + [
            pltpu.SemaphoreType.DMA((GATHER_REMOTES,)),
            pltpu.SemaphoreType.DMA((GATHER_REMOTES,)),
            pltpu.SemaphoreType.DMA((2,)),
            pltpu.SemaphoreType.DMA,
            pltpu.SemaphoreType.DMA((5, 3)),
        ],
        compiler_params=params(collective_id),
        cost_estimate=cost(10**9, 10**8),
    )(length, cot, routes, route_gates, w_query, w_key, w_value, w_out, tokens, attn_gain, ffn_gain, cos, sin)


def attend_back_kernel(
    d_mixed, heads, length, cos, sin, parts, up, up_one, gate, first, d_attn, normed_one, mixed, tokens, gain, d_hidden,
    ffn_term, w_query_in, w_key_in, w_value_in, down,
    input_grad, routed, up_final, gate_out, dense_out, up_out, down_out,
    land, kept, d_key, d_value, result, home, a, b, c, d, e, up_land, up_work, one_land, gate_other, first_land,
    pair_rows, d_qkv, pair_qkv, right, out_right, out_terms, out_land, weights, total, late, up_sum, first_sum, second,
    z_land, f_land, y_land, y_sum, x_land, u_land, v_land, v_sum, w_land, t_land, tz_land, t_sum, tx_land,
    gains, gx_land, gx_sum, gy_land, sums, stage, final_land, up_other, d_land, d_work, d_other,
    s1, r1, o1, s2, r2, o2, s3, r3, o3, s4, r4, o4, load_sem, weight_sem,
):
    where = place()
    x, y, z, core = where
    ctx = lax.axis_index("ctx")
    x_peers = [device((x + 1) % 4, y, z, core), device((x + 3) % 4, y, z, core)]
    load_heads = pltpu.make_async_copy(heads, kept, load_sem)
    load_heads.start()

    def fetch(index):
        rows = slice(256 * index, 256 * index + 256)
        return [
            pltpu.make_async_copy(source.at[rows], weights.at[index % 2, kind], weight_sem.at[index % 2, kind])
            for kind, source in enumerate((w_query_in, w_key_in, w_value_in))
        ]

    for index in range(2):
        for copy in fetch(index):
            copy.start()
    spot = z * 2 + core
    spot_peers = [device(x, y, ((spot + d) % 8) // 2, (spot + d) % 2) for d in range(1, 8)]
    more_peers = [
        device(x, y, (z + 2) % 4, core), device(x, y, (z + 2) % 4, 1 - core),
        device(x, y, (z + 1) % 4, 1 - core), device(x, y, (z + 3) % 4, 1 - core),
    ]
    y_peers = [device(x, (y + step) % 4, z, core) for step in (1, 2, 3)]
    pair_peer = device(x, (y // 2) * 2 + 1 - y % 2, z, core)
    cross_peer = device(x, (y // 2) * 2 + 2 + 1 - y % 2 - 4 * (y // 2), z, core)
    greet([ctx_device((ctx + step) % 8) for step in range(1, 8)] + exp_peers(where) + [cross_peer] + more_peers)
    owners = ToOwners(Exchange(s1, r1, o1), lambda head: d_mixed.at[head], lambda slot, at: land.at[slot, at])
    for head in (8, 9, 0, 1, 2, 3, 4, 5, 6, 7):
        owners.start(head)
    copies = Copies(s3, r3, o3)
    scatter = Scatter(copies, where, parts, a, b, c, d, e)
    back = Home(Exchange(s2, r2, o2), lambda slot, at: result.at[slot, :, at], lambda head: home.at[:, head])
    y_low = y % 2

    def one_add(out, *terms):
        add_into(out, (), *terms, rows=(16, 5))

    ring_one = RingSum(
        copies, x, x_peers[0], x_peers[1], lambda chunk, half: up_one.at[chunk, 80 * half : 80 * half + 80],
        one_land, None, one_add, resident=True,
    )
    ring = RingSum(
        copies, x, x_peers[0], x_peers[1], lambda chunk, half: up.at[half_rows(2 * chunk + half, 160)],
        up_land, up_work, up_add,
    )
    swap = copies.remote(gate.at[:, half_rows(1 - y_low, 160)], gate_other, pair_peer)
    z_peers = [device(x, y, (z + 1) % 4, core), device(x, y, (z + 3) % 4, core)]

    block_add = add_blocks((2, 4))
    pair = device(x, y, z, 1 - core)
    pairs = [copies.remote(src, pair_rows.at[i], pair) for i, src in enumerate((normed_one, mixed, d_attn))]
    for copy in pairs:
        copy.wait_recv()
    at = pl.ds(pl.multiple_of(core * 640, 128), 640)
    out_right[0:128] = d_attn[:, at]
    out_right[128:256] = pair_rows[2, :, at]

    def spread_blocks(value, tile, panels):
        for lane, ref in enumerate(panels):
            for block in range(8):
                part = value[80 * block : 80 * block + 80, lane * 128 : lane * 128 + 128]
                ref[2 * tile + block // 4, block % 4] = part.astype(BF16)

    @pl.loop(0, 2)
    def _(tile):
        at = pl.ds(pl.multiple_of(tile * 640, 128), 640)
        value = dot_tn(jnp.concatenate([mixed[:, at], pair_rows[1, :, at]], axis=0), out_right[...])
        spread_blocks(value, tile, [out_terms.at[panel] for panel in range(4)] + [late.at[3, 3]])

    scatter.first()
    load_heads.wait()
    owners.arrived()

    def run(slot):
        d_key[...] = jnp.zeros_like(d_key)
        d_value[...] = jnp.zeros_like(d_value)
        for block in range(8):
            width = (block + 1) * 128
            query, upstream = kept[slot, 0, block], land[slot, block]
            key = kept[slot, 1, 0 : block + 1].reshape(width, HEAD_DIM)
            value = kept[slot, 2, 0 : block + 1].reshape(width, HEAD_DIM)
            row = lax.broadcasted_iota(jnp.int32, (width, 128), 0)
            column = lax.broadcasted_iota(jnp.int32, (width, 128), 1) + block * 128
            scores = jnp.where(
                (row <= column) & (row < length[0]), dot_nt(key, query) * SCALE, -1e30
            )
            weight = jnp.exp(scores - jnp.max(scores, axis=0, keepdims=True))
            probs = weight * (1.0 / jnp.sum(weight, axis=0, keepdims=True))
            d_probs = dot_nt(value, upstream)
            delta = jnp.sum(probs * d_probs, axis=0, keepdims=True)
            d_scores = (probs * (d_probs - delta)).astype(BF16)
            rows = slice(block * 128, block * 128 + 128)
            d_query = dot_tn(d_scores, key) * SCALE
            result[slot, 0, block] = turned(d_query, cos[rows], sin[rows]).astype(BF16)
            d_key[0:width] += dot(d_scores, query)
            d_value[0:width] += dot(probs.astype(BF16), upstream)
        for block in range(8):
            rows = slice(block * 128, block * 128 + 128)
            result[slot, 1, block] = turned(d_key[rows] * SCALE, cos[rows], sin[rows]).astype(BF16)
            result[slot, 2, block] = d_value[rows].astype(BF16)
        back.start(slot)

    run(0)
    scatter.merge_rest()
    scatter.second()

    @pl.when(owns_extra(ctx))
    def _():
        run(1)

    first_copies = [
        copies.remote(first.at[:, :, order((y + step) % 4)], first_land.at[step - 1], y_peers[step - 1])
        for step in (1, 2, 3)
    ]
    ring_one.raw()
    ring_one.forward()
    ring.raw()
    outs = RingSum(
        copies, z, z_peers[0], z_peers[1], lambda chunk, half: out_terms.at[chunk, 2 * half : 2 * half + 2],
        out_land, None, block_add, resident=True,
    )
    outs.raw()
    ring.forward()
    scatter.third()
    back.finish()
    outs.forward()
    for head in range(10):
        for kind in range(3):
            at = kind * 1280 + head * HEAD_DIM
            d_qkv[:, at : at + HEAD_DIM] = home[kind, head]
    swap_qkv = copies.remote(d_qkv, pair_qkv, pair)
    for index in range(5):
        for copy in fetch(index):
            copy.wait()
        value = dot_nt(d_qkv[:, 0:1280], weights[index % 2, 0])
        value += dot_nt(d_qkv[:, 1280:2560], weights[index % 2, 1])
        value += dot_nt(d_qkv[:, 2560:3840], weights[index % 2, 2])
        total[:, 256 * index : 256 * index + 256] = value
        if index + 2 < 5:
            for copy in fetch(index + 2):
                copy.start()

    swap_qkv.wait_recv()
    at = pl.ds(pl.multiple_of(core * 1920, 128), 1920)
    right[0:128] = d_qkv[:, at]
    right[128:256] = pair_qkv[:, at]

    @pl.loop(0, 2)
    def _(tile):
        at = pl.ds(pl.multiple_of(tile * 640, 128), 640)
        left = jnp.concatenate([normed_one[:, at], pair_rows[0, :, at]], axis=0)
        for group in range(5):
            value = dot_tn(left, right[:, 384 * group : 384 * group + 384])
            spread_blocks(value, tile, [late.at[p // 4, p % 4] for p in range(3 * group, 3 * group + 3)])

    last = Copies(s4, r4, o4)

    def direct(part, me, land, peers):
        return [last.remote(part((me + d) % 4), land.at[d - 1], peers[d - 1]) for d in (1, 2, 3)]

    def landed(arrivals):
        for copy in arrivals:
            copy.wait_recv()

    all_z = [z_peers[0], more_peers[0], z_peers[1]]
    all_x = [x_peers[0], device((x + 2) % 4, y, z, core), x_peers[1]]

    def z_ring(panel):
        return RingSum(
            last, z, z_peers[0], z_peers[1], lambda chunk, half: late.at[chunk, panel, 2 * half : 2 * half + 2],
            z_land.at[panel], None, block_add, resident=True,
        )

    ring_a, ring_b = z_ring(0), z_ring(1)
    ring_a.raw()
    tall = RingSum(
        last, y, y_peers[0], y_peers[2], lambda chunk, half: late.at[2 * half : 2 * half + 2, 3, :, order(chunk)],
        t_land, None, block_add, resident=True,
    )
    tall.raw()
    side = RingSum(
        last, x, x_peers[0], x_peers[1], lambda chunk, half: late.at[2 * half : 2 * half + 2, 2, chunk],
        u_land, None, block_add, resident=True,
    )
    side.raw()

    grad, term = normed_back(tokens[...].astype(F32), gain[...].reshape(1, -1), total[...])
    input_grad[...] = d_hidden[...] + grad
    column = lax.broadcasted_iota(jnp.int32, (128, 1280), 1)
    group = lax.broadcasted_iota(jnp.int32, (128, 1280), 0)
    inside = (column >= group * 10) & (column < group * 10 + 10)
    rest = lax.broadcasted_iota(jnp.int32, (1280, 128), 0) % 10
    lane = lax.broadcasted_iota(jnp.int32, (1280, 128), 1)
    lines = jnp.zeros((128, 128), F32)
    for offset, values in ((0, term), (10, ffn_term[...])):
        spots = jnp.where(inside, values, 0.0)
        high = spots.astype(BF16)
        low = (spots - high.astype(F32)).astype(BF16)
        pick = jnp.where(lane == rest + offset, 1.0, 0.0).astype(BF16)
        lines += dot(high, pick) + dot(low, pick)
    gains[...] = lines.reshape(4, 4, 8, 128)
    gain_x = direct(lambda c: gains.at[c], x, gx_land, all_x)

    def down_add(out, *terms):
        add_into(out, (), *terms, rows=(16, 7))

    downs = RingSum(
        last, x, x_peers[0], x_peers[1], lambda c, h: down.at[half_rows(2 * c + h, 112)], d_land, d_work, down_add
    )
    downs.raw()
    scatter.last(routed)
    outs.finish([second.at[0:2], second.at[2:4]])
    y_copies = {0: direct(lambda c: second.at[:, order(c)], y, y_land.at[0], y_peers)}
    ring_a.forward()
    ring_b.raw()
    tall.forward()
    for copy in first_copies:
        copy.wait_recv()
    add_into(first_sum, (3, 4), first.at[:, :, order(y)], first_land.at[0], first_land.at[1], first_land.at[2])
    x_copies = {3: direct(lambda c: first_sum.at[:, c], x, f_land, all_x)}
    ring_b.forward()
    swap.wait_recv()
    add_into(gate_out, (2,), gate.at[:, half_rows(y_low, 160)], gate_other, rows=(16, 10))
    ring_one.finish([up_final.at[0:80], up_final.at[80:160]])
    ring.finish([up_sum.at[0], up_sum.at[1]])
    swap_up = last.remote(up_sum.at[1 - y_low], up_other, pair_peer)
    side.forward()
    landed(gain_x)
    gx_sum[...] = gains[x] + gx_land[0] + gx_land[1] + gx_land[2]
    gain_y = direct(lambda c: gx_sum.at[order(c)], y, gy_land, y_peers)
    downs.forward()

    def start_x(t, mine):
        landed(y_copies[t])
        add_into(y_sum.at[t], (4,), mine, y_land.at[t, 0], y_land.at[t, 1], y_land.at[t, 2])
        x_copies[t] = direct(lambda c: y_sum.at[t, c], x, x_land.at[t], all_x)

    ring_a.finish(ring_a.own[2:4])
    y_copies[1] = direct(lambda c: late.at[z, 0, :, order(c)], y, y_land.at[1], y_peers)
    tall.finish(tall.own[2:4])
    tall_z = direct(lambda c: late.at[c, 3, :, order(y)], z, tz_land, all_z)
    start_x(0, second.at[:, order(y)])
    ring_b.finish(ring_b.own[2:4])
    y_copies[2] = direct(lambda c: late.at[z, 1, :, order(c)], y, y_land.at[2], y_peers)
    side.finish(side.own[2:4])
    side_z = direct(lambda c: late.at[c, 2, x], z, v_land, all_z)
    start_x(1, late.at[z, 0, :, order(y)])
    landed(tall_z)
    add_into(t_sum, (4,), late.at[z, 3, :, order(y)], tz_land.at[0], tz_land.at[1], tz_land.at[2])
    tall_x = direct(lambda c: t_sum.at[c], x, tx_land, all_x)
    start_x(2, late.at[z, 1, :, order(y)])
    landed(side_z)
    add_into(v_sum, (4,), late.at[z, 2, x], v_land.at[0], v_land.at[1], v_land.at[2])
    side_y = direct(lambda c: v_sum.at[order(c)], y, w_land, y_peers)
    downs.finish([d_work.at[2], d_work.at[3]])
    swap_down = last.remote(d_work.at[2 + 1 - y_low], d_other, pair_peer)
    swap_up.wait_recv()
    add_into(up_out, (), up_sum.at[y_low], up_other, rows=(16, 10))

    def summed(panel, first_part, land, *index):
        value = first_part.astype(F32)
        for d in range(3):
            value = value + land[(d,) + index].astype(F32)
        sums[panel, 0:80] = value
        sums[panel, 80:96] = jnp.zeros((16, 128), F32)

    landed(gain_y)
    both_gains = gx_sum[order(y)] + gy_land[0] + gy_land[1] + gy_land[2]
    landed(x_copies[3])
    for panel in range(3):
        summed(panel, first_sum[panel, x], f_land, panel)
    for t in range(3):
        landed(x_copies[t])
        summed(3 + t, y_sum[t, x], x_land.at[t])
    landed(tall_x)
    summed(7, t_sum[x], tx_land)
    landed(side_y)
    summed(6, v_sum[order(y)], w_land)
    for j in range(8):
        for panel in range(8):
            stage[j, panel] = sums[panel, 10 * j : 10 * j + 16]
        stage[j, 0, 10:11] = both_gains[j : j + 1]
    finals = [
        last.remote(stage.at[(spot + d) % 8], final_land.at[d], spot_peers[d - 1]) for d in range(1, 8)
    ]
    swap_down.wait_recv()
    add_into(down_out, (), d_work.at[2 + y_low], d_other, rows=(16, 7))
    dense_out[spot] = stage[spot]
    for d, copy in enumerate(finals):
        copy.wait_recv()
        dense_out[(spot + 7 - d) % 8] = final_land[d + 1]
    owners.sent()
    copies.drain()
    last.drain()


def attend_back(
    d_mixed, heads, length, cos, sin, parts, up, up_one, gate, first, d_attn, normed_one, mixed, tokens, gain, d_hidden,
    ffn_term, w_query, w_key, w_value, down, collective_id,
):
    rows, width = tokens.shape
    hidden = up.shape[1]
    ring_land = pltpu.VMEM((6, 2, 4, 80, 128), BF16)
    return pl.pallas_call(
        attend_back_kernel,
        name="attend_back",
        out_shape=(
            jax.ShapeDtypeStruct((rows, width), F32),
            jax.ShapeDtypeStruct((rows, width), F32),
            jax.ShapeDtypeStruct((160, hidden), F32),
            jax.ShapeDtypeStruct((2, 160, hidden), F32),
            jax.ShapeDtypeStruct((8, 8, 16, 128), F32),
            jax.ShapeDtypeStruct((160, hidden), F32),
            jax.ShapeDtypeStruct((112, width), F32),
        ),
        in_specs=[ANYWHERE, ANYWHERE, SMEM, VMEM, VMEM, ANYWHERE, ANYWHERE, VMEM, VMEM, VMEM]
        + [VMEM] * 7
        + [ANYWHERE] * 4,
        out_specs=(VMEM,) * 7,
        scratch_shapes=[
            pltpu.VMEM((2, 8, 128, HEAD_DIM), BF16),
            pltpu.VMEM((2, 3, 8, 128, HEAD_DIM), BF16),
            pltpu.VMEM((1024, HEAD_DIM), F32),
            pltpu.VMEM((1024, HEAD_DIM), F32),
            pltpu.VMEM((2, 3, 8, 128, HEAD_DIM), BF16),
            pltpu.VMEM((3, 10, 128, HEAD_DIM), BF16),
        ]
        + SCATTER_SCRATCH
        + [
            pltpu.VMEM((6, 160, hidden), BF16),
            pltpu.VMEM((4, 160, hidden), BF16),
            pltpu.VMEM((6, 80, hidden), BF16),
            pltpu.VMEM((2, 160, hidden), BF16),
            pltpu.VMEM((3, 3, 4, 80, 128), BF16),
            pltpu.VMEM((3, rows, width), BF16),
            pltpu.VMEM((rows, 3 * width), BF16),
            pltpu.VMEM((rows, 3 * width), BF16),
            pltpu.VMEM((2 * rows, 1920), BF16),
            pltpu.VMEM((2 * rows, 640), BF16),
            pltpu.VMEM((4, 4, 4, 80, 128), BF16),
            ring_land,
            pltpu.VMEM((2, 3, 256, width), BF16),
            pltpu.VMEM((rows, width), F32),
            pltpu.VMEM((4, 4, 4, 4, 80, 128), BF16),
            pltpu.VMEM((2, 160, hidden), BF16),
            pltpu.VMEM((3, 4, 80, 128), BF16),
            pltpu.VMEM((4, 4, 80, 128), BF16),
            pltpu.VMEM((2, 6, 2, 4, 80, 128), BF16),
            pltpu.VMEM((3, 3, 80, 128), BF16),
            pltpu.VMEM((3, 3, 4, 80, 128), BF16),
            pltpu.VMEM((3, 4, 80, 128), BF16),
            pltpu.VMEM((3, 3, 80, 128), BF16),
            ring_land,
            pltpu.VMEM((3, 4, 80, 128), BF16),
            pltpu.VMEM((4, 80, 128), BF16),
            pltpu.VMEM((3, 80, 128), BF16),
            ring_land,
            pltpu.VMEM((3, 4, 80, 128), BF16),
            pltpu.VMEM((4, 80, 128), BF16),
            pltpu.VMEM((3, 80, 128), BF16),
            pltpu.VMEM((4, 4, 8, 128), F32),
            pltpu.VMEM((3, 4, 8, 128), F32),
            pltpu.VMEM((4, 8, 128), F32),
            pltpu.VMEM((3, 8, 128), F32),
            pltpu.VMEM((8, 96, 128), F32),
            pltpu.VMEM((8, 8, 16, 128), F32),
            pltpu.VMEM((8, 8, 16, 128), F32),
            pltpu.VMEM((160, hidden), BF16),
            pltpu.VMEM((6, 112, width), BF16),
            pltpu.VMEM((4, 112, width), BF16),
            pltpu.VMEM((112, width), BF16),
        ]
        + exchange_semaphores()
        + exchange_semaphores()
        + [
            pltpu.SemaphoreType.DMA((SCATTER_REMOTES + 26,)),
            pltpu.SemaphoreType.DMA((SCATTER_REMOTES + 26,)),
            pltpu.SemaphoreType.DMA((SCATTER_LOCALS + 4,)),
            pltpu.SemaphoreType.DMA((GRAD_REMOTES,)),
            pltpu.SemaphoreType.DMA((GRAD_REMOTES,)),
            pltpu.SemaphoreType.DMA((4,)),
            pltpu.SemaphoreType.DMA,
            pltpu.SemaphoreType.DMA((2, 3)),
        ],
        compiler_params=params(collective_id),
        cost_estimate=cost(10**9, 10**8),
    )(
        d_mixed, heads, length, cos, sin, parts, up, up_one, gate, first, d_attn, normed_one, mixed,
        tokens, gain, d_hidden, ffn_term, w_query, w_key, w_value, down,
    )


def gated(gate, up):
    squash = 1.0 / (1.0 + jnp.exp(-gate))
    silu = gate * squash
    slope = squash * (1.0 + gate * (1.0 - squash))
    return silu, slope


SLOTS = 48
DEPTH = 4
SLOT_ROWS = 16 * SLOTS


def slot_lines(meta):
    member = jnp.where(meta[...].reshape(32, 128) > 0, 1.0, 0.0)
    before = lax.broadcasted_iota(jnp.int32, (128, 128), 0) < lax.broadcasted_iota(jnp.int32, (128, 128), 1)
    count = dot(member.astype(BF16), jnp.where(before, 1.0, 0.0).astype(BF16))
    return jnp.where(member > 0, count, -1.0)


def experts_kernel(
    meta, weight, rows, cots, gate_w, up_w, down_w, early, out, d_rows, kept_act, kept_back, down_sum, first_sum,
    gate_up, down, slot_rows, slot_cots, slot_out, slot_back, lines, columns, act, back,
    out_buf, term, land, z_land, z_work, in_sem, out_sem, weight_sem, keep_sem, send, recv, own,
):
    hidden = down.shape[1]
    x, y, z, core = place()
    x_peers = [device((x + 1) % 4, y, z, core), device((x + 3) % 4, y, z, core)]

    def load(expert):
        return [
            pltpu.make_async_copy(gate_w.at[expert], gate_up.at[expert, :, 0:hidden], weight_sem.at[expert, 0]),
            pltpu.make_async_copy(up_w.at[expert], gate_up.at[expert, :, hidden : 2 * hidden], weight_sem.at[expert, 1]),
            pltpu.make_async_copy(down_w.at[expert], down.at[expert], weight_sem.at[expert, 2]),
        ]

    def fetch(expert):
        return [
            pltpu.make_async_copy(rows.at[expert], slot_rows.at[expert], in_sem.at[expert, 0]),
            pltpu.make_async_copy(cots.at[expert], slot_cots.at[expert], in_sem.at[expert, 1]),
        ]

    for copy in fetch(0) + load(0):
        copy.start()
    z_peers = [device(x, y, (z + 1) % 4, core), device(x, y, (z + 3) % 4, core)]
    greet(x_peers + z_peers)
    copies = Copies(send, recv, own)

    def panel_add(out, *terms):
        add_into(out, (), *terms, rows=(80, 8))

    dense = [
        RingSum(
            copies, z, z_peers[0], z_peers[1],
            lambda chunk, half, panel=panel: early.at[
                2 * chunk + panel if panel < 2 else 8 + chunk, 640 * half : 640 * half + 640
            ],
            z_land.at[panel], z_work.at[panel], panel_add,
        )
        for panel in range(3)
    ]
    for panel in dense:
        panel.raw()
    lines[...] = slot_lines(meta).reshape(16, 2, 128)
    columns[...] = jnp.concatenate([lines[...].reshape(32, 128), jnp.zeros((96, 128), F32)], axis=0).T
    def keep(expert):
        return [
            pltpu.make_async_copy(act.at[expert], kept_act.at[expert], keep_sem.at[expert, 0]),
            pltpu.make_async_copy(back.at[expert], kept_back.at[expert], keep_sem.at[expert, 1]),
        ]

    def main(expert):
        for copy in fetch(expert) + load(expert):
            copy.wait()
        if expert == 0:
            for copy in fetch(1) + load(1):
                copy.start()

        tile = 256

        @pl.loop(0, SLOT_ROWS // tile)
        def _(index):
            at = pl.ds(pl.multiple_of(index * tile, tile), tile)
            both = dot(slot_rows[expert, at], gate_up[expert])
            gate, up = both[:, :hidden], both[:, hidden:]
            silu, slope = gated(gate, up)
            activated = (silu * up).astype(BF16)
            act[expert, at] = activated
            produced = dot(activated, down[expert]).astype(BF16).astype(F32)
            slot_out[expert, at] = (produced * weight[expert, at][:, 0:1]).astype(BF16)
            d_act = dot_nt(slot_cots[expert, at], down[expert])
            back[expert, at, 0:hidden] = (d_act * up * slope).astype(BF16)
            back[expert, at, hidden : 2 * hidden] = (d_act * silu).astype(BF16)
            slot_back[expert, at] = dot_nt(back[expert, at], gate_up[expert]).astype(BF16)

    main(0)
    for copy in keep(0):
        copy.start()

    @pl.loop(0, hidden // 128)
    def _(index):
        at = pl.ds(pl.multiple_of(index * 128, 128), 128)
        term[at] = dot_tn(act[0, :, at], slot_cots[0]).astype(BF16)

    def part(chunk, half):
        return term.at[pl.ds(pl.multiple_of(chunk * 224 + half * 112, 112), 112)]

    def add(out, *terms):
        add_into(out, (), *terms, rows=(16, 7))

    ring = RingSum(copies, x, x_peers[0], x_peers[1], part, land, None, add, resident=True)
    ring.raw()
    for panel in dense:
        panel.forward()
    main(1)
    ring.forward()
    for copy in keep(1):
        copy.start()

    def store(block):
        slot = block % DEPTH
        return [
            pltpu.make_async_copy(out_buf.at[slot, 0], out.at[block], out_sem.at[slot, 0]),
            pltpu.make_async_copy(out_buf.at[slot, 1], d_rows.at[block], out_sem.at[slot, 1]),
        ]

    lane = lax.broadcasted_iota(jnp.int32, (128, 2 * SLOTS), 1).astype(F32)
    for block in range(16):
        slot = block % DEPTH
        first, second = columns[:, 2 * block : 2 * block + 1], columns[:, 2 * block + 1 : 2 * block + 2]
        hit = ((lane < SLOTS) & (lane == first)) | ((lane >= SLOTS) & (lane - SLOTS == second))
        both = jnp.where(hit, 1.0, 0.0).astype(BF16)
        if block >= DEPTH:
            for copy in store(block - DEPTH):
                copy.wait()
        at = slice(block * SLOTS, (block + 1) * SLOTS)
        for index, source in enumerate((slot_out, slot_back)):
            value = jnp.concatenate([source[0, at], source[1, at]], axis=0)
            out_buf[slot, index] = dot(both, value).astype(BF16)
        for copy in store(block):
            copy.start()
    for block in range(16 - DEPTH, 16):
        for copy in store(block):
            copy.wait()
    for panel in range(3):
        dense[panel].finish([first_sum.at[panel, 0:640], first_sum.at[panel, 640:1280]])
    ring.finish([down_sum.at[0:112], down_sum.at[112:224]])
    copies.drain()
    for copy in keep(0) + keep(1):
        copy.wait()


def experts(meta, weight, rows, cots, gate_w, up_w, down_w, early, collective_id):
    width, hidden = gate_w.shape[1:]
    return pl.pallas_call(
        experts_kernel,
        name="experts",
        out_shape=(
            jax.ShapeDtypeStruct((16, 128, width), BF16),
            jax.ShapeDtypeStruct((16, 128, width), BF16),
            jax.ShapeDtypeStruct((2, SLOT_ROWS, hidden), BF16),
            jax.ShapeDtypeStruct((2, SLOT_ROWS, 2 * hidden), BF16),
            jax.ShapeDtypeStruct((hidden // 4, width), BF16),
            jax.ShapeDtypeStruct((3, width, 128), BF16),
        ),
        in_specs=[VMEM, VMEM] + [ANYWHERE] * 6,
        out_specs=[ANYWHERE] * 4 + [VMEM, VMEM],
        scratch_shapes=[
            pltpu.VMEM((2, width, 2 * hidden), BF16),
            pltpu.VMEM((2, hidden, width), BF16),
            pltpu.VMEM((2, SLOT_ROWS, width), BF16),
            pltpu.VMEM((2, SLOT_ROWS, width), BF16),
            pltpu.VMEM((2, SLOT_ROWS, width), BF16),
            pltpu.VMEM((2, SLOT_ROWS, width), BF16),
            pltpu.VMEM((16, 2, 128), F32),
            pltpu.VMEM((128, 128), F32),
            pltpu.VMEM((2, SLOT_ROWS, hidden), BF16),
            pltpu.VMEM((2, SLOT_ROWS, 2 * hidden), BF16),
            pltpu.VMEM((DEPTH, 2, 128, width), BF16),
            pltpu.VMEM((hidden, width), BF16),
            pltpu.VMEM((6, hidden // 8, width), BF16),
            pltpu.VMEM((3, 6, width // 2, 128), BF16),
            pltpu.VMEM((3, 4, width // 2, 128), BF16),
            pltpu.SemaphoreType.DMA((2, 2)),
            pltpu.SemaphoreType.DMA((DEPTH, 2)),
            pltpu.SemaphoreType.DMA((2, 3)),
            pltpu.SemaphoreType.DMA((2, 2)),
            pltpu.SemaphoreType.DMA((24,)),
            pltpu.SemaphoreType.DMA((24,)),
            pltpu.SemaphoreType.DMA((12,)),
        ],
        compiler_params=params(collective_id),
        cost_estimate=cost(12 * 2 * SLOT_ROWS * width * hidden, 6 * 10**7),
    )(meta, weight, rows, cots, gate_w, up_w, down_w, early)


def finish_kernel(
    packed, hidden, shared_out, routed, gate, up_zero, up_one, down_zero, down_one, grad,
    block_out, input_grad, attn_gain, query, key, value, out, ffn_gain, s_gate, s_up, s_down, gate_grad, up_grad, down_grad,
):
    input_grad[...] = grad[...]
    gate_grad[...] = gate[...]
    up_grad[0] = up_zero[...]
    up_grad[1] = up_one[...]
    down_grad[0] = down_zero[...]
    down_grad[1] = down_one[...]
    block_out[...] = hidden[...] + shared_out[...] + routed[...]
    gains = packed[0, 0, 10:11]
    for source in range(1, 8):
        gains = gains + packed[source, 0, 10:11]
    attn_gain[...] = gains[:, 0:10]
    ffn_gain[...] = gains[:, 10:20]
    for core in range(2):
        for panel in range(20):
            if panel < 15:
                part = packed[2 * (panel // 4) + core, 4 + panel % 4, 0:10]
                at = core * 1920 + panel * 128
                (query, key, value)[at // 1280][:, at % 1280 : at % 1280 + 128] = part
            else:
                part = packed[2 * (panel - 15) + core, 3, 0:10] if panel < 19 else packed[6 + core, 7, 0:10]
                at = core * 640 + (panel - 15) * 128
                out[:, at : at + 128] = part
        for panel in range(12):
            where = (panel // 2, panel % 2) if panel < 8 else (panel - 8, 2)
            part = packed[2 * where[0] + core, where[1], 0:10]
            if panel < 7:
                (s_gate, s_up)[core][:, panel * 128 : panel * 128 + 128] = part
            else:
                at = core * 640 + (panel - 7) * 128
                s_down[:, at : at + 128] = part[0:7]


def finish(packed, *values):
    def shape(*dims):
        return jax.ShapeDtypeStruct(dims, F32)

    return pl.pallas_call(
        finish_kernel,
        name="finish",
        out_shape=(
            shape(128, 1280), shape(128, 1280), shape(1, 10),
            shape(10, 1280), shape(10, 1280), shape(10, 1280), shape(10, 1280), shape(1, 10),
            shape(10, 896), shape(10, 896), shape(7, 1280),
            shape(2, 160, 896), shape(2, 160, 896), shape(2, 112, 1280),
        ),
        in_specs=[VMEM] * 10,
        out_specs=(VMEM,) * 14,
        compiler_params=params(),
        cost_estimate=cost(10**7, 12 * 10**6),
    )(packed, *values)


def local(
    tokens,
    lengths,
    routes,
    route_gates,
    attn_gain,
    w_query,
    w_key,
    w_value,
    w_out,
    ffn_gain,
    shared_gate,
    shared_up,
    shared_down,
    expert_gate,
    expert_up,
    expert_down,
    cotangent,
):
    resident, cot = tokens[0], cotangent[0]
    rows = resident.shape[0]
    all_cos, all_sin = turn_tables(8 * rows)
    back_sin = jnp.asarray(-all_sin)
    all_cos, all_sin = jnp.asarray(all_cos), jnp.asarray(all_sin)
    normed_one, mixed, heads, cots, hidden, normed_two = attend(
        lengths, cot, routes[0].T, route_gates[0].T, w_query, w_key, w_value, w_out, resident, attn_gain, ffn_gain, all_cos, all_sin, 1
    )
    slot_rows, slot_cots, meta, weight, shared_out, d_shared, early = gather_rows(
        normed_two, cot, cots, shared_gate, shared_up, shared_down, 2
    )
    parts, d_parts, kept_act, kept_back, down_one, first = experts(
        meta, weight, slot_rows, slot_cots, expert_gate, expert_up, expert_down, early, 5
    )
    first = first.reshape(3, 4, 4, 80, 128)
    gate_sum, up_term, up_one, down_term, down_zero, d_mixed, d_hidden, d_attn, ffn_term = scatter_rows(
        d_parts, slot_rows, slot_cots, kept_act, kept_back, d_shared, hidden, ffn_gain, cot, w_out, down_one, 3
    )
    grad, routed, up_last, gate_grad, packed, up_first, down_last = attend_back(
        d_mixed, heads, lengths, all_cos, back_sin, parts, up_term, up_one, gate_sum, first, d_attn, normed_one,
        mixed, resident, attn_gain, d_hidden, ffn_term, w_query, w_key, w_value, down_term, 4,
    )
    outs = finish(
        packed, hidden, shared_out, routed, gate_grad, up_first, up_last, down_zero, down_last, grad
    )
    return (outs[0][None], outs[1][None], outs[2][0], *outs[3:7], outs[7][0], *outs[8:])


def solution(mesh):
    in_specs = (
        P("exp", "ctx", None),
        P("exp"),
        P("exp", "ctx", None),
        P("exp", "ctx", None),
        P(),
        P(),
        P(),
        P(),
        P(),
        P(),
        P(),
        P(),
        P(),
        P("exp", None, None),
        P("exp", None, None),
        P("exp", None, None),
        P("exp", "ctx", None),
    )
    out_specs = (
        P("exp", "ctx", None),
        P("exp", "ctx", None),
        P(("ctx", "exp")),
        P(("ctx", "exp"), None),
        P(("ctx", "exp"), None),
        P(("ctx", "exp"), None),
        P(("ctx", "exp"), None),
        P(("ctx", "exp")),
        P(("ctx", "exp"), None),
        P(("ctx", "exp"), None),
        P(("ctx", "exp"), None),
        P("exp", "ctx", None),
        P("exp", "ctx", None),
        P("exp", "ctx", None),
    )
    return jax.shard_map(local, mesh=mesh, in_specs=in_specs, out_specs=out_specs, check_vma=False)
```

```python
import functools
import math

import jax
import jax.numpy as jnp
import numpy as np
from jax import lax
from jax.experimental import pallas as pl
from jax.experimental.pallas import tpu as pltpu
from jax.sharding import PartitionSpec as P

MESH = pl.DeviceIdType.MESH
HEAD_DIM = 128
VMEM_LIMIT = 60 * 2**20
F32, BF16 = jnp.float32, jnp.bfloat16


def place():
    ctx, exp = lax.axis_index("ctx"), lax.axis_index("exp")
    return ctx // 2, (exp // 8) * 2 + ctx % 2, (exp // 2) % 4, exp % 2


def device(x, y, z, core):
    return (x * 2 + y % 2, (y // 2) * 8 + z * 2 + core)


def greet(devices):
    barrier = pltpu.get_barrier_semaphore()
    for target in devices:
        pl.semaphore_signal(barrier, inc=1, device_id=target, device_id_type=MESH)
    pl.semaphore_wait(barrier, len(devices))


class Copies:
    def __init__(self, send, recv, own):
        self.send, self.recv, self.own = send, recv, own
        self.remotes, self.locals = 0, 0
        self.started = []

    def remote(self, src, dst, target):
        index = self.remotes
        self.remotes += 1
        copy = pltpu.make_async_remote_copy(
            src_ref=src,
            dst_ref=dst,
            send_sem=self.send.at[index],
            recv_sem=self.recv.at[index],
            device_id=target,
            device_id_type=MESH,
        )
        copy.start()
        self.started.append(copy)
        return copy

    def local(self, src, dst):
        index = self.locals
        self.locals += 1
        copy = pltpu.make_async_copy(src, dst, self.own.at[index])
        copy.start()
        return copy

    def drain(self):
        for copy in self.started:
            copy.wait_send()


def each(shape, body):
    @pl.loop(0, math.prod(shape))
    def _(step):
        index = []
        for size in reversed(shape):
            index.append(step % size)
            step = step // size
        body(tuple(reversed(index)))


def add_into(out, shape, *terms, rows=None):
    def body(index):
        total = terms[0][index].astype(F32)
        for term in terms[1:]:
            total = total + term[index].astype(F32)
        out[index] = total.astype(out.dtype)

    if rows is None:
        each(shape, body)
    else:
        step, count = rows
        each(shape + (count,), lambda i: body(i[:-1] + (pl.ds(pl.multiple_of(i[-1] * step, step), step),)))


class RingSum:
    def __init__(self, copies, me, right, left, part, land, work, add, resident=None):
        self.copies, self.right, self.left, self.land, self.work, self.add = copies, right, left, land, work, add
        self.part = part
        self.after, self.before, across = (me + 1) % 4, (me + 3) % 4, (me + 2) % 4
        self.one = copies.remote(part(across, 0), land.at[0], right)
        self.two = copies.remote(part(across, 1), land.at[1], left)
        sources = [part(self.after, 0), part(self.before, 1), part(me, 0), part(me, 1)]
        if resident is None:
            self.loads = [copies.local(source, work.at[i]) for i, source in enumerate(sources)]
            self.own = [work.at[i] for i in range(4)]
        else:
            self.loads = []
            self.own = sources

    def raw(self):
        self.three = self.copies.remote(self.part(self.after, 1), self.land.at[2], self.right)
        self.four = self.copies.remote(self.part(self.before, 0), self.land.at[4], self.left)

    def forward(self):
        for load in self.loads:
            load.wait()
        self.one.wait_recv()
        self.add(self.land.at[0], self.land.at[0], self.own[0])
        self.five = self.copies.remote(self.land.at[0], self.land.at[3], self.right)
        self.two.wait_recv()
        self.add(self.land.at[1], self.land.at[1], self.own[1])
        self.six = self.copies.remote(self.land.at[1], self.land.at[5], self.left)

    def finish(self, outs):
        for copy in (self.three, self.four, self.five, self.six):
            copy.wait_recv()
        self.add(outs[0], self.own[2], self.land.at[3], self.land.at[4])
        self.add(outs[1], self.own[3], self.land.at[2], self.land.at[5])


GRAD_REMOTES = 5 * 6 + 2 + 3 * 4 + 3 * 5 + 6 + 3 * 2 + 7


def add_blocks(shape):
    def add(out, *terms):
        add_into(out, shape, *terms)

    return add


def half_rows(which, size):
    return pl.ds(pl.multiple_of(which * size, size), size)


def order(y):
    return (y % 2) * 2 + y // 2


VMEM = pl.BlockSpec(memory_space=pltpu.VMEM)
ANYWHERE = pl.BlockSpec(memory_space=pl.ANY)
SMEM = pl.BlockSpec(memory_space=pltpu.SMEM)
SCALE = HEAD_DIM ** (-0.5)


def params(collective_id=None):
    if collective_id is None:
        return pltpu.CompilerParams(vmem_limit_bytes=VMEM_LIMIT)
    return pltpu.CompilerParams(
        collective_id=collective_id, has_side_effects=True, vmem_limit_bytes=VMEM_LIMIT
    )


def cost(flops, bytes_accessed):
    return pl.CostEstimate(flops=int(flops), bytes_accessed=int(bytes_accessed), transcendentals=0)


def dot(left, right):
    return jnp.dot(left, right, preferred_element_type=F32)


def dot_nt(left, right):
    return lax.dot_general(left, right, (((1,), (1,)), ((), ())), preferred_element_type=F32)


def dot_tn(left, right):
    return lax.dot_general(left, right, (((0,), (0,)), ((), ())), preferred_element_type=F32)


def normed(values, gain):
    return values * lax.rsqrt(jnp.mean(values * values, axis=-1, keepdims=True) + 1e-06) * gain


def normed_back(values, gain, upstream):
    factor = lax.rsqrt(jnp.mean(values * values, axis=-1, keepdims=True) + 1e-06)
    scaled = upstream * gain
    inner = jnp.mean(scaled * values, axis=-1, keepdims=True)
    term = jnp.sum(upstream * values * factor, axis=0, keepdims=True)
    return factor * scaled - values * factor * factor * factor * inner, term


def turned(values, cos, sin):
    return values * cos + pltpu.roll(values, HEAD_DIM // 2, 1) * sin


def turn_tables(count):
    half = HEAD_DIM // 2
    frequency = np.exp(np.arange(half, dtype=np.float32) * np.float32(-2.0 * math.log(10000.0) / HEAD_DIM))
    angle = np.arange(count, dtype=np.float32)[:, None] * frequency[None, :]
    cos, sin = np.cos(angle), np.sin(angle)
    return np.concatenate([cos, cos], axis=1), np.concatenate([-sin, sin], axis=1)


def rank(y_half, z, core):
    return y_half * 8 + z * 2 + core


class Gather:
    def __init__(self, copies, where, src, out, cut, far, far_cut):
        x, y, z, core = where
        self.copies, self.out, self.cut, self.far_rows, self.far_cut = copies, out, cut, far, far_cut
        self.rows = out.shape[1]
        self.split = far < self.rows
        self.y_half, self.z, self.core = y // 2, z, core
        self.pair = device(x, y, z, 1 - core)
        self.across = device(x, (y + 2) % 4, z, core)
        self.right, self.left = device(x, y, (z + 1) % 4, core), device(x, y, (z + 3) % 4, core)
        me = rank(self.y_half, z, core)
        self.mine = copies.local(src, out.at[me])
        self.over = copies.remote(src, out.at[me], self.across)
        self.to_right = copies.remote(src, out.at[me], self.right)
        self.to_left = copies.remote(src, out.at[me], self.left)
        self.pairs = [copies.remote(src, out.at[me], self.pair)]
        self.seen = 0

    def shard(self, other, dz):
        y_half = 1 - self.y_half if other else self.y_half
        return rank(y_half, (self.z + dz + 4) % 4, self.core)

    def send(self, ref, target):
        return self.copies.remote(ref, ref, target)

    def share(self, ref):
        self.pairs.append(self.send(ref, self.pair))

    def near(self):
        self.to_right.wait_recv()
        index = self.shard(False, -1)
        self.on_right = self.send(self.out.at[index, 0 : self.cut], self.right)
        if self.split:
            self.side_before = self.send(self.out.at[index, self.far_rows : self.rows], self.across)
        self.share(self.out.at[index])
        self.to_left.wait_recv()
        index = self.shard(False, 1)
        self.on_left = self.send(self.out.at[index, self.cut : self.rows], self.left)
        if self.split:
            self.side_after = self.send(self.out.at[index, self.far_rows : self.rows], self.across)
        self.share(self.out.at[index])

    def far(self):
        self.over.wait_recv()
        index = self.shard(True, 0)
        self.far_right = self.send(self.out.at[index, 0 : self.far_rows], self.right)
        self.far_left = self.send(self.out.at[index, 0 : self.far_rows], self.left)
        self.share(self.out.at[index])

    def middle(self):
        index = self.shard(False, 2)
        self.on_right.wait_recv()
        self.share(self.out.at[index, 0 : self.cut])
        self.on_left.wait_recv()
        if self.split:
            self.side_middle = self.send(self.out.at[index, self.far_rows : self.rows], self.across)
        self.share(self.out.at[index, self.cut : self.rows])

    def third(self):
        self.far_right.wait_recv()
        index = self.shard(True, -1)
        self.far_on_right = self.send(self.out.at[index, 0 : self.far_cut], self.right)
        self.share(self.out.at[index, 0 : self.far_rows])
        self.far_left.wait_recv()
        index = self.shard(True, 1)
        self.far_on_left = self.send(self.out.at[index, self.far_cut : self.far_rows], self.left)
        self.share(self.out.at[index, 0 : self.far_rows])

    def sides(self):
        for copy, dz in ((self.side_before, -1), (self.side_after, 1)):
            copy.wait_recv()
            self.share(self.out.at[self.shard(True, dz), self.far_rows : self.rows])

    def pairs_arrived(self, count):
        for copy in self.pairs[self.seen : count]:
            copy.wait_recv()
        self.seen = count

    def last(self):
        index = self.shard(True, 2)
        self.far_on_right.wait_recv()
        self.share(self.out.at[index, 0 : self.far_cut])
        self.far_on_left.wait_recv()
        self.share(self.out.at[index, self.far_cut : self.far_rows])
        if self.split:
            self.side_middle.wait_recv()
            self.share(self.out.at[index, self.far_rows : self.rows])
        self.pairs_arrived(len(self.pairs))


GATHER_REMOTES = 3 + 2 + 2 + 2 + 8 + 2


def exp_peers(where):
    x, y, z, core = where
    return [
        device(x, y, z, 1 - core),
        device(x, (y + 2) % 4, z, core),
        device(x, y, (z + 1) % 4, core),
        device(x, y, (z + 3) % 4, core),
    ]


class Scatter:
    def __init__(self, copies, where, parts, pair_land, work, ring_land, far_land, y_land):
        x, y, z, core = where
        self.copies, self.work, self.pair_land = copies, work, pair_land
        self.ring_land, self.far_land, self.y_land = ring_land, far_land, y_land
        self.across = device(x, (y + 2) % 4, z, core)
        self.right, self.left = device(x, y, (z + 1) % 4, core), device(x, y, (z + 3) % 4, core)
        pair = device(x, y, z, 1 - core)
        self.pairs, self.loads = {}, {}
        for slot in ((0, 2), (1, 2), (0, 1), (0, 3), (1, 1), (1, 3), (0, 0), (1, 0)):
            y_half = 1 - y // 2 if slot[0] == 0 else y // 2
            at = (z + slot[1]) % 4
            self.pairs[slot] = copies.remote(parts.at[rank(y_half, at, 1 - core)], pair_land.at[slot], pair)
            self.loads[slot] = copies.local(parts.at[rank(y_half, at, core)], work.at[slot])

    def merge(self, slot):
        self.loads[slot].wait()
        self.pairs[slot].wait_recv()
        rows_add(self.work.at[slot], 0, 128, self.work.at[slot], self.pair_land.at[slot])

    def first(self):
        self.ring = {}
        for far in range(2):
            self.merge((far, 2))
            self.ring[far] = (
                self.copies.remote(self.work.at[far, 2, 0:64], self.ring_land.at[far, 0], self.right),
                self.copies.remote(self.work.at[far, 2, 64:128], self.ring_land.at[far, 1], self.left),
            )

    def merge_rest(self):
        for far in range(2):
            self.merge((far, 1))
            self.merge((far, 3))
            self.merge((far, 0))

    def second(self):
        self.final = {}
        for far in range(2):
            self.ring[far][0].wait_recv()
            rows_add(self.work.at[far, 1, 0:64], 0, 64, self.work.at[far, 1, 0:64], self.ring_land.at[far, 0])
            to_right = self.copies.remote(self.work.at[far, 1], self.far_land.at[far, 0], self.right)
            self.ring[far][1].wait_recv()
            rows_add(self.work.at[far, 3, 64:128], 0, 64, self.work.at[far, 3, 64:128], self.ring_land.at[far, 1])
            to_left = self.copies.remote(self.work.at[far, 3], self.far_land.at[far, 1], self.left)
            self.final[far] = (to_right, to_left)

    def third(self):
        for far in range(2):
            for copy in self.final[far]:
                copy.wait_recv()
            rows_add(self.work.at[far, 0], 0, 128, self.work.at[far, 0], self.far_land.at[far, 0], self.far_land.at[far, 1])
            if far == 0:
                self.over = self.copies.remote(self.work.at[0, 0], self.y_land, self.across)

    def last(self, out):
        self.over.wait_recv()
        rows_add(out, 0, 128, self.work.at[1, 0], self.y_land)


def rows_add(out, first, rows, *terms):
    @pl.loop(0, rows // 16)
    def _(step):
        at = pl.ds(pl.multiple_of(step * 16, 16), 16)
        value = terms[0][at].astype(F32)
        for term in terms[1:]:
            value = value + term[at].astype(F32)
        out[at] = value.astype(out.dtype)


SCATTER_REMOTES, SCATTER_LOCALS = 8 + 4 + 4 + 1, 8
SCATTER_SCRATCH = [
    pltpu.VMEM((2, 4, 128, 1280), BF16),
    pltpu.VMEM((2, 4, 128, 1280), BF16),
    pltpu.VMEM((2, 2, 64, 1280), BF16),
    pltpu.VMEM((2, 2, 128, 1280), BF16),
    pltpu.VMEM((128, 1280), BF16),
]


def up_add(out, *terms):
    add_into(out, (), *terms, rows=(16, 10))


def scatter_kernel(
    parts, rows_in, cots_in, act_in, back_in, d_shared, hidden_rows, gain, cot, w_out_in, down_one,
    gate_sum, up_out, up_one, down_out, down_final, d_mixed, d_hidden, d_attn, gain_term,
    a, b, c, d, e, rows, cots, act, back, gate, up, down, land, w_out, d_routed, up_land, one_other,
    send, recv, own, load_sem, keep_sem,
):
    where = place()
    x, y, z, core = where
    x_peers = [device((x + 1) % 4, y, z, core), device((x + 3) % 4, y, z, core)]
    loads = [
        pltpu.make_async_copy(src, dst, load_sem.at[i])
        for i, (src, dst) in enumerate(
            (
                (rows_in.at[0], rows.at[0]), (back_in.at[0], back.at[0]), (rows_in.at[1], rows.at[1]),
                (back_in.at[1], back.at[1]), (act_in.at[1], act), (cots_in.at[1], cots), (w_out_in, w_out),
            )
        )
    ]
    for load in loads:
        load.start()
    greet(exp_peers(where) + x_peers + [device(x, (y // 2) * 2 + 1 - y % 2, z, core)])
    copies = Copies(send, recv, own)
    scatter = Scatter(copies, where, parts, a, b, c, d, e)
    hidden = act.shape[1]
    loads[0].wait()
    loads[1].wait()

    y_low = y % 2
    pair = device(x, (y // 2) * 2 + 1 - y_low, z, core)

    def term(dst, lanes, first, last):
        @pl.loop(first, last)
        def _(index):
            expert = index // 5
            at = pl.ds(pl.multiple_of((index % 5) * 256, 256), 256)
            dst[expert, at] = dot_tn(rows[expert, :, at], back[expert, :, lanes]).astype(BF16)

    def up_rows(chunk, which):
        return pl.ds(pl.multiple_of(chunk * 320 + which * 160, 160), 160)

    swap_one = copies.remote(down_one.at[half_rows(1 - y_low, 112)], one_other, pair)

    def gate_ring(expert):
        return RingSum(
            copies, x, x_peers[0], x_peers[1], lambda chunk, half: gate.at[expert, half_rows(2 * chunk + half, 160)],
            land.at[expert], None, up_add, resident=True,
        )

    term(gate, slice(0, hidden), 0, 5)
    rings = [gate_ring(0)]
    rings[0].raw()
    scatter.first()
    scatter.merge_rest()
    loads[2].wait()
    loads[3].wait()
    term(up, slice(hidden, 2 * hidden), 5, 10)
    over = [copies.remote(up.at[1, up_rows(chunk, 1 - y_low)], up_land.at[chunk], pair) for chunk in range(4)]
    term(gate, slice(0, hidden), 5, 10)
    rings.append(gate_ring(1))
    rings[1].raw()
    scatter.second()
    rings[0].forward()
    term(up, slice(hidden, 2 * hidden), 0, 5)
    keep_up = pltpu.make_async_copy(up.at[0], up_out, keep_sem.at[0])
    keep_up.start()
    loads[4].wait()
    loads[5].wait()

    @pl.loop(0, hidden // 128)
    def _(index):
        at = pl.ds(pl.multiple_of(index * 128, 128), 128)
        down[at] = dot_tn(act[:, at], cots[...]).astype(BF16)

    keep_down = pltpu.make_async_copy(down, down_out, keep_sem.at[1])
    keep_down.start()
    rings[1].forward()
    scatter.third()
    scatter.last(d_routed)
    grad, term_sum = normed_back(hidden_rows[...], gain[...].reshape(1, -1), d_shared[...] + d_routed[...])
    whole = cot[...].astype(F32) + grad
    d_hidden[...] = whole
    d_attn[...] = whole.astype(BF16)
    gain_term[...] = term_sum
    loads[6].wait()

    @pl.loop(0, 5)
    def _(index):
        value = dot_nt(d_attn[...], w_out[pl.ds(pl.multiple_of(index * 256, 256), 256)]).astype(BF16)
        d_mixed[2 * index] = value[:, :HEAD_DIM]
        d_mixed[2 * index + 1] = value[:, HEAD_DIM:]

    for chunk, copy in enumerate(over):
        copy.wait_recv()
        add_into(up_one.at[chunk], (), up.at[1, up_rows(chunk, y_low)], up_land.at[chunk], rows=(16, 10))
    for expert in range(2):
        rings[expert].finish([gate_sum.at[expert, 0:160], gate_sum.at[expert, 160:320]])
    swap_one.wait_recv()
    add_into(down_final, (), down_one.at[half_rows(y_low, 112)], one_other, rows=(16, 7))
    copies.drain()
    keep_up.wait()
    keep_down.wait()


def scatter_rows(parts, kept_rows, kept_cots, kept_act, kept_back, d_shared, hidden_rows, gain, cot, w_out, down_one, collective_id):
    width, hidden = kept_rows.shape[2], kept_act.shape[2]
    count = cot.shape[0]
    return pl.pallas_call(
        scatter_kernel,
        name="scatter_rows",
        out_shape=(
            jax.ShapeDtypeStruct((2, 320, hidden), BF16),
            jax.ShapeDtypeStruct((width, hidden), BF16),
            jax.ShapeDtypeStruct((4, 160, hidden), BF16),
            jax.ShapeDtypeStruct((hidden, width), BF16),
            jax.ShapeDtypeStruct((112, width), F32),
            jax.ShapeDtypeStruct((10, count, HEAD_DIM), BF16),
            jax.ShapeDtypeStruct((count, width), F32),
            jax.ShapeDtypeStruct((count, width), BF16),
            jax.ShapeDtypeStruct((1, width), F32),
        ),
        in_specs=[ANYWHERE] * 5 + [VMEM] * 4 + [ANYWHERE, VMEM],
        out_specs=(VMEM, ANYWHERE, VMEM, ANYWHERE) + (VMEM,) * 5,
        scratch_shapes=SCATTER_SCRATCH
        + [
            pltpu.VMEM(kept_rows.shape, BF16),
            pltpu.VMEM(kept_cots.shape[1:], BF16),
            pltpu.VMEM(kept_act.shape[1:], BF16),
            pltpu.VMEM(kept_back.shape, BF16),
            pltpu.VMEM((2, width, hidden), BF16),
            pltpu.VMEM((2, width, hidden), BF16),
            pltpu.VMEM((hidden, width), BF16),
            pltpu.VMEM((2, 6, 160, hidden), BF16),
            pltpu.VMEM(w_out.shape, BF16),
            pltpu.VMEM((count, width), F32),
            pltpu.VMEM((4, 160, hidden), BF16),
            pltpu.VMEM((112, width), BF16),
            pltpu.SemaphoreType.DMA((SCATTER_REMOTES + 17,)),
            pltpu.SemaphoreType.DMA((SCATTER_REMOTES + 17,)),
            pltpu.SemaphoreType.DMA((SCATTER_LOCALS,)),
            pltpu.SemaphoreType.DMA((7,)),
            pltpu.SemaphoreType.DMA((2,)),
        ],
        compiler_params=params(collective_id),
        cost_estimate=cost(10**10, 10**8),
    )(
        parts, kept_rows, kept_cots, kept_act, kept_back,
        d_shared, hidden_rows, gain, cot, w_out, down_one,
    )


def ctx_device(ctx):
    return (ctx, lax.axis_index("exp"))


def extra_owner(head):
    core = lax.axis_index("exp") % 2
    return 3 * core if head == 8 else 5 + core


def owns_extra(ctx):
    return (ctx == extra_owner(8)) | (ctx == extra_owner(9))


def extra_head(ctx):
    return 8 + (ctx == extra_owner(9)).astype(jnp.int32)


class Exchange:
    def __init__(self, send, recv, own):
        self.send, self.recv, self.own = send, recv, own
        self.ctx = lax.axis_index("ctx")

    def copy(self, src, dst, slot, d):
        return pltpu.make_async_remote_copy(
            src_ref=src,
            dst_ref=dst,
            send_sem=self.send.at[slot, d],
            recv_sem=self.recv.at[slot, d],
            device_id=ctx_device((self.ctx + d) % 8),
            device_id_type=MESH,
        )


class ToOwners:
    def __init__(self, exchange, block, land):
        self.exchange, self.block, self.land, self.ctx = exchange, block, land, exchange.ctx

    def mine(self, slot, head):
        return pltpu.make_async_copy(self.block(head), self.land(slot, self.ctx), self.exchange.own.at[slot])

    def start(self, head):
        slot, owner = (0, head) if head < 8 else (1, extra_owner(head))
        d = (owner + 8 - self.ctx) % 8

        @pl.when(d == 0)
        def _():
            self.mine(slot, head).start()

        @pl.when(d != 0)
        def _():
            self.exchange.copy(self.block(head), self.land(slot, self.ctx), slot, d).start()

    def any(self, slot, d):
        return self.exchange.copy(self.block(0), self.land(slot, self.ctx), slot, d)

    def arrived(self):
        self.mine(0, 0).wait()
        for d in range(1, 8):
            self.any(0, d).wait_recv()

        @pl.when(owns_extra(self.ctx))
        def _():
            self.mine(1, 0).wait()
            for d in range(1, 8):
                self.any(1, d).wait_recv()

    def sent(self):
        for d in range(1, 8):
            self.any(0, d).wait_send()

            @pl.when(owns_extra((self.ctx + d) % 8))
            def _():
                self.any(1, d).wait_send()


class Home:
    def __init__(self, exchange, block, land):
        self.exchange, self.block, self.land = exchange, block, land
        self.ctx = exchange.ctx

    def head(self, slot):
        return self.ctx if slot == 0 else extra_head(self.ctx)

    def start(self, slot):
        for d in range(1, 8):
            self.exchange.copy(self.block(slot, (self.ctx + d) % 8), self.land(self.head(slot)), slot, d).start()
        self.mine(slot).start()

    def mine(self, slot):
        return pltpu.make_async_copy(
            self.block(slot, self.ctx), self.land(self.head(slot)), self.exchange.own.at[slot]
        )

    def finish(self):
        self.mine(0).wait()
        for d in range(1, 8):
            copy = self.exchange.copy(self.block(0, 0), self.land(0), 0, d)
            copy.wait_send()
            copy.wait_recv()

            @pl.when(owns_extra((self.ctx + 8 - d) % 8))
            def _():
                self.exchange.copy(self.block(1, 0), self.land(0), 1, d).wait_recv()

        @pl.when(owns_extra(self.ctx))
        def _():
            self.mine(1).wait()
            for d in range(1, 8):
                self.exchange.copy(self.block(1, 0), self.land(0), 1, d).wait_send()


def attend_kernel(
    length, cot, routes, route_gates, w_query, w_key, w_value, w_out_in, tokens, attn_gain, ffn_gain, cos, sin,
    gate_w, up_w, down_w, spread,
    normed_one, mixed, heads, hidden, slot_rows, slot_cots, meta, weight, shared_out, d_shared, early,
    sent_cot, qkv, weights, land, result, home, w_out, rows, every, cots_in, gate, up, down, spread_in,
    filled_rows, filled_cots, lines, act, d_gates, pair_act, pair_gates, right, act_left, panels,
    s1, r1, o1, s2, r2, o2, s3, r3, o3, s4, r4, o4, load_sem, weight_sem, shared_sem, keep_sem, early_sem,
):
    def fetch(index):
        return [
            pltpu.make_async_copy(source.at[:, 256 * index : 256 * index + 256], weights.at[index, kind], weight_sem.at[index, kind])
            for kind, source in enumerate((w_query, w_key, w_value))
        ]

    pairs_of_heads = (4, 0, 1, 2, 3)
    for index in pairs_of_heads:
        for copy in fetch(index):
            copy.start()
    load = pltpu.make_async_copy(w_out_in, w_out, load_sem)
    load.start()
    loads = [
        pltpu.make_async_copy(src, dst, shared_sem.at[i])
        for i, (src, dst) in enumerate(((gate_w, gate), (up_w, up), (down_w, down), (spread, spread_in)))
    ]
    for copy in loads:
        copy.start()
    where = place()
    ctx = lax.axis_index("ctx")
    greet([ctx_device((ctx + d) % 8) for d in range(1, 8)] + exp_peers(where))
    copies = Copies(s3, r3, o3)
    expert = lax.broadcasted_iota(jnp.int32, (32, 128), 0)
    table = jnp.zeros((32, 128), F32)
    for choice in range(routes.shape[0]):
        table += jnp.where(expert == routes[choice], route_gates[choice], 0.0)
    position = lax.broadcasted_iota(jnp.int32, (32, 128), 1) + ctx * 128
    table = jnp.where(position < length[0], table, 0.0)
    high = table.astype(BF16)
    low = (table - high.astype(F32)).astype(BF16)
    sent_cot[0:128] = cot[...]
    sent_cot[128:144] = jnp.zeros((16, cot.shape[1]), BF16)
    for index, part in enumerate((high[0:16], high[16:32], low[0:16], low[16:32])):
        sent_cot[128:144, index * 128 : index * 128 + 128] = part
    first = Gather(copies, where, sent_cot, cots_in, 80, 144, 80)
    owners = ToOwners(Exchange(s1, r1, o1), lambda head: qkv.at[head], lambda slot, c: land.at[slot, :, c])
    normed_one[...] = normed(tokens[...].astype(F32), attn_gain[...].reshape(1, -1)).astype(BF16)
    positions = pl.ds(pl.multiple_of(ctx * 128, 128), 128)
    for index in pairs_of_heads:
        for copy in fetch(index):
            copy.wait()
        parts = [dot(normed_one[...], weights[index, kind]) for kind in range(3)]
        for half in range(2):
            head, lanes = 2 * index + half, slice(half * HEAD_DIM, (half + 1) * HEAD_DIM)
            qkv[head, 0] = turned(parts[0][:, lanes], cos[positions], sin[positions]).astype(BF16)
            qkv[head, 1] = turned(parts[1][:, lanes], cos[positions], sin[positions]).astype(BF16)
            qkv[head, 2] = parts[2][:, lanes].astype(BF16)
            owners.start(head)
    back = Home(Exchange(s2, r2, o2), lambda slot, c: result.at[slot, c], lambda head: home.at[head])
    keep = pltpu.make_async_copy(land, heads, o3.at[1])

    def run(slot, blocks):
        for block in blocks:
            width = (block + 1) * 128
            query = land[slot, 0, block]
            key = land[slot, 1, 0 : block + 1].reshape(width, HEAD_DIM)
            value = land[slot, 2, 0 : block + 1].reshape(width, HEAD_DIM)
            row = lax.broadcasted_iota(jnp.int32, (width, 128), 0)
            column = lax.broadcasted_iota(jnp.int32, (width, 128), 1) + block * 128
            scores = jnp.where(
                (row <= column) & (row < length[0]), dot_nt(key, query) * SCALE, -1e30
            )
            weights = jnp.exp(scores - jnp.max(scores, axis=0, keepdims=True))
            probs = weights * (1.0 / jnp.sum(weights, axis=0, keepdims=True))
            result[slot, block] = dot_tn(probs.astype(BF16), value).astype(BF16)

    first.near()
    first.far()
    owners.arrived()
    run(0, range(8))
    back.start(0)

    @pl.when(owns_extra(ctx))
    def _():
        run(1, range(8))
        back.start(1)

    @pl.when(jnp.logical_not(owns_extra(ctx)))
    def _():
        land[1] = jnp.zeros_like(land[1])

    keep.start()
    first.middle()
    first.third()
    first.mine.wait()
    back.finish()
    for head in range(10):
        mixed[:, head * HEAD_DIM : (head + 1) * HEAD_DIM] = home[head]
    load.wait()

    @pl.loop(0, 5)
    def _(index):
        at = pl.ds(pl.multiple_of(index * 256, 256), 256)
        hidden[:, at] = tokens[:, at].astype(F32) + dot(mixed[...], w_out[:, at])

    rows[...] = normed(hidden[...], ffn_gain[...].reshape(1, -1)).astype(BF16)

    core, y_half = where[3], where[1] // 2
    me = lax.axis_index("exp")
    other = me + 1 - 2 * core
    more = Copies(s4, r4, o4)
    gather = Gather(more, where, rows, every, 64, 80, 48)
    first.last()
    shared_out[...] = jnp.zeros_like(shared_out)
    d_shared[...] = jnp.zeros_like(d_shared)

    def shared(first, last):
        @pl.loop(first, last)
        def _(step):
            at = pl.ds(pl.multiple_of(step * 128, 128), 128)
            value = rows[...]
            gate_pre, up_pre = dot(value, gate[:, at]), dot(value, up[:, at])
            silu, slope = gated(gate_pre, up_pre)
            activated = (silu * up_pre).astype(BF16)
            act[:, at] = activated
            shared_out[...] += dot(activated, down[at])
            d_act = dot_nt(cot[...], down[at])
            gate_back = (d_act * up_pre * slope).astype(BF16)
            up_back = (d_act * silu).astype(BF16)
            d_gates[0, :, at] = gate_back
            d_gates[1, :, at] = up_back
            d_shared[...] += dot_nt(gate_back, gate[:, at]) + dot_nt(up_back, up[:, at])

    def meta_lines():
        @pl.loop(0, 16)
        def _(block):
            high = cots_in[block, 128:144, pl.ds(pl.multiple_of(y_half * 128, 128), 128)].astype(F32)
            low = cots_in[block, 128:144, pl.ds(pl.multiple_of(256 + y_half * 128, 128), 128)].astype(F32)
            line = lax.broadcasted_iota(jnp.int32, (16, 128), 0)
            for expert in range(2):
                mine = line == 2 * (me % 8) + expert
                meta[block, expert : expert + 1] = jnp.sum(jnp.where(mine, high + low, 0.0), axis=0, keepdims=True)

        lines[...] = slot_lines(meta).reshape(16, 2, 128)

    def hot(block):
        slot = lax.broadcasted_iota(jnp.int32, (SLOTS, 128), 0).astype(F32)
        return [jnp.where(slot == lines[block, e : e + 1], 1.0, 0.0) for e in range(2)]

    def fill(block, source, out, column=None):
        value = dot(jnp.concatenate(hot(block), axis=0).astype(BF16), source)
        if column is not None:
            value = value * column
        value = value.astype(BF16)
        at = pl.ds(pl.multiple_of(block * SLOTS, SLOTS), SLOTS)
        for expert in range(2):
            out[expert, at] = value[expert * SLOTS : (expert + 1) * SLOTS]

    def fill_cots(block):
        column = jnp.concatenate(
            [jnp.sum(one * meta[block, e : e + 1], axis=1, keepdims=True) for e, one in enumerate(hot(block))], axis=0
        )
        at = pl.ds(pl.multiple_of(block * SLOTS, SLOTS), SLOTS)
        for expert in range(2):
            weight[expert, at] = jnp.broadcast_to(column[expert * SLOTS : (expert + 1) * SLOTS], (SLOTS, 128))
        fill(block, cots_in[block, 0:128], filled_cots, column)

    def fill_rows(far, dz):
        own_block = gather.shard(far, dz)
        for block in (own_block, own_block + 1 - 2 * core):
            fill(block, every[block], filled_rows)

    meta_lines()

    @pl.loop(0, 8, unroll=4)
    def _(block):
        fill_cots(block)

    for load in loads[:3]:
        load.wait()
    gather.near()
    gather.far()
    shared(0, 7)
    pair = device(where[0], where[1], where[2], 1 - core)
    from_pair = [more.remote(act, pair_act, pair), more.remote(d_gates.at[1 - core], pair_gates, pair)]
    gather.middle()

    @pl.loop(8, 16, unroll=4)
    def _(block):
        fill_cots(block)

    gather.third()
    keep_cots = pltpu.make_async_copy(filled_cots, slot_cots, keep_sem.at[0])
    keep_cots.start()
    gather.pairs_arrived(4)
    for copy in from_pair:
        copy.wait_recv()
    loads[3].wait()
    right[0:128, 0:896] = d_gates[core]
    right[128:256, 0:896] = pair_gates[...]
    at = pl.ds(pl.multiple_of(core * 640, 128), 640)
    right[0:128, 896:1536] = cot[:, at]
    right[128:256, 896:1536] = cots_in[other, 0:128, at]
    act_left[...] = dot(jnp.concatenate([act[...], pair_act[...]], axis=0), spread_in[...]).astype(BF16)

    def store(index):
        return pltpu.make_async_copy(
            panels.at[index], early.at[:, pl.ds(pl.multiple_of(index * 256, 256), 256)], early_sem.at[index]
        )

    @pl.loop(0, 5)
    def _(index):
        at = pl.ds(pl.multiple_of(index * 256, 256), 256)
        value = dot_tn(jnp.concatenate([rows[:, at], every[other, :, at]], axis=0), right[:, 0:896])
        for panel in range(7):
            panels[index, panel] = value[:, panel * 128 : panel * 128 + 128].astype(BF16)
        value = dot_tn(act_left[:, at], right[:, 896:1536])
        for panel in range(5):
            panels[index, 7 + panel] = value[:, panel * 128 : panel * 128 + 128].astype(BF16)
        store(index).start()

    gather.mine.wait()
    gather.sides()
    gather.pairs_arrived(6)
    for far, dz in ((False, 0), (False, -1), (False, 1), (True, 0), (False, 2)):
        fill_rows(far, dz)
    gather.pairs_arrived(10)
    for dz in (-1, 1):
        fill_rows(True, dz)
    gather.last()
    fill_rows(True, 2)
    keep_rows = pltpu.make_async_copy(filled_rows, slot_rows, keep_sem.at[1])
    keep_rows.start()
    owners.sent()
    keep.wait()
    copies.drain()
    more.drain()
    keep_cots.wait()
    keep_rows.wait()
    for index in range(5):
        store(index).wait()


def exchange_semaphores():
    return [
        pltpu.SemaphoreType.DMA((2, 8)),
        pltpu.SemaphoreType.DMA((2, 8)),
        pltpu.SemaphoreType.DMA((2,)),
    ]


def attend(
    length, cot, routes, route_gates, w_query, w_key, w_value, w_out, tokens, attn_gain, ffn_gain, cos, sin,
    gate_w, up_w, down_w, collective_id,
):
    rows, width = tokens.shape
    hidden = gate_w.shape[1]
    spread = np.zeros((128, 7, 128, 10), np.float32)
    for group in range(128):
        spread[group, np.arange(7), group, np.arange(7)] = 1.0
    spread = jnp.asarray(spread.reshape(hidden, width), BF16)
    return pl.pallas_call(
        attend_kernel,
        name="attend",
        out_shape=(
            jax.ShapeDtypeStruct((rows, width), BF16),
            jax.ShapeDtypeStruct((rows, width), BF16),
            jax.ShapeDtypeStruct((2, 3, 8, rows, HEAD_DIM), BF16),
            jax.ShapeDtypeStruct((rows, width), F32),
            jax.ShapeDtypeStruct((2, SLOT_ROWS, width), BF16),
            jax.ShapeDtypeStruct((2, SLOT_ROWS, width), BF16),
            jax.ShapeDtypeStruct((16, 2, 128), F32),
            jax.ShapeDtypeStruct((2, SLOT_ROWS, 128), F32),
            jax.ShapeDtypeStruct((rows, width), F32),
            jax.ShapeDtypeStruct((rows, width), F32),
            jax.ShapeDtypeStruct((12, width, 128), BF16),
        ),
        in_specs=[SMEM] + [VMEM] * 3 + [ANYWHERE] * 4 + [VMEM] * 5 + [ANYWHERE] * 4,
        out_specs=(VMEM, VMEM, ANYWHERE, VMEM, ANYWHERE, ANYWHERE, VMEM, VMEM, VMEM, VMEM, ANYWHERE),
        scratch_shapes=[
            pltpu.VMEM((rows + 16, width), BF16),
            pltpu.VMEM((10, 3, rows, HEAD_DIM), BF16),
            pltpu.VMEM((5, 3, width, 256), BF16),
            pltpu.VMEM((2, 3, 8, rows, HEAD_DIM), BF16),
            pltpu.VMEM((2, 8, rows, HEAD_DIM), BF16),
            pltpu.VMEM((10, rows, HEAD_DIM), BF16),
            pltpu.VMEM(w_out.shape, BF16),
            pltpu.VMEM((rows, width), BF16),
            pltpu.VMEM((16, rows, width), BF16),
            pltpu.VMEM((16, rows + 16, width), BF16),
            pltpu.VMEM(gate_w.shape, BF16),
            pltpu.VMEM(up_w.shape, BF16),
            pltpu.VMEM(down_w.shape, BF16),
            pltpu.VMEM(spread.shape, BF16),
            pltpu.VMEM((2, SLOT_ROWS, width), BF16),
            pltpu.VMEM((2, SLOT_ROWS, width), BF16),
            pltpu.VMEM((16, 2, 128), F32),
            pltpu.VMEM((rows, hidden), BF16),
            pltpu.VMEM((2, rows, hidden), BF16),
            pltpu.VMEM((rows, hidden), BF16),
            pltpu.VMEM((rows, hidden), BF16),
            pltpu.VMEM((2 * rows, 1536), BF16),
            pltpu.VMEM((2 * rows, width), BF16),
            pltpu.VMEM((5, 12, 256, 128), BF16),
        ]
        + exchange_semaphores()
        + exchange_semaphores()
        + [
            pltpu.SemaphoreType.DMA((GATHER_REMOTES,)),
            pltpu.SemaphoreType.DMA((GATHER_REMOTES,)),
            pltpu.SemaphoreType.DMA((2,)),
            pltpu.SemaphoreType.DMA((GATHER_REMOTES + 8,)),
            pltpu.SemaphoreType.DMA((GATHER_REMOTES + 8,)),
            pltpu.SemaphoreType.DMA((1,)),
            pltpu.SemaphoreType.DMA,
            pltpu.SemaphoreType.DMA((5, 3)),
            pltpu.SemaphoreType.DMA((4,)),
            pltpu.SemaphoreType.DMA((2,)),
            pltpu.SemaphoreType.DMA((5,)),
        ],
        compiler_params=params(collective_id),
        cost_estimate=cost(10**9, 10**8),
    )(
        length, cot, routes, route_gates, w_query, w_key, w_value, w_out, tokens, attn_gain, ffn_gain, cos, sin,
        gate_w, up_w, down_w, spread,
    )


def attend_back_kernel(
    d_mixed, heads, length, cos, sin, parts, up, up_one, gate, first, d_attn, normed_one, mixed, tokens, gain, d_hidden,
    ffn_term, w_query_in, w_key_in, w_value_in, down,
    input_grad, routed, up_final, gate_out, dense_out, up_out, down_out,
    land, kept, d_key, d_value, result, home, a, b, c, d, e, up_land, up_work, one_land, gate_other, first_land,
    pair_rows, d_qkv, pair_qkv, right, out_right, out_terms, out_land, weights, total, late, up_sum, first_sum, second,
    z_land, f_land, y_land, y_sum, x_land, t_land, tz_land, t_sum, tx_land,
    gains, gx_land, gx_sum, gy_land, sums, stage, final_land, up_other, d_land, d_work, d_other,
    s1, r1, o1, s2, r2, o2, s3, r3, o3, s4, r4, o4, load_sem, weight_sem,
):
    where = place()
    x, y, z, core = where
    ctx = lax.axis_index("ctx")
    x_peers = [device((x + 1) % 4, y, z, core), device((x + 3) % 4, y, z, core)]
    load_heads = pltpu.make_async_copy(heads, kept, load_sem)
    load_heads.start()

    def fetch(index):
        rows = slice(256 * index, 256 * index + 256)
        return [
            pltpu.make_async_copy(source.at[rows], weights.at[index % 2, kind], weight_sem.at[index % 2, kind])
            for kind, source in enumerate((w_query_in, w_key_in, w_value_in))
        ]

    for index in range(2):
        for copy in fetch(index):
            copy.start()
    spot = z * 2 + core
    spot_peers = [device(x, y, ((spot + d) % 8) // 2, (spot + d) % 2) for d in range(1, 8)]
    more_peers = [
        device(x, y, (z + 2) % 4, core), device(x, y, (z + 2) % 4, 1 - core),
        device(x, y, (z + 1) % 4, 1 - core), device(x, y, (z + 3) % 4, 1 - core),
    ]
    y_peers = [device(x, (y + step) % 4, z, core) for step in (1, 2, 3)]
    pair_peer = device(x, (y // 2) * 2 + 1 - y % 2, z, core)
    cross_peer = device(x, (y // 2) * 2 + 2 + 1 - y % 2 - 4 * (y // 2), z, core)
    greet([ctx_device((ctx + step) % 8) for step in range(1, 8)] + exp_peers(where) + [cross_peer] + more_peers)
    owners = ToOwners(Exchange(s1, r1, o1), lambda head: d_mixed.at[head], lambda slot, at: land.at[slot, at])
    for head in (8, 9, 0, 1, 2, 3, 4, 5, 6, 7):
        owners.start(head)
    copies = Copies(s3, r3, o3)
    scatter = Scatter(copies, where, parts, a, b, c, d, e)
    back = Home(Exchange(s2, r2, o2), lambda slot, at: result.at[slot, :, at], lambda head: home.at[:, head])
    y_low = y % 2

    def one_add(out, *terms):
        add_into(out, (), *terms, rows=(16, 5))

    ring_one = RingSum(
        copies, x, x_peers[0], x_peers[1], lambda chunk, half: up_one.at[chunk, 80 * half : 80 * half + 80],
        one_land, None, one_add, resident=True,
    )
    ring = RingSum(
        copies, x, x_peers[0], x_peers[1], lambda chunk, half: up.at[half_rows(2 * chunk + half, 160)],
        up_land, up_work, up_add,
    )
    swap = copies.remote(gate.at[:, half_rows(1 - y_low, 160)], gate_other, pair_peer)
    z_peers = [device(x, y, (z + 1) % 4, core), device(x, y, (z + 3) % 4, core)]

    block_add = add_blocks((2, 4))
    pair = device(x, y, z, 1 - core)
    pairs = [copies.remote(src, pair_rows.at[i], pair) for i, src in enumerate((normed_one, mixed, d_attn))]
    for copy in pairs:
        copy.wait_recv()
    at = pl.ds(pl.multiple_of(core * 640, 128), 640)
    out_right[0:128] = d_attn[:, at]
    out_right[128:256] = pair_rows[2, :, at]

    def spread_blocks(value, tile, panels):
        for lane, ref in enumerate(panels):
            for block in range(8):
                part = value[80 * block : 80 * block + 80, lane * 128 : lane * 128 + 128]
                ref[2 * tile + block // 4, block % 4] = part.astype(BF16)

    @pl.loop(0, 2)
    def _(tile):
        at = pl.ds(pl.multiple_of(tile * 640, 128), 640)
        value = dot_tn(jnp.concatenate([mixed[:, at], pair_rows[1, :, at]], axis=0), out_right[...])
        spread_blocks(value, tile, [out_terms.at[panel] for panel in range(4)] + [late.at[3, 3]])

    scatter.first()
    load_heads.wait()
    owners.arrived()

    def run(slot):
        d_key[...] = jnp.zeros_like(d_key)
        d_value[...] = jnp.zeros_like(d_value)
        for block in range(8):
            width = (block + 1) * 128
            query, upstream = kept[slot, 0, block], land[slot, block]
            key = kept[slot, 1, 0 : block + 1].reshape(width, HEAD_DIM)
            value = kept[slot, 2, 0 : block + 1].reshape(width, HEAD_DIM)
            row = lax.broadcasted_iota(jnp.int32, (width, 128), 0)
            column = lax.broadcasted_iota(jnp.int32, (width, 128), 1) + block * 128
            scores = jnp.where(
                (row <= column) & (row < length[0]), dot_nt(key, query) * SCALE, -1e30
            )
            weight = jnp.exp(scores - jnp.max(scores, axis=0, keepdims=True))
            probs = weight * (1.0 / jnp.sum(weight, axis=0, keepdims=True))
            d_probs = dot_nt(value, upstream)
            delta = jnp.sum(probs * d_probs, axis=0, keepdims=True)
            d_scores = (probs * (d_probs - delta)).astype(BF16)
            rows = slice(block * 128, block * 128 + 128)
            d_query = dot_tn(d_scores, key) * SCALE
            result[slot, 0, block] = turned(d_query, cos[rows], sin[rows]).astype(BF16)
            d_key[0:width] += dot(d_scores, query)
            d_value[0:width] += dot(probs.astype(BF16), upstream)
        for block in range(8):
            rows = slice(block * 128, block * 128 + 128)
            result[slot, 1, block] = turned(d_key[rows] * SCALE, cos[rows], sin[rows]).astype(BF16)
            result[slot, 2, block] = d_value[rows].astype(BF16)
        back.start(slot)

    run(0)
    scatter.merge_rest()
    scatter.second()

    @pl.when(owns_extra(ctx))
    def _():
        run(1)

    first_copies = [
        copies.remote(first.at[:, :, order((y + step) % 4)], first_land.at[step - 1], y_peers[step - 1])
        for step in (1, 2, 3)
    ]
    ring_one.raw()
    ring_one.forward()
    ring.raw()
    outs = RingSum(
        copies, z, z_peers[0], z_peers[1], lambda chunk, half: out_terms.at[chunk, 2 * half : 2 * half + 2],
        out_land, None, block_add, resident=True,
    )
    outs.raw()
    ring.forward()
    scatter.third()
    back.finish()
    outs.forward()
    for head in range(10):
        for kind in range(3):
            at = kind * 1280 + head * HEAD_DIM
            d_qkv[:, at : at + HEAD_DIM] = home[kind, head]
    swap_qkv = copies.remote(d_qkv, pair_qkv, pair)
    for index in range(5):
        for copy in fetch(index):
            copy.wait()
        value = dot_nt(d_qkv[:, 0:1280], weights[index % 2, 0])
        value += dot_nt(d_qkv[:, 1280:2560], weights[index % 2, 1])
        value += dot_nt(d_qkv[:, 2560:3840], weights[index % 2, 2])
        total[:, 256 * index : 256 * index + 256] = value
        if index + 2 < 5:
            for copy in fetch(index + 2):
                copy.start()

    swap_qkv.wait_recv()
    at = pl.ds(pl.multiple_of(core * 1920, 128), 1920)
    right[0:128] = d_qkv[:, at]
    right[128:256] = pair_qkv[:, at]

    @pl.loop(0, 2)
    def _(tile):
        at = pl.ds(pl.multiple_of(tile * 640, 128), 640)
        left = jnp.concatenate([normed_one[:, at], pair_rows[0, :, at]], axis=0)
        for group in range(5):
            value = dot_tn(left, right[:, 384 * group : 384 * group + 384])
            spread_blocks(value, tile, [late.at[p // 4, p % 4] for p in range(3 * group, 3 * group + 3)])

    last = Copies(s4, r4, o4)

    def direct(part, me, land, peers):
        return [last.remote(part((me + d) % 4), land.at[d - 1], peers[d - 1]) for d in (1, 2, 3)]

    def landed(arrivals):
        for copy in arrivals:
            copy.wait_recv()

    all_z = [z_peers[0], more_peers[0], z_peers[1]]
    all_x = [x_peers[0], device((x + 2) % 4, y, z, core), x_peers[1]]

    def z_ring(panel):
        return RingSum(
            last, z, z_peers[0], z_peers[1], lambda chunk, half: late.at[chunk, panel, 2 * half : 2 * half + 2],
            z_land.at[panel], None, block_add, resident=True,
        )

    ring_a, ring_b = z_ring(0), z_ring(1)
    ring_a.raw()
    tall = RingSum(
        last, y, y_peers[0], y_peers[2], lambda chunk, half: late.at[2 * half : 2 * half + 2, 3, :, order(chunk)],
        t_land, None, block_add, resident=True,
    )
    tall.raw()
    grad, term = normed_back(tokens[...].astype(F32), gain[...].reshape(1, -1), total[...])
    input_grad[...] = d_hidden[...] + grad
    column = lax.broadcasted_iota(jnp.int32, (128, 1280), 1)
    group = lax.broadcasted_iota(jnp.int32, (128, 1280), 0)
    inside = (column >= group * 10) & (column < group * 10 + 10)
    rest = lax.broadcasted_iota(jnp.int32, (1280, 128), 0) % 10
    lane = lax.broadcasted_iota(jnp.int32, (1280, 128), 1)
    lines = jnp.zeros((128, 128), F32)
    for offset, values in ((0, term), (10, ffn_term[...])):
        spots = jnp.where(inside, values, 0.0)
        high = spots.astype(BF16)
        low = (spots - high.astype(F32)).astype(BF16)
        pick = jnp.where(lane == rest + offset, 1.0, 0.0).astype(BF16)
        lines += dot(high, pick) + dot(low, pick)
    gains[...] = lines.reshape(4, 4, 8, 128)
    gain_x = direct(lambda c: gains.at[c], x, gx_land, all_x)

    def down_add(out, *terms):
        add_into(out, (), *terms, rows=(16, 7))

    downs = RingSum(
        last, x, x_peers[0], x_peers[1], lambda c, h: down.at[half_rows(2 * c + h, 112)], d_land, d_work, down_add
    )
    downs.raw()
    scatter.last(routed)
    outs.finish([second.at[0:2], second.at[2:4]])
    y_copies = {0: direct(lambda c: second.at[:, order(c)], y, y_land.at[0], y_peers)}
    ring_a.forward()
    ring_b.raw()
    ring_c = z_ring(2)
    ring_c.raw()
    tall.forward()
    for copy in first_copies:
        copy.wait_recv()
    add_into(first_sum, (3, 4), first.at[:, :, order(y)], first_land.at[0], first_land.at[1], first_land.at[2])
    x_copies = {4: direct(lambda c: first_sum.at[:, c], x, f_land, all_x)}
    ring_b.forward()
    swap.wait_recv()
    add_into(gate_out, (2,), gate.at[:, half_rows(y_low, 160)], gate_other, rows=(16, 10))
    ring_one.finish([up_final.at[0:80], up_final.at[80:160]])
    ring.finish([up_sum.at[0], up_sum.at[1]])
    swap_up = last.remote(up_sum.at[1 - y_low], up_other, pair_peer)
    ring_c.forward()
    landed(gain_x)
    gx_sum[...] = gains[x] + gx_land[0] + gx_land[1] + gx_land[2]
    gain_y = direct(lambda c: gx_sum.at[order(c)], y, gy_land, y_peers)
    downs.forward()

    def start_x(t, mine):
        landed(y_copies[t])
        add_into(y_sum.at[t], (4,), mine, y_land.at[t, 0], y_land.at[t, 1], y_land.at[t, 2])
        x_copies[t] = direct(lambda c: y_sum.at[t, c], x, x_land.at[t], all_x)

    ring_a.finish(ring_a.own[2:4])
    y_copies[1] = direct(lambda c: late.at[z, 0, :, order(c)], y, y_land.at[1], y_peers)
    tall.finish(tall.own[2:4])
    tall_z = direct(lambda c: late.at[c, 3, :, order(y)], z, tz_land, all_z)
    start_x(0, second.at[:, order(y)])
    ring_b.finish(ring_b.own[2:4])
    y_copies[2] = direct(lambda c: late.at[z, 1, :, order(c)], y, y_land.at[2], y_peers)
    start_x(1, late.at[z, 0, :, order(y)])
    landed(tall_z)
    add_into(t_sum, (4,), late.at[z, 3, :, order(y)], tz_land.at[0], tz_land.at[1], tz_land.at[2])
    tall_x = direct(lambda c: t_sum.at[c], x, tx_land, all_x)
    start_x(2, late.at[z, 1, :, order(y)])
    ring_c.finish(ring_c.own[2:4])
    y_copies[3] = direct(lambda c: late.at[z, 2, :, order(c)], y, y_land.at[3], y_peers)
    downs.finish([d_work.at[2], d_work.at[3]])
    swap_down = last.remote(d_work.at[2 + 1 - y_low], d_other, pair_peer)
    start_x(3, late.at[z, 2, :, order(y)])
    swap_up.wait_recv()
    add_into(up_out, (), up_sum.at[y_low], up_other, rows=(16, 10))

    def summed(panel, first_part, land, *index):
        value = first_part.astype(F32)
        for d in range(3):
            value = value + land[(d,) + index].astype(F32)
        sums[panel, 0:80] = value
        sums[panel, 80:96] = jnp.zeros((16, 128), F32)

    landed(gain_y)
    both_gains = gx_sum[order(y)] + gy_land[0] + gy_land[1] + gy_land[2]
    landed(x_copies[4])
    for panel in range(3):
        summed(panel, first_sum[panel, x], f_land, panel)
    for t in range(3):
        landed(x_copies[t])
        summed(3 + t, y_sum[t, x], x_land.at[t])
    landed(tall_x)
    summed(7, t_sum[x], tx_land)
    landed(x_copies[3])
    summed(6, y_sum[3, x], x_land.at[3])
    for j in range(8):
        for panel in range(8):
            stage[j, panel] = sums[panel, 10 * j : 10 * j + 16]
        stage[j, 0, 10:11] = both_gains[j : j + 1]
    finals = [
        last.remote(stage.at[(spot + d) % 8], final_land.at[d], spot_peers[d - 1]) for d in range(1, 8)
    ]
    swap_down.wait_recv()
    add_into(down_out, (), d_work.at[2 + y_low], d_other, rows=(16, 7))
    dense_out[spot] = stage[spot]
    for d, copy in enumerate(finals):
        copy.wait_recv()
        dense_out[(spot + 7 - d) % 8] = final_land[d + 1]
    owners.sent()
    copies.drain()
    last.drain()


def attend_back(
    d_mixed, heads, length, cos, sin, parts, up, up_one, gate, first, d_attn, normed_one, mixed, tokens, gain, d_hidden,
    ffn_term, w_query, w_key, w_value, down, collective_id,
):
    rows, width = tokens.shape
    hidden = up.shape[1]
    ring_land = pltpu.VMEM((6, 2, 4, 80, 128), BF16)
    return pl.pallas_call(
        attend_back_kernel,
        name="attend_back",
        out_shape=(
            jax.ShapeDtypeStruct((rows, width), F32),
            jax.ShapeDtypeStruct((rows, width), F32),
            jax.ShapeDtypeStruct((160, hidden), F32),
            jax.ShapeDtypeStruct((2, 160, hidden), F32),
            jax.ShapeDtypeStruct((8, 8, 16, 128), F32),
            jax.ShapeDtypeStruct((160, hidden), F32),
            jax.ShapeDtypeStruct((112, width), F32),
        ),
        in_specs=[ANYWHERE, ANYWHERE, SMEM, VMEM, VMEM, ANYWHERE, ANYWHERE, VMEM, VMEM, VMEM]
        + [VMEM] * 7
        + [ANYWHERE] * 4,
        out_specs=(VMEM,) * 7,
        scratch_shapes=[
            pltpu.VMEM((2, 8, 128, HEAD_DIM), BF16),
            pltpu.VMEM((2, 3, 8, 128, HEAD_DIM), BF16),
            pltpu.VMEM((1024, HEAD_DIM), F32),
            pltpu.VMEM((1024, HEAD_DIM), F32),
            pltpu.VMEM((2, 3, 8, 128, HEAD_DIM), BF16),
            pltpu.VMEM((3, 10, 128, HEAD_DIM), BF16),
        ]
        + SCATTER_SCRATCH
        + [
            pltpu.VMEM((6, 160, hidden), BF16),
            pltpu.VMEM((4, 160, hidden), BF16),
            pltpu.VMEM((6, 80, hidden), BF16),
            pltpu.VMEM((2, 160, hidden), BF16),
            pltpu.VMEM((3, 3, 4, 80, 128), BF16),
            pltpu.VMEM((3, rows, width), BF16),
            pltpu.VMEM((rows, 3 * width), BF16),
            pltpu.VMEM((rows, 3 * width), BF16),
            pltpu.VMEM((2 * rows, 1920), BF16),
            pltpu.VMEM((2 * rows, 640), BF16),
            pltpu.VMEM((4, 4, 4, 80, 128), BF16),
            ring_land,
            pltpu.VMEM((2, 3, 256, width), BF16),
            pltpu.VMEM((rows, width), F32),
            pltpu.VMEM((4, 4, 4, 4, 80, 128), BF16),
            pltpu.VMEM((2, 160, hidden), BF16),
            pltpu.VMEM((3, 4, 80, 128), BF16),
            pltpu.VMEM((4, 4, 80, 128), BF16),
            pltpu.VMEM((3, 6, 2, 4, 80, 128), BF16),
            pltpu.VMEM((3, 3, 80, 128), BF16),
            pltpu.VMEM((4, 3, 4, 80, 128), BF16),
            pltpu.VMEM((4, 4, 80, 128), BF16),
            pltpu.VMEM((4, 3, 80, 128), BF16),
            ring_land,
            pltpu.VMEM((3, 4, 80, 128), BF16),
            pltpu.VMEM((4, 80, 128), BF16),
            pltpu.VMEM((3, 80, 128), BF16),
            pltpu.VMEM((4, 4, 8, 128), F32),
            pltpu.VMEM((3, 4, 8, 128), F32),
            pltpu.VMEM((4, 8, 128), F32),
            pltpu.VMEM((3, 8, 128), F32),
            pltpu.VMEM((8, 96, 128), F32),
            pltpu.VMEM((8, 8, 16, 128), F32),
            pltpu.VMEM((8, 8, 16, 128), F32),
            pltpu.VMEM((160, hidden), BF16),
            pltpu.VMEM((6, 112, width), BF16),
            pltpu.VMEM((4, 112, width), BF16),
            pltpu.VMEM((112, width), BF16),
        ]
        + exchange_semaphores()
        + exchange_semaphores()
        + [
            pltpu.SemaphoreType.DMA((SCATTER_REMOTES + 26,)),
            pltpu.SemaphoreType.DMA((SCATTER_REMOTES + 26,)),
            pltpu.SemaphoreType.DMA((SCATTER_LOCALS + 4,)),
            pltpu.SemaphoreType.DMA((GRAD_REMOTES,)),
            pltpu.SemaphoreType.DMA((GRAD_REMOTES,)),
            pltpu.SemaphoreType.DMA((4,)),
            pltpu.SemaphoreType.DMA,
            pltpu.SemaphoreType.DMA((2, 3)),
        ],
        compiler_params=params(collective_id),
        cost_estimate=cost(10**9, 10**8),
    )(
        d_mixed, heads, length, cos, sin, parts, up, up_one, gate, first, d_attn, normed_one, mixed,
        tokens, gain, d_hidden, ffn_term, w_query, w_key, w_value, down,
    )


def gated(gate, up):
    squash = 1.0 / (1.0 + jnp.exp(-gate))
    silu = gate * squash
    slope = squash * (1.0 + gate * (1.0 - squash))
    return silu, slope


SLOTS = 48
DEPTH = 4
SLOT_ROWS = 16 * SLOTS


def slot_lines(meta):
    member = jnp.where(meta[...].reshape(32, 128) > 0, 1.0, 0.0)
    before = lax.broadcasted_iota(jnp.int32, (128, 128), 0) < lax.broadcasted_iota(jnp.int32, (128, 128), 1)
    count = dot(member.astype(BF16), jnp.where(before, 1.0, 0.0).astype(BF16))
    return jnp.where(member > 0, count, -1.0)


def experts_kernel(
    meta, weight, rows, cots, gate_w, up_w, down_w, early, out, d_rows, kept_act, kept_back, down_sum, first_sum,
    gate_up, down, slot_rows, slot_cots, slot_out, slot_back, lines, columns, act, back,
    out_buf, term, land, z_land, z_work, in_sem, out_sem, weight_sem, keep_sem, send, recv, own,
):
    hidden = down.shape[1]
    x, y, z, core = place()
    x_peers = [device((x + 1) % 4, y, z, core), device((x + 3) % 4, y, z, core)]

    def load(expert):
        return [
            pltpu.make_async_copy(gate_w.at[expert], gate_up.at[expert, :, 0:hidden], weight_sem.at[expert, 0]),
            pltpu.make_async_copy(up_w.at[expert], gate_up.at[expert, :, hidden : 2 * hidden], weight_sem.at[expert, 1]),
            pltpu.make_async_copy(down_w.at[expert], down.at[expert], weight_sem.at[expert, 2]),
        ]

    def fetch(expert):
        return [
            pltpu.make_async_copy(rows.at[expert], slot_rows.at[expert], in_sem.at[expert, 0]),
            pltpu.make_async_copy(cots.at[expert], slot_cots.at[expert], in_sem.at[expert, 1]),
        ]

    for copy in fetch(0) + load(0):
        copy.start()
    z_peers = [device(x, y, (z + 1) % 4, core), device(x, y, (z + 3) % 4, core)]
    greet(x_peers + z_peers)
    copies = Copies(send, recv, own)

    def panel_add(out, *terms):
        add_into(out, (), *terms, rows=(80, 8))

    dense = [
        RingSum(
            copies, z, z_peers[0], z_peers[1],
            lambda chunk, half, panel=panel: early.at[
                2 * chunk + panel if panel < 2 else 8 + chunk, 640 * half : 640 * half + 640
            ],
            z_land.at[panel], z_work.at[panel], panel_add,
        )
        for panel in range(3)
    ]
    for panel in dense:
        panel.raw()
    lines[...] = slot_lines(meta).reshape(16, 2, 128)
    columns[...] = jnp.concatenate([lines[...].reshape(32, 128), jnp.zeros((96, 128), F32)], axis=0).T
    def keep(expert):
        return [
            pltpu.make_async_copy(act.at[expert], kept_act.at[expert], keep_sem.at[expert, 0]),
            pltpu.make_async_copy(back.at[expert], kept_back.at[expert], keep_sem.at[expert, 1]),
        ]

    def main(expert):
        for copy in fetch(expert) + load(expert):
            copy.wait()
        if expert == 0:
            for copy in fetch(1) + load(1):
                copy.start()

        tile = 256

        @pl.loop(0, SLOT_ROWS // tile)
        def _(index):
            at = pl.ds(pl.multiple_of(index * tile, tile), tile)
            both = dot(slot_rows[expert, at], gate_up[expert])
            gate, up = both[:, :hidden], both[:, hidden:]
            silu, slope = gated(gate, up)
            activated = (silu * up).astype(BF16)
            act[expert, at] = activated
            produced = dot(activated, down[expert]).astype(BF16).astype(F32)
            slot_out[expert, at] = (produced * weight[expert, at][:, 0:1]).astype(BF16)
            d_act = dot_nt(slot_cots[expert, at], down[expert])
            back[expert, at, 0:hidden] = (d_act * up * slope).astype(BF16)
            back[expert, at, hidden : 2 * hidden] = (d_act * silu).astype(BF16)
            slot_back[expert, at] = dot_nt(back[expert, at], gate_up[expert]).astype(BF16)

    main(0)
    for copy in keep(0):
        copy.start()

    @pl.loop(0, hidden // 128)
    def _(index):
        at = pl.ds(pl.multiple_of(index * 128, 128), 128)
        term[at] = dot_tn(act[0, :, at], slot_cots[0]).astype(BF16)

    def part(chunk, half):
        return term.at[pl.ds(pl.multiple_of(chunk * 224 + half * 112, 112), 112)]

    def add(out, *terms):
        add_into(out, (), *terms, rows=(16, 7))

    ring = RingSum(copies, x, x_peers[0], x_peers[1], part, land, None, add, resident=True)
    ring.raw()
    for panel in dense:
        panel.forward()
    main(1)
    ring.forward()
    for copy in keep(1):
        copy.start()

    def store(block):
        slot = block % DEPTH
        return [
            pltpu.make_async_copy(out_buf.at[slot, 0], out.at[block], out_sem.at[slot, 0]),
            pltpu.make_async_copy(out_buf.at[slot, 1], d_rows.at[block], out_sem.at[slot, 1]),
        ]

    lane = lax.broadcasted_iota(jnp.int32, (128, 2 * SLOTS), 1).astype(F32)
    for block in range(16):
        slot = block % DEPTH
        first, second = columns[:, 2 * block : 2 * block + 1], columns[:, 2 * block + 1 : 2 * block + 2]
        hit = ((lane < SLOTS) & (lane == first)) | ((lane >= SLOTS) & (lane - SLOTS == second))
        both = jnp.where(hit, 1.0, 0.0).astype(BF16)
        if block >= DEPTH:
            for copy in store(block - DEPTH):
                copy.wait()
        at = slice(block * SLOTS, (block + 1) * SLOTS)
        for index, source in enumerate((slot_out, slot_back)):
            value = jnp.concatenate([source[0, at], source[1, at]], axis=0)
            out_buf[slot, index] = dot(both, value).astype(BF16)
        for copy in store(block):
            copy.start()
    for block in range(16 - DEPTH, 16):
        for copy in store(block):
            copy.wait()
    for panel in range(3):
        dense[panel].finish([first_sum.at[panel, 0:640], first_sum.at[panel, 640:1280]])
    ring.finish([down_sum.at[0:112], down_sum.at[112:224]])
    copies.drain()
    for copy in keep(0) + keep(1):
        copy.wait()


def experts(meta, weight, rows, cots, gate_w, up_w, down_w, early, collective_id):
    width, hidden = gate_w.shape[1:]
    return pl.pallas_call(
        experts_kernel,
        name="experts",
        out_shape=(
            jax.ShapeDtypeStruct((16, 128, width), BF16),
            jax.ShapeDtypeStruct((16, 128, width), BF16),
            jax.ShapeDtypeStruct((2, SLOT_ROWS, hidden), BF16),
            jax.ShapeDtypeStruct((2, SLOT_ROWS, 2 * hidden), BF16),
            jax.ShapeDtypeStruct((hidden // 4, width), BF16),
            jax.ShapeDtypeStruct((3, width, 128), BF16),
        ),
        in_specs=[VMEM, VMEM] + [ANYWHERE] * 6,
        out_specs=[ANYWHERE] * 4 + [VMEM, VMEM],
        scratch_shapes=[
            pltpu.VMEM((2, width, 2 * hidden), BF16),
            pltpu.VMEM((2, hidden, width), BF16),
            pltpu.VMEM((2, SLOT_ROWS, width), BF16),
            pltpu.VMEM((2, SLOT_ROWS, width), BF16),
            pltpu.VMEM((2, SLOT_ROWS, width), BF16),
            pltpu.VMEM((2, SLOT_ROWS, width), BF16),
            pltpu.VMEM((16, 2, 128), F32),
            pltpu.VMEM((128, 128), F32),
            pltpu.VMEM((2, SLOT_ROWS, hidden), BF16),
            pltpu.VMEM((2, SLOT_ROWS, 2 * hidden), BF16),
            pltpu.VMEM((DEPTH, 2, 128, width), BF16),
            pltpu.VMEM((hidden, width), BF16),
            pltpu.VMEM((6, hidden // 8, width), BF16),
            pltpu.VMEM((3, 6, width // 2, 128), BF16),
            pltpu.VMEM((3, 4, width // 2, 128), BF16),
            pltpu.SemaphoreType.DMA((2, 2)),
            pltpu.SemaphoreType.DMA((DEPTH, 2)),
            pltpu.SemaphoreType.DMA((2, 3)),
            pltpu.SemaphoreType.DMA((2, 2)),
            pltpu.SemaphoreType.DMA((24,)),
            pltpu.SemaphoreType.DMA((24,)),
            pltpu.SemaphoreType.DMA((12,)),
        ],
        compiler_params=params(collective_id),
        cost_estimate=cost(12 * 2 * SLOT_ROWS * width * hidden, 6 * 10**7),
    )(meta, weight, rows, cots, gate_w, up_w, down_w, early)


def finish_kernel(
    packed, hidden, shared_out, routed, gate, up_zero, up_one, down_zero, down_one, grad,
    block_out, input_grad, attn_gain, query, key, value, out, ffn_gain, s_gate, s_up, s_down, gate_grad, up_grad, down_grad,
):
    input_grad[...] = grad[...]
    gate_grad[...] = gate[...]
    up_grad[0] = up_zero[...]
    up_grad[1] = up_one[...]
    down_grad[0] = down_zero[...]
    down_grad[1] = down_one[...]
    block_out[...] = hidden[...] + shared_out[...] + routed[...]
    gains = packed[0, 0, 10:11]
    for source in range(1, 8):
        gains = gains + packed[source, 0, 10:11]
    attn_gain[...] = gains[:, 0:10]
    ffn_gain[...] = gains[:, 10:20]
    for core in range(2):
        for panel in range(20):
            if panel < 15:
                part = packed[2 * (panel // 4) + core, 4 + panel % 4, 0:10]
                at = core * 1920 + panel * 128
                (query, key, value)[at // 1280][:, at % 1280 : at % 1280 + 128] = part
            else:
                part = packed[2 * (panel - 15) + core, 3, 0:10] if panel < 19 else packed[6 + core, 7, 0:10]
                at = core * 640 + (panel - 15) * 128
                out[:, at : at + 128] = part
        for panel in range(12):
            where = (panel // 2, panel % 2) if panel < 8 else (panel - 8, 2)
            part = packed[2 * where[0] + core, where[1], 0:10]
            if panel < 7:
                (s_gate, s_up)[core][:, panel * 128 : panel * 128 + 128] = part
            else:
                at = core * 640 + (panel - 7) * 128
                s_down[:, at : at + 128] = part[0:7]


def finish(packed, *values):
    def shape(*dims):
        return jax.ShapeDtypeStruct(dims, F32)

    return pl.pallas_call(
        finish_kernel,
        name="finish",
        out_shape=(
            shape(128, 1280), shape(128, 1280), shape(1, 10),
            shape(10, 1280), shape(10, 1280), shape(10, 1280), shape(10, 1280), shape(1, 10),
            shape(10, 896), shape(10, 896), shape(7, 1280),
            shape(2, 160, 896), shape(2, 160, 896), shape(2, 112, 1280),
        ),
        in_specs=[VMEM] * 10,
        out_specs=(VMEM,) * 14,
        compiler_params=params(),
        cost_estimate=cost(10**7, 12 * 10**6),
    )(packed, *values)


def local(
    tokens,
    lengths,
    routes,
    route_gates,
    attn_gain,
    w_query,
    w_key,
    w_value,
    w_out,
    ffn_gain,
    shared_gate,
    shared_up,
    shared_down,
    expert_gate,
    expert_up,
    expert_down,
    cotangent,
):
    resident, cot = tokens[0], cotangent[0]
    rows = resident.shape[0]
    all_cos, all_sin = turn_tables(8 * rows)
    back_sin = jnp.asarray(-all_sin)
    all_cos, all_sin = jnp.asarray(all_cos), jnp.asarray(all_sin)
    normed_one, mixed, heads, hidden, slot_rows, slot_cots, meta, weight, shared_out, d_shared, early = attend(
        lengths, cot, routes.transpose(2, 0, 1), route_gates.transpose(2, 0, 1), w_query, w_key, w_value, w_out, resident,
        attn_gain, ffn_gain, all_cos, all_sin, shared_gate, shared_up, shared_down, 1,
    )
    parts, d_parts, kept_act, kept_back, down_one, first = experts(
        meta, weight, slot_rows, slot_cots, expert_gate, expert_up, expert_down, early, 5
    )
    first = first.reshape(3, 4, 4, 80, 128)
    gate_sum, up_term, up_one, down_term, down_zero, d_mixed, d_hidden, d_attn, ffn_term = scatter_rows(
        d_parts, slot_rows, slot_cots, kept_act, kept_back, d_shared, hidden, ffn_gain, cot, w_out, down_one, 3
    )
    grad, routed, up_last, gate_grad, packed, up_first, down_last = attend_back(
        d_mixed, heads, lengths, all_cos, back_sin, parts, up_term, up_one, gate_sum, first, d_attn, normed_one,
        mixed, resident, attn_gain, d_hidden, ffn_term, w_query, w_key, w_value, down_term, 4,
    )
    outs = finish(
        packed, hidden, shared_out, routed, gate_grad, up_first, up_last, down_zero, down_last, grad
    )
    return (outs[0][None], outs[1][None], outs[2][0], *outs[3:7], outs[7][0], *outs[8:])


def solution(mesh):
    in_specs = (
        P("exp", "ctx", None),
        P("exp"),
        P("exp", "ctx", None),
        P("exp", "ctx", None),
        P(),
        P(),
        P(),
        P(),
        P(),
        P(),
        P(),
        P(),
        P(),
        P("exp", None, None),
        P("exp", None, None),
        P("exp", None, None),
        P("exp", "ctx", None),
    )
    out_specs = (
        P("exp", "ctx", None),
        P("exp", "ctx", None),
        P(("ctx", "exp")),
        P(("ctx", "exp"), None),
        P(("ctx", "exp"), None),
        P(("ctx", "exp"), None),
        P(("ctx", "exp"), None),
        P(("ctx", "exp")),
        P(("ctx", "exp"), None),
        P(("ctx", "exp"), None),
        P(("ctx", "exp"), None),
        P("exp", "ctx", None),
        P("exp", "ctx", None),
        P("exp", "ctx", None),
    )
    return jax.shard_map(local, mesh=mesh, in_specs=in_specs, out_specs=out_specs, check_vma=False)
```

```python
import functools
import math

import jax
import jax.numpy as jnp
import numpy as np
from jax import lax
from jax.experimental import pallas as pl
from jax.experimental.pallas import tpu as pltpu
from jax.sharding import PartitionSpec as P

MESH = pl.DeviceIdType.MESH
HEAD_DIM = 128
VMEM_LIMIT = 60 * 2**20
F32, BF16 = jnp.float32, jnp.bfloat16


def place():
    ctx, exp = lax.axis_index("ctx"), lax.axis_index("exp")
    return ctx // 2, (exp // 8) * 2 + ctx % 2, (exp // 2) % 4, exp % 2


def device(x, y, z, core):
    return (x * 2 + y % 2, (y // 2) * 8 + z * 2 + core)


def greet(devices):
    barrier = pltpu.get_barrier_semaphore()
    for target in devices:
        pl.semaphore_signal(barrier, inc=1, device_id=target, device_id_type=MESH)
    pl.semaphore_wait(barrier, len(devices))


class Copies:
    def __init__(self, send, recv, own):
        self.send, self.recv, self.own = send, recv, own
        self.remotes, self.locals = 0, 0
        self.started = []

    def remote(self, src, dst, target):
        index = self.remotes
        self.remotes += 1
        copy = pltpu.make_async_remote_copy(
            src_ref=src,
            dst_ref=dst,
            send_sem=self.send.at[index],
            recv_sem=self.recv.at[index],
            device_id=target,
            device_id_type=MESH,
        )
        copy.start()
        self.started.append(copy)
        return copy

    def local(self, src, dst):
        index = self.locals
        self.locals += 1
        copy = pltpu.make_async_copy(src, dst, self.own.at[index])
        copy.start()
        return copy

    def drain(self):
        for copy in self.started:
            copy.wait_send()


def each(shape, body):
    @pl.loop(0, math.prod(shape))
    def _(step):
        index = []
        for size in reversed(shape):
            index.append(step % size)
            step = step // size
        body(tuple(reversed(index)))


def add_into(out, shape, *terms, rows=None):
    def body(index):
        total = terms[0][index].astype(F32)
        for term in terms[1:]:
            total = total + term[index].astype(F32)
        out[index] = total.astype(out.dtype)

    if rows is None:
        each(shape, body)
    else:
        step, count = rows
        each(shape + (count,), lambda i: body(i[:-1] + (pl.ds(pl.multiple_of(i[-1] * step, step), step),)))


class RingSum:
    def __init__(self, copies, me, right, left, part, land, work, add, resident=None):
        self.copies, self.right, self.left, self.land, self.work, self.add = copies, right, left, land, work, add
        self.part = part
        self.after, self.before, across = (me + 1) % 4, (me + 3) % 4, (me + 2) % 4
        self.one = copies.remote(part(across, 0), land.at[0], right)
        self.two = copies.remote(part(across, 1), land.at[1], left)
        sources = [part(self.after, 0), part(self.before, 1), part(me, 0), part(me, 1)]
        if resident is None:
            self.loads = [copies.local(source, work.at[i]) for i, source in enumerate(sources)]
            self.own = [work.at[i] for i in range(4)]
        else:
            self.loads = []
            self.own = sources

    def raw(self):
        self.three = self.copies.remote(self.part(self.after, 1), self.land.at[2], self.right)
        self.four = self.copies.remote(self.part(self.before, 0), self.land.at[4], self.left)

    def forward(self):
        for load in self.loads:
            load.wait()
        self.one.wait_recv()
        self.add(self.land.at[0], self.land.at[0], self.own[0])
        self.five = self.copies.remote(self.land.at[0], self.land.at[3], self.right)
        self.two.wait_recv()
        self.add(self.land.at[1], self.land.at[1], self.own[1])
        self.six = self.copies.remote(self.land.at[1], self.land.at[5], self.left)

    def finish(self, outs):
        for copy in (self.three, self.four, self.five, self.six):
            copy.wait_recv()
        self.add(outs[0], self.own[2], self.land.at[3], self.land.at[4])
        self.add(outs[1], self.own[3], self.land.at[2], self.land.at[5])


GRAD_REMOTES = 5 * 6 + 2 + 3 * 3 + 3 * 4 + 6 + 3 * 4 + 7


def add_blocks(shape):
    def add(out, *terms):
        add_into(out, shape, *terms)

    return add


def half_rows(which, size):
    return pl.ds(pl.multiple_of(which * size, size), size)


def order(y):
    return (y % 2) * 2 + y // 2


VMEM = pl.BlockSpec(memory_space=pltpu.VMEM)
ANYWHERE = pl.BlockSpec(memory_space=pl.ANY)
SMEM = pl.BlockSpec(memory_space=pltpu.SMEM)
SCALE = HEAD_DIM ** (-0.5)


def params(collective_id=None):
    if collective_id is None:
        return pltpu.CompilerParams(vmem_limit_bytes=VMEM_LIMIT)
    return pltpu.CompilerParams(
        collective_id=collective_id, has_side_effects=True, vmem_limit_bytes=VMEM_LIMIT
    )


def cost(flops, bytes_accessed):
    return pl.CostEstimate(flops=int(flops), bytes_accessed=int(bytes_accessed), transcendentals=0)


def dot(left, right):
    return jnp.dot(left, right, preferred_element_type=F32)


def dot_nt(left, right):
    return lax.dot_general(left, right, (((1,), (1,)), ((), ())), preferred_element_type=F32)


def dot_tn(left, right):
    return lax.dot_general(left, right, (((0,), (0,)), ((), ())), preferred_element_type=F32)


def normed(values, gain):
    return values * lax.rsqrt(jnp.mean(values * values, axis=-1, keepdims=True) + 1e-06) * gain


def normed_back(values, gain, upstream):
    factor = lax.rsqrt(jnp.mean(values * values, axis=-1, keepdims=True) + 1e-06)
    scaled = upstream * gain
    inner = jnp.mean(scaled * values, axis=-1, keepdims=True)
    term = jnp.sum(upstream * values * factor, axis=0, keepdims=True)
    return factor * scaled - values * factor * factor * factor * inner, term


def turned(values, cos, sin):
    return values * cos + pltpu.roll(values, HEAD_DIM // 2, 1) * sin


def turn_tables(count):
    half = HEAD_DIM // 2
    frequency = np.exp(np.arange(half, dtype=np.float32) * np.float32(-2.0 * math.log(10000.0) / HEAD_DIM))
    angle = np.arange(count, dtype=np.float32)[:, None] * frequency[None, :]
    cos, sin = np.cos(angle), np.sin(angle)
    return np.concatenate([cos, cos], axis=1), np.concatenate([-sin, sin], axis=1)


def rank(y_half, z, core):
    return y_half * 8 + z * 2 + core


class Gather:
    def __init__(self, copies, where, src, out, cut, far, far_cut):
        x, y, z, core = where
        self.copies, self.out, self.cut, self.far_rows, self.far_cut = copies, out, cut, far, far_cut
        self.rows = out.shape[1]
        self.split = far < self.rows
        self.y_half, self.z, self.core = y // 2, z, core
        self.pair = device(x, y, z, 1 - core)
        self.across = device(x, (y + 2) % 4, z, core)
        self.right, self.left = device(x, y, (z + 1) % 4, core), device(x, y, (z + 3) % 4, core)
        me = rank(self.y_half, z, core)
        self.mine = copies.local(src, out.at[me])
        self.over = copies.remote(src, out.at[me], self.across)
        self.to_right = copies.remote(src, out.at[me], self.right)
        self.to_left = copies.remote(src, out.at[me], self.left)
        self.pairs = [copies.remote(src, out.at[me], self.pair)]
        self.seen = 0

    def shard(self, other, dz):
        y_half = 1 - self.y_half if other else self.y_half
        return rank(y_half, (self.z + dz + 4) % 4, self.core)

    def send(self, ref, target):
        return self.copies.remote(ref, ref, target)

    def share(self, ref):
        self.pairs.append(self.send(ref, self.pair))

    def near(self):
        self.to_right.wait_recv()
        index = self.shard(False, -1)
        self.on_right = self.send(self.out.at[index, 0 : self.cut], self.right)
        if self.split:
            self.side_before = self.send(self.out.at[index, self.far_rows : self.rows], self.across)
        self.share(self.out.at[index])
        self.to_left.wait_recv()
        index = self.shard(False, 1)
        self.on_left = self.send(self.out.at[index, self.cut : self.rows], self.left)
        if self.split:
            self.side_after = self.send(self.out.at[index, self.far_rows : self.rows], self.across)
        self.share(self.out.at[index])

    def far(self):
        self.over.wait_recv()
        index = self.shard(True, 0)
        self.far_right = self.send(self.out.at[index, 0 : self.far_rows], self.right)
        self.far_left = self.send(self.out.at[index, 0 : self.far_rows], self.left)
        self.share(self.out.at[index])

    def middle(self):
        index = self.shard(False, 2)
        self.on_right.wait_recv()
        self.share(self.out.at[index, 0 : self.cut])
        self.on_left.wait_recv()
        if self.split:
            self.side_middle = self.send(self.out.at[index, self.far_rows : self.rows], self.across)
        self.share(self.out.at[index, self.cut : self.rows])

    def third(self):
        self.far_right.wait_recv()
        index = self.shard(True, -1)
        self.far_on_right = self.send(self.out.at[index, 0 : self.far_cut], self.right)
        self.share(self.out.at[index, 0 : self.far_rows])
        self.far_left.wait_recv()
        index = self.shard(True, 1)
        self.far_on_left = self.send(self.out.at[index, self.far_cut : self.far_rows], self.left)
        self.share(self.out.at[index, 0 : self.far_rows])

    def sides(self):
        for copy, dz in ((self.side_before, -1), (self.side_after, 1)):
            copy.wait_recv()
            self.share(self.out.at[self.shard(True, dz), self.far_rows : self.rows])

    def pairs_arrived(self, count):
        for copy in self.pairs[self.seen : count]:
            copy.wait_recv()
        self.seen = count

    def last(self):
        index = self.shard(True, 2)
        self.far_on_right.wait_recv()
        self.share(self.out.at[index, 0 : self.far_cut])
        self.far_on_left.wait_recv()
        self.share(self.out.at[index, self.far_cut : self.far_rows])
        if self.split:
            self.side_middle.wait_recv()
            self.share(self.out.at[index, self.far_rows : self.rows])
        self.pairs_arrived(len(self.pairs))


GATHER_REMOTES = 3 + 2 + 2 + 2 + 8 + 2


def exp_peers(where):
    x, y, z, core = where
    return [
        device(x, y, z, 1 - core),
        device(x, (y + 2) % 4, z, core),
        device(x, y, (z + 1) % 4, core),
        device(x, y, (z + 3) % 4, core),
    ]


class Scatter:
    def __init__(self, copies, where, parts, pair_land, work, ring_land, far_land, y_land):
        x, y, z, core = where
        self.copies, self.work, self.pair_land = copies, work, pair_land
        self.ring_land, self.far_land, self.y_land = ring_land, far_land, y_land
        self.across = device(x, (y + 2) % 4, z, core)
        self.right, self.left = device(x, y, (z + 1) % 4, core), device(x, y, (z + 3) % 4, core)
        pair = device(x, y, z, 1 - core)
        self.pairs, self.loads = {}, {}
        for slot in ((0, 2), (1, 2), (0, 1), (0, 3), (1, 1), (1, 3), (0, 0), (1, 0)):
            y_half = 1 - y // 2 if slot[0] == 0 else y // 2
            at = (z + slot[1]) % 4
            self.pairs[slot] = copies.remote(parts.at[rank(y_half, at, 1 - core)], pair_land.at[slot], pair)
            self.loads[slot] = copies.local(parts.at[rank(y_half, at, core)], work.at[slot])

    def merge(self, slot):
        self.loads[slot].wait()
        self.pairs[slot].wait_recv()
        rows_add(self.work.at[slot], 0, 128, self.work.at[slot], self.pair_land.at[slot])

    def first(self):
        self.ring = {}
        for far in range(2):
            self.merge((far, 2))
            self.ring[far] = (
                self.copies.remote(self.work.at[far, 2, 0:64], self.ring_land.at[far, 0], self.right),
                self.copies.remote(self.work.at[far, 2, 64:128], self.ring_land.at[far, 1], self.left),
            )

    def merge_rest(self):
        for far in range(2):
            self.merge((far, 1))
            self.merge((far, 3))
            self.merge((far, 0))

    def second(self):
        self.final = {}
        for far in range(2):
            self.ring[far][0].wait_recv()
            rows_add(self.work.at[far, 1, 0:64], 0, 64, self.work.at[far, 1, 0:64], self.ring_land.at[far, 0])
            to_right = self.copies.remote(self.work.at[far, 1], self.far_land.at[far, 0], self.right)
            self.ring[far][1].wait_recv()
            rows_add(self.work.at[far, 3, 64:128], 0, 64, self.work.at[far, 3, 64:128], self.ring_land.at[far, 1])
            to_left = self.copies.remote(self.work.at[far, 3], self.far_land.at[far, 1], self.left)
            self.final[far] = (to_right, to_left)

    def third(self):
        for far in range(2):
            for copy in self.final[far]:
                copy.wait_recv()
            rows_add(self.work.at[far, 0], 0, 128, self.work.at[far, 0], self.far_land.at[far, 0], self.far_land.at[far, 1])
            if far == 0:
                self.over = self.copies.remote(self.work.at[0, 0], self.y_land, self.across)

    def last(self, out):
        self.over.wait_recv()
        rows_add(out, 0, 128, self.work.at[1, 0], self.y_land)


def rows_add(out, first, rows, *terms):
    @pl.loop(0, rows // 16)
    def _(step):
        at = pl.ds(pl.multiple_of(step * 16, 16), 16)
        value = terms[0][at].astype(F32)
        for term in terms[1:]:
            value = value + term[at].astype(F32)
        out[at] = value.astype(out.dtype)


SCATTER_REMOTES, SCATTER_LOCALS = 8 + 4 + 4 + 1, 8
SCATTER_SCRATCH = [
    pltpu.VMEM((2, 4, 128, 1280), BF16),
    pltpu.VMEM((2, 4, 128, 1280), BF16),
    pltpu.VMEM((2, 2, 64, 1280), BF16),
    pltpu.VMEM((2, 2, 128, 1280), BF16),
    pltpu.VMEM((128, 1280), BF16),
]


def up_add(out, *terms):
    add_into(out, (), *terms, rows=(16, 10))


def scatter_kernel(
    parts, rows_in, cots_in, act_in, back_in, d_shared, hidden_rows, gain, cot, w_out_in, down_one,
    gate_sum, up_out, up_one, down_out, down_final, d_mixed, d_hidden, d_attn, gain_term,
    a, b, c, d, e, rows, cots, act, back, gate, up, down, land, w_out, d_routed, up_land, one_other,
    send, recv, own, load_sem, keep_sem,
):
    where = place()
    x, y, z, core = where
    x_peers = [device((x + 1) % 4, y, z, core), device((x + 3) % 4, y, z, core)]
    loads = [
        pltpu.make_async_copy(src, dst, load_sem.at[i])
        for i, (src, dst) in enumerate(
            (
                (rows_in.at[0], rows.at[0]), (back_in.at[0], back.at[0]), (rows_in.at[1], rows.at[1]),
                (back_in.at[1], back.at[1]), (act_in.at[1], act), (cots_in.at[1], cots), (w_out_in, w_out),
            )
        )
    ]
    for load in loads:
        load.start()
    greet(exp_peers(where) + x_peers + [device(x, (y // 2) * 2 + 1 - y % 2, z, core)])
    copies = Copies(send, recv, own)
    scatter = Scatter(copies, where, parts, a, b, c, d, e)
    hidden = act.shape[1]
    loads[0].wait()
    loads[1].wait()

    y_low = y % 2
    pair = device(x, (y // 2) * 2 + 1 - y_low, z, core)

    def term(dst, lanes, first, last):
        @pl.loop(first, last)
        def _(index):
            expert = index // 5
            at = pl.ds(pl.multiple_of((index % 5) * 256, 256), 256)
            dst[expert, at] = dot_tn(rows[expert, :, at], back[expert, :, lanes]).astype(BF16)

    def up_rows(chunk, which):
        return pl.ds(pl.multiple_of(chunk * 320 + which * 160, 160), 160)

    swap_one = copies.remote(down_one.at[half_rows(1 - y_low, 112)], one_other, pair)

    def gate_ring(expert):
        return RingSum(
            copies, x, x_peers[0], x_peers[1], lambda chunk, half: gate.at[expert, half_rows(2 * chunk + half, 160)],
            land.at[expert], None, up_add, resident=True,
        )

    term(gate, slice(0, hidden), 0, 5)
    rings = [gate_ring(0)]
    rings[0].raw()
    scatter.first()
    scatter.merge_rest()
    loads[2].wait()
    loads[3].wait()
    term(up, slice(hidden, 2 * hidden), 5, 10)
    over = [copies.remote(up.at[1, up_rows(chunk, 1 - y_low)], up_land.at[chunk], pair) for chunk in range(4)]
    term(gate, slice(0, hidden), 5, 10)
    rings.append(gate_ring(1))
    rings[1].raw()
    scatter.second()
    rings[0].forward()
    term(up, slice(hidden, 2 * hidden), 0, 5)
    keep_up = pltpu.make_async_copy(up.at[0], up_out, keep_sem.at[0])
    keep_up.start()
    loads[4].wait()
    loads[5].wait()

    @pl.loop(0, hidden // 128)
    def _(index):
        at = pl.ds(pl.multiple_of(index * 128, 128), 128)
        down[at] = dot_tn(act[:, at], cots[...]).astype(BF16)

    keep_down = pltpu.make_async_copy(down, down_out, keep_sem.at[1])
    keep_down.start()
    rings[1].forward()
    scatter.third()
    scatter.last(d_routed)
    grad, term_sum = normed_back(hidden_rows[...], gain[...].reshape(1, -1), d_shared[...] + d_routed[...])
    whole = cot[...].astype(F32) + grad
    d_hidden[...] = whole
    d_attn[...] = whole.astype(BF16)
    gain_term[...] = term_sum
    loads[6].wait()

    @pl.loop(0, 5)
    def _(index):
        value = dot_nt(d_attn[...], w_out[pl.ds(pl.multiple_of(index * 256, 256), 256)]).astype(BF16)
        d_mixed[2 * index] = value[:, :HEAD_DIM]
        d_mixed[2 * index + 1] = value[:, HEAD_DIM:]

    for chunk, copy in enumerate(over):
        copy.wait_recv()
        add_into(up_one.at[chunk], (), up.at[1, up_rows(chunk, y_low)], up_land.at[chunk], rows=(16, 10))
    for expert in range(2):
        rings[expert].finish([gate_sum.at[expert, 0:160], gate_sum.at[expert, 160:320]])
    swap_one.wait_recv()
    add_into(down_final, (), down_one.at[half_rows(y_low, 112)], one_other, rows=(16, 7))
    copies.drain()
    keep_up.wait()
    keep_down.wait()


def scatter_rows(parts, kept_rows, kept_cots, kept_act, kept_back, d_shared, hidden_rows, gain, cot, w_out, down_one, collective_id):
    width, hidden = kept_rows.shape[2], kept_act.shape[2]
    count = cot.shape[0]
    return pl.pallas_call(
        scatter_kernel,
        name="scatter_rows",
        out_shape=(
            jax.ShapeDtypeStruct((2, 320, hidden), BF16),
            jax.ShapeDtypeStruct((width, hidden), BF16),
            jax.ShapeDtypeStruct((4, 160, hidden), BF16),
            jax.ShapeDtypeStruct((hidden, width), BF16),
            jax.ShapeDtypeStruct((112, width), F32),
            jax.ShapeDtypeStruct((10, count, HEAD_DIM), BF16),
            jax.ShapeDtypeStruct((count, width), F32),
            jax.ShapeDtypeStruct((count, width), BF16),
            jax.ShapeDtypeStruct((1, width), F32),
        ),
        in_specs=[ANYWHERE] * 5 + [VMEM] * 4 + [ANYWHERE, VMEM],
        out_specs=(VMEM, ANYWHERE, VMEM, ANYWHERE) + (VMEM,) * 5,
        scratch_shapes=SCATTER_SCRATCH
        + [
            pltpu.VMEM(kept_rows.shape, BF16),
            pltpu.VMEM(kept_cots.shape[1:], BF16),
            pltpu.VMEM(kept_act.shape[1:], BF16),
            pltpu.VMEM(kept_back.shape, BF16),
            pltpu.VMEM((2, width, hidden), BF16),
            pltpu.VMEM((2, width, hidden), BF16),
            pltpu.VMEM((hidden, width), BF16),
            pltpu.VMEM((2, 6, 160, hidden), BF16),
            pltpu.VMEM(w_out.shape, BF16),
            pltpu.VMEM((count, width), F32),
            pltpu.VMEM((4, 160, hidden), BF16),
            pltpu.VMEM((112, width), BF16),
            pltpu.SemaphoreType.DMA((SCATTER_REMOTES + 17,)),
            pltpu.SemaphoreType.DMA((SCATTER_REMOTES + 17,)),
            pltpu.SemaphoreType.DMA((SCATTER_LOCALS,)),
            pltpu.SemaphoreType.DMA((7,)),
            pltpu.SemaphoreType.DMA((2,)),
        ],
        compiler_params=params(collective_id),
        cost_estimate=cost(10**10, 10**8),
    )(
        parts, kept_rows, kept_cots, kept_act, kept_back,
        d_shared, hidden_rows, gain, cot, w_out, down_one,
    )


def ctx_device(ctx):
    return (ctx, lax.axis_index("exp"))


def extra_owner(head):
    core = lax.axis_index("exp") % 2
    return 3 * core if head == 8 else 5 + core


def owns_extra(ctx):
    return (ctx == extra_owner(8)) | (ctx == extra_owner(9))


def extra_head(ctx):
    return 8 + (ctx == extra_owner(9)).astype(jnp.int32)


class Exchange:
    def __init__(self, send, recv, own):
        self.send, self.recv, self.own = send, recv, own
        self.ctx = lax.axis_index("ctx")

    def copy(self, src, dst, slot, d):
        return pltpu.make_async_remote_copy(
            src_ref=src,
            dst_ref=dst,
            send_sem=self.send.at[slot, d],
            recv_sem=self.recv.at[slot, d],
            device_id=ctx_device((self.ctx + d) % 8),
            device_id_type=MESH,
        )


class ToOwners:
    def __init__(self, exchange, block, land):
        self.exchange, self.block, self.land, self.ctx = exchange, block, land, exchange.ctx

    def mine(self, slot, head):
        return pltpu.make_async_copy(self.block(head), self.land(slot, self.ctx), self.exchange.own.at[slot])

    def start(self, head):
        slot, owner = (0, head) if head < 8 else (1, extra_owner(head))
        d = (owner + 8 - self.ctx) % 8

        @pl.when(d == 0)
        def _():
            self.mine(slot, head).start()

        @pl.when(d != 0)
        def _():
            self.exchange.copy(self.block(head), self.land(slot, self.ctx), slot, d).start()

    def any(self, slot, d):
        return self.exchange.copy(self.block(0), self.land(slot, self.ctx), slot, d)

    def arrived(self):
        self.mine(0, 0).wait()
        for d in range(1, 8):
            self.any(0, d).wait_recv()

        @pl.when(owns_extra(self.ctx))
        def _():
            self.mine(1, 0).wait()
            for d in range(1, 8):
                self.any(1, d).wait_recv()

    def sent(self):
        for d in range(1, 8):
            self.any(0, d).wait_send()

            @pl.when(owns_extra((self.ctx + d) % 8))
            def _():
                self.any(1, d).wait_send()


class Home:
    def __init__(self, exchange, block, land):
        self.exchange, self.block, self.land = exchange, block, land
        self.ctx = exchange.ctx

    def head(self, slot):
        return self.ctx if slot == 0 else extra_head(self.ctx)

    def start(self, slot):
        for d in range(1, 8):
            self.exchange.copy(self.block(slot, (self.ctx + d) % 8), self.land(self.head(slot)), slot, d).start()
        self.mine(slot).start()

    def mine(self, slot):
        return pltpu.make_async_copy(
            self.block(slot, self.ctx), self.land(self.head(slot)), self.exchange.own.at[slot]
        )

    def finish(self):
        self.mine(0).wait()
        for d in range(1, 8):
            copy = self.exchange.copy(self.block(0, 0), self.land(0), 0, d)
            copy.wait_send()
            copy.wait_recv()

            @pl.when(owns_extra((self.ctx + 8 - d) % 8))
            def _():
                self.exchange.copy(self.block(1, 0), self.land(0), 1, d).wait_recv()

        @pl.when(owns_extra(self.ctx))
        def _():
            self.mine(1).wait()
            for d in range(1, 8):
                self.exchange.copy(self.block(1, 0), self.land(0), 1, d).wait_send()


def attend_kernel(
    length, cot, routes, route_gates, w_query, w_key, w_value, w_out_in, tokens, attn_gain, ffn_gain, cos, sin,
    gate_w, up_w, down_w, spread,
    normed_one, mixed, heads, hidden, slot_rows, slot_cots, meta, weight, shared_out, d_shared, early,
    sent_cot, qkv, weights, land, result, home, w_out, rows, every, cots_in, gate, up, down, spread_in,
    filled_rows, filled_cots, lines, act, d_gates, pair_act, pair_gates, right, act_left, panels,
    s1, r1, o1, s2, r2, o2, s3, r3, o3, s4, r4, o4, load_sem, weight_sem, shared_sem, keep_sem, early_sem,
):
    def fetch(index):
        return [
            pltpu.make_async_copy(source.at[:, 256 * index : 256 * index + 256], weights.at[index, kind], weight_sem.at[index, kind])
            for kind, source in enumerate((w_query, w_key, w_value))
        ]

    pairs_of_heads = (4, 0, 1, 2, 3)
    for index in pairs_of_heads:
        for copy in fetch(index):
            copy.start()
    load = pltpu.make_async_copy(w_out_in, w_out, load_sem)
    load.start()
    loads = [
        pltpu.make_async_copy(src, dst, shared_sem.at[i])
        for i, (src, dst) in enumerate(((gate_w, gate), (up_w, up), (down_w, down), (spread, spread_in)))
    ]
    for copy in loads:
        copy.start()
    where = place()
    ctx = lax.axis_index("ctx")
    greet([ctx_device((ctx + d) % 8) for d in range(1, 8)] + exp_peers(where))
    copies = Copies(s3, r3, o3)
    expert = lax.broadcasted_iota(jnp.int32, (32, 128), 0)
    table = jnp.zeros((32, 128), F32)
    for choice in range(routes.shape[0]):
        table += jnp.where(expert == routes[choice], route_gates[choice], 0.0)
    position = lax.broadcasted_iota(jnp.int32, (32, 128), 1) + ctx * 128
    table = jnp.where(position < length[0], table, 0.0)
    high = table.astype(BF16)
    low = (table - high.astype(F32)).astype(BF16)
    sent_cot[0:128] = cot[...]
    sent_cot[128:144] = jnp.zeros((16, cot.shape[1]), BF16)
    for index, part in enumerate((high[0:16], high[16:32], low[0:16], low[16:32])):
        sent_cot[128:144, index * 128 : index * 128 + 128] = part
    first = Gather(copies, where, sent_cot, cots_in, 80, 144, 80)
    owners = ToOwners(Exchange(s1, r1, o1), lambda head: qkv.at[head], lambda slot, c: land.at[slot, :, c])
    normed_one[...] = normed(tokens[...].astype(F32), attn_gain[...].reshape(1, -1)).astype(BF16)
    positions = pl.ds(pl.multiple_of(ctx * 128, 128), 128)
    for index in pairs_of_heads:
        for copy in fetch(index):
            copy.wait()
        parts = [dot(normed_one[...], weights[index, kind]) for kind in range(3)]
        for half in range(2):
            head, lanes = 2 * index + half, slice(half * HEAD_DIM, (half + 1) * HEAD_DIM)
            qkv[head, 0] = turned(parts[0][:, lanes], cos[positions], sin[positions]).astype(BF16)
            qkv[head, 1] = turned(parts[1][:, lanes], cos[positions], sin[positions]).astype(BF16)
            qkv[head, 2] = parts[2][:, lanes].astype(BF16)
            owners.start(head)
    back = Home(Exchange(s2, r2, o2), lambda slot, c: result.at[slot, c], lambda head: home.at[head])
    keep = pltpu.make_async_copy(land, heads, o3.at[1])

    def run(slot, blocks):
        for block in blocks:
            width = (block + 1) * 128
            query = land[slot, 0, block]
            key = land[slot, 1, 0 : block + 1].reshape(width, HEAD_DIM)
            value = land[slot, 2, 0 : block + 1].reshape(width, HEAD_DIM)
            row = lax.broadcasted_iota(jnp.int32, (width, 128), 0)
            column = lax.broadcasted_iota(jnp.int32, (width, 128), 1) + block * 128
            scores = jnp.where(
                (row <= column) & (row < length[0]), dot_nt(key, query) * SCALE, -1e30
            )
            weights = jnp.exp(scores - jnp.max(scores, axis=0, keepdims=True))
            probs = weights * (1.0 / jnp.sum(weights, axis=0, keepdims=True))
            result[slot, block] = dot_tn(probs.astype(BF16), value).astype(BF16)

    first.near()
    first.far()
    owners.arrived()
    run(0, range(8))
    back.start(0)

    @pl.when(owns_extra(ctx))
    def _():
        run(1, range(8))
        back.start(1)

    @pl.when(jnp.logical_not(owns_extra(ctx)))
    def _():
        land[1] = jnp.zeros_like(land[1])

    keep.start()
    first.middle()
    first.third()
    first.mine.wait()
    back.finish()
    for head in range(10):
        mixed[:, head * HEAD_DIM : (head + 1) * HEAD_DIM] = home[head]
    load.wait()

    @pl.loop(0, 5)
    def _(index):
        at = pl.ds(pl.multiple_of(index * 256, 256), 256)
        hidden[:, at] = tokens[:, at].astype(F32) + dot(mixed[...], w_out[:, at])

    rows[...] = normed(hidden[...], ffn_gain[...].reshape(1, -1)).astype(BF16)

    core, y_half = where[3], where[1] // 2
    me = lax.axis_index("exp")
    other = me + 1 - 2 * core
    more = Copies(s4, r4, o4)
    gather = Gather(more, where, rows, every, 64, 80, 48)
    first.last()
    shared_out[...] = jnp.zeros_like(shared_out)
    d_shared[...] = jnp.zeros_like(d_shared)

    def shared(first, last):
        @pl.loop(first, last)
        def _(step):
            at = pl.ds(pl.multiple_of(step * 128, 128), 128)
            value = rows[...]
            gate_pre, up_pre = dot(value, gate[:, at]), dot(value, up[:, at])
            silu, slope = gated(gate_pre, up_pre)
            activated = (silu * up_pre).astype(BF16)
            act[:, at] = activated
            shared_out[...] += dot(activated, down[at])
            d_act = dot_nt(cot[...], down[at])
            gate_back = (d_act * up_pre * slope).astype(BF16)
            up_back = (d_act * silu).astype(BF16)
            d_gates[0, :, at] = gate_back
            d_gates[1, :, at] = up_back
            d_shared[...] += dot_nt(gate_back, gate[:, at]) + dot_nt(up_back, up[:, at])

    def meta_lines():
        @pl.loop(0, 16)
        def _(block):
            high = cots_in[block, 128:144, pl.ds(pl.multiple_of(y_half * 128, 128), 128)].astype(F32)
            low = cots_in[block, 128:144, pl.ds(pl.multiple_of(256 + y_half * 128, 128), 128)].astype(F32)
            line = lax.broadcasted_iota(jnp.int32, (16, 128), 0)
            for expert in range(2):
                mine = line == 2 * (me % 8) + expert
                meta[block, expert : expert + 1] = jnp.sum(jnp.where(mine, high + low, 0.0), axis=0, keepdims=True)

        lines[...] = slot_lines(meta).reshape(16, 2, 128)

    def hot(block):
        slot = lax.broadcasted_iota(jnp.int32, (SLOTS, 128), 0).astype(F32)
        return [jnp.where(slot == lines[block, e : e + 1], 1.0, 0.0) for e in range(2)]

    def fill(block, source, out, column=None):
        value = dot(jnp.concatenate(hot(block), axis=0).astype(BF16), source)
        if column is not None:
            value = value * column
        value = value.astype(BF16)
        at = pl.ds(pl.multiple_of(block * SLOTS, SLOTS), SLOTS)
        for expert in range(2):
            out[expert, at] = value[expert * SLOTS : (expert + 1) * SLOTS]

    def fill_cots(block):
        column = jnp.concatenate(
            [jnp.sum(one * meta[block, e : e + 1], axis=1, keepdims=True) for e, one in enumerate(hot(block))], axis=0
        )
        at = pl.ds(pl.multiple_of(block * SLOTS, SLOTS), SLOTS)
        for expert in range(2):
            weight[expert, at] = jnp.broadcast_to(column[expert * SLOTS : (expert + 1) * SLOTS], (SLOTS, 128))
        fill(block, cots_in[block, 0:128], filled_cots, column)

    def fill_rows(far, dz):
        own_block = gather.shard(far, dz)
        for block in (own_block, own_block + 1 - 2 * core):
            fill(block, every[block], filled_rows)

    meta_lines()

    @pl.loop(0, 8, unroll=4)
    def _(block):
        fill_cots(block)

    for load in loads[:3]:
        load.wait()
    gather.near()
    gather.far()
    shared(0, 7)
    pair = device(where[0], where[1], where[2], 1 - core)
    from_pair = [more.remote(act, pair_act, pair), more.remote(d_gates.at[1 - core], pair_gates, pair)]
    gather.middle()

    @pl.loop(8, 16, unroll=4)
    def _(block):
        fill_cots(block)

    gather.third()
    keep_cots = pltpu.make_async_copy(filled_cots, slot_cots, keep_sem.at[0])
    keep_cots.start()
    gather.pairs_arrived(4)
    for copy in from_pair:
        copy.wait_recv()
    loads[3].wait()
    right[0:128, 0:896] = d_gates[core]
    right[128:256, 0:896] = pair_gates[...]
    at = pl.ds(pl.multiple_of(core * 640, 128), 640)
    right[0:128, 896:1536] = cot[:, at]
    right[128:256, 896:1536] = cots_in[other, 0:128, at]
    act_left[...] = dot(jnp.concatenate([act[...], pair_act[...]], axis=0), spread_in[...]).astype(BF16)

    def store(index):
        return pltpu.make_async_copy(
            panels.at[index], early.at[:, pl.ds(pl.multiple_of(index * 256, 256), 256)], early_sem.at[index]
        )

    @pl.loop(0, 5)
    def _(index):
        at = pl.ds(pl.multiple_of(index * 256, 256), 256)
        value = dot_tn(jnp.concatenate([rows[:, at], every[other, :, at]], axis=0), right[:, 0:896])
        for panel in range(7):
            panels[index, panel] = value[:, panel * 128 : panel * 128 + 128].astype(BF16)
        value = dot_tn(act_left[:, at], right[:, 896:1536])
        for panel in range(5):
            panels[index, 7 + panel] = value[:, panel * 128 : panel * 128 + 128].astype(BF16)
        store(index).start()

    gather.mine.wait()
    gather.sides()
    gather.pairs_arrived(6)
    for far, dz in ((False, 0), (False, -1), (False, 1), (True, 0), (False, 2)):
        fill_rows(far, dz)
    gather.pairs_arrived(10)
    for dz in (-1, 1):
        fill_rows(True, dz)
    gather.last()
    fill_rows(True, 2)
    keep_rows = pltpu.make_async_copy(filled_rows, slot_rows, keep_sem.at[1])
    keep_rows.start()
    owners.sent()
    keep.wait()
    copies.drain()
    more.drain()
    keep_cots.wait()
    keep_rows.wait()
    for index in range(5):
        store(index).wait()


def exchange_semaphores():
    return [
        pltpu.SemaphoreType.DMA((2, 8)),
        pltpu.SemaphoreType.DMA((2, 8)),
        pltpu.SemaphoreType.DMA((2,)),
    ]


def attend(
    length, cot, routes, route_gates, w_query, w_key, w_value, w_out, tokens, attn_gain, ffn_gain, cos, sin,
    gate_w, up_w, down_w, collective_id,
):
    rows, width = tokens.shape
    hidden = gate_w.shape[1]
    spread = np.zeros((128, 7, 128, 10), np.float32)
    for group in range(128):
        spread[group, np.arange(7), group, np.arange(7)] = 1.0
    spread = jnp.asarray(spread.reshape(hidden, width), BF16)
    return pl.pallas_call(
        attend_kernel,
        name="attend",
        out_shape=(
            jax.ShapeDtypeStruct((rows, width), BF16),
            jax.ShapeDtypeStruct((rows, width), BF16),
            jax.ShapeDtypeStruct((2, 3, 8, rows, HEAD_DIM), BF16),
            jax.ShapeDtypeStruct((rows, width), F32),
            jax.ShapeDtypeStruct((2, SLOT_ROWS, width), BF16),
            jax.ShapeDtypeStruct((2, SLOT_ROWS, width), BF16),
            jax.ShapeDtypeStruct((16, 2, 128), F32),
            jax.ShapeDtypeStruct((2, SLOT_ROWS, 128), F32),
            jax.ShapeDtypeStruct((rows, width), F32),
            jax.ShapeDtypeStruct((rows, width), F32),
            jax.ShapeDtypeStruct((12, width, 128), BF16),
        ),
        in_specs=[SMEM] + [VMEM] * 3 + [ANYWHERE] * 4 + [VMEM] * 5 + [ANYWHERE] * 4,
        out_specs=(VMEM, VMEM, ANYWHERE, VMEM, ANYWHERE, ANYWHERE, VMEM, VMEM, VMEM, VMEM, ANYWHERE),
        scratch_shapes=[
            pltpu.VMEM((rows + 16, width), BF16),
            pltpu.VMEM((10, 3, rows, HEAD_DIM), BF16),
            pltpu.VMEM((5, 3, width, 256), BF16),
            pltpu.VMEM((2, 3, 8, rows, HEAD_DIM), BF16),
            pltpu.VMEM((2, 8, rows, HEAD_DIM), BF16),
            pltpu.VMEM((10, rows, HEAD_DIM), BF16),
            pltpu.VMEM(w_out.shape, BF16),
            pltpu.VMEM((rows, width), BF16),
            pltpu.VMEM((16, rows, width), BF16),
            pltpu.VMEM((16, rows + 16, width), BF16),
            pltpu.VMEM(gate_w.shape, BF16),
            pltpu.VMEM(up_w.shape, BF16),
            pltpu.VMEM(down_w.shape, BF16),
            pltpu.VMEM(spread.shape, BF16),
            pltpu.VMEM((2, SLOT_ROWS, width), BF16),
            pltpu.VMEM((2, SLOT_ROWS, width), BF16),
            pltpu.VMEM((16, 2, 128), F32),
            pltpu.VMEM((rows, hidden), BF16),
            pltpu.VMEM((2, rows, hidden), BF16),
            pltpu.VMEM((rows, hidden), BF16),
            pltpu.VMEM((rows, hidden), BF16),
            pltpu.VMEM((2 * rows, 1536), BF16),
            pltpu.VMEM((2 * rows, width), BF16),
            pltpu.VMEM((5, 12, 256, 128), BF16),
        ]
        + exchange_semaphores()
        + exchange_semaphores()
        + [
            pltpu.SemaphoreType.DMA((GATHER_REMOTES,)),
            pltpu.SemaphoreType.DMA((GATHER_REMOTES,)),
            pltpu.SemaphoreType.DMA((2,)),
            pltpu.SemaphoreType.DMA((GATHER_REMOTES + 8,)),
            pltpu.SemaphoreType.DMA((GATHER_REMOTES + 8,)),
            pltpu.SemaphoreType.DMA((1,)),
            pltpu.SemaphoreType.DMA,
            pltpu.SemaphoreType.DMA((5, 3)),
            pltpu.SemaphoreType.DMA((4,)),
            pltpu.SemaphoreType.DMA((2,)),
            pltpu.SemaphoreType.DMA((5,)),
        ],
        compiler_params=params(collective_id),
        cost_estimate=cost(10**9, 10**8),
    )(
        length, cot, routes, route_gates, w_query, w_key, w_value, w_out, tokens, attn_gain, ffn_gain, cos, sin,
        gate_w, up_w, down_w, spread,
    )


def attend_back_kernel(
    d_mixed, heads, length, cos, sin, parts, up, up_one, gate, first, d_attn, normed_one, mixed, tokens, gain, d_hidden,
    ffn_term, w_query_in, w_key_in, w_value_in, down,
    input_grad, routed, up_final, gate_out, dense_out, up_out, down_out,
    land, kept, d_key, d_value, result, home, a, b, c, d, e, up_land, up_work, one_land, gate_other, first_land,
    pair_rows, d_qkv, pair_qkv, right, out_right, out_terms, out_land, weights, total, late, up_sum, first_sum, second,
    z_land, f_land, y_land, y_sum, x_land, u_land, v_land, v_sum, w_land, t_land, tz_land, t_sum, tx_land,
    gains, gx_land, gx_sum, gy_land, sums, stage, final_land, up_other, d_land, d_work, d_other,
    s1, r1, o1, s2, r2, o2, s3, r3, o3, s4, r4, o4, load_sem, weight_sem,
):
    where = place()
    x, y, z, core = where
    ctx = lax.axis_index("ctx")
    x_peers = [device((x + 1) % 4, y, z, core), device((x + 3) % 4, y, z, core)]
    load_heads = pltpu.make_async_copy(heads, kept, load_sem)
    load_heads.start()

    def fetch(index):
        rows = slice(256 * index, 256 * index + 256)
        return [
            pltpu.make_async_copy(source.at[rows], weights.at[index % 2, kind], weight_sem.at[index % 2, kind])
            for kind, source in enumerate((w_query_in, w_key_in, w_value_in))
        ]

    for index in range(2):
        for copy in fetch(index):
            copy.start()
    spot = z * 2 + core
    spot_peers = [device(x, y, ((spot + d) % 8) // 2, (spot + d) % 2) for d in range(1, 8)]
    more_peers = [
        device(x, y, (z + 2) % 4, core), device(x, y, (z + 2) % 4, 1 - core),
        device(x, y, (z + 1) % 4, 1 - core), device(x, y, (z + 3) % 4, 1 - core),
    ]
    y_peers = [device(x, (y + step) % 4, z, core) for step in (1, 2, 3)]
    pair_peer = device(x, (y // 2) * 2 + 1 - y % 2, z, core)
    cross_peer = device(x, (y // 2) * 2 + 2 + 1 - y % 2 - 4 * (y // 2), z, core)
    greet([ctx_device((ctx + step) % 8) for step in range(1, 8)] + exp_peers(where) + [cross_peer] + more_peers)
    owners = ToOwners(Exchange(s1, r1, o1), lambda head: d_mixed.at[head], lambda slot, at: land.at[slot, at])
    for head in (8, 9, 0, 1, 2, 3, 4, 5, 6, 7):
        owners.start(head)
    copies = Copies(s3, r3, o3)
    scatter = Scatter(copies, where, parts, a, b, c, d, e)
    back = Home(Exchange(s2, r2, o2), lambda slot, at: result.at[slot, :, at], lambda head: home.at[:, head])
    y_low = y % 2

    def one_add(out, *terms):
        add_into(out, (), *terms, rows=(16, 5))

    ring_one = RingSum(
        copies, x, x_peers[0], x_peers[1], lambda chunk, half: up_one.at[chunk, 80 * half : 80 * half + 80],
        one_land, None, one_add, resident=True,
    )
    ring = RingSum(
        copies, x, x_peers[0], x_peers[1], lambda chunk, half: up.at[half_rows(2 * chunk + half, 160)],
        up_land, up_work, up_add,
    )
    swap = copies.remote(gate.at[:, half_rows(1 - y_low, 160)], gate_other, pair_peer)
    z_peers = [device(x, y, (z + 1) % 4, core), device(x, y, (z + 3) % 4, core)]

    block_add = add_blocks((2, 4))
    pair = device(x, y, z, 1 - core)
    pairs = [copies.remote(src, pair_rows.at[i], pair) for i, src in enumerate((normed_one, mixed, d_attn))]
    for copy in pairs:
        copy.wait_recv()
    at = pl.ds(pl.multiple_of(core * 640, 128), 640)
    out_right[0:128] = d_attn[:, at]
    out_right[128:256] = pair_rows[2, :, at]

    def spread_blocks(value, tile, panels):
        for lane, ref in enumerate(panels):
            for block in range(8):
                part = value[80 * block : 80 * block + 80, lane * 128 : lane * 128 + 128]
                ref[2 * tile + block // 4, block % 4] = part.astype(BF16)

    @pl.loop(0, 2)
    def _(tile):
        at = pl.ds(pl.multiple_of(tile * 640, 128), 640)
        value = dot_tn(jnp.concatenate([mixed[:, at], pair_rows[1, :, at]], axis=0), out_right[...])
        spread_blocks(value, tile, [out_terms.at[panel] for panel in range(4)] + [late.at[3, 3]])

    scatter.first()
    load_heads.wait()
    owners.arrived()

    def run(slot):
        d_key[...] = jnp.zeros_like(d_key)
        d_value[...] = jnp.zeros_like(d_value)
        for block in range(8):
            width = (block + 1) * 128
            query, upstream = kept[slot, 0, block], land[slot, block]
            key = kept[slot, 1, 0 : block + 1].reshape(width, HEAD_DIM)
            value = kept[slot, 2, 0 : block + 1].reshape(width, HEAD_DIM)
            row = lax.broadcasted_iota(jnp.int32, (width, 128), 0)
            column = lax.broadcasted_iota(jnp.int32, (width, 128), 1) + block * 128
            scores = jnp.where(
                (row <= column) & (row < length[0]), dot_nt(key, query) * SCALE, -1e30
            )
            weight = jnp.exp(scores - jnp.max(scores, axis=0, keepdims=True))
            probs = weight * (1.0 / jnp.sum(weight, axis=0, keepdims=True))
            d_probs = dot_nt(value, upstream)
            delta = jnp.sum(probs * d_probs, axis=0, keepdims=True)
            d_scores = (probs * (d_probs - delta)).astype(BF16)
            rows = slice(block * 128, block * 128 + 128)
            d_query = dot_tn(d_scores, key) * SCALE
            result[slot, 0, block] = turned(d_query, cos[rows], sin[rows]).astype(BF16)
            d_key[0:width] += dot(d_scores, query)
            d_value[0:width] += dot(probs.astype(BF16), upstream)
        for block in range(8):
            rows = slice(block * 128, block * 128 + 128)
            result[slot, 1, block] = turned(d_key[rows] * SCALE, cos[rows], sin[rows]).astype(BF16)
            result[slot, 2, block] = d_value[rows].astype(BF16)
        back.start(slot)

    run(0)
    scatter.merge_rest()
    scatter.second()

    @pl.when(owns_extra(ctx))
    def _():
        run(1)

    first_copies = [
        copies.remote(first.at[:, :, order((y + step) % 4)], first_land.at[step - 1], y_peers[step - 1])
        for step in (1, 2, 3)
    ]
    ring_one.raw()
    ring_one.forward()
    ring.raw()
    outs = RingSum(
        copies, z, z_peers[0], z_peers[1], lambda chunk, half: out_terms.at[chunk, 2 * half : 2 * half + 2],
        out_land, None, block_add, resident=True,
    )
    outs.raw()
    ring.forward()
    scatter.third()
    back.finish()
    outs.forward()
    for head in range(10):
        for kind in range(3):
            at = kind * 1280 + head * HEAD_DIM
            d_qkv[:, at : at + HEAD_DIM] = home[kind, head]
    swap_qkv = copies.remote(d_qkv, pair_qkv, pair)
    for index in range(5):
        for copy in fetch(index):
            copy.wait()
        value = dot_nt(d_qkv[:, 0:1280], weights[index % 2, 0])
        value += dot_nt(d_qkv[:, 1280:2560], weights[index % 2, 1])
        value += dot_nt(d_qkv[:, 2560:3840], weights[index % 2, 2])
        total[:, 256 * index : 256 * index + 256] = value
        if index + 2 < 5:
            for copy in fetch(index + 2):
                copy.start()

    swap_qkv.wait_recv()
    at = pl.ds(pl.multiple_of(core * 1920, 128), 1920)
    right[0:128] = d_qkv[:, at]
    right[128:256] = pair_qkv[:, at]

    @pl.loop(0, 2)
    def _(tile):
        at = pl.ds(pl.multiple_of(tile * 640, 128), 640)
        left = jnp.concatenate([normed_one[:, at], pair_rows[0, :, at]], axis=0)
        for group in range(5):
            value = dot_tn(left, right[:, 384 * group : 384 * group + 384])
            spread_blocks(value, tile, [late.at[p // 4, p % 4] for p in range(3 * group, 3 * group + 3)])

    last = Copies(s4, r4, o4)

    def direct(part, me, land, peers):
        return [last.remote(part((me + d) % 4), land.at[d - 1], peers[d - 1]) for d in (1, 2, 3)]

    def landed(arrivals):
        for copy in arrivals:
            copy.wait_recv()

    all_z = [z_peers[0], more_peers[0], z_peers[1]]
    all_x = [x_peers[0], device((x + 2) % 4, y, z, core), x_peers[1]]

    def z_ring(panel):
        return RingSum(
            last, z, z_peers[0], z_peers[1], lambda chunk, half: late.at[chunk, panel, 2 * half : 2 * half + 2],
            z_land.at[panel], None, block_add, resident=True,
        )

    ring_a, ring_b = z_ring(0), z_ring(1)
    ring_a.raw()
    tall = RingSum(
        last, y, y_peers[0], y_peers[2], lambda chunk, half: late.at[2 * half : 2 * half + 2, 3, :, order(chunk)],
        t_land, None, block_add, resident=True,
    )
    tall.raw()
    side = RingSum(
        last, x, x_peers[0], x_peers[1], lambda chunk, half: late.at[2 * half : 2 * half + 2, 2, chunk],
        u_land, None, block_add, resident=True,
    )
    side.raw()

    grad, term = normed_back(tokens[...].astype(F32), gain[...].reshape(1, -1), total[...])
    input_grad[...] = d_hidden[...] + grad
    column = lax.broadcasted_iota(jnp.int32, (128, 1280), 1)
    group = lax.broadcasted_iota(jnp.int32, (128, 1280), 0)
    inside = (column >= group * 10) & (column < group * 10 + 10)
    rest = lax.broadcasted_iota(jnp.int32, (1280, 128), 0) % 10
    lane = lax.broadcasted_iota(jnp.int32, (1280, 128), 1)
    lines = jnp.zeros((128, 128), F32)
    for offset, values in ((0, term), (10, ffn_term[...])):
        spots = jnp.where(inside, values, 0.0)
        high = spots.astype(BF16)
        low = (spots - high.astype(F32)).astype(BF16)
        pick = jnp.where(lane == rest + offset, 1.0, 0.0).astype(BF16)
        lines += dot(high, pick) + dot(low, pick)
    gains[...] = lines.reshape(4, 4, 8, 128)
    gain_x = direct(lambda c: gains.at[c], x, gx_land, all_x)

    def down_add(out, *terms):
        add_into(out, (), *terms, rows=(16, 7))

    downs = RingSum(
        last, x, x_peers[0], x_peers[1], lambda c, h: down.at[half_rows(2 * c + h, 112)], d_land, d_work, down_add
    )
    downs.raw()
    scatter.last(routed)
    outs.finish([second.at[0:2], second.at[2:4]])
    y_copies = {0: direct(lambda c: second.at[:, order(c)], y, y_land.at[0], y_peers)}
    ring_a.forward()
    ring_b.raw()
    tall.forward()
    for copy in first_copies:
        copy.wait_recv()
    add_into(first_sum, (3, 4), first.at[:, :, order(y)], first_land.at[0], first_land.at[1], first_land.at[2])
    x_copies = {3: direct(lambda c: first_sum.at[:, c], x, f_land, all_x)}
    ring_b.forward()
    swap.wait_recv()
    add_into(gate_out, (2,), gate.at[:, half_rows(y_low, 160)], gate_other, rows=(16, 10))
    ring_one.finish([up_final.at[0:80], up_final.at[80:160]])
    ring.finish([up_sum.at[0], up_sum.at[1]])
    swap_up = last.remote(up_sum.at[1 - y_low], up_other, pair_peer)
    side.forward()
    landed(gain_x)
    gx_sum[...] = gains[x] + gx_land[0] + gx_land[1] + gx_land[2]
    gain_y = direct(lambda c: gx_sum.at[order(c)], y, gy_land, y_peers)
    downs.forward()

    def start_x(t, mine):
        landed(y_copies[t])
        add_into(y_sum.at[t], (4,), mine, y_land.at[t, 0], y_land.at[t, 1], y_land.at[t, 2])
        x_copies[t] = direct(lambda c: y_sum.at[t, c], x, x_land.at[t], all_x)

    ring_a.finish(ring_a.own[2:4])
    y_copies[1] = direct(lambda c: late.at[z, 0, :, order(c)], y, y_land.at[1], y_peers)
    tall.finish(tall.own[2:4])
    tall_z = direct(lambda c: late.at[c, 3, :, order(y)], z, tz_land, all_z)
    start_x(0, second.at[:, order(y)])
    ring_b.finish(ring_b.own[2:4])
    y_copies[2] = direct(lambda c: late.at[z, 1, :, order(c)], y, y_land.at[2], y_peers)
    side.finish(side.own[2:4])
    side_z = direct(lambda c: late.at[c, 2, x], z, v_land, all_z)
    start_x(1, late.at[z, 0, :, order(y)])
    landed(tall_z)
    add_into(t_sum, (4,), late.at[z, 3, :, order(y)], tz_land.at[0], tz_land.at[1], tz_land.at[2])
    tall_x = direct(lambda c: t_sum.at[c], x, tx_land, all_x)
    start_x(2, late.at[z, 1, :, order(y)])
    landed(side_z)
    add_into(v_sum, (4,), late.at[z, 2, x], v_land.at[0], v_land.at[1], v_land.at[2])
    side_y = direct(lambda c: v_sum.at[order(c)], y, w_land, y_peers)
    downs.finish([d_work.at[2], d_work.at[3]])
    swap_down = last.remote(d_work.at[2 + 1 - y_low], d_other, pair_peer)
    swap_up.wait_recv()
    add_into(up_out, (), up_sum.at[y_low], up_other, rows=(16, 10))

    def summed(panel, first_part, land, *index):
        value = first_part.astype(F32)
        for d in range(3):
            value = value + land[(d,) + index].astype(F32)
        sums[panel, 0:80] = value
        sums[panel, 80:96] = jnp.zeros((16, 128), F32)

    landed(gain_y)
    both_gains = gx_sum[order(y)] + gy_land[0] + gy_land[1] + gy_land[2]
    landed(x_copies[3])
    for panel in range(3):
        summed(panel, first_sum[panel, x], f_land, panel)
    for t in range(3):
        landed(x_copies[t])
        summed(3 + t, y_sum[t, x], x_land.at[t])
    landed(tall_x)
    summed(7, t_sum[x], tx_land)
    landed(side_y)
    summed(6, v_sum[order(y)], w_land)
    for j in range(8):
        for panel in range(8):
            stage[j, panel] = sums[panel, 10 * j : 10 * j + 16]
        stage[j, 0, 10:11] = both_gains[j : j + 1]
    finals = [
        last.remote(stage.at[(spot + d) % 8], final_land.at[d], spot_peers[d - 1]) for d in range(1, 8)
    ]
    swap_down.wait_recv()
    add_into(down_out, (), d_work.at[2 + y_low], d_other, rows=(16, 7))
    dense_out[spot] = stage[spot]
    for d, copy in enumerate(finals):
        copy.wait_recv()
        dense_out[(spot + 7 - d) % 8] = final_land[d + 1]
    owners.sent()
    copies.drain()
    last.drain()


def attend_back(
    d_mixed, heads, length, cos, sin, parts, up, up_one, gate, first, d_attn, normed_one, mixed, tokens, gain, d_hidden,
    ffn_term, w_query, w_key, w_value, down, collective_id,
):
    rows, width = tokens.shape
    hidden = up.shape[1]
    ring_land = pltpu.VMEM((6, 2, 4, 80, 128), BF16)
    return pl.pallas_call(
        attend_back_kernel,
        name="attend_back",
        out_shape=(
            jax.ShapeDtypeStruct((rows, width), F32),
            jax.ShapeDtypeStruct((rows, width), F32),
            jax.ShapeDtypeStruct((160, hidden), F32),
            jax.ShapeDtypeStruct((2, 160, hidden), F32),
            jax.ShapeDtypeStruct((8, 8, 16, 128), F32),
            jax.ShapeDtypeStruct((160, hidden), F32),
            jax.ShapeDtypeStruct((112, width), F32),
        ),
        in_specs=[ANYWHERE, ANYWHERE, SMEM, VMEM, VMEM, ANYWHERE, ANYWHERE, VMEM, VMEM, VMEM]
        + [VMEM] * 7
        + [ANYWHERE] * 4,
        out_specs=(VMEM,) * 7,
        scratch_shapes=[
            pltpu.VMEM((2, 8, 128, HEAD_DIM), BF16),
            pltpu.VMEM((2, 3, 8, 128, HEAD_DIM), BF16),
            pltpu.VMEM((1024, HEAD_DIM), F32),
            pltpu.VMEM((1024, HEAD_DIM), F32),
            pltpu.VMEM((2, 3, 8, 128, HEAD_DIM), BF16),
            pltpu.VMEM((3, 10, 128, HEAD_DIM), BF16),
        ]
        + SCATTER_SCRATCH
        + [
            pltpu.VMEM((6, 160, hidden), BF16),
            pltpu.VMEM((4, 160, hidden), BF16),
            pltpu.VMEM((6, 80, hidden), BF16),
            pltpu.VMEM((2, 160, hidden), BF16),
            pltpu.VMEM((3, 3, 4, 80, 128), BF16),
            pltpu.VMEM((3, rows, width), BF16),
            pltpu.VMEM((rows, 3 * width), BF16),
            pltpu.VMEM((rows, 3 * width), BF16),
            pltpu.VMEM((2 * rows, 1920), BF16),
            pltpu.VMEM((2 * rows, 640), BF16),
            pltpu.VMEM((4, 4, 4, 80, 128), BF16),
            ring_land,
            pltpu.VMEM((2, 3, 256, width), BF16),
            pltpu.VMEM((rows, width), F32),
            pltpu.VMEM((4, 4, 4, 4, 80, 128), BF16),
            pltpu.VMEM((2, 160, hidden), BF16),
            pltpu.VMEM((3, 4, 80, 128), BF16),
            pltpu.VMEM((4, 4, 80, 128), BF16),
            pltpu.VMEM((2, 6, 2, 4, 80, 128), BF16),
            pltpu.VMEM((3, 3, 80, 128), BF16),
            pltpu.VMEM((3, 3, 4, 80, 128), BF16),
            pltpu.VMEM((3, 4, 80, 128), BF16),
            pltpu.VMEM((3, 3, 80, 128), BF16),
            ring_land,
            pltpu.VMEM((3, 4, 80, 128), BF16),
            pltpu.VMEM((4, 80, 128), BF16),
            pltpu.VMEM((3, 80, 128), BF16),
            ring_land,
            pltpu.VMEM((3, 4, 80, 128), BF16),
            pltpu.VMEM((4, 80, 128), BF16),
            pltpu.VMEM((3, 80, 128), BF16),
            pltpu.VMEM((4, 4, 8, 128), F32),
            pltpu.VMEM((3, 4, 8, 128), F32),
            pltpu.VMEM((4, 8, 128), F32),
            pltpu.VMEM((3, 8, 128), F32),
            pltpu.VMEM((8, 96, 128), F32),
            pltpu.VMEM((8, 8, 16, 128), F32),
            pltpu.VMEM((8, 8, 16, 128), F32),
            pltpu.VMEM((160, hidden), BF16),
            pltpu.VMEM((6, 112, width), BF16),
            pltpu.VMEM((4, 112, width), BF16),
            pltpu.VMEM((112, width), BF16),
        ]
        + exchange_semaphores()
        + exchange_semaphores()
        + [
            pltpu.SemaphoreType.DMA((SCATTER_REMOTES + 26,)),
            pltpu.SemaphoreType.DMA((SCATTER_REMOTES + 26,)),
            pltpu.SemaphoreType.DMA((SCATTER_LOCALS + 4,)),
            pltpu.SemaphoreType.DMA((GRAD_REMOTES,)),
            pltpu.SemaphoreType.DMA((GRAD_REMOTES,)),
            pltpu.SemaphoreType.DMA((4,)),
            pltpu.SemaphoreType.DMA,
            pltpu.SemaphoreType.DMA((2, 3)),
        ],
        compiler_params=params(collective_id),
        cost_estimate=cost(10**9, 10**8),
    )(
        d_mixed, heads, length, cos, sin, parts, up, up_one, gate, first, d_attn, normed_one, mixed,
        tokens, gain, d_hidden, ffn_term, w_query, w_key, w_value, down,
    )


def gated(gate, up):
    squash = 1.0 / (1.0 + jnp.exp(-gate))
    silu = gate * squash
    slope = squash * (1.0 + gate * (1.0 - squash))
    return silu, slope


SLOTS = 48
DEPTH = 4
SLOT_ROWS = 16 * SLOTS


def slot_lines(meta):
    member = jnp.where(meta[...].reshape(32, 128) > 0, 1.0, 0.0)
    before = lax.broadcasted_iota(jnp.int32, (128, 128), 0) < lax.broadcasted_iota(jnp.int32, (128, 128), 1)
    count = dot(member.astype(BF16), jnp.where(before, 1.0, 0.0).astype(BF16))
    return jnp.where(member > 0, count, -1.0)


def experts_kernel(
    meta, weight, rows, cots, gate_w, up_w, down_w, early, out, d_rows, kept_act, kept_back, down_sum, first_sum,
    gate_up, down, slot_rows, slot_cots, slot_out, slot_back, lines, columns, act, back,
    out_buf, term, land, z_land, z_work, in_sem, out_sem, weight_sem, keep_sem, send, recv, own,
):
    hidden = down.shape[1]
    x, y, z, core = place()
    x_peers = [device((x + 1) % 4, y, z, core), device((x + 3) % 4, y, z, core)]

    def load(expert):
        return [
            pltpu.make_async_copy(gate_w.at[expert], gate_up.at[expert, :, 0:hidden], weight_sem.at[expert, 0]),
            pltpu.make_async_copy(up_w.at[expert], gate_up.at[expert, :, hidden : 2 * hidden], weight_sem.at[expert, 1]),
            pltpu.make_async_copy(down_w.at[expert], down.at[expert], weight_sem.at[expert, 2]),
        ]

    def fetch(expert):
        return [
            pltpu.make_async_copy(rows.at[expert], slot_rows.at[expert], in_sem.at[expert, 0]),
            pltpu.make_async_copy(cots.at[expert], slot_cots.at[expert], in_sem.at[expert, 1]),
        ]

    for copy in fetch(0) + load(0):
        copy.start()
    z_peers = [device(x, y, (z + 1) % 4, core), device(x, y, (z + 3) % 4, core)]
    greet(x_peers + z_peers)
    copies = Copies(send, recv, own)

    def panel_add(out, *terms):
        add_into(out, (), *terms, rows=(80, 8))

    dense = [
        RingSum(
            copies, z, z_peers[0], z_peers[1],
            lambda chunk, half, panel=panel: early.at[
                2 * chunk + panel if panel < 2 else 8 + chunk, 640 * half : 640 * half + 640
            ],
            z_land.at[panel], z_work.at[panel], panel_add,
        )
        for panel in range(3)
    ]
    for panel in dense:
        panel.raw()
    lines[...] = slot_lines(meta).reshape(16, 2, 128)
    columns[...] = jnp.concatenate([lines[...].reshape(32, 128), jnp.zeros((96, 128), F32)], axis=0).T
    def keep(expert):
        return [
            pltpu.make_async_copy(act.at[expert], kept_act.at[expert], keep_sem.at[expert, 0]),
            pltpu.make_async_copy(back.at[expert], kept_back.at[expert], keep_sem.at[expert, 1]),
        ]

    def main(expert):
        for copy in fetch(expert) + load(expert):
            copy.wait()
        if expert == 0:
            for copy in fetch(1) + load(1):
                copy.start()

        tile = 256

        @pl.loop(0, SLOT_ROWS // tile)
        def _(index):
            at = pl.ds(pl.multiple_of(index * tile, tile), tile)
            both = dot(slot_rows[expert, at], gate_up[expert])
            gate, up = both[:, :hidden], both[:, hidden:]
            silu, slope = gated(gate, up)
            activated = (silu * up).astype(BF16)
            act[expert, at] = activated
            produced = dot(activated, down[expert]).astype(BF16).astype(F32)
            slot_out[expert, at] = (produced * weight[expert, at][:, 0:1]).astype(BF16)
            d_act = dot_nt(slot_cots[expert, at], down[expert])
            back[expert, at, 0:hidden] = (d_act * up * slope).astype(BF16)
            back[expert, at, hidden : 2 * hidden] = (d_act * silu).astype(BF16)
            slot_back[expert, at] = dot_nt(back[expert, at], gate_up[expert]).astype(BF16)

    main(0)
    for copy in keep(0):
        copy.start()

    @pl.loop(0, hidden // 128)
    def _(index):
        at = pl.ds(pl.multiple_of(index * 128, 128), 128)
        term[at] = dot_tn(act[0, :, at], slot_cots[0]).astype(BF16)

    def part(chunk, half):
        return term.at[pl.ds(pl.multiple_of(chunk * 224 + half * 112, 112), 112)]

    def add(out, *terms):
        add_into(out, (), *terms, rows=(16, 7))

    ring = RingSum(copies, x, x_peers[0], x_peers[1], part, land, None, add, resident=True)
    ring.raw()
    for panel in dense:
        panel.forward()
    main(1)
    ring.forward()
    for copy in keep(1):
        copy.start()

    def store(block):
        slot = block % DEPTH
        return [
            pltpu.make_async_copy(out_buf.at[slot, 0], out.at[block], out_sem.at[slot, 0]),
            pltpu.make_async_copy(out_buf.at[slot, 1], d_rows.at[block], out_sem.at[slot, 1]),
        ]

    lane = lax.broadcasted_iota(jnp.int32, (128, 2 * SLOTS), 1).astype(F32)
    for block in range(16):
        slot = block % DEPTH
        first, second = columns[:, 2 * block : 2 * block + 1], columns[:, 2 * block + 1 : 2 * block + 2]
        hit = ((lane < SLOTS) & (lane == first)) | ((lane >= SLOTS) & (lane - SLOTS == second))
        both = jnp.where(hit, 1.0, 0.0).astype(BF16)
        if block >= DEPTH:
            for copy in store(block - DEPTH):
                copy.wait()
        at = slice(block * SLOTS, (block + 1) * SLOTS)
        for index, source in enumerate((slot_out, slot_back)):
            value = jnp.concatenate([source[0, at], source[1, at]], axis=0)
            out_buf[slot, index] = dot(both, value).astype(BF16)
        for copy in store(block):
            copy.start()
    for block in range(16 - DEPTH, 16):
        for copy in store(block):
            copy.wait()
    for panel in range(3):
        dense[panel].finish([first_sum.at[panel, 0:640], first_sum.at[panel, 640:1280]])
    ring.finish([down_sum.at[0:112], down_sum.at[112:224]])
    copies.drain()
    for copy in keep(0) + keep(1):
        copy.wait()


def experts(meta, weight, rows, cots, gate_w, up_w, down_w, early, collective_id):
    width, hidden = gate_w.shape[1:]
    return pl.pallas_call(
        experts_kernel,
        name="experts",
        out_shape=(
            jax.ShapeDtypeStruct((16, 128, width), BF16),
            jax.ShapeDtypeStruct((16, 128, width), BF16),
            jax.ShapeDtypeStruct((2, SLOT_ROWS, hidden), BF16),
            jax.ShapeDtypeStruct((2, SLOT_ROWS, 2 * hidden), BF16),
            jax.ShapeDtypeStruct((hidden // 4, width), BF16),
            jax.ShapeDtypeStruct((3, width, 128), BF16),
        ),
        in_specs=[VMEM, VMEM] + [ANYWHERE] * 6,
        out_specs=[ANYWHERE] * 4 + [VMEM, VMEM],
        scratch_shapes=[
            pltpu.VMEM((2, width, 2 * hidden), BF16),
            pltpu.VMEM((2, hidden, width), BF16),
            pltpu.VMEM((2, SLOT_ROWS, width), BF16),
            pltpu.VMEM((2, SLOT_ROWS, width), BF16),
            pltpu.VMEM((2, SLOT_ROWS, width), BF16),
            pltpu.VMEM((2, SLOT_ROWS, width), BF16),
            pltpu.VMEM((16, 2, 128), F32),
            pltpu.VMEM((128, 128), F32),
            pltpu.VMEM((2, SLOT_ROWS, hidden), BF16),
            pltpu.VMEM((2, SLOT_ROWS, 2 * hidden), BF16),
            pltpu.VMEM((DEPTH, 2, 128, width), BF16),
            pltpu.VMEM((hidden, width), BF16),
            pltpu.VMEM((6, hidden // 8, width), BF16),
            pltpu.VMEM((3, 6, width // 2, 128), BF16),
            pltpu.VMEM((3, 4, width // 2, 128), BF16),
            pltpu.SemaphoreType.DMA((2, 2)),
            pltpu.SemaphoreType.DMA((DEPTH, 2)),
            pltpu.SemaphoreType.DMA((2, 3)),
            pltpu.SemaphoreType.DMA((2, 2)),
            pltpu.SemaphoreType.DMA((24,)),
            pltpu.SemaphoreType.DMA((24,)),
            pltpu.SemaphoreType.DMA((12,)),
        ],
        compiler_params=params(collective_id),
        cost_estimate=cost(12 * 2 * SLOT_ROWS * width * hidden, 6 * 10**7),
    )(meta, weight, rows, cots, gate_w, up_w, down_w, early)


def finish_kernel(
    packed, hidden, shared_out, routed, gate, up_zero, up_one, down_zero, down_one, grad,
    block_out, input_grad, attn_gain, query, key, value, out, ffn_gain, s_gate, s_up, s_down, gate_grad, up_grad, down_grad,
):
    input_grad[...] = grad[...]
    gate_grad[...] = gate[...]
    up_grad[0] = up_zero[...]
    up_grad[1] = up_one[...]
    down_grad[0] = down_zero[...]
    down_grad[1] = down_one[...]
    block_out[...] = hidden[...] + shared_out[...] + routed[...]
    gains = packed[0, 0, 10:11]
    for source in range(1, 8):
        gains = gains + packed[source, 0, 10:11]
    attn_gain[...] = gains[:, 0:10]
    ffn_gain[...] = gains[:, 10:20]
    for core in range(2):
        for panel in range(20):
            if panel < 15:
                part = packed[2 * (panel // 4) + core, 4 + panel % 4, 0:10]
                at = core * 1920 + panel * 128
                (query, key, value)[at // 1280][:, at % 1280 : at % 1280 + 128] = part
            else:
                part = packed[2 * (panel - 15) + core, 3, 0:10] if panel < 19 else packed[6 + core, 7, 0:10]
                at = core * 640 + (panel - 15) * 128
                out[:, at : at + 128] = part
        for panel in range(12):
            where = (panel // 2, panel % 2) if panel < 8 else (panel - 8, 2)
            part = packed[2 * where[0] + core, where[1], 0:10]
            if panel < 7:
                (s_gate, s_up)[core][:, panel * 128 : panel * 128 + 128] = part
            else:
                at = core * 640 + (panel - 7) * 128
                s_down[:, at : at + 128] = part[0:7]


def finish(packed, *values):
    def shape(*dims):
        return jax.ShapeDtypeStruct(dims, F32)

    return pl.pallas_call(
        finish_kernel,
        name="finish",
        out_shape=(
            shape(128, 1280), shape(128, 1280), shape(1, 10),
            shape(10, 1280), shape(10, 1280), shape(10, 1280), shape(10, 1280), shape(1, 10),
            shape(10, 896), shape(10, 896), shape(7, 1280),
            shape(2, 160, 896), shape(2, 160, 896), shape(2, 112, 1280),
        ),
        in_specs=[VMEM] * 10,
        out_specs=(VMEM,) * 14,
        compiler_params=params(),
        cost_estimate=cost(10**7, 12 * 10**6),
    )(packed, *values)


def local(
    tokens,
    lengths,
    routes,
    route_gates,
    attn_gain,
    w_query,
    w_key,
    w_value,
    w_out,
    ffn_gain,
    shared_gate,
    shared_up,
    shared_down,
    expert_gate,
    expert_up,
    expert_down,
    cotangent,
):
    resident, cot = tokens[0], cotangent[0]
    rows = resident.shape[0]
    all_cos, all_sin = turn_tables(8 * rows)
    back_sin = jnp.asarray(-all_sin)
    all_cos, all_sin = jnp.asarray(all_cos), jnp.asarray(all_sin)
    normed_one, mixed, heads, hidden, slot_rows, slot_cots, meta, weight, shared_out, d_shared, early = attend(
        lengths, cot, routes.transpose(2, 0, 1), route_gates.transpose(2, 0, 1), w_query, w_key, w_value, w_out, resident,
        attn_gain, ffn_gain, all_cos, all_sin, shared_gate, shared_up, shared_down, 1,
    )
    parts, d_parts, kept_act, kept_back, down_one, first = experts(
        meta, weight, slot_rows, slot_cots, expert_gate, expert_up, expert_down, early, 5
    )
    first = first.reshape(3, 4, 4, 80, 128)
    gate_sum, up_term, up_one, down_term, down_zero, d_mixed, d_hidden, d_attn, ffn_term = scatter_rows(
        d_parts, slot_rows, slot_cots, kept_act, kept_back, d_shared, hidden, ffn_gain, cot, w_out, down_one, 3
    )
    grad, routed, up_last, gate_grad, packed, up_first, down_last = attend_back(
        d_mixed, heads, lengths, all_cos, back_sin, parts, up_term, up_one, gate_sum, first, d_attn, normed_one,
        mixed, resident, attn_gain, d_hidden, ffn_term, w_query, w_key, w_value, down_term, 4,
    )
    outs = finish(
        packed, hidden, shared_out, routed, gate_grad, up_first, up_last, down_zero, down_last, grad
    )
    return (outs[0][None], outs[1][None], outs[2][0], *outs[3:7], outs[7][0], *outs[8:])


def solution(mesh):
    in_specs = (
        P("exp", "ctx", None),
        P("exp"),
        P("exp", "ctx", None),
        P("exp", "ctx", None),
        P(),
        P(),
        P(),
        P(),
        P(),
        P(),
        P(),
        P(),
        P(),
        P("exp", None, None),
        P("exp", None, None),
        P("exp", None, None),
        P("exp", "ctx", None),
    )
    out_specs = (
        P("exp", "ctx", None),
        P("exp", "ctx", None),
        P(("ctx", "exp")),
        P(("ctx", "exp"), None),
        P(("ctx", "exp"), None),
        P(("ctx", "exp"), None),
        P(("ctx", "exp"), None),
        P(("ctx", "exp")),
        P(("ctx", "exp"), None),
        P(("ctx", "exp"), None),
        P(("ctx", "exp"), None),
        P("exp", "ctx", None),
        P("exp", "ctx", None),
        P("exp", "ctx", None),
    )
    return jax.shard_map(local, mesh=mesh, in_specs=in_specs, out_specs=out_specs, check_vma=False)
```
